32 devices in a mesh: grp: 2 (over core), row: 16 (over z, y, x), col: 1.
Axes of the slice: x: 2, y: 2, z: 4, core: 2. Of those that a mesh axis runs over, the one named last changes fastest.
Arguments:
- pair_rep: bfloat16 [256, 128, 128], P(('grp', 'row'), 'col'), parts along dimension 0, may hold values from -6 to 6
- w_left: bfloat16 [128, 128], replicated, may hold values from -0.5 to 0.5
- w_left_gate: bfloat16 [128, 128], replicated, may hold values from -0.5 to 0.5
- w_right: bfloat16 [128, 128], replicated, may hold values from -0.5 to 0.5
- w_right_gate: bfloat16 [128, 128], replicated, may hold values from -0.5 to 0.5
- w_tri_gate: bfloat16 [128, 128], replicated, may hold values from -0.5 to 0.5
- w_tri_out: bfloat16 [128, 128], replicated, may hold values from -0.5 to 0.5
- w_query: bfloat16 [128, 128], replicated, may hold values from -1 to 1
- w_key: bfloat16 [128, 128], replicated, may hold values from -1 to 1
- w_value: bfloat16 [128, 128], replicated, may hold values from -0.5 to 0.5
- w_bias: bfloat16 [128, 4], replicated, may hold values from -54 to 54
- w_att_gate: bfloat16 [128, 128], replicated, may hold values from -0.5 to 0.5
- w_att_out: bfloat16 [128, 128], replicated, may hold values from -0.5 to 0.5
Outputs:
- updated_pair: bfloat16 [256, 128, 128], P(('grp', 'row'), 'col'), parts along dimension 0
The draws below stay inside these ranges and needn't reach their ends.
There are 2 independent parts, one for each index of `grp`. The reference program is written for one: setup_inputs(seed, part) draws one part's arguments, and reference() takes and returns one part's arrays. A program takes and returns all parts, laid end to end along the dimension named above; an argument that names none is the same for every part. Nothing has to cross between parts.
All inputs are finite; a program needn't handle non-finite values.
Results may differ from the reference program's by a relative error of at most 0.023.
The reference program's roundings to bfloat16 on the way (of `normed`, `left_act`, `triangle`, `tri_norm`, `att_norm`, `queries`, `weights` and `gated`) count: a program that leaves them out, or rounds other values in their place, can miss the bound.
Values may be sent and summed in bfloat16 or wider, within the bound.
No kernel may reach another device: no remote copies, remote signals or barrier semaphores. Data moves between devices by JAX's collectives and lax.ppermute only.
A program may use at most 64 MiB of HBM per device.

```python
import math
import jax
import jax.numpy as jnp
from jax import lax

PAIR_C = 128
TRI_C = 128
HEADS = 4
HEAD_DIM = 32
RESIDUES = 128


def draw_w_bias(key, part):
    key = jax.random.fold_in(key, 7)
    values = jnp.clip(jax.random.normal(key, (PAIR_C, HEADS), jnp.float32), -5.0, 5.0)
    return (values * 1.5 / math.sqrt(PAIR_C)).astype(jnp.bfloat16)


def block_scale(key, dims, cuts, smallest, top_value):
    def one(position, shards_of):
        heights = jax.random.uniform(jax.random.fold_in(jax.random.fold_in(key, 6), position), (shards_of,), jnp.float32, smallest / len(cuts), top_value / len(cuts))
        return jnp.repeat(jnp.exp(heights), dims[position] // shards_of).reshape((-1,) + (1,) * (len(dims) - position - 1))

    loudness = one(*cuts[0])
    for cut in cuts[1:]:
        loudness = loudness * one(*cut)
    return loudness


def scatter_about(rng, extent, deviation, reach, shards=(), held_as=jnp.bfloat16):
    level = block_scale(rng, extent, shards, -0.22, 0.18) if shards else 1.0
    entries = jax.random.normal(rng, extent, jnp.float32) * deviation * level
    return jnp.minimum(jnp.maximum(entries, -reach), reach).astype(held_as)


def setup_inputs(seed: int = 0, part: int = 0) -> dict:
    splits = jax.random.split(jax.random.key(seed), 14)
    part_keys = jax.random.split(jax.random.fold_in(splits[13], part), 14)
    pair_rep = scatter_about(part_keys[0], (RESIDUES, RESIDUES, PAIR_C), 1.0, 6.0, ((0, 16),))
    w_left = scatter_about(splits[1], (PAIR_C, TRI_C), PAIR_C ** -0.5, 0.5)
    w_left_gate = scatter_about(splits[2], (PAIR_C, TRI_C), PAIR_C ** -0.5, 0.5)
    w_right = scatter_about(splits[3], (PAIR_C, TRI_C), PAIR_C ** -0.5, 0.5)
    w_right_gate = scatter_about(splits[4], (PAIR_C, TRI_C), PAIR_C ** -0.5, 0.5)
    w_tri_gate = scatter_about(splits[5], (PAIR_C, PAIR_C), PAIR_C ** -0.5, 0.5)
    w_tri_out = scatter_about(splits[6], (TRI_C, PAIR_C), TRI_C ** -0.5, 0.5)
    w_query = scatter_about(splits[7], (PAIR_C, HEADS * HEAD_DIM), (PAIR_C // 3) ** -0.5, 1.0)
    w_key = scatter_about(splits[8], (PAIR_C, HEADS * HEAD_DIM), (PAIR_C // 3) ** -0.5, 1.0)
    w_value = scatter_about(splits[9], (PAIR_C, HEADS * HEAD_DIM), PAIR_C ** -0.5, 0.5)
    w_bias = draw_w_bias(jax.random.fold_in(splits[13], 71), part)
    w_att_gate = scatter_about(splits[11], (PAIR_C, HEADS * HEAD_DIM), PAIR_C ** -0.5, 0.5)
    w_att_out = scatter_about(splits[12], (HEADS * HEAD_DIM, PAIR_C), (HEADS * HEAD_DIM) ** -0.5, 0.5)
    return dict(pair_rep=pair_rep, w_left=w_left, w_left_gate=w_left_gate, w_right=w_right, w_right_gate=w_right_gate, w_tri_gate=w_tri_gate, w_tri_out=w_tri_out, w_query=w_query, w_key=w_key, w_value=w_value, w_bias=w_bias, w_att_gate=w_att_gate, w_att_out=w_att_out)


def layer_norm(values, reduce_axes):
    average = lax.optimization_barrier(jnp.mean(values, axis=reduce_axes, keepdims=True))
    centered = values - average
    variance = lax.optimization_barrier(jnp.mean(centered * centered, axis=reduce_axes, keepdims=True))
    return centered * lax.rsqrt(variance + 1e-05)

def project(source, weight):
    return jnp.dot(source, weight, preferred_element_type=jnp.float32)

def reference(pair_rep, w_left, w_left_gate, w_right, w_right_gate, w_tri_gate, w_tri_out, w_query, w_key, w_value, w_bias, w_att_gate, w_att_out):
    normed = layer_norm(pair_rep.astype(jnp.float32), -1).astype(jnp.bfloat16)
    left_act = (jax.nn.sigmoid(project(normed, w_left_gate)) * project(normed, w_left)).astype(jnp.bfloat16)
    right_act = (jax.nn.sigmoid(project(normed, w_right_gate)) * project(normed, w_right)).astype(jnp.bfloat16)
    left_major = jnp.moveaxis(left_act, -1, 0)
    right_major = jnp.moveaxis(right_act, -1, 0)

    def channel_product(pieces):
        return jnp.dot(pieces[0], pieces[1].T, preferred_element_type=jnp.float32).astype(jnp.bfloat16)
    triangle = lax.map(channel_product, (left_major, right_major))
    tri_norm = layer_norm(triangle.astype(jnp.float32), 0).astype(jnp.bfloat16)
    update = jnp.einsum('cij,cd->ijd', tri_norm.astype(jnp.float32), w_tri_out.astype(jnp.float32))
    first_pass = pair_rep.astype(jnp.float32) + jax.nn.sigmoid(project(normed, w_tri_gate)) * update
    att_norm = layer_norm(first_pass, -1).astype(jnp.bfloat16)
    queries = project(att_norm, w_query).astype(jnp.bfloat16)
    key_proj = project(att_norm, w_key).astype(jnp.bfloat16)
    value_proj = project(att_norm, w_value).astype(jnp.bfloat16)
    bias_heads = jnp.moveaxis(project(att_norm, w_bias).astype(jnp.bfloat16), -1, 0).astype(jnp.float32)
    att_gate = jax.nn.sigmoid(project(att_norm, w_att_gate))
    score_scale = 1.0 / HEAD_DIM ** 0.5
    count = queries.shape[1]

    def attend_row(row_items):
        query_row = row_items[0].astype(jnp.float32).reshape(count, HEADS, HEAD_DIM)
        key_row = row_items[1].astype(jnp.float32).reshape(count, HEADS, HEAD_DIM)
        value_row = row_items[2].astype(jnp.float32).reshape(count, HEADS, HEAD_DIM)
        scores = jnp.einsum('jhd,khd->hjk', query_row, key_row) * score_scale + bias_heads
        row_peak = lax.optimization_barrier(jnp.max(scores, axis=-1, keepdims=True))
        shifted = jnp.exp(scores - row_peak)
        row_total = lax.optimization_barrier(jnp.sum(shifted, axis=-1, keepdims=True))
        weights = (shifted / row_total).astype(jnp.bfloat16).astype(jnp.float32)
        return jnp.einsum('hjk,khd->jhd', weights, value_row).reshape(count, HEADS * HEAD_DIM)
    attended = lax.map(attend_row, (queries, key_proj, value_proj))
    gated = (attended * att_gate).astype(jnp.bfloat16)
    return (first_pass + project(gated, w_att_out)).astype(jnp.bfloat16)
```

```python
import jax
import jax.numpy as jnp
from jax import lax
from jax.sharding import PartitionSpec as P

HEADS = 4
HEAD_DIM = 32


def layer_norm(values, reduce_axes):
    average = jnp.mean(values, axis=reduce_axes, keepdims=True)
    centered = values - average
    variance = jnp.mean(centered * centered, axis=reduce_axes, keepdims=True)
    return centered * lax.rsqrt(variance + 1e-05)


def project(source, weight):
    return jnp.dot(source, weight, preferred_element_type=jnp.float32)


def channel_major(source, weight):
    return jnp.einsum("ijc,cm->mij", source, weight, preferred_element_type=jnp.float32)


def body(
    pair_rep,
    w_left,
    w_left_gate,
    w_right,
    w_right_gate,
    w_tri_gate,
    w_tri_out,
    w_query,
    w_key,
    w_value,
    w_bias,
    w_att_gate,
    w_att_out,
):
    col_count = pair_rep.shape[1]
    normed = layer_norm(pair_rep.astype(jnp.float32), -1).astype(jnp.bfloat16)
    left_act = (
        jax.nn.sigmoid(channel_major(normed, w_left_gate)) * channel_major(normed, w_left)
    ).astype(jnp.bfloat16)
    right_act = (
        jax.nn.sigmoid(channel_major(normed, w_right_gate)) * channel_major(normed, w_right)
    ).astype(jnp.bfloat16)
    stacked = jnp.stack((left_act, right_act))
    spread = lax.all_to_all(stacked, "row", split_axis=1, concat_axis=2, tiled=True)
    partial_sums = jnp.einsum(
        "cik,cjk->cij", spread[0], spread[1], preferred_element_type=jnp.float32
    )
    summed = lax.psum_scatter(partial_sums, "col", scatter_dimension=2, tiled=True).astype(
        jnp.bfloat16
    )
    returned = lax.all_to_all(summed, "row", split_axis=1, concat_axis=0, tiled=True)
    tri_norm = layer_norm(returned.astype(jnp.float32), 0).astype(jnp.bfloat16)
    update = jnp.einsum("cij,cd->ijd", tri_norm, w_tri_out, preferred_element_type=jnp.float32)
    first_pass = pair_rep.astype(jnp.float32) + jax.nn.sigmoid(project(normed, w_tri_gate)) * update
    att_norm = layer_norm(first_pass, -1).astype(jnp.bfloat16)
    queries = project(att_norm, w_query).astype(jnp.bfloat16)
    key_proj = project(att_norm, w_key).astype(jnp.bfloat16)
    value_proj = project(att_norm, w_value).astype(jnp.bfloat16)
    att_gate = jax.nn.sigmoid(project(att_norm, w_att_gate))
    bias_local = jnp.einsum(
        "ijc,ch->hij", att_norm, w_bias, preferred_element_type=jnp.float32
    ).astype(jnp.bfloat16)
    row_parts = lax.axis_size("row")
    copies = jnp.broadcast_to(bias_local[None], (row_parts, *bias_local.shape))
    every_row = lax.all_to_all(copies, "row", split_axis=0, concat_axis=2, tiled=True)[0]
    bias_full = lax.all_to_all(every_row, "col", split_axis=1, concat_axis=2, tiled=True).astype(
        jnp.float32
    )
    key_value = lax.all_gather(jnp.stack((key_proj, value_proj)), "col", axis=2, tiled=True)
    total_keys = key_value.shape[2]
    score_scale = 1.0 / HEAD_DIM**0.5

    def attend_row(row_items):
        query_row = row_items[0].reshape(col_count, HEADS, HEAD_DIM)
        key_row = row_items[1].reshape(total_keys, HEADS, HEAD_DIM)
        value_row = row_items[2].reshape(total_keys, HEADS, HEAD_DIM)
        scores = (
            jnp.einsum("jhd,khd->hjk", query_row, key_row, preferred_element_type=jnp.float32)
            * score_scale
            + bias_full
        )
        row_peak = jnp.max(scores, axis=-1, keepdims=True)
        shifted = jnp.exp(scores - row_peak)
        row_total = jnp.sum(shifted, axis=-1, keepdims=True)
        weights = (shifted / row_total).astype(jnp.bfloat16)
        return jnp.einsum(
            "hjk,khd->jhd", weights, value_row, preferred_element_type=jnp.float32
        ).reshape(col_count, HEADS * HEAD_DIM)

    attended = lax.map(attend_row, (queries, key_value[0], key_value[1]))
    gated = (attended * att_gate).astype(jnp.bfloat16)
    return (first_pass + project(gated, w_att_out)).astype(jnp.bfloat16)


def solution(mesh):
    in_specs = (
        P(("grp", "row"), "col", None),
        P(),
        P(),
        P(),
        P(),
        P(),
        P(),
        P(),
        P(),
        P(),
        P(),
        P(),
        P(),
    )
    out_specs = P(("grp", "row"), "col", None)
    return jax.shard_map(body, mesh=mesh, in_specs=in_specs, out_specs=out_specs, check_vma=False)
```

```python
import jax
import jax.numpy as jnp
from jax import lax
from jax.sharding import PartitionSpec as P

HEADS = 4
HEAD_DIM = 32


def layer_norm(values, reduce_axes):
    average = jnp.mean(values, axis=reduce_axes, keepdims=True)
    centered = values - average
    variance = jnp.mean(centered * centered, axis=reduce_axes, keepdims=True)
    return centered * lax.rsqrt(variance + 1e-05)


def project(source, weight):
    return jnp.dot(source, weight, preferred_element_type=jnp.float32)


def channel_major(source, weight):
    return jnp.einsum("ijc,cm->mij", source, weight, preferred_element_type=jnp.float32)


def body(
    pair_rep,
    w_left,
    w_left_gate,
    w_right,
    w_right_gate,
    w_tri_gate,
    w_tri_out,
    w_query,
    w_key,
    w_value,
    w_bias,
    w_att_gate,
    w_att_out,
):
    col_count = pair_rep.shape[1]
    normed = layer_norm(pair_rep.astype(jnp.float32), -1).astype(jnp.bfloat16)
    left_act = (
        jax.nn.sigmoid(channel_major(normed, w_left_gate)) * channel_major(normed, w_left)
    ).astype(jnp.bfloat16)
    right_act = (
        jax.nn.sigmoid(channel_major(normed, w_right_gate)) * channel_major(normed, w_right)
    ).astype(jnp.bfloat16)
    stacked = jnp.stack((left_act, right_act))
    spread = lax.all_to_all(stacked, "row", split_axis=1, concat_axis=2, tiled=True)
    partial_sums = jnp.einsum(
        "cik,cjk->cij", spread[0], spread[1], preferred_element_type=jnp.float32
    )
    summed = lax.psum_scatter(partial_sums, "col", scatter_dimension=2, tiled=True).astype(
        jnp.bfloat16
    )
    returned = lax.all_to_all(summed, "row", split_axis=1, concat_axis=0, tiled=True)
    tri_norm = layer_norm(returned.astype(jnp.float32), 0).astype(jnp.bfloat16)
    update = jnp.einsum("cij,cd->ijd", tri_norm, w_tri_out, preferred_element_type=jnp.float32)
    first_pass = pair_rep.astype(jnp.float32) + jax.nn.sigmoid(project(normed, w_tri_gate)) * update
    att_norm = layer_norm(first_pass, -1).astype(jnp.bfloat16)
    queries = project(att_norm, w_query).astype(jnp.bfloat16)
    key_proj = project(att_norm, w_key).astype(jnp.bfloat16)
    value_proj = project(att_norm, w_value).astype(jnp.bfloat16)
    att_gate = jax.nn.sigmoid(project(att_norm, w_att_gate))
    bias_local = jnp.einsum(
        "ijc,ch->hij", att_norm, w_bias, preferred_element_type=jnp.float32
    ).astype(jnp.bfloat16)
    row_parts = lax.axis_size("row")
    pieces = [bias_local]
    for shift in range(1, row_parts):
        pairs = [(r, (r + row_parts - shift) % row_parts) for r in range(row_parts)]
        pieces.append(lax.ppermute(bias_local, "row", pairs))
    twice = jnp.concatenate(pieces + pieces, axis=1)
    first = (row_parts - lax.axis_index("row")) * bias_local.shape[1]
    every_row = lax.dynamic_slice_in_dim(twice, first, row_parts * bias_local.shape[1], axis=1)
    bias_full = lax.all_to_all(every_row, "col", split_axis=1, concat_axis=2, tiled=True).astype(
        jnp.float32
    )
    key_value = lax.all_gather(jnp.stack((key_proj, value_proj)), "col", axis=2, tiled=True)
    total_keys = key_value.shape[2]
    score_scale = 1.0 / HEAD_DIM**0.5

    def attend_row(row_items):
        query_row = row_items[0].reshape(col_count, HEADS, HEAD_DIM)
        key_row = row_items[1].reshape(total_keys, HEADS, HEAD_DIM)
        value_row = row_items[2].reshape(total_keys, HEADS, HEAD_DIM)
        scores = (
            jnp.einsum("jhd,khd->hjk", query_row, key_row, preferred_element_type=jnp.float32)
            * score_scale
            + bias_full
        )
        row_peak = jnp.max(scores, axis=-1, keepdims=True)
        shifted = jnp.exp(scores - row_peak)
        row_total = jnp.sum(shifted, axis=-1, keepdims=True)
        weights = (shifted / row_total).astype(jnp.bfloat16)
        return jnp.einsum(
            "hjk,khd->jhd", weights, value_row, preferred_element_type=jnp.float32
        ).reshape(col_count, HEADS * HEAD_DIM)

    attended = lax.map(attend_row, (queries, key_value[0], key_value[1]))
    gated = (attended * att_gate).astype(jnp.bfloat16)
    return (first_pass + project(gated, w_att_out)).astype(jnp.bfloat16)


def solution(mesh):
    in_specs = (
        P(("grp", "row"), "col", None),
        P(),
        P(),
        P(),
        P(),
        P(),
        P(),
        P(),
        P(),
        P(),
        P(),
        P(),
        P(),
    )
    out_specs = P(("grp", "row"), "col", None)
    return jax.shard_map(body, mesh=mesh, in_specs=in_specs, out_specs=out_specs, check_vma=False)
```

```python
import functools

import jax
import jax.numpy as jnp
from jax import lax
from jax.experimental import pallas as pl
from jax.experimental.pallas import tpu as pltpu
from jax.sharding import PartitionSpec as P

HEADS = 4
HEAD_DIM = 32
LANES = 128
LOG2_E = 1.4426950408889634
F32 = jnp.float32
BF16 = jnp.bfloat16
NN = (((1,), (0,)), ((), ()))
NT = (((1,), (1,)), ((), ()))
TN = (((0,), (0,)), ((), ()))


def dot(left, right, dims=NN):
    return lax.dot_general(left, right, dims, preferred_element_type=F32)


def sigmoid(values):
    return 0.5 * jnp.tanh(0.5 * values) + 0.5


def flipped(weight):
    return weight.astype(F32).T.astype(BF16)


def lane_tiles(values):
    lanes = values.shape[1]
    return [(t, slice(t * LANES, (t + 1) * LANES)) for t in range(lanes // LANES)]


def lane_norm(values):
    centered = values - jnp.mean(values, axis=-1, keepdims=True)
    variance = jnp.mean(centered * centered, axis=-1, keepdims=True)
    return (centered * lax.rsqrt(variance + 1e-05)).astype(BF16)


def edges_kernel(pair, w_left, w_left_gate, w_right, w_right_gate, out, held):
    rows = pair.shape[0]
    channels = w_left.shape[1]
    weights = jnp.concatenate(
        [flipped(w[...]) for w in (w_left, w_left_gate, w_right, w_right_gate)], axis=0
    )
    for i in range(rows):
        normed = lane_norm(pair[i].astype(F32))
        both = dot(weights, normed, NT)
        for side in range(2):
            base = 2 * side * channels
            act = sigmoid(both[base + channels : base + 2 * channels]) * both[base : base + channels]
            for tile, lanes in lane_tiles(act):
                held[tile, pl.ds(side * rows + i, channels, stride=2 * rows), :] = act[:, lanes]
    block = out.shape[1]
    for owner in range(out.shape[0]):
        for tile, lanes in lane_tiles(pair):
            out[owner, :, lanes] = held[tile, owner * block : (owner + 1) * block, :].astype(BF16)


def gate_kernel(pair, w_tri_gate, out):
    for i in range(pair.shape[0]):
        out[i] = sigmoid(dot(lane_norm(pair[i].astype(F32)), w_tri_gate[...]))


def triangle_sides(edges, rows, channel):
    sides = [[], []]
    for source in range(edges.shape[0]):
        block = edges[source, channel * 2 * rows : (channel + 1) * 2 * rows, :].astype(F32)
        sides[0].append(block[:rows])
        sides[1].append(block[rows:])
    return [jnp.concatenate(side, axis=0).astype(BF16) for side in sides]


def triangle_kernel(rows, edges, out):
    for pair_of in range(0, out.shape[1] // rows, 2):
        products = [dot(*triangle_sides(edges, rows, pair_of + o), NT) for o in range(2)]
        for owner in range(out.shape[0]):
            mine = slice(owner * rows, (owner + 1) * rows)
            out[owner, pair_of * rows : (pair_of + 2) * rows, :] = jnp.concatenate(
                [p[mine] for p in products], axis=0
            ).astype(BF16)


def partial_kernel(rows, edges, out):
    for channel in range(out.shape[0]):
        out[channel] = dot(*triangle_sides(edges, rows, channel), NT)


def update_kernel(returned, gate, pair, w_tri_out, w_bias_t, first_pass, att_norm, bias, held, bias_held):
    rows, cols = pair.shape[0], pair.shape[1]
    owners, block = returned.shape[0], returned.shape[1]
    channels = owners * block // rows
    total = jnp.zeros((rows, cols), F32)
    for owner in range(owners):
        total += jnp.sum(returned[owner].astype(F32).reshape(block // rows, rows, cols), axis=0)
    average = total / channels
    square = jnp.zeros((rows, cols), F32)
    for owner in range(owners):
        centered = returned[owner].astype(F32).reshape(block // rows, rows, cols) - average
        square += jnp.sum(centered * centered, axis=0)
        for tile, lanes in lane_tiles(pair):
            held[tile, owner * block : (owner + 1) * block, :] = centered.reshape(block, cols)[:, lanes]
    scale = lax.rsqrt(square / channels + 1e-05)
    for i in range(rows):
        tri_norm = jnp.concatenate(
            [held[tile, pl.ds(i, channels, stride=rows), :] for tile, _ in lane_tiles(pair)], axis=1
        )
        tri_norm = tri_norm * scale[i : i + 1]
        update = dot(tri_norm.T.astype(BF16), w_tri_out[...])
        passed = pair[i].astype(F32) + gate[i] * update
        first_pass[i] = passed
        normed = lane_norm(passed)
        att_norm[i] = normed
        row_bias = dot(w_bias_t[...], normed, NT)
        for head in range(HEADS):
            bias_held[head * rows + i : head * rows + i + 1, :] = row_bias[head : head + 1]
    rounded = bias_held[...].astype(BF16)
    for owner in range(bias.shape[0]):
        bias[owner] = rounded


def project_kernel(att_norm, w_query, w_key, w_value, w_att_gate, query, key, value_t, gate_t):
    w_direct = jnp.concatenate([w_query[...], w_key[...]], axis=1)
    w_flipped = jnp.concatenate([flipped(w_value[...]), flipped(w_att_gate[...])], axis=0)
    split = query.shape[2]
    for i in range(att_norm.shape[0]):
        normed = att_norm[i]
        direct = dot(normed, w_direct).astype(BF16)
        query[i] = direct[:, :split]
        key[i] = direct[:, split:]
        turned = dot(w_flipped, normed, NT)
        value_t[i] = turned[:split].astype(BF16)
        gate_t[i] = sigmoid(turned[split:])


def attend_kernel(query, key, value_t, gate_t, first_pass, bias, w_att_out, out, bias_t):
    rows, cols, width = query.shape
    head_rows = bias.shape[1] // HEADS
    for head in range(HEADS):
        parts = [
            bias[owner].astype(F32)[head * head_rows : (head + 1) * head_rows]
            for owner in range(bias.shape[0])
        ]
        bias_t[head] = jnp.concatenate(parts, axis=0).T * LOG2_E
    lane = lax.broadcasted_iota(jnp.int32, (1, width), 1)
    score_scale = LOG2_E / HEAD_DIM**0.5
    ones = jnp.ones((16, key.shape[1]), BF16)
    for i in range(rows):
        keys = key[i]
        queries = query[i]
        gated = []
        for head in range(HEADS):
            inside = (lane >= head * HEAD_DIM) & (lane < (head + 1) * HEAD_DIM)
            chosen = jnp.where(inside, queries, jnp.zeros_like(queries))
            scores = dot(keys, chosen, NT) * score_scale + bias_t[head]
            peak = jnp.max(scores, axis=0, keepdims=True)
            weights = jnp.exp2(scores - peak).astype(BF16)
            mine = slice(head * HEAD_DIM, (head + 1) * HEAD_DIM)
            summed = dot(jnp.concatenate([value_t[i, mine, :], ones], axis=0), weights)
            total = summed[HEAD_DIM : HEAD_DIM + 1]
            gated.append(summed[:HEAD_DIM] * (1.0 / total) * gate_t[i, mine, :])
        gated_t = jnp.concatenate(gated, axis=0)
        result = first_pass[i] + dot(gated_t.T.astype(BF16), w_att_out[...])
        out[i] = result.astype(BF16)


def call(kernel, outs, scratch, flops, *operands):
    vmem = pl.BlockSpec(memory_space=pltpu.VMEM)
    shapes = [jax.ShapeDtypeStruct(shape, dtype) for shape, dtype in outs]
    moved = sum(o.size * o.dtype.itemsize for o in operands)
    got = pl.pallas_call(
        kernel,
        out_shape=shapes,
        in_specs=[vmem] * len(operands),
        out_specs=[vmem] * len(shapes),
        scratch_shapes=[pltpu.VMEM(shape, dtype) for shape, dtype in scratch],
        compiler_params=pltpu.CompilerParams(vmem_limit_bytes=48 * 2**20),
        cost_estimate=pl.CostEstimate(flops=flops, bytes_accessed=moved, transcendentals=0),
    )(*operands)
    return got if len(got) > 1 else got[0]


def body(
    pair_rep,
    w_left,
    w_left_gate,
    w_right,
    w_right_gate,
    w_tri_gate,
    w_tri_out,
    w_query,
    w_key,
    w_value,
    w_bias,
    w_att_gate,
    w_att_out,
):
    rows, cols, width = pair_rep.shape
    channels = w_left.shape[1]
    owners, col_parts = lax.axis_size("row"), lax.axis_size("col")
    own = channels // owners
    residues = owners * rows
    cells = rows * cols

    edges = call(
        edges_kernel,
        [((owners, own * 2 * rows, cols), BF16)],
        [((cols // LANES, channels * 2 * rows, LANES), F32)],
        8 * cells * width * channels,
        pair_rep,
        w_left,
        w_left_gate,
        w_right,
        w_right_gate,
    )
    spread = lax.all_to_all(edges, "row", split_axis=0, concat_axis=0, tiled=True)
    gate = call(
        gate_kernel, [((rows, cols, width), F32)], [], 2 * cells * width * width, pair_rep, w_tri_gate
    )
    flops = 2 * own * residues * residues * cols
    if col_parts == 1:
        summed = call(
            functools.partial(triangle_kernel, rows),
            [((owners, own * rows, residues), BF16)],
            [],
            flops,
            spread,
        )
    else:
        partial_sums = call(
            functools.partial(partial_kernel, rows),
            [((own, residues, residues), F32)],
            [],
            flops,
            spread,
        )
        summed = lax.psum_scatter(partial_sums, "col", scatter_dimension=2, tiled=True).astype(BF16)
        summed = summed.reshape(own, owners, rows, cols).swapaxes(0, 1)
        summed = summed.reshape(owners, own * rows, cols)
    returned = lax.all_to_all(summed, "row", split_axis=0, concat_axis=0, tiled=True)
    first_pass, att_norm, bias_copies = call(
        update_kernel,
        [
            ((rows, cols, width), F32),
            ((rows, cols, width), BF16),
            ((owners, HEADS * rows, cols), BF16),
        ],
        [((cols // LANES, channels * rows, LANES), F32), ((HEADS * rows, cols), F32)],
        2 * cells * channels * width,
        returned,
        gate,
        pair_rep,
        w_tri_out,
        w_bias.T,
    )
    bias = lax.all_to_all(bias_copies, "row", split_axis=0, concat_axis=0, tiled=True)
    query, key, value_t, gate_t = call(
        project_kernel,
        [
            ((rows, cols, width), BF16),
            ((rows, cols, width), BF16),
            ((rows, width, cols), BF16),
            ((rows, width, cols), F32),
        ],
        [],
        8 * cells * width * width,
        att_norm,
        w_query,
        w_key,
        w_value,
        w_att_gate,
    )
    if col_parts > 1:
        bias = lax.all_to_all(bias, "col", split_axis=0, concat_axis=2, tiled=True)
        key = lax.all_gather(key, "col", axis=1, tiled=True)
        value_t = lax.all_gather(value_t, "col", axis=2, tiled=True)
    return call(
        attend_kernel,
        [((rows, cols, width), BF16)],
        [((HEADS, key.shape[1], cols), F32)],
        4 * cells * key.shape[1] * width,
        query,
        key,
        value_t,
        gate_t,
        first_pass,
        bias,
        w_att_out,
    )


def solution(mesh):
    in_specs = (P(("grp", "row"), "col", None),) + (P(),) * 12
    out_specs = P(("grp", "row"), "col", None)
    return jax.shard_map(body, mesh=mesh, in_specs=in_specs, out_specs=out_specs, check_vma=False)
```

```python
import functools

import jax
import jax.numpy as jnp
from jax import lax
from jax.experimental import pallas as pl
from jax.experimental.pallas import tpu as pltpu
from jax.sharding import PartitionSpec as P

HEADS = 4
HEAD_DIM = 32
LANES = 128
LOG2_E = 1.4426950408889634
F32 = jnp.float32
BF16 = jnp.bfloat16
NN = (((1,), (0,)), ((), ()))
NT = (((1,), (1,)), ((), ()))
TN = (((0,), (0,)), ((), ()))


def dot(left, right, dims=NN):
    return lax.dot_general(left, right, dims, preferred_element_type=F32)


def sigmoid(values):
    return 0.5 * jnp.tanh(0.5 * values) + 0.5


def flipped(weight):
    return weight.astype(F32).T.astype(BF16)


def lane_tiles(values):
    lanes = values.shape[1]
    return [(t, slice(t * LANES, (t + 1) * LANES)) for t in range(lanes // LANES)]


def lane_norm(values):
    centered = values - jnp.mean(values, axis=-1, keepdims=True)
    variance = jnp.mean(centered * centered, axis=-1, keepdims=True)
    return (centered * lax.rsqrt(variance + 1e-05)).astype(BF16)


def edges_kernel(pair, w_left, w_left_gate, w_right, w_right_gate, out, held):
    rows = pair.shape[0]
    channels = w_left.shape[1]
    weights = jnp.concatenate(
        [flipped(w[...]) for w in (w_left, w_left_gate, w_right, w_right_gate)], axis=0
    )
    for i in range(rows):
        normed = lane_norm(pair[i].astype(F32))
        both = dot(weights, normed, NT)
        for side in range(2):
            base = 2 * side * channels
            act = sigmoid(both[base + channels : base + 2 * channels]) * both[base : base + channels]
            for tile, lanes in lane_tiles(act):
                held[tile, pl.ds(side * rows + i, channels, stride=2 * rows), :] = act[:, lanes]
    block = out.shape[1]
    for owner in range(out.shape[0]):
        for tile, lanes in lane_tiles(pair):
            out[owner, :, lanes] = held[tile, owner * block : (owner + 1) * block, :].astype(BF16)


def gate_kernel(pair, w_tri_gate, out):
    for i in range(pair.shape[0]):
        out[i] = sigmoid(dot(lane_norm(pair[i].astype(F32)), w_tri_gate[...]))


def triangle_sides(edges, rows, channel):
    sides = [[], []]
    for source in range(edges.shape[0]):
        block = edges[source, channel * 2 * rows : (channel + 1) * 2 * rows, :].astype(F32)
        sides[0].append(block[:rows])
        sides[1].append(block[rows:])
    return [jnp.concatenate(side, axis=0).astype(BF16) for side in sides]


def triangle_kernel(rows, edges, out):
    for pair_of in range(0, out.shape[1] // rows, 2):
        products = [dot(*triangle_sides(edges, rows, pair_of + o), NT) for o in range(2)]
        for owner in range(out.shape[0]):
            mine = slice(owner * rows, (owner + 1) * rows)
            out[owner, pair_of * rows : (pair_of + 2) * rows, :] = jnp.concatenate(
                [p[mine] for p in products], axis=0
            ).astype(BF16)


def partial_kernel(rows, edges, out):
    for channel in range(out.shape[0]):
        out[channel] = dot(*triangle_sides(edges, rows, channel), NT)


def update_kernel(returned, gate, pair, w_tri_out, w_bias_t, first_pass, att_norm, bias, held, bias_held):
    rows, cols = pair.shape[0], pair.shape[1]
    owners, block = returned.shape[0], returned.shape[1]
    channels = owners * block // rows
    total = jnp.zeros((rows, cols), F32)
    for owner in range(owners):
        total += jnp.sum(returned[owner].astype(F32).reshape(block // rows, rows, cols), axis=0)
    average = total / channels
    square = jnp.zeros((rows, cols), F32)
    for owner in range(owners):
        centered = returned[owner].astype(F32).reshape(block // rows, rows, cols) - average
        square += jnp.sum(centered * centered, axis=0)
        for tile, lanes in lane_tiles(pair):
            held[tile, owner * block : (owner + 1) * block, :] = centered.reshape(block, cols)[:, lanes]
    scale = lax.rsqrt(square / channels + 1e-05)
    for i in range(rows):
        tri_norm = jnp.concatenate(
            [held[tile, pl.ds(i, channels, stride=rows), :] for tile, _ in lane_tiles(pair)], axis=1
        )
        tri_norm = tri_norm * scale[i : i + 1]
        update = dot(tri_norm.T.astype(BF16), w_tri_out[...])
        passed = pair[i].astype(F32) + gate[i] * update
        first_pass[i] = passed
        normed = lane_norm(passed)
        att_norm[i] = normed
        row_bias = dot(w_bias_t[...], normed, NT)
        for head in range(HEADS):
            bias_held[head * rows + i : head * rows + i + 1, :] = row_bias[head : head + 1]
    rounded = bias_held[...].astype(BF16)
    for owner in range(bias.shape[0]):
        bias[owner] = rounded


def project_kernel(att_norm, w_query, w_key, w_value, w_att_gate, query, key, value_t, gate_t):
    w_direct = jnp.concatenate([w_query[...], w_key[...]], axis=1)
    w_flipped = jnp.concatenate([flipped(w_value[...]), flipped(w_att_gate[...])], axis=0)
    split = query.shape[2]
    for i in range(att_norm.shape[0]):
        normed = att_norm[i]
        direct = dot(normed, w_direct).astype(BF16)
        query[i] = direct[:, :split]
        key[i] = direct[:, split:]
        turned = dot(w_flipped, normed, NT)
        value_t[i] = turned[:split].astype(BF16)
        gate_t[i] = sigmoid(turned[split:])


def attend_kernel(query, key, value_t, gate_t, first_pass, bias, w_att_out, out, bias_t):
    rows, cols, width = query.shape
    head_rows = bias.shape[1] // HEADS
    for head in range(HEADS):
        parts = [
            bias[owner].astype(F32)[head * head_rows : (head + 1) * head_rows]
            for owner in range(bias.shape[0])
        ]
        bias_t[head] = jnp.concatenate(parts, axis=0).T * LOG2_E
    lane = lax.broadcasted_iota(jnp.int32, (1, width), 1)
    score_scale = LOG2_E / HEAD_DIM**0.5
    ones = jnp.ones((16, key.shape[1]), BF16)
    for i in range(rows):
        keys = key[i]
        queries = query[i]
        gated = []
        for head in range(HEADS):
            inside = (lane >= head * HEAD_DIM) & (lane < (head + 1) * HEAD_DIM)
            chosen = jnp.where(inside, queries, jnp.zeros_like(queries))
            scores = dot(keys, chosen, NT) * score_scale + bias_t[head]
            peak = jnp.max(scores, axis=0, keepdims=True)
            weights = jnp.exp2(scores - peak).astype(BF16)
            mine = slice(head * HEAD_DIM, (head + 1) * HEAD_DIM)
            summed = dot(jnp.concatenate([value_t[i, mine, :], ones], axis=0), weights)
            total = summed[HEAD_DIM : HEAD_DIM + 1]
            gated.append(summed[:HEAD_DIM] * (1.0 / total) * gate_t[i, mine, :])
        gated_t = jnp.concatenate(gated, axis=0)
        result = first_pass[i] + dot(gated_t.T.astype(BF16), w_att_out[...])
        out[i] = result.astype(BF16)


def call(kernel, outs, scratch, flops, *operands):
    vmem = pl.BlockSpec(memory_space=pltpu.VMEM)
    shapes = [jax.ShapeDtypeStruct(shape, dtype) for shape, dtype in outs]
    moved = sum(o.size * o.dtype.itemsize for o in operands)
    got = pl.pallas_call(
        kernel,
        out_shape=shapes,
        in_specs=[vmem] * len(operands),
        out_specs=[vmem] * len(shapes),
        scratch_shapes=[pltpu.VMEM(shape, dtype) for shape, dtype in scratch],
        compiler_params=pltpu.CompilerParams(vmem_limit_bytes=48 * 2**20),
        cost_estimate=pl.CostEstimate(flops=flops, bytes_accessed=moved, transcendentals=0),
    )(*operands)
    return got if len(got) > 1 else got[0]


def stages(owners):
    near = 1 << (owners.bit_length() // 2)
    far = owners // near
    lines = [[f * near + c for f in range(far)] for c in range(near)]
    planes = [[f * near + c for c in range(near)] for f in range(far)]
    return far, near, lines, planes


def swap(blocks, groups, axis):
    return lax.all_to_all(
        blocks, "row", split_axis=axis, concat_axis=axis, axis_index_groups=groups, tiled=True
    )


def exchange(blocks):
    far, near, lines, planes = stages(blocks.shape[0])
    split = blocks.reshape(far, near, *blocks.shape[1:])
    return swap(swap(split, lines, 0), planes, 1).reshape(blocks.shape)


def gather(copies, owners):
    far, near, lines, planes = stages(owners)
    plane = swap(copies, planes, 0)
    plane = jnp.broadcast_to(plane[None], (far, *plane.shape))
    return swap(plane, lines, 0).reshape(owners, *copies.shape[1:])


def body(
    pair_rep,
    w_left,
    w_left_gate,
    w_right,
    w_right_gate,
    w_tri_gate,
    w_tri_out,
    w_query,
    w_key,
    w_value,
    w_bias,
    w_att_gate,
    w_att_out,
):
    rows, cols, width = pair_rep.shape
    channels = w_left.shape[1]
    owners, col_parts = lax.axis_size("row"), lax.axis_size("col")
    own = channels // owners
    residues = owners * rows
    cells = rows * cols

    edges = call(
        edges_kernel,
        [((owners, own * 2 * rows, cols), BF16)],
        [((cols // LANES, channels * 2 * rows, LANES), F32)],
        8 * cells * width * channels,
        pair_rep,
        w_left,
        w_left_gate,
        w_right,
        w_right_gate,
    )
    spread = exchange(edges)
    gate = call(
        gate_kernel, [((rows, cols, width), F32)], [], 2 * cells * width * width, pair_rep, w_tri_gate
    )
    flops = 2 * own * residues * residues * cols
    if col_parts == 1:
        summed = call(
            functools.partial(triangle_kernel, rows),
            [((owners, own * rows, residues), BF16)],
            [],
            flops,
            spread,
        )
    else:
        partial_sums = call(
            functools.partial(partial_kernel, rows),
            [((own, residues, residues), F32)],
            [],
            flops,
            spread,
        )
        summed = lax.psum_scatter(partial_sums, "col", scatter_dimension=2, tiled=True).astype(BF16)
        summed = summed.reshape(own, owners, rows, cols).swapaxes(0, 1)
        summed = summed.reshape(owners, own * rows, cols)
    returned = exchange(summed)
    first_pass, att_norm, bias_copies = call(
        update_kernel,
        [
            ((rows, cols, width), F32),
            ((rows, cols, width), BF16),
            ((stages(owners)[1], HEADS * rows, cols), BF16),
        ],
        [((cols // LANES, channels * rows, LANES), F32), ((HEADS * rows, cols), F32)],
        2 * cells * channels * width,
        returned,
        gate,
        pair_rep,
        w_tri_out,
        w_bias.T,
    )
    bias = gather(bias_copies, owners)
    query, key, value_t, gate_t = call(
        project_kernel,
        [
            ((rows, cols, width), BF16),
            ((rows, cols, width), BF16),
            ((rows, width, cols), BF16),
            ((rows, width, cols), F32),
        ],
        [],
        8 * cells * width * width,
        att_norm,
        w_query,
        w_key,
        w_value,
        w_att_gate,
    )
    if col_parts > 1:
        bias = lax.all_to_all(bias, "col", split_axis=0, concat_axis=2, tiled=True)
        key = lax.all_gather(key, "col", axis=1, tiled=True)
        value_t = lax.all_gather(value_t, "col", axis=2, tiled=True)
    return call(
        attend_kernel,
        [((rows, cols, width), BF16)],
        [((HEADS, key.shape[1], cols), F32)],
        4 * cells * key.shape[1] * width,
        query,
        key,
        value_t,
        gate_t,
        first_pass,
        bias,
        w_att_out,
    )


def solution(mesh):
    in_specs = (P(("grp", "row"), "col", None),) + (P(),) * 12
    out_specs = P(("grp", "row"), "col", None)
    return jax.shard_map(body, mesh=mesh, in_specs=in_specs, out_specs=out_specs, check_vma=False)
```

```python
import functools

import jax
import jax.numpy as jnp
from jax import lax
from jax.experimental import pallas as pl
from jax.experimental.pallas import tpu as pltpu
from jax.sharding import PartitionSpec as P

HEADS = 4
HEAD_DIM = 32
LANES = 128
LOG2_E = 1.4426950408889634
F32 = jnp.float32
BF16 = jnp.bfloat16
NN = (((1,), (0,)), ((), ()))
NT = (((1,), (1,)), ((), ()))
TN = (((0,), (0,)), ((), ()))


def dot(left, right, dims=NN):
    return lax.dot_general(left, right, dims, preferred_element_type=F32)


def sigmoid(values):
    return 0.5 * jnp.tanh(0.5 * values) + 0.5


def flipped(weight):
    return weight.astype(F32).T.astype(BF16)


def lane_tiles(values):
    lanes = values.shape[1]
    return [(t, slice(t * LANES, (t + 1) * LANES)) for t in range(lanes // LANES)]


def lane_norm(values):
    centered = values - jnp.mean(values, axis=-1, keepdims=True)
    variance = jnp.mean(centered * centered, axis=-1, keepdims=True)
    return (centered * lax.rsqrt(variance + 1e-05)).astype(BF16)


def pipeline(rows, *steps):
    for tick in range(rows + len(steps) - 1):
        for late, step in enumerate(steps):
            if 0 <= tick - late < rows:
                step(tick - late)


def edges_kernel(*refs):
    given, (out, gate), (pair, weights, normed, held, sems) = refs[:6], refs[6:8], refs[8:]
    copies = [
        pltpu.make_async_copy(source, target, sems.at[n])
        for n, (source, target) in enumerate(zip(given, [weights.at[n] for n in range(5)] + [pair]))
    ]
    for copy in copies:
        copy.start()
    for copy in copies:
        copy.wait()
    rows = pair.shape[0]
    channels = weights.shape[2]
    turned = jnp.concatenate([flipped(weights[n]) for n in range(4)], axis=0)
    for i in range(rows):
        normed[i] = lane_norm(pair[i].astype(F32))
    for i in range(rows):
        both = dot(turned, normed[i], NT)
        for side in range(2):
            base = 2 * side * channels
            act = sigmoid(both[base + channels : base + 2 * channels]) * both[base : base + channels]
            for tile, lanes in lane_tiles(act):
                held[tile, pl.ds(side * rows + i, channels, stride=2 * rows), :] = act[:, lanes]
        gate[i] = sigmoid(dot(normed[i], weights[4]))
    block = out.shape[1]
    for owner in range(out.shape[0]):
        for tile, lanes in lane_tiles(pair):
            out[owner, :, lanes] = held[tile, owner * block : (owner + 1) * block, :].astype(BF16)


def triangle_sides(edges, rows, channel):
    sides = [[], []]
    for source in range(edges.shape[0]):
        block = edges[source, channel * 2 * rows : (channel + 1) * 2 * rows, :].astype(F32)
        sides[0].append(block[:rows])
        sides[1].append(block[rows:])
    return [jnp.concatenate(side, axis=0).astype(BF16) for side in sides]


def triangle_kernel(rows, edges, out):
    for pair_of in range(0, out.shape[1] // rows, 2):
        products = [dot(*triangle_sides(edges, rows, pair_of + o), NT) for o in range(2)]
        for owner in range(out.shape[0]):
            mine = slice(owner * rows, (owner + 1) * rows)
            out[owner, pair_of * rows : (pair_of + 2) * rows, :] = jnp.concatenate(
                [p[mine] for p in products], axis=0
            ).astype(BF16)


def partial_kernel(rows, edges, out):
    for channel in range(out.shape[0]):
        out[channel] = dot(*triangle_sides(edges, rows, channel), NT)


def update_kernel(
    returned, gate, pair, w_tri_out, w_bias_t, first_pass, att_norm, bias, held, bias_held, turned
):
    rows, cols = pair.shape[0], pair.shape[1]
    owners, block = returned.shape[0], returned.shape[1]
    channels = owners * block // rows
    total = jnp.zeros((rows, cols), F32)
    for owner in range(owners):
        total += jnp.sum(returned[owner].astype(F32).reshape(block // rows, rows, cols), axis=0)
    average = total / channels
    square = jnp.zeros((rows, cols), F32)
    for owner in range(owners):
        centered = returned[owner].astype(F32).reshape(block // rows, rows, cols) - average
        square += jnp.sum(centered * centered, axis=0)
        for tile, lanes in lane_tiles(pair):
            held[tile, owner * block : (owner + 1) * block, :] = centered.reshape(block, cols)[:, lanes]
    scale = lax.rsqrt(square / channels + 1e-05)

    def turn(i):
        tri_norm = jnp.concatenate(
            [held[tile, pl.ds(i, channels, stride=rows), :] for tile, _ in lane_tiles(pair)], axis=1
        )
        turned[i % 2] = (tri_norm * scale[i : i + 1]).T.astype(BF16)

    def update(i):
        first_pass[i] = pair[i].astype(F32) + gate[i] * dot(turned[i % 2], w_tri_out[...])

    def norm(i):
        att_norm[i] = lane_norm(first_pass[i])

    def project_bias(i):
        row_bias = dot(w_bias_t[...], att_norm[i], NT)
        for head in range(HEADS):
            bias_held[head * rows + i : head * rows + i + 1, :] = row_bias[head : head + 1]

    pipeline(rows, turn, update, norm, project_bias)
    rounded = bias_held[...].astype(BF16)
    for owner in range(bias.shape[0]):
        bias[owner] = rounded


def project_kernel(att_norm, w_query, w_key, w_value, w_att_gate, query_t, key, value_t, gate_t):
    w_turned = jnp.concatenate([flipped(w[...]) for w in (w_query, w_value, w_att_gate)], axis=0)
    width = w_query.shape[1]
    for i in range(att_norm.shape[0]):
        normed = att_norm[i]
        key[i] = dot(normed, w_key[...]).astype(BF16)
        turned = dot(w_turned, normed, NT)
        query_t[i] = turned[:width].astype(BF16)
        value_t[i] = turned[width : 2 * width].astype(BF16)
        gate_t[i] = sigmoid(turned[2 * width :])


def attend_kernel(
    query_t, key, value_t, gate_t, first_pass, bias, w_att_out, out, bias_t, scores, weights, gated
):
    rows, width, cols = query_t.shape
    head_rows = bias.shape[1] // HEADS
    score_scale = LOG2_E / HEAD_DIM**0.5
    ones = jnp.ones((16, key.shape[1]), BF16)
    heads = [
        (slice(h * HEAD_DIM, (h + 1) * HEAD_DIM), slice(h * cols, (h + 1) * cols)) for h in range(HEADS)
    ]

    def score(i):
        blocks = []
        for mine, _ in heads:
            above = jnp.zeros((mine.start, cols), BF16)
            below = jnp.zeros((width - mine.stop, cols), BF16)
            parts = [p for p in (above, query_t[i, mine, :], below) if p.shape[0]]
            blocks.append(jnp.concatenate(parts, axis=0))
        scores[i % 2] = dot(key[i], jnp.concatenate(blocks, axis=1)) * score_scale

    def soften(i):
        for _, span in heads:
            biased = scores[i % 2, :, span] + bias_t[:, span]
            peak = jnp.max(biased, axis=0, keepdims=True)
            weights[i % 2, :, span] = jnp.exp2(biased - peak).astype(BF16)

    def collect(i):
        for mine, span in heads:
            values = jnp.concatenate([value_t[i, mine, :], ones], axis=0)
            summed = dot(values, weights[i % 2, :, span])
            share = 1.0 / summed[HEAD_DIM : HEAD_DIM + 1]
            gated[i % 2, mine, :] = summed[:HEAD_DIM] * share * gate_t[i, mine, :]

    def finish(i):
        turned = gated[i % 2].T.astype(BF16)
        out[i] = (first_pass[i] + dot(turned, w_att_out[...])).astype(BF16)

    for head, (_, span) in enumerate(heads):
        parts = [
            bias[owner].astype(F32)[head * head_rows : (head + 1) * head_rows]
            for owner in range(bias.shape[0])
        ]
        bias_t[:, span] = jnp.concatenate(parts, axis=0).T * LOG2_E
    pipeline(rows, score, soften, collect, finish)


def call(kernel, outs, scratch, flops, *operands, copied=False):
    vmem = pl.BlockSpec(memory_space=pltpu.VMEM)
    given = pl.BlockSpec(memory_space=pltpu.HBM) if copied else vmem
    shapes = [jax.ShapeDtypeStruct(shape, dtype) for shape, dtype in outs]
    moved = sum(o.size * o.dtype.itemsize for o in operands)
    got = pl.pallas_call(
        kernel,
        out_shape=shapes,
        in_specs=[given] * len(operands),
        out_specs=[vmem] * len(shapes),
        scratch_shapes=[pltpu.VMEM(*s) if isinstance(s, tuple) else s for s in scratch],
        compiler_params=pltpu.CompilerParams(vmem_limit_bytes=48 * 2**20),
        cost_estimate=pl.CostEstimate(flops=flops, bytes_accessed=moved, transcendentals=0),
    )(*operands)
    return got if len(got) > 1 else got[0]


def body(
    pair_rep,
    w_left,
    w_left_gate,
    w_right,
    w_right_gate,
    w_tri_gate,
    w_tri_out,
    w_query,
    w_key,
    w_value,
    w_bias,
    w_att_gate,
    w_att_out,
):
    rows, cols, width = pair_rep.shape
    channels = w_left.shape[1]
    owners, col_parts = lax.axis_size("row"), lax.axis_size("col")
    own = channels // owners
    residues = owners * rows
    cells = rows * cols

    edges, gate = call(
        edges_kernel,
        [((owners, own * 2 * rows, cols), BF16), ((rows, cols, width), F32)],
        [
            (pair_rep.shape, BF16),
            ((5, width, channels), BF16),
            (pair_rep.shape, BF16),
            ((cols // LANES, channels * 2 * rows, LANES), F32),
            pltpu.SemaphoreType.DMA((6,)),
        ],
        10 * cells * width * channels,
        w_left,
        w_left_gate,
        w_right,
        w_right_gate,
        w_tri_gate,
        pair_rep,
        copied=True,
    )
    spread = lax.all_to_all(edges, "row", split_axis=0, concat_axis=0, tiled=True)
    flops = 2 * own * residues * residues * cols
    if col_parts == 1:
        summed = call(
            functools.partial(triangle_kernel, rows),
            [((owners, own * rows, residues), BF16)],
            [],
            flops,
            spread,
        )
    else:
        partial_sums = call(
            functools.partial(partial_kernel, rows),
            [((own, residues, residues), F32)],
            [],
            flops,
            spread,
        )
        summed = lax.psum_scatter(partial_sums, "col", scatter_dimension=2, tiled=True).astype(BF16)
        summed = summed.reshape(own, owners, rows, cols).swapaxes(0, 1)
        summed = summed.reshape(owners, own * rows, cols)
    returned = lax.all_to_all(summed, "row", split_axis=0, concat_axis=0, tiled=True)
    first_pass, att_norm, bias_copies = call(
        update_kernel,
        [
            ((rows, cols, width), F32),
            ((rows, cols, width), BF16),
            ((owners, HEADS * rows, cols), BF16),
        ],
        [
            ((cols // LANES, channels * rows, LANES), F32),
            ((HEADS * rows, cols), F32),
            ((2, cols, channels), BF16),
        ],
        2 * cells * channels * width,
        returned,
        gate,
        pair_rep,
        w_tri_out,
        w_bias.T,
    )
    bias = lax.all_to_all(bias_copies, "row", split_axis=0, concat_axis=0, tiled=True)
    att_norm, bias = lax.optimization_barrier((att_norm, bias))
    query_t, key, value_t, gate_t = call(
        project_kernel,
        [
            ((rows, width, cols), BF16),
            ((rows, cols, width), BF16),
            ((rows, width, cols), BF16),
            ((rows, width, cols), F32),
        ],
        [],
        8 * cells * width * width,
        att_norm,
        w_query,
        w_key,
        w_value,
        w_att_gate,
    )
    if col_parts > 1:
        bias = lax.all_to_all(bias, "col", split_axis=0, concat_axis=2, tiled=True)
        key = lax.all_gather(key, "col", axis=1, tiled=True)
        value_t = lax.all_gather(value_t, "col", axis=2, tiled=True)
    keys = key.shape[1]
    return call(
        attend_kernel,
        [((rows, cols, width), BF16)],
        [
            ((keys, HEADS * cols), F32),
            ((2, keys, HEADS * cols), F32),
            ((2, keys, HEADS * cols), BF16),
            ((2, width, cols), F32),
        ],
        4 * cells * keys * width,
        query_t,
        key,
        value_t,
        gate_t,
        first_pass,
        bias,
        w_att_out,
    )


def solution(mesh):
    in_specs = (P(("grp", "row"), "col", None),) + (P(),) * 12
    out_specs = P(("grp", "row"), "col", None)
    return jax.shard_map(body, mesh=mesh, in_specs=in_specs, out_specs=out_specs, check_vma=False)
```

```python
import functools

import jax
import jax.numpy as jnp
from jax import lax
from jax.experimental import pallas as pl
from jax.experimental.pallas import tpu as pltpu
from jax.sharding import PartitionSpec as P

HEADS = 4
HEAD_DIM = 32
LANES = 128
LOG2_E = 1.4426950408889634
F32 = jnp.float32
BF16 = jnp.bfloat16
NN = (((1,), (0,)), ((), ()))
NT = (((1,), (1,)), ((), ()))
TN = (((0,), (0,)), ((), ()))


def dot(left, right, dims=NN):
    return lax.dot_general(left, right, dims, preferred_element_type=F32)


def sigmoid(values):
    return 0.5 * jnp.tanh(0.5 * values) + 0.5


def flipped(weight):
    return weight.astype(F32).T.astype(BF16)


def slot(rank, ranks):
    return ranks - 1 - rank


def swap(blocks):
    ranks = blocks.shape[0]
    order = [slot(rank, ranks) for rank in range(ranks)]
    return lax.all_to_all(
        blocks, "row", split_axis=0, concat_axis=0, axis_index_groups=[order], tiled=True
    )


def lane_tiles(values):
    lanes = values.shape[1]
    return [(t, slice(t * LANES, (t + 1) * LANES)) for t in range(lanes // LANES)]


def lane_norm(values):
    centered = values - jnp.mean(values, axis=-1, keepdims=True)
    variance = jnp.mean(centered * centered, axis=-1, keepdims=True)
    return (centered * lax.rsqrt(variance + 1e-05)).astype(BF16)


def pipeline(rows, *steps):
    for tick in range(rows + len(steps) - 1):
        for late, step in enumerate(steps):
            if 0 <= tick - late < rows:
                step(tick - late)


def edges_kernel(*refs):
    given, (out, gate), (pair, weights, normed, held, sems) = refs[:6], refs[6:8], refs[8:]
    copies = [
        pltpu.make_async_copy(source, target, sems.at[n])
        for n, (source, target) in enumerate(zip(given, [weights.at[n] for n in range(5)] + [pair]))
    ]
    for copy in copies:
        copy.start()
    for copy in copies:
        copy.wait()
    rows = pair.shape[0]
    channels = weights.shape[2]
    turned = jnp.concatenate([flipped(weights[n]) for n in range(4)], axis=0)
    for i in range(rows):
        normed[i] = lane_norm(pair[i].astype(F32))
    for i in range(rows):
        both = dot(turned, normed[i], NT)
        for side in range(2):
            base = 2 * side * channels
            act = sigmoid(both[base + channels : base + 2 * channels]) * both[base : base + channels]
            for tile, lanes in lane_tiles(act):
                held[tile, pl.ds(side * rows + i, channels, stride=2 * rows), :] = act[:, lanes]
        gate[i] = sigmoid(dot(normed[i], weights[4]))
    owners, block = out.shape[0], out.shape[1]
    for owner in range(owners):
        for tile, lanes in lane_tiles(pair):
            out[slot(owner, owners), :, lanes] = held[tile, owner * block : (owner + 1) * block, :].astype(BF16)


def triangle_sides(edges, rows, channel):
    sides = [[], []]
    sources = edges.shape[0]
    for source in range(sources):
        block = edges[slot(source, sources), channel * 2 * rows : (channel + 1) * 2 * rows, :].astype(F32)
        sides[0].append(block[:rows])
        sides[1].append(block[rows:])
    return [jnp.concatenate(side, axis=0).astype(BF16) for side in sides]


def triangle_kernel(rows, edges, out):
    for pair_of in range(0, out.shape[1] // rows, 2):
        products = [dot(*triangle_sides(edges, rows, pair_of + o), NT) for o in range(2)]
        owners = out.shape[0]
        for owner in range(owners):
            mine = slice(owner * rows, (owner + 1) * rows)
            out[slot(owner, owners), pair_of * rows : (pair_of + 2) * rows, :] = jnp.concatenate(
                [p[mine] for p in products], axis=0
            ).astype(BF16)


def partial_kernel(rows, edges, out):
    for channel in range(out.shape[0]):
        out[channel] = dot(*triangle_sides(edges, rows, channel), NT)


def update_kernel(
    w_tri_out_given,
    w_bias_given,
    returned,
    gate,
    pair,
    first_pass,
    att_norm,
    bias,
    held,
    bias_held,
    turned,
    w_tri_out,
    w_bias_t,
    sems,
):
    copies = [
        pltpu.make_async_copy(w_tri_out_given, w_tri_out, sems.at[0]),
        pltpu.make_async_copy(w_bias_given, w_bias_t, sems.at[1]),
    ]
    for copy in copies:
        copy.start()
    rows, cols = pair.shape[0], pair.shape[1]
    owners, block = returned.shape[0], returned.shape[1]
    channels = owners * block // rows
    total = jnp.zeros((rows, cols), F32)
    for owner in range(owners):
        total += jnp.sum(returned[owner].astype(F32).reshape(block // rows, rows, cols), axis=0)
    average = total / channels
    square = jnp.zeros((rows, cols), F32)
    for owner in range(owners):
        centered = returned[slot(owner, owners)].astype(F32).reshape(block // rows, rows, cols) - average
        square += jnp.sum(centered * centered, axis=0)
        for tile, lanes in lane_tiles(pair):
            held[tile, owner * block : (owner + 1) * block, :] = centered.reshape(block, cols)[:, lanes]
    scale = lax.rsqrt(square / channels + 1e-05)
    for copy in copies:
        copy.wait()

    def turn(i):
        tri_norm = jnp.concatenate(
            [held[tile, pl.ds(i, channels, stride=rows), :] for tile, _ in lane_tiles(pair)], axis=1
        )
        turned[i % 2] = (tri_norm * scale[i : i + 1]).T.astype(BF16)

    def update(i):
        first_pass[i] = pair[i].astype(F32) + gate[i] * dot(turned[i % 2], w_tri_out[...])

    def norm(i):
        att_norm[i] = lane_norm(first_pass[i])

    def project_bias(i):
        row_bias = dot(w_bias_t[...], att_norm[i], NT)
        for head in range(HEADS):
            bias_held[head * rows + i : head * rows + i + 1, :] = row_bias[head : head + 1]

    pipeline(rows, turn, update, norm, project_bias)
    rounded = bias_held[...].astype(BF16)
    for owner in range(bias.shape[0]):
        bias[owner] = rounded


def project_kernel(att_norm, w_query, w_key, w_value, w_att_gate, query_t, key, value_t, gate_t):
    w_turned = jnp.concatenate([flipped(w[...]) for w in (w_query, w_value, w_att_gate)], axis=0)
    width = w_query.shape[1]
    for i in range(att_norm.shape[0]):
        normed = att_norm[i]
        key[i] = dot(normed, w_key[...]).astype(BF16)
        turned = dot(w_turned, normed, NT)
        query_t[i] = turned[:width].astype(BF16)
        value_t[i] = turned[width : 2 * width].astype(BF16)
        gate_t[i] = sigmoid(turned[2 * width :])


def attend_kernel(
    query_t, key, value_t, gate_t, first_pass, bias, w_att_out, out, bias_t, scores, weights, gated
):
    rows, width, cols = query_t.shape
    head_rows = bias.shape[1] // HEADS
    score_scale = LOG2_E / HEAD_DIM**0.5
    ones = jnp.ones((16, key.shape[1]), BF16)
    heads = [
        (slice(h * HEAD_DIM, (h + 1) * HEAD_DIM), slice(h * cols, (h + 1) * cols)) for h in range(HEADS)
    ]

    def score(i):
        blocks = []
        for mine, _ in heads:
            above = jnp.zeros((mine.start, cols), BF16)
            below = jnp.zeros((width - mine.stop, cols), BF16)
            parts = [p for p in (above, query_t[i, mine, :], below) if p.shape[0]]
            blocks.append(jnp.concatenate(parts, axis=0))
        scores[i % 2] = dot(key[i], jnp.concatenate(blocks, axis=1)) * score_scale

    def soften(i):
        for _, span in heads:
            biased = scores[i % 2, :, span] + bias_t[:, span]
            peak = jnp.max(biased, axis=0, keepdims=True)
            weights[i % 2, :, span] = jnp.exp2(biased - peak).astype(BF16)

    def collect(i):
        for mine, span in heads:
            values = jnp.concatenate([value_t[i, mine, :], ones], axis=0)
            summed = dot(values, weights[i % 2, :, span])
            share = 1.0 / summed[HEAD_DIM : HEAD_DIM + 1]
            gated[i % 2, mine, :] = summed[:HEAD_DIM] * share * gate_t[i, mine, :]

    def finish(i):
        turned = gated[i % 2].T.astype(BF16)
        out[i] = (first_pass[i] + dot(turned, w_att_out[...])).astype(BF16)

    for head, (_, span) in enumerate(heads):
        parts = [
            bias[slot(owner, bias.shape[0])].astype(F32)[head * head_rows : (head + 1) * head_rows]
            for owner in range(bias.shape[0])
        ]
        bias_t[:, span] = jnp.concatenate(parts, axis=0).T * LOG2_E
    pipeline(rows, score, soften, collect, finish)


def call(kernel, outs, scratch, flops, *operands, fetched=0):
    vmem = pl.BlockSpec(memory_space=pltpu.VMEM)
    far = pl.BlockSpec(memory_space=pltpu.HBM)
    shapes = [jax.ShapeDtypeStruct(shape, dtype) for shape, dtype in outs]
    moved = sum(o.size * o.dtype.itemsize for o in operands)
    operands = [
        pltpu.with_memory_space_constraint(o, pltpu.HBM) if n < fetched else o
        for n, o in enumerate(operands)
    ]
    got = pl.pallas_call(
        kernel,
        out_shape=shapes,
        in_specs=[far] * fetched + [vmem] * (len(operands) - fetched),
        out_specs=[vmem] * len(shapes),
        scratch_shapes=[pltpu.VMEM(*s) if isinstance(s, tuple) else s for s in scratch],
        compiler_params=pltpu.CompilerParams(vmem_limit_bytes=48 * 2**20),
        cost_estimate=pl.CostEstimate(flops=flops, bytes_accessed=moved, transcendentals=0),
    )(*operands)
    return got if len(got) > 1 else got[0]


def body(
    pair_rep,
    w_left,
    w_left_gate,
    w_right,
    w_right_gate,
    w_tri_gate,
    w_tri_out,
    w_query,
    w_key,
    w_value,
    w_bias,
    w_att_gate,
    w_att_out,
):
    rows, cols, width = pair_rep.shape
    channels = w_left.shape[1]
    owners, col_parts = lax.axis_size("row"), lax.axis_size("col")
    own = channels // owners
    residues = owners * rows
    cells = rows * cols

    edges, gate = call(
        edges_kernel,
        [((owners, own * 2 * rows, cols), BF16), ((rows, cols, width), F32)],
        [
            (pair_rep.shape, BF16),
            ((5, width, channels), BF16),
            (pair_rep.shape, BF16),
            ((cols // LANES, channels * 2 * rows, LANES), F32),
            pltpu.SemaphoreType.DMA((6,)),
        ],
        10 * cells * width * channels,
        w_left,
        w_left_gate,
        w_right,
        w_right_gate,
        w_tri_gate,
        pair_rep,
        fetched=6,
    )
    spread = swap(edges)
    flops = 2 * own * residues * residues * cols
    if col_parts == 1:
        summed = call(
            functools.partial(triangle_kernel, rows),
            [((owners, own * rows, residues), BF16)],
            [],
            flops,
            spread,
        )
    else:
        partial_sums = call(
            functools.partial(partial_kernel, rows),
            [((own, residues, residues), F32)],
            [],
            flops,
            spread,
        )
        summed = lax.psum_scatter(partial_sums, "col", scatter_dimension=2, tiled=True).astype(BF16)
        summed = summed.reshape(own, owners, rows, cols).swapaxes(0, 1)[::-1]
        summed = summed.reshape(owners, own * rows, cols)
    returned = swap(summed)
    first_pass, att_norm, bias_copies = call(
        update_kernel,
        [
            ((rows, cols, width), F32),
            ((rows, cols, width), BF16),
            ((owners, HEADS * rows, cols), BF16),
        ],
        [
            ((cols // LANES, channels * rows, LANES), F32),
            ((HEADS * rows, cols), F32),
            ((2, cols, channels), BF16),
            (w_tri_out.shape, BF16),
            (w_bias.shape[::-1], BF16),
            pltpu.SemaphoreType.DMA((2,)),
        ],
        2 * cells * channels * width,
        w_tri_out,
        w_bias.T,
        returned,
        gate,
        pair_rep,
        fetched=2,
    )
    bias = swap(bias_copies)
    att_norm, bias = lax.optimization_barrier((att_norm, bias))
    query_t, key, value_t, gate_t = call(
        project_kernel,
        [
            ((rows, width, cols), BF16),
            ((rows, cols, width), BF16),
            ((rows, width, cols), BF16),
            ((rows, width, cols), F32),
        ],
        [],
        8 * cells * width * width,
        att_norm,
        w_query,
        w_key,
        w_value,
        w_att_gate,
    )
    if col_parts > 1:
        bias = lax.all_to_all(bias[::-1], "col", split_axis=0, concat_axis=2, tiled=True)[::-1]
        key = lax.all_gather(key, "col", axis=1, tiled=True)
        value_t = lax.all_gather(value_t, "col", axis=2, tiled=True)
    keys = key.shape[1]
    return call(
        attend_kernel,
        [((rows, cols, width), BF16)],
        [
            ((keys, HEADS * cols), F32),
            ((2, keys, HEADS * cols), F32),
            ((2, keys, HEADS * cols), BF16),
            ((2, width, cols), F32),
        ],
        4 * cells * keys * width,
        query_t,
        key,
        value_t,
        gate_t,
        first_pass,
        bias,
        w_att_out,
    )


def solution(mesh):
    in_specs = (P(("grp", "row"), "col", None),) + (P(),) * 12
    out_specs = P(("grp", "row"), "col", None)
    return jax.shard_map(body, mesh=mesh, in_specs=in_specs, out_specs=out_specs, check_vma=False)
```

```python
import functools

import jax
import jax.numpy as jnp
import numpy as np
from jax import lax
from jax.experimental import pallas as pl
from jax.experimental.pallas import tpu as pltpu
from jax.sharding import PartitionSpec as P

HEADS = 4
HEAD_DIM = 32
LANES = 128
LOG2_E = 1.4426950408889634
F32 = jnp.float32
BF16 = jnp.bfloat16
NN = (((1,), (0,)), ((), ()))
NT = (((1,), (1,)), ((), ()))
TN = (((0,), (0,)), ((), ()))


def dot(left, right, dims=NN):
    return lax.dot_general(left, right, dims, preferred_element_type=F32)


def sigmoid(values):
    return 0.5 * jnp.tanh(0.5 * values) + 0.5


def flipped(weight):
    return weight.astype(F32).T.astype(BF16)


def listing(ranks):
    first = ranks - 1 - ranks // 4
    return [first] + [rank for rank in range(ranks - 1, -1, -1) if rank != first]


def slot(rank, ranks):
    return listing(ranks).index(rank)


def swap(blocks):
    return lax.all_to_all(
        blocks,
        "row",
        split_axis=0,
        concat_axis=0,
        axis_index_groups=[listing(blocks.shape[0])],
        tiled=True,
    )


def by_rank(blocks):
    return blocks[np.array([slot(r, blocks.shape[0]) for r in range(blocks.shape[0])])]


def by_slot(blocks):
    return blocks[np.array(listing(blocks.shape[0]))]


def lane_tiles(values):
    lanes = values.shape[1]
    return [(t, slice(t * LANES, (t + 1) * LANES)) for t in range(lanes // LANES)]


def lane_norm(values):
    centered = values - jnp.mean(values, axis=-1, keepdims=True)
    variance = jnp.mean(centered * centered, axis=-1, keepdims=True)
    return (centered * lax.rsqrt(variance + 1e-05)).astype(BF16)


def pipeline(rows, *steps):
    for tick in range(rows + len(steps) - 1):
        for late, step in enumerate(steps):
            if 0 <= tick - late < rows:
                step(tick - late)


def edges_kernel(*refs):
    given, (out, gate, *staged), (pair, weights, normed, held, sems) = refs[:13], refs[13:22], refs[22:]
    targets = [pair, *(weights.at[n] for n in range(5)), *staged]
    copies = [
        pltpu.make_async_copy(source, target, sems.at[n])
        for n, (source, target) in enumerate(zip(given, targets))
    ]
    for copy in copies:
        copy.start()
    for copy in copies[:6]:
        copy.wait()
    rows = pair.shape[0]
    channels = weights.shape[2]
    turned = jnp.concatenate([flipped(weights[n]) for n in range(4)], axis=0)
    for i in range(rows):
        normed[i] = lane_norm(pair[i].astype(F32))
    for i in range(rows):
        both = dot(turned, normed[i], NT)
        for side in range(2):
            base = 2 * side * channels
            act = sigmoid(both[base + channels : base + 2 * channels]) * both[base : base + channels]
            for tile, lanes in lane_tiles(act):
                held[tile, pl.ds(side * rows + i, channels, stride=2 * rows), :] = act[:, lanes]
        gate[i] = sigmoid(dot(normed[i], weights[4]))
    owners, block = out.shape[0], out.shape[1]
    for owner in range(owners):
        for tile, lanes in lane_tiles(pair):
            out[slot(owner, owners), :, lanes] = held[tile, owner * block : (owner + 1) * block, :].astype(BF16)
    for copy in copies[6:]:
        copy.wait()


def triangle_sides(edges, rows, channel):
    sides = [[], []]
    sources = edges.shape[0]
    for source in range(sources):
        block = edges[slot(source, sources), channel * 2 * rows : (channel + 1) * 2 * rows, :].astype(F32)
        sides[0].append(block[:rows])
        sides[1].append(block[rows:])
    return [jnp.concatenate(side, axis=0).astype(BF16) for side in sides]


def triangle_kernel(rows, edges, out):
    for pair_of in range(0, out.shape[1] // rows, 2):
        products = [dot(*triangle_sides(edges, rows, pair_of + o), NT) for o in range(2)]
        owners = out.shape[0]
        for owner in range(owners):
            mine = slice(owner * rows, (owner + 1) * rows)
            out[slot(owner, owners), pair_of * rows : (pair_of + 2) * rows, :] = jnp.concatenate(
                [p[mine] for p in products], axis=0
            ).astype(BF16)


def partial_kernel(rows, edges, out):
    for channel in range(out.shape[0]):
        out[channel] = dot(*triangle_sides(edges, rows, channel), NT)


def update_kernel(
    returned, gate, pair, w_tri_out, w_bias_t, first_pass, att_norm, bias, held, bias_held, turned
):
    rows, cols = pair.shape[0], pair.shape[1]
    owners, block = returned.shape[0], returned.shape[1]
    channels = owners * block // rows
    total = jnp.zeros((rows, cols), F32)
    for owner in range(owners):
        total += jnp.sum(returned[owner].astype(F32).reshape(block // rows, rows, cols), axis=0)
    average = total / channels
    square = jnp.zeros((rows, cols), F32)
    for owner in range(owners):
        centered = returned[slot(owner, owners)].astype(F32).reshape(block // rows, rows, cols) - average
        square += jnp.sum(centered * centered, axis=0)
        for tile, lanes in lane_tiles(pair):
            held[tile, owner * block : (owner + 1) * block, :] = centered.reshape(block, cols)[:, lanes]
    scale = lax.rsqrt(square / channels + 1e-05)

    def turn(i):
        tri_norm = jnp.concatenate(
            [held[tile, pl.ds(i, channels, stride=rows), :] for tile, _ in lane_tiles(pair)], axis=1
        )
        turned[i % 2] = (tri_norm * scale[i : i + 1]).T.astype(BF16)

    def update(i):
        first_pass[i] = pair[i].astype(F32) + gate[i] * dot(turned[i % 2], w_tri_out[...])

    def norm(i):
        att_norm[i] = lane_norm(first_pass[i])

    def project_bias(i):
        row_bias = dot(w_bias_t[...], att_norm[i], NT)
        for head in range(HEADS):
            bias_held[head * rows + i : head * rows + i + 1, :] = row_bias[head : head + 1]

    pipeline(rows, turn, update, norm, project_bias)
    rounded = bias_held[...].astype(BF16)
    for owner in range(bias.shape[0]):
        bias[owner] = rounded


def projector(att_norm, w_query, w_key, w_value, w_att_gate, query_t, key, value_t, gate_t):
    w_turned = jnp.concatenate([flipped(w[...]) for w in (w_query, w_value, w_att_gate)], axis=0)
    width = w_query.shape[1]

    def project(i):
        normed = att_norm[i]
        key[i] = dot(normed, w_key[...]).astype(BF16)
        turned = dot(w_turned, normed, NT)
        query_t[i] = turned[:width].astype(BF16)
        value_t[i] = turned[width : 2 * width].astype(BF16)
        gate_t[i] = sigmoid(turned[2 * width :])

    return project


def project_kernel(*refs):
    pipeline(refs[0].shape[0], projector(*refs))


def whole_kernel(att_norm, w_query, w_key, w_value, w_att_gate, *refs):
    given, projected, held = refs[:4], refs[4:8], refs[8:]
    project = projector(att_norm, w_query, w_key, w_value, w_att_gate, *projected)
    attend_kernel(*projected, *given, *held, before=(project,))


def attend_kernel(
    query_t,
    key,
    value_t,
    gate_t,
    first_pass,
    bias,
    w_att_out,
    out,
    bias_t,
    scores,
    weights,
    gated,
    before=(),
):
    rows, width, cols = query_t.shape
    head_rows = bias.shape[1] // HEADS
    score_scale = LOG2_E / HEAD_DIM**0.5
    ones = jnp.ones((16, key.shape[1]), BF16)
    heads = [
        (slice(h * HEAD_DIM, (h + 1) * HEAD_DIM), slice(h * cols, (h + 1) * cols)) for h in range(HEADS)
    ]

    def score(i):
        blocks = []
        for mine, _ in heads:
            above = jnp.zeros((mine.start, cols), BF16)
            below = jnp.zeros((width - mine.stop, cols), BF16)
            parts = [p for p in (above, query_t[i, mine, :], below) if p.shape[0]]
            blocks.append(jnp.concatenate(parts, axis=0))
        scores[i % 2] = dot(key[i], jnp.concatenate(blocks, axis=1)) * score_scale

    def soften(i):
        for _, span in heads:
            biased = scores[i % 2, :, span] + bias_t[:, span]
            peak = jnp.max(biased, axis=0, keepdims=True)
            weights[i % 2, :, span] = jnp.exp2(biased - peak).astype(BF16)

    def collect(i):
        for mine, span in heads:
            values = jnp.concatenate([value_t[i, mine, :], ones], axis=0)
            summed = dot(values, weights[i % 2, :, span])
            share = 1.0 / summed[HEAD_DIM : HEAD_DIM + 1]
            gated[i % 2, mine, :] = summed[:HEAD_DIM] * share * gate_t[i, mine, :]

    def finish(i):
        turned = gated[i % 2].T.astype(BF16)
        out[i] = (first_pass[i] + dot(turned, w_att_out[...])).astype(BF16)

    for head, (_, span) in enumerate(heads):
        parts = [
            bias[slot(owner, bias.shape[0])].astype(F32)[head * head_rows : (head + 1) * head_rows]
            for owner in range(bias.shape[0])
        ]
        bias_t[:, span] = jnp.concatenate(parts, axis=0).T * LOG2_E
    pipeline(rows, *before, score, soften, collect, finish)


def call(kernel, outs, scratch, flops, *operands, fetched=0):
    vmem = pl.BlockSpec(memory_space=pltpu.VMEM)
    far = pl.BlockSpec(memory_space=pltpu.HBM)
    shapes = [jax.ShapeDtypeStruct(shape, dtype) for shape, dtype in outs]
    moved = sum(o.size * o.dtype.itemsize for o in operands)
    operands = [
        pltpu.with_memory_space_constraint(o, pltpu.HBM) if n < fetched else o
        for n, o in enumerate(operands)
    ]
    got = pl.pallas_call(
        kernel,
        out_shape=shapes,
        in_specs=[far] * fetched + [vmem] * (len(operands) - fetched),
        out_specs=[vmem] * len(shapes),
        scratch_shapes=[pltpu.VMEM(*s) if isinstance(s, tuple) else s for s in scratch],
        compiler_params=pltpu.CompilerParams(vmem_limit_bytes=48 * 2**20),
        cost_estimate=pl.CostEstimate(flops=flops, bytes_accessed=moved, transcendentals=0),
    )(*operands)
    return got if len(got) > 1 else got[0]


def body(
    pair_rep,
    w_left,
    w_left_gate,
    w_right,
    w_right_gate,
    w_tri_gate,
    w_tri_out,
    w_query,
    w_key,
    w_value,
    w_bias,
    w_att_gate,
    w_att_out,
):
    rows, cols, width = pair_rep.shape
    channels = w_left.shape[1]
    owners, col_parts = lax.axis_size("row"), lax.axis_size("col")
    own = channels // owners
    residues = owners * rows
    cells = rows * cols

    edges, gate, w_tri_out, w_query, w_key, w_value, w_att_gate, w_att_out, w_bias_t = call(
        edges_kernel,
        [
            ((owners, own * 2 * rows, cols), BF16),
            ((rows, cols, width), F32),
            *[(w.shape, BF16) for w in (w_tri_out, w_query, w_key, w_value, w_att_gate, w_att_out)],
            (w_bias.shape[::-1], BF16),
        ],
        [
            (pair_rep.shape, BF16),
            ((5, width, channels), BF16),
            (pair_rep.shape, BF16),
            ((cols // LANES, channels * 2 * rows, LANES), F32),
            pltpu.SemaphoreType.DMA((13,)),
        ],
        10 * cells * width * channels,
        pair_rep,
        w_left,
        w_left_gate,
        w_right,
        w_right_gate,
        w_tri_gate,
        w_tri_out,
        w_query,
        w_key,
        w_value,
        w_att_gate,
        w_att_out,
        w_bias.T,
        fetched=13,
    )
    spread = swap(edges)
    flops = 2 * own * residues * residues * cols
    if col_parts == 1:
        summed = call(
            functools.partial(triangle_kernel, rows),
            [((owners, own * rows, residues), BF16)],
            [],
            flops,
            spread,
        )
    else:
        partial_sums = call(
            functools.partial(partial_kernel, rows),
            [((own, residues, residues), F32)],
            [],
            flops,
            spread,
        )
        summed = lax.psum_scatter(partial_sums, "col", scatter_dimension=2, tiled=True).astype(BF16)
        summed = by_slot(summed.reshape(own, owners, rows, cols).swapaxes(0, 1))
        summed = summed.reshape(owners, own * rows, cols)
    returned = swap(summed)
    first_pass, att_norm, bias_copies = call(
        update_kernel,
        [
            ((rows, cols, width), F32),
            ((rows, cols, width), BF16),
            ((owners, HEADS * rows, cols), BF16),
        ],
        [
            ((cols // LANES, channels * rows, LANES), F32),
            ((HEADS * rows, cols), F32),
            ((2, cols, channels), BF16),
        ],
        2 * cells * channels * width,
        returned,
        gate,
        pair_rep,
        w_tri_out,
        w_bias_t,
    )
    bias = swap(bias_copies)
    projected = [
        ((rows, width, cols), BF16),
        ((rows, cols, width), BF16),
        ((rows, width, cols), BF16),
        ((rows, width, cols), F32),
    ]
    projecting = (att_norm, w_query, w_key, w_value, w_att_gate)
    residues = cols * col_parts
    out = [((rows, cols, width), BF16)]
    held = [
        ((residues, HEADS * cols), F32),
        ((2, residues, HEADS * cols), F32),
        ((2, residues, HEADS * cols), BF16),
        ((2, width, cols), F32),
    ]
    project_flops, attend_flops = 8 * cells * width * width, 4 * cells * residues * width
    if col_parts == 1:
        flops = project_flops + attend_flops
        given = (first_pass, bias, w_att_out)
        return call(whole_kernel, out, projected + held, flops, *projecting, *given)
    query_t, key, value_t, gate_t = call(project_kernel, projected, [], project_flops, *projecting)
    bias = by_slot(lax.all_to_all(by_rank(bias), "col", split_axis=0, concat_axis=2, tiled=True))
    key = lax.all_gather(key, "col", axis=1, tiled=True)
    value_t = lax.all_gather(value_t, "col", axis=2, tiled=True)
    given = (query_t, key, value_t, gate_t, first_pass, bias, w_att_out)
    return call(attend_kernel, out, held, attend_flops, *given)


def solution(mesh):
    in_specs = (P(("grp", "row"), "col", None),) + (P(),) * 12
    out_specs = P(("grp", "row"), "col", None)
    return jax.shard_map(body, mesh=mesh, in_specs=in_specs, out_specs=out_specs, check_vma=False)
```

```python
import functools

import jax
import jax.numpy as jnp
import numpy as np
from jax import lax
from jax.experimental import pallas as pl
from jax.experimental.pallas import tpu as pltpu
from jax.sharding import PartitionSpec as P

HEADS = 4
HEAD_DIM = 32
LANES = 128
LOG2_E = 1.4426950408889634
F32 = jnp.float32
BF16 = jnp.bfloat16
NN = (((1,), (0,)), ((), ()))
NT = (((1,), (1,)), ((), ()))
TN = (((0,), (0,)), ((), ()))


def dot(left, right, dims=NN):
    return lax.dot_general(left, right, dims, preferred_element_type=F32)


def sigmoid(values):
    return 0.5 * jnp.tanh(0.5 * values) + 0.5


def flipped(weight):
    return weight.astype(F32).T.astype(BF16)


def listing(step, ranks):
    first, order = {
        "edges": (5 * ranks // 8, -1),
        "triangle": (ranks - 1 - ranks // 4, 1),
        "bias": (ranks // 2 - 1, -1),
    }[step]
    return [first] + [rank for rank in range(ranks)[::order] if rank != first]


def slot(step, rank, ranks):
    return listing(step, ranks).index(rank)


def swap(step, blocks):
    return lax.all_to_all(
        blocks,
        "row",
        split_axis=0,
        concat_axis=0,
        axis_index_groups=[listing(step, blocks.shape[0])],
        tiled=True,
    )


def by_rank(step, blocks):
    return blocks[np.array([slot(step, r, blocks.shape[0]) for r in range(blocks.shape[0])])]


def by_slot(step, blocks):
    return blocks[np.array(listing(step, blocks.shape[0]))]


def lane_tiles(values):
    lanes = values.shape[1]
    return [(t, slice(t * LANES, (t + 1) * LANES)) for t in range(lanes // LANES)]


def lane_norm(values):
    centered = values - jnp.mean(values, axis=-1, keepdims=True)
    variance = jnp.mean(centered * centered, axis=-1, keepdims=True)
    return (centered * lax.rsqrt(variance + 1e-05)).astype(BF16)


def pipeline(rows, *steps):
    for tick in range(rows + len(steps) - 1):
        for late, step in enumerate(steps):
            if 0 <= tick - late < rows:
                step(tick - late)


def edges_kernel(*refs):
    given, (out, gate, *staged), (pair, weights, normed, held, sems) = refs[:13], refs[13:22], refs[22:]
    targets = [pair, *(weights.at[n] for n in range(5)), *staged]
    copies = [
        pltpu.make_async_copy(source, target, sems.at[n])
        for n, (source, target) in enumerate(zip(given, targets))
    ]
    for copy in copies:
        copy.start()
    for copy in copies[:6]:
        copy.wait()
    rows = pair.shape[0]
    channels = weights.shape[2]
    turned = jnp.concatenate([flipped(weights[n]) for n in range(4)], axis=0)
    for i in range(rows):
        normed[i] = lane_norm(pair[i].astype(F32))
    for i in range(rows):
        both = dot(turned, normed[i], NT)
        for side in range(2):
            base = 2 * side * channels
            act = sigmoid(both[base + channels : base + 2 * channels]) * both[base : base + channels]
            for tile, lanes in lane_tiles(act):
                held[tile, pl.ds(side * rows + i, channels, stride=2 * rows), :] = act[:, lanes]
        gate[i] = sigmoid(dot(normed[i], weights[4]))
    owners, block = out.shape[0], out.shape[1]
    for owner in range(owners):
        for tile, lanes in lane_tiles(pair):
            out[slot("edges", owner, owners), :, lanes] = held[tile, owner * block : (owner + 1) * block, :].astype(BF16)
    for copy in copies[6:]:
        copy.wait()


def triangle_sides(edges, rows, channel):
    sides = [[], []]
    sources = edges.shape[0]
    for source in range(sources):
        block = edges[slot("edges", source, sources), channel * 2 * rows : (channel + 1) * 2 * rows, :].astype(F32)
        sides[0].append(block[:rows])
        sides[1].append(block[rows:])
    return [jnp.concatenate(side, axis=0).astype(BF16) for side in sides]


def triangle_kernel(rows, edges, out):
    for pair_of in range(0, out.shape[1] // rows, 2):
        products = [dot(*triangle_sides(edges, rows, pair_of + o), NT) for o in range(2)]
        owners = out.shape[0]
        for owner in range(owners):
            mine = slice(owner * rows, (owner + 1) * rows)
            out[slot("triangle", owner, owners), pair_of * rows : (pair_of + 2) * rows, :] = jnp.concatenate(
                [p[mine] for p in products], axis=0
            ).astype(BF16)


def partial_kernel(rows, edges, out):
    for channel in range(out.shape[0]):
        out[channel] = dot(*triangle_sides(edges, rows, channel), NT)


def update_kernel(
    returned, gate, pair, w_tri_out, w_bias_t, first_pass, att_norm, bias, held, bias_held, turned
):
    rows, cols = pair.shape[0], pair.shape[1]
    owners, block = returned.shape[0], returned.shape[1]
    channels = owners * block // rows
    total = jnp.zeros((rows, cols), F32)
    for owner in range(owners):
        total += jnp.sum(returned[owner].astype(F32).reshape(block // rows, rows, cols), axis=0)
    average = total / channels
    square = jnp.zeros((rows, cols), F32)
    for owner in range(owners):
        block_now = returned[slot("triangle", owner, owners)].astype(F32)
        centered = block_now.reshape(block // rows, rows, cols) - average
        square += jnp.sum(centered * centered, axis=0)
        for tile, lanes in lane_tiles(pair):
            held[tile, owner * block : (owner + 1) * block, :] = centered.reshape(block, cols)[:, lanes]
    scale = lax.rsqrt(square / channels + 1e-05)

    def turn(i):
        tri_norm = jnp.concatenate(
            [held[tile, pl.ds(i, channels, stride=rows), :] for tile, _ in lane_tiles(pair)], axis=1
        )
        turned[i % 2] = (tri_norm * scale[i : i + 1]).T.astype(BF16)

    def update(i):
        first_pass[i] = pair[i].astype(F32) + gate[i] * dot(turned[i % 2], w_tri_out[...])

    def norm(i):
        att_norm[i] = lane_norm(first_pass[i])

    def project_bias(i):
        row_bias = dot(w_bias_t[...], att_norm[i], NT)
        for head in range(HEADS):
            bias_held[head * rows + i : head * rows + i + 1, :] = row_bias[head : head + 1]

    pipeline(rows, turn, update, norm, project_bias)
    rounded = bias_held[...].astype(BF16)
    for owner in range(bias.shape[0]):
        bias[owner] = rounded


def projector(att_norm, w_query, w_key, w_value, w_att_gate, query_t, key, value_t, gate_t):
    w_turned = jnp.concatenate([flipped(w[...]) for w in (w_query, w_value, w_att_gate)], axis=0)
    width = w_query.shape[1]

    def project(i):
        normed = att_norm[i]
        key[i] = dot(normed, w_key[...]).astype(BF16)
        turned = dot(w_turned, normed, NT)
        query_t[i] = turned[:width].astype(BF16)
        value_t[i] = turned[width : 2 * width].astype(BF16)
        gate_t[i] = sigmoid(turned[2 * width :])

    return project


def project_kernel(*refs):
    pipeline(refs[0].shape[0], projector(*refs))


def whole_kernel(att_norm, w_query, w_key, w_value, w_att_gate, *refs):
    given, projected, held = refs[:4], refs[4:8], refs[8:]
    project = projector(att_norm, w_query, w_key, w_value, w_att_gate, *projected)
    attend_kernel(*projected, *given, *held, before=(project,))


def attend_kernel(
    query_t,
    key,
    value_t,
    gate_t,
    first_pass,
    bias,
    w_att_out,
    out,
    bias_t,
    scores,
    weights,
    gated,
    before=(),
):
    rows, width, cols = query_t.shape
    head_rows = bias.shape[1] // HEADS
    score_scale = LOG2_E / HEAD_DIM**0.5
    ones = jnp.ones((16, key.shape[1]), BF16)
    heads = [
        (slice(h * HEAD_DIM, (h + 1) * HEAD_DIM), slice(h * cols, (h + 1) * cols)) for h in range(HEADS)
    ]

    def score(i):
        blocks = []
        for mine, _ in heads:
            above = jnp.zeros((mine.start, cols), BF16)
            below = jnp.zeros((width - mine.stop, cols), BF16)
            parts = [p for p in (above, query_t[i, mine, :], below) if p.shape[0]]
            blocks.append(jnp.concatenate(parts, axis=0))
        scores[i % 2] = dot(key[i], jnp.concatenate(blocks, axis=1)) * score_scale

    def soften(i):
        for _, span in heads:
            biased = scores[i % 2, :, span] + bias_t[:, span]
            peak = jnp.max(biased, axis=0, keepdims=True)
            weights[i % 2, :, span] = jnp.exp2(biased - peak).astype(BF16)

    def collect(i):
        for mine, span in heads:
            values = jnp.concatenate([value_t[i, mine, :], ones], axis=0)
            summed = dot(values, weights[i % 2, :, span])
            share = 1.0 / summed[HEAD_DIM : HEAD_DIM + 1]
            gated[i % 2, mine, :] = summed[:HEAD_DIM] * share * gate_t[i, mine, :]

    def finish(i):
        turned = gated[i % 2].T.astype(BF16)
        out[i] = (first_pass[i] + dot(turned, w_att_out[...])).astype(BF16)

    for head, (_, span) in enumerate(heads):
        parts = [
            bias[slot("bias", owner, bias.shape[0])].astype(F32)[head * head_rows : (head + 1) * head_rows]
            for owner in range(bias.shape[0])
        ]
        bias_t[:, span] = jnp.concatenate(parts, axis=0).T * LOG2_E
    pipeline(rows, *before, score, soften, collect, finish)


def call(kernel, outs, scratch, flops, *operands, fetched=0):
    vmem = pl.BlockSpec(memory_space=pltpu.VMEM)
    far = pl.BlockSpec(memory_space=pltpu.HBM)
    shapes = [jax.ShapeDtypeStruct(shape, dtype) for shape, dtype in outs]
    moved = sum(o.size * o.dtype.itemsize for o in operands)
    operands = [
        pltpu.with_memory_space_constraint(o, pltpu.HBM) if n < fetched else o
        for n, o in enumerate(operands)
    ]
    got = pl.pallas_call(
        kernel,
        out_shape=shapes,
        in_specs=[far] * fetched + [vmem] * (len(operands) - fetched),
        out_specs=[vmem] * len(shapes),
        scratch_shapes=[pltpu.VMEM(*s) if isinstance(s, tuple) else s for s in scratch],
        compiler_params=pltpu.CompilerParams(vmem_limit_bytes=48 * 2**20),
        cost_estimate=pl.CostEstimate(flops=flops, bytes_accessed=moved, transcendentals=0),
    )(*operands)
    return got if len(got) > 1 else got[0]


def body(
    pair_rep,
    w_left,
    w_left_gate,
    w_right,
    w_right_gate,
    w_tri_gate,
    w_tri_out,
    w_query,
    w_key,
    w_value,
    w_bias,
    w_att_gate,
    w_att_out,
):
    rows, cols, width = pair_rep.shape
    channels = w_left.shape[1]
    owners, col_parts = lax.axis_size("row"), lax.axis_size("col")
    own = channels // owners
    residues = owners * rows
    cells = rows * cols

    edges, gate, w_tri_out, w_query, w_key, w_value, w_att_gate, w_att_out, w_bias_t = call(
        edges_kernel,
        [
            ((owners, own * 2 * rows, cols), BF16),
            ((rows, cols, width), F32),
            *[(w.shape, BF16) for w in (w_tri_out, w_query, w_key, w_value, w_att_gate, w_att_out)],
            (w_bias.shape[::-1], BF16),
        ],
        [
            (pair_rep.shape, BF16),
            ((5, width, channels), BF16),
            (pair_rep.shape, BF16),
            ((cols // LANES, channels * 2 * rows, LANES), F32),
            pltpu.SemaphoreType.DMA((13,)),
        ],
        10 * cells * width * channels,
        pair_rep,
        w_left,
        w_left_gate,
        w_right,
        w_right_gate,
        w_tri_gate,
        w_tri_out,
        w_query,
        w_key,
        w_value,
        w_att_gate,
        w_att_out,
        w_bias.T,
        fetched=13,
    )
    spread = swap("edges", edges)
    flops = 2 * own * residues * residues * cols
    if col_parts == 1:
        summed = call(
            functools.partial(triangle_kernel, rows),
            [((owners, own * rows, residues), BF16)],
            [],
            flops,
            spread,
        )
    else:
        partial_sums = call(
            functools.partial(partial_kernel, rows),
            [((own, residues, residues), F32)],
            [],
            flops,
            spread,
        )
        summed = lax.psum_scatter(partial_sums, "col", scatter_dimension=2, tiled=True).astype(BF16)
        summed = by_slot("triangle", summed.reshape(own, owners, rows, cols).swapaxes(0, 1))
        summed = summed.reshape(owners, own * rows, cols)
    returned = swap("triangle", summed)
    first_pass, att_norm, bias_copies = call(
        update_kernel,
        [
            ((rows, cols, width), F32),
            ((rows, cols, width), BF16),
            ((owners, HEADS * rows, cols), BF16),
        ],
        [
            ((cols // LANES, channels * rows, LANES), F32),
            ((HEADS * rows, cols), F32),
            ((2, cols, channels), BF16),
        ],
        2 * cells * channels * width,
        returned,
        gate,
        pair_rep,
        w_tri_out,
        w_bias_t,
    )
    bias = swap("bias", bias_copies)
    projected = [
        ((rows, width, cols), BF16),
        ((rows, cols, width), BF16),
        ((rows, width, cols), BF16),
        ((rows, width, cols), F32),
    ]
    projecting = (att_norm, w_query, w_key, w_value, w_att_gate)
    residues = cols * col_parts
    out = [((rows, cols, width), BF16)]
    held = [
        ((residues, HEADS * cols), F32),
        ((2, residues, HEADS * cols), F32),
        ((2, residues, HEADS * cols), BF16),
        ((2, width, cols), F32),
    ]
    project_flops, attend_flops = 8 * cells * width * width, 4 * cells * residues * width
    if col_parts == 1:
        flops = project_flops + attend_flops
        given = (first_pass, bias, w_att_out)
        return call(whole_kernel, out, projected + held, flops, *projecting, *given)
    query_t, key, value_t, gate_t = call(project_kernel, projected, [], project_flops, *projecting)
    bias = by_slot(
        "bias", lax.all_to_all(by_rank("bias", bias), "col", split_axis=0, concat_axis=2, tiled=True)
    )
    key = lax.all_gather(key, "col", axis=1, tiled=True)
    value_t = lax.all_gather(value_t, "col", axis=2, tiled=True)
    given = (query_t, key, value_t, gate_t, first_pass, bias, w_att_out)
    return call(attend_kernel, out, held, attend_flops, *given)


def solution(mesh):
    in_specs = (P(("grp", "row"), "col", None),) + (P(),) * 12
    out_specs = P(("grp", "row"), "col", None)
    return jax.shard_map(body, mesh=mesh, in_specs=in_specs, out_specs=out_specs, check_vma=False)
```

```python
import functools

import jax
import jax.numpy as jnp
import numpy as np
from jax import lax
from jax.experimental import pallas as pl
from jax.experimental.pallas import tpu as pltpu
from jax.sharding import PartitionSpec as P

HEADS = 4
HEAD_DIM = 32
LANES = 128
LOG2_E = 1.4426950408889634
F32 = jnp.float32
BF16 = jnp.bfloat16
NN = (((1,), (0,)), ((), ()))
NT = (((1,), (1,)), ((), ()))
TN = (((0,), (0,)), ((), ()))


def dot(left, right, dims=NN):
    return lax.dot_general(left, right, dims, preferred_element_type=F32)


def sigmoid(values):
    return 0.5 * jnp.tanh(0.5 * values) + 0.5


def twice(weight):
    zeros = jnp.zeros_like(weight)
    return jnp.concatenate(
        [jnp.concatenate([weight, zeros], axis=1), jnp.concatenate([zeros, weight], axis=1)], axis=0
    )


def listing(ranks):
    first = ranks - 1 - ranks // 4
    return [first] + [rank for rank in range(ranks - 1, -1, -1) if rank != first]


def slot(rank, ranks):
    return listing(ranks).index(rank)


def swap(blocks):
    return lax.all_to_all(
        blocks,
        "row",
        split_axis=0,
        concat_axis=0,
        axis_index_groups=[listing(blocks.shape[0])],
        tiled=True,
    )


def by_rank(blocks):
    return blocks[np.array([slot(r, blocks.shape[0]) for r in range(blocks.shape[0])])]


def by_slot(blocks):
    return blocks[np.array(listing(blocks.shape[0]))]


def lane_tiles(values):
    lanes = values.shape[1]
    return [(t, slice(t * LANES, (t + 1) * LANES)) for t in range(lanes // LANES)]


def lane_norm(values):
    centered = values - jnp.mean(values, axis=-1, keepdims=True)
    variance = jnp.mean(centered * centered, axis=-1, keepdims=True)
    return (centered * lax.rsqrt(variance + 1e-05)).astype(BF16)


def side_by_side(held, i):
    return jnp.concatenate([held[i], held[i + 1]], axis=1)


def pipeline(rows, *steps):
    for tick in range(len(rows) + len(steps) - 1):
        for late, step in enumerate(steps):
            if 0 <= tick - late < len(rows):
                step(rows[tick - late])


def edges_kernel(*refs):
    given, (out, gate, *staged), (pair, weights, normed, held, sems) = refs[:13], refs[13:22], refs[22:]
    targets = [pair, *(weights.at[n] for n in range(5)), *staged]
    copies = [
        pltpu.make_async_copy(source, target, sems.at[n])
        for n, (source, target) in enumerate(zip(given, targets))
    ]
    for copy in copies:
        copy.start()
    for copy in copies[:6]:
        copy.wait()
    rows, width = pair.shape[0], pair.shape[2]
    channels = weights.shape[2]
    cols = pair.shape[1]
    turned = jnp.concatenate([weights[n].T for n in range(4)], axis=0)
    gate_weight = twice(weights[4])

    def norm(i):
        normed[i] = lane_norm(pair[i].astype(F32))
        normed[i + 1] = lane_norm(pair[i + 1].astype(F32))

    def project(i):
        both = dot(turned, jnp.concatenate([normed[i], normed[i + 1]], axis=0), NT)
        for side in range(2):
            base = 2 * side * channels
            act = sigmoid(both[base + channels : base + 2 * channels]) * both[base : base + channels]
            for tile, lanes in lane_tiles(act):
                row, part = divmod(tile, cols // LANES)
                place = pl.ds(side * rows + i + row, channels, stride=2 * rows)
                held[part, place, :] = act[:, lanes]
        opened = sigmoid(dot(side_by_side(normed, i), gate_weight))
        gate[i] = opened[:, :width]
        gate[i + 1] = opened[:, width:]

    pipeline(range(0, rows, 2), norm, project)
    owners, block = out.shape[0], out.shape[1]
    for owner in range(owners):
        for tile, lanes in lane_tiles(pair):
            out[slot(owner, owners), :, lanes] = held[tile, owner * block : (owner + 1) * block, :].astype(BF16)
    for copy in copies[6:]:
        copy.wait()


def triangle_sides(edges, rows, channel):
    sides = [[], []]
    sources = edges.shape[0]
    for source in range(sources):
        block = edges[slot(source, sources), channel * 2 * rows : (channel + 1) * 2 * rows, :].astype(F32)
        sides[0].append(block[:rows])
        sides[1].append(block[rows:])
    return [jnp.concatenate(side, axis=0).astype(BF16) for side in sides]


def triangle_kernel(rows, edges, out):
    for pair_of in range(0, out.shape[1] // rows, 2):
        products = [dot(*triangle_sides(edges, rows, pair_of + o), NT) for o in range(2)]
        owners = out.shape[0]
        for owner in range(owners):
            mine = slice(owner * rows, (owner + 1) * rows)
            out[slot(owner, owners), pair_of * rows : (pair_of + 2) * rows, :] = jnp.concatenate(
                [p[mine] for p in products], axis=0
            ).astype(BF16)


def partial_kernel(rows, edges, out):
    for channel in range(out.shape[0]):
        out[channel] = dot(*triangle_sides(edges, rows, channel), NT)


def update_kernel(
    returned, gate, pair, w_tri_out, w_bias_t, first_pass, att_norm, bias, held, bias_held, turned
):
    rows, cols, width = pair.shape
    owners, block = returned.shape[0], returned.shape[1]
    channels = owners * block // rows
    total = jnp.zeros((rows, cols), F32)
    for owner in range(owners):
        total += jnp.sum(returned[owner].astype(F32).reshape(block // rows, rows, cols), axis=0)
    average = total / channels
    square = jnp.zeros((rows, cols), F32)
    for owner in range(owners):
        centered = returned[slot(owner, owners)].astype(F32).reshape(block // rows, rows, cols) - average
        square += jnp.sum(centered * centered, axis=0)
        for tile, lanes in lane_tiles(pair):
            held[tile, owner * block : (owner + 1) * block, :] = centered.reshape(block, cols)[:, lanes]
    scale = lax.rsqrt(square / channels + 1e-05)

    weight = twice(w_tri_out[...])

    def turn(i):
        for row in (i, i + 1):
            tri_norm = jnp.concatenate(
                [held[tile, pl.ds(row, channels, stride=rows), :] for tile, _ in lane_tiles(pair)], axis=1
            )
            turned[row % 4] = (tri_norm * scale[row : row + 1]).astype(BF16).T

    def update(i):
        both = dot(side_by_side(turned, i % 4), weight)
        first_pass[i] = pair[i].astype(F32) + gate[i] * both[:, :width]
        first_pass[i + 1] = pair[i + 1].astype(F32) + gate[i + 1] * both[:, width:]

    def norm(i):
        for row in (i, i + 1):
            att_norm[row] = lane_norm(first_pass[row])

    def project_bias(i):
        both = dot(w_bias_t[...], jnp.concatenate([att_norm[i], att_norm[i + 1]], axis=0), NT)
        for row in range(2):
            for head in range(HEADS):
                place = head * rows + i + row
                bias_held[place : place + 1, :] = both[head : head + 1, row * cols : (row + 1) * cols]

    pipeline(range(0, rows, 2), turn, update, norm, project_bias)
    rounded = bias_held[...].astype(BF16)
    for owner in range(bias.shape[0]):
        bias[owner] = rounded


def projector(att_norm, w_query, w_key, w_value, w_att_gate, query_t, key, value_t, gate_t):
    w_turned = jnp.concatenate([w[...].T for w in (w_query, w_value, w_att_gate)], axis=0)
    w_direct = twice(w_key[...])
    cols, width = att_norm.shape[1], w_query.shape[1]

    def project(i):
        if i % 2:
            return
        keys = dot(side_by_side(att_norm, i), w_direct).astype(BF16)
        turned = dot(w_turned, jnp.concatenate([att_norm[i], att_norm[i + 1]], axis=0), NT)
        for row in range(2):
            key[i + row] = keys[:, row * width : (row + 1) * width]
            mine = turned[:, row * cols : (row + 1) * cols]
            query_t[i + row] = mine[:width].astype(BF16)
            value_t[i + row] = mine[width : 2 * width].astype(BF16)
            gate_t[i + row] = sigmoid(mine[2 * width :])

    return project


def project_kernel(*refs):
    pipeline(range(refs[0].shape[0]), projector(*refs))


def whole_kernel(att_norm, w_query, w_key, w_value, w_att_gate, *refs):
    given, projected, held = refs[:4], refs[4:8], refs[8:]
    project = projector(att_norm, w_query, w_key, w_value, w_att_gate, *projected)
    attend_kernel(*projected, *given, *held, before=(project,))


def attend_kernel(
    query_t,
    key,
    value_t,
    gate_t,
    first_pass,
    bias,
    w_att_out,
    out,
    bias_t,
    scores,
    weights,
    gated,
    before=(),
):
    rows, width, cols = query_t.shape
    head_rows = bias.shape[1] // HEADS
    score_scale = LOG2_E / HEAD_DIM**0.5
    ones = jnp.ones((16, key.shape[1]), BF16)
    heads = [
        (slice(h * HEAD_DIM, (h + 1) * HEAD_DIM), slice(h * cols, (h + 1) * cols)) for h in range(HEADS)
    ]

    def score(i):
        blocks = []
        for mine, _ in heads:
            above = jnp.zeros((mine.start, cols), BF16)
            below = jnp.zeros((width - mine.stop, cols), BF16)
            parts = [p for p in (above, query_t[i, mine, :], below) if p.shape[0]]
            blocks.append(jnp.concatenate(parts, axis=0))
        scores[i % 2] = dot(key[i], jnp.concatenate(blocks, axis=1)) * score_scale

    def turn_bias():
        for head, (_, span) in enumerate(heads):
            parts = [
                bias[slot(owner, bias.shape[0])].astype(F32)[head * head_rows : (head + 1) * head_rows]
                for owner in range(bias.shape[0])
            ]
            bias_t[:, span] = jnp.concatenate(parts, axis=0).T * LOG2_E

    def soften(i):
        if i == 0:
            turn_bias()
        for _, span in heads:
            biased = scores[i % 2, :, span] + bias_t[:, span]
            peak = jnp.max(biased, axis=0, keepdims=True)
            weights[i % 2, :, span] = jnp.exp2(biased - peak).astype(BF16)

    def collect(i):
        for head in range(0, HEADS, 2):
            (first, left), (second, right) = heads[head : head + 2]
            values = jnp.concatenate([value_t[i, first.start : second.stop, :], ones], axis=0)
            summed = dot(values, weights[i % 2, :, left.start : right.stop])
            share = 1.0 / summed[2 * HEAD_DIM : 2 * HEAD_DIM + 1]
            for mine, there, lanes in (
                (first, slice(0, HEAD_DIM), slice(0, cols)),
                (second, slice(HEAD_DIM, 2 * HEAD_DIM), slice(cols, 2 * cols)),
            ):
                attended = summed[there, lanes] * share[:, lanes] * gate_t[i, mine, :]
                gated[i % 4, mine, :] = attended.astype(BF16)

    def finish(i):
        if i % 2 == 0:
            return
        turned = jnp.concatenate([gated[(i - 1) % 4].T, gated[i % 4].T], axis=1)
        both = dot(turned, w_last)
        out[i - 1] = (first_pass[i - 1] + both[:, :width]).astype(BF16)
        out[i] = (first_pass[i] + both[:, width:]).astype(BF16)

    w_last = twice(w_att_out[...])
    pipeline(range(rows), *before, score, soften, collect, finish)


def call(kernel, outs, scratch, flops, *operands, fetched=0):
    vmem = pl.BlockSpec(memory_space=pltpu.VMEM)
    far = pl.BlockSpec(memory_space=pltpu.HBM)
    shapes = [jax.ShapeDtypeStruct(shape, dtype) for shape, dtype in outs]
    moved = sum(o.size * o.dtype.itemsize for o in operands)
    operands = [
        pltpu.with_memory_space_constraint(o, pltpu.HBM) if n < fetched else o
        for n, o in enumerate(operands)
    ]
    got = pl.pallas_call(
        kernel,
        out_shape=shapes,
        in_specs=[far] * fetched + [vmem] * (len(operands) - fetched),
        out_specs=[vmem] * len(shapes),
        scratch_shapes=[pltpu.VMEM(*s) if isinstance(s, tuple) else s for s in scratch],
        compiler_params=pltpu.CompilerParams(vmem_limit_bytes=48 * 2**20),
        cost_estimate=pl.CostEstimate(flops=flops, bytes_accessed=moved, transcendentals=0),
    )(*operands)
    return got if len(got) > 1 else got[0]


def body(
    pair_rep,
    w_left,
    w_left_gate,
    w_right,
    w_right_gate,
    w_tri_gate,
    w_tri_out,
    w_query,
    w_key,
    w_value,
    w_bias,
    w_att_gate,
    w_att_out,
):
    rows, cols, width = pair_rep.shape
    channels = w_left.shape[1]
    owners, col_parts = lax.axis_size("row"), lax.axis_size("col")
    own = channels // owners
    residues = owners * rows
    cells = rows * cols

    edges, gate, w_tri_out, w_query, w_key, w_value, w_att_gate, w_att_out, w_bias_t = call(
        edges_kernel,
        [
            ((owners, own * 2 * rows, cols), BF16),
            ((rows, cols, width), F32),
            *[(w.shape, BF16) for w in (w_tri_out, w_query, w_key, w_value, w_att_gate, w_att_out)],
            (w_bias.shape[::-1], BF16),
        ],
        [
            (pair_rep.shape, BF16),
            ((5, width, channels), BF16),
            (pair_rep.shape, BF16),
            ((cols // LANES, channels * 2 * rows, LANES), F32),
            pltpu.SemaphoreType.DMA((13,)),
        ],
        10 * cells * width * channels,
        pair_rep,
        w_left,
        w_left_gate,
        w_right,
        w_right_gate,
        w_tri_gate,
        w_tri_out,
        w_query,
        w_key,
        w_value,
        w_att_gate,
        w_att_out,
        w_bias.T,
        fetched=13,
    )
    spread = swap(edges)
    flops = 2 * own * residues * residues * cols
    if col_parts == 1:
        summed = call(
            functools.partial(triangle_kernel, rows),
            [((owners, own * rows, residues), BF16)],
            [],
            flops,
            spread,
        )
    else:
        partial_sums = call(
            functools.partial(partial_kernel, rows),
            [((own, residues, residues), F32)],
            [],
            flops,
            spread,
        )
        summed = lax.psum_scatter(partial_sums, "col", scatter_dimension=2, tiled=True).astype(BF16)
        summed = by_slot(summed.reshape(own, owners, rows, cols).swapaxes(0, 1))
        summed = summed.reshape(owners, own * rows, cols)
    returned = swap(summed)
    first_pass, att_norm, bias_copies = call(
        update_kernel,
        [
            ((rows, cols, width), F32),
            ((rows, cols, width), BF16),
            ((owners, HEADS * rows, cols), BF16),
        ],
        [
            ((cols // LANES, channels * rows, LANES), F32),
            ((HEADS * rows, cols), F32),
            ((4, cols, channels), BF16),
        ],
        2 * cells * channels * width,
        returned,
        gate,
        pair_rep,
        w_tri_out,
        w_bias_t,
    )
    bias = swap(bias_copies)
    projected = [
        ((rows, width, cols), BF16),
        ((rows, cols, width), BF16),
        ((rows, width, cols), BF16),
        ((rows, width, cols), F32),
    ]
    projecting = (att_norm, w_query, w_key, w_value, w_att_gate)
    residues = cols * col_parts
    out = [((rows, cols, width), BF16)]
    held = [
        ((residues, HEADS * cols), F32),
        ((2, residues, HEADS * cols), F32),
        ((2, residues, HEADS * cols), BF16),
        ((4, width, cols), BF16),
    ]
    project_flops, attend_flops = 8 * cells * width * width, 4 * cells * residues * width
    if col_parts == 1:
        flops = project_flops + attend_flops
        given = (first_pass, bias, w_att_out)
        return call(whole_kernel, out, projected + held, flops, *projecting, *given)
    query_t, key, value_t, gate_t = call(project_kernel, projected, [], project_flops, *projecting)
    bias = by_slot(lax.all_to_all(by_rank(bias), "col", split_axis=0, concat_axis=2, tiled=True))
    key = lax.all_gather(key, "col", axis=1, tiled=True)
    value_t = lax.all_gather(value_t, "col", axis=2, tiled=True)
    given = (query_t, key, value_t, gate_t, first_pass, bias, w_att_out)
    return call(attend_kernel, out, held, attend_flops, *given)


def solution(mesh):
    in_specs = (P(("grp", "row"), "col", None),) + (P(),) * 12
    out_specs = P(("grp", "row"), "col", None)
    return jax.shard_map(body, mesh=mesh, in_specs=in_specs, out_specs=out_specs, check_vma=False)
```

```python
import functools

import jax
import jax.numpy as jnp
import numpy as np
from jax import lax
from jax.experimental import pallas as pl
from jax.experimental.pallas import tpu as pltpu
from jax.sharding import PartitionSpec as P

HEADS = 4
HEAD_DIM = 32
LANES = 128
LOG2_E = 1.4426950408889634
F32 = jnp.float32
BF16 = jnp.bfloat16
NN = (((1,), (0,)), ((), ()))
NT = (((1,), (1,)), ((), ()))
TN = (((0,), (0,)), ((), ()))


def dot(left, right, dims=NN):
    return lax.dot_general(left, right, dims, preferred_element_type=F32)


def sigmoid(values):
    return 0.5 * jnp.tanh(0.5 * values) + 0.5


def twice(weight):
    zeros = jnp.zeros_like(weight)
    return jnp.concatenate(
        [jnp.concatenate([weight, zeros], axis=1), jnp.concatenate([zeros, weight], axis=1)], axis=0
    )


def listing(ranks):
    first = ranks - 1 - ranks // 4
    return [first] + [rank for rank in range(ranks - 1, -1, -1) if rank != first]


def slot(rank, ranks):
    return listing(ranks).index(rank)


def swap(blocks, ranks):
    members = blocks.shape[0]
    order = listing(members)
    groups = [[first + member for member in order] for first in range(0, ranks, members)]
    return lax.all_to_all(
        blocks, "row", split_axis=0, concat_axis=0, axis_index_groups=groups, tiled=True
    )


def by_rank(blocks):
    return blocks[np.array([slot(r, blocks.shape[0]) for r in range(blocks.shape[0])])]


def by_slot(blocks):
    return blocks[np.array(listing(blocks.shape[0]))]


def lane_tiles(values):
    lanes = values.shape[1]
    return [(t, slice(t * LANES, (t + 1) * LANES)) for t in range(lanes // LANES)]


def lane_norm(values):
    centered = values - jnp.mean(values, axis=-1, keepdims=True)
    variance = jnp.mean(centered * centered, axis=-1, keepdims=True)
    return (centered * lax.rsqrt(variance + 1e-05)).astype(BF16)


def side_by_side(held, i):
    return jnp.concatenate([held[i], held[i + 1]], axis=1)


def pipeline(rows, *steps):
    for tick in range(len(rows) + len(steps) - 1):
        for late, step in enumerate(steps):
            if 0 <= tick - late < len(rows):
                step(rows[tick - late])


def edges_kernel(*refs):
    given, (left, right, gate, *staged) = refs[:13], refs[13:23]
    pair, weights, normed, held, sems = refs[23:]
    targets = [pair, *(weights.at[n] for n in range(5)), *staged]
    copies = [
        pltpu.make_async_copy(source, target, sems.at[n])
        for n, (source, target) in enumerate(zip(given, targets))
    ]
    for copy in copies:
        copy.start()
    for copy in copies[:6]:
        copy.wait()
    rows, width = pair.shape[0], pair.shape[2]
    channels = weights.shape[2]
    cols = pair.shape[1]
    turned = jnp.concatenate([weights[n].T for n in range(4)], axis=0)
    gate_weight = twice(weights[4])

    def norm(i):
        normed[i] = lane_norm(pair[i].astype(F32))
        normed[i + 1] = lane_norm(pair[i + 1].astype(F32))

    def project(i):
        both = dot(turned, jnp.concatenate([normed[i], normed[i + 1]], axis=0), NT)
        for side in range(2):
            base = 2 * side * channels
            act = sigmoid(both[base + channels : base + 2 * channels]) * both[base : base + channels]
            for tile, lanes in lane_tiles(act):
                row, part = divmod(tile, cols // LANES)
                held[part, side, pl.ds(i + row, channels, stride=rows), :] = act[:, lanes]
        opened = sigmoid(dot(side_by_side(normed, i), gate_weight))
        gate[i] = opened[:, :width]
        gate[i + 1] = opened[:, width:]

    pipeline(range(0, rows, 2), norm, project)
    half, block = left.shape[0], left.shape[1]
    for member in range(half):
        mine = slice(member * block, (member + 1) * block)
        for tile, lanes in lane_tiles(pair):
            left[slot(member, half), :, lanes] = held[tile, 0, mine, :].astype(BF16)
            sent = held[tile, 1, mine, :].astype(BF16)
            for owner in range(member, right.shape[0], half):
                right[slot(owner, right.shape[0]), :, lanes] = sent
    for copy in copies[6:]:
        copy.wait()


def channel_rows(edges, rows, channel):
    sources = edges.shape[0]
    mine = slice(channel * rows, (channel + 1) * rows)
    both = slice(channel // 2 * 2 * rows, (channel // 2 + 1) * 2 * rows)
    inner = slice(mine.start - both.start, mine.stop - both.start)
    parts = [edges[slot(r, sources), both, :].astype(F32)[inner] for r in range(sources)]
    return jnp.concatenate(parts, axis=0).astype(BF16)


def triangle_product(left, right, rows, channel):
    return dot(channel_rows(left, rows, channel), channel_rows(right, rows, channel), NT)


def triangle_kernel(rows, left, right, out):
    owners = out.shape[0]
    for channel in range(0, out.shape[1] // rows, 2):
        products = [triangle_product(left, right, rows, channel + o) for o in range(2)]
        for owner in range(owners):
            mine = slice(owner * rows, (owner + 1) * rows)
            out[slot(owner, owners), channel * rows : (channel + 2) * rows, :] = jnp.concatenate(
                [p[mine] for p in products], axis=0
            ).astype(BF16)


def partial_kernel(rows, left, right, out):
    for channel in range(out.shape[0]):
        out[channel] = triangle_product(left, right, rows, channel)


def update_kernel(
    returned, gate, pair, w_tri_out, w_bias_t, first_pass, att_norm, bias, held, bias_held, turned
):
    rows, cols, width = pair.shape
    owners, block = returned.shape[0], returned.shape[1]
    channels = owners * block // rows
    total = jnp.zeros((rows, cols), F32)
    for owner in range(owners):
        total += jnp.sum(returned[owner].astype(F32).reshape(block // rows, rows, cols), axis=0)
    average = total / channels
    square = jnp.zeros((rows, cols), F32)
    for owner in range(owners):
        centered = returned[slot(owner, owners)].astype(F32).reshape(block // rows, rows, cols) - average
        square += jnp.sum(centered * centered, axis=0)
        for tile, lanes in lane_tiles(pair):
            held[tile, owner * block : (owner + 1) * block, :] = centered.reshape(block, cols)[:, lanes]
    scale = lax.rsqrt(square / channels + 1e-05)

    weight = twice(w_tri_out[...])

    def turn(i):
        for row in (i, i + 1):
            tri_norm = jnp.concatenate(
                [held[tile, pl.ds(row, channels, stride=rows), :] for tile, _ in lane_tiles(pair)], axis=1
            )
            turned[row % 4] = (tri_norm * scale[row : row + 1]).astype(BF16).T

    def update(i):
        both = dot(side_by_side(turned, i % 4), weight)
        first_pass[i] = pair[i].astype(F32) + gate[i] * both[:, :width]
        first_pass[i + 1] = pair[i + 1].astype(F32) + gate[i + 1] * both[:, width:]

    def norm(i):
        for row in (i, i + 1):
            att_norm[row] = lane_norm(first_pass[row])

    def project_bias(i):
        both = dot(w_bias_t[...], jnp.concatenate([att_norm[i], att_norm[i + 1]], axis=0), NT)
        for row in range(2):
            for head in range(HEADS):
                place = head * rows + i + row
                bias_held[place : place + 1, :] = both[head : head + 1, row * cols : (row + 1) * cols]

    pipeline(range(0, rows, 2), turn, update, norm, project_bias)
    rounded = bias_held[...].astype(BF16)
    for owner in range(bias.shape[0]):
        bias[owner] = rounded


def projector(att_norm, w_query, w_key, w_value, w_att_gate, query_t, key, value_t, gate_t):
    w_turned = jnp.concatenate([w[...].T for w in (w_query, w_value, w_att_gate)], axis=0)
    w_direct = twice(w_key[...])
    cols, width = att_norm.shape[1], w_query.shape[1]

    def project(i):
        if i % 2:
            return
        keys = dot(side_by_side(att_norm, i), w_direct).astype(BF16)
        turned = dot(w_turned, jnp.concatenate([att_norm[i], att_norm[i + 1]], axis=0), NT)
        for row in range(2):
            key[i + row] = keys[:, row * width : (row + 1) * width]
            mine = turned[:, row * cols : (row + 1) * cols]
            query_t[i + row] = mine[:width].astype(BF16)
            value_t[i + row] = mine[width : 2 * width].astype(BF16)
            gate_t[i + row] = sigmoid(mine[2 * width :])

    return project


def project_kernel(*refs):
    pipeline(range(refs[0].shape[0]), projector(*refs))


def whole_kernel(att_norm, w_query, w_key, w_value, w_att_gate, *refs):
    given, projected, held = refs[:4], refs[4:8], refs[8:]
    project = projector(att_norm, w_query, w_key, w_value, w_att_gate, *projected)
    attend_kernel(*projected, *given, *held, before=(project,))


def attend_kernel(
    query_t,
    key,
    value_t,
    gate_t,
    first_pass,
    bias,
    w_att_out,
    out,
    bias_t,
    scores,
    weights,
    gated,
    before=(),
):
    rows, width, cols = query_t.shape
    head_rows = bias.shape[1] // HEADS
    score_scale = LOG2_E / HEAD_DIM**0.5
    ones = jnp.ones((16, key.shape[1]), BF16)
    heads = [
        (slice(h * HEAD_DIM, (h + 1) * HEAD_DIM), slice(h * cols, (h + 1) * cols)) for h in range(HEADS)
    ]

    def score(i):
        blocks = []
        for mine, _ in heads:
            above = jnp.zeros((mine.start, cols), BF16)
            below = jnp.zeros((width - mine.stop, cols), BF16)
            parts = [p for p in (above, query_t[i, mine, :], below) if p.shape[0]]
            blocks.append(jnp.concatenate(parts, axis=0))
        scores[i % 2] = dot(key[i], jnp.concatenate(blocks, axis=1)) * score_scale

    def turn_bias():
        for head, (_, span) in enumerate(heads):
            parts = [
                bias[slot(owner, bias.shape[0])].astype(F32)[head * head_rows : (head + 1) * head_rows]
                for owner in range(bias.shape[0])
            ]
            bias_t[:, span] = jnp.concatenate(parts, axis=0).T * LOG2_E

    def soften(i):
        if i == 0:
            turn_bias()
        for _, span in heads:
            biased = scores[i % 2, :, span] + bias_t[:, span]
            peak = jnp.max(biased, axis=0, keepdims=True)
            weights[i % 2, :, span] = jnp.exp2(biased - peak).astype(BF16)

    def collect(i):
        for head in range(0, HEADS, 2):
            (first, left), (second, right) = heads[head : head + 2]
            values = jnp.concatenate([value_t[i, first.start : second.stop, :], ones], axis=0)
            summed = dot(values, weights[i % 2, :, left.start : right.stop])
            share = 1.0 / summed[2 * HEAD_DIM : 2 * HEAD_DIM + 1]
            for mine, there, lanes in (
                (first, slice(0, HEAD_DIM), slice(0, cols)),
                (second, slice(HEAD_DIM, 2 * HEAD_DIM), slice(cols, 2 * cols)),
            ):
                attended = summed[there, lanes] * share[:, lanes] * gate_t[i, mine, :]
                gated[i % 4, mine, :] = attended.astype(BF16)

    def finish(i):
        if i % 2 == 0:
            return
        turned = jnp.concatenate([gated[(i - 1) % 4].T, gated[i % 4].T], axis=1)
        both = dot(turned, w_last)
        out[i - 1] = (first_pass[i - 1] + both[:, :width]).astype(BF16)
        out[i] = (first_pass[i] + both[:, width:]).astype(BF16)

    w_last = twice(w_att_out[...])
    pipeline(range(rows), *before, score, soften, collect, finish)


def call(kernel, outs, scratch, flops, *operands, fetched=0):
    vmem = pl.BlockSpec(memory_space=pltpu.VMEM)
    far = pl.BlockSpec(memory_space=pltpu.HBM)
    shapes = [jax.ShapeDtypeStruct(shape, dtype) for shape, dtype in outs]
    moved = sum(o.size * o.dtype.itemsize for o in operands)
    operands = [
        pltpu.with_memory_space_constraint(o, pltpu.HBM) if n < fetched else o
        for n, o in enumerate(operands)
    ]
    got = pl.pallas_call(
        kernel,
        out_shape=shapes,
        in_specs=[far] * fetched + [vmem] * (len(operands) - fetched),
        out_specs=[vmem] * len(shapes),
        scratch_shapes=[pltpu.VMEM(*s) if isinstance(s, tuple) else s for s in scratch],
        compiler_params=pltpu.CompilerParams(vmem_limit_bytes=48 * 2**20),
        cost_estimate=pl.CostEstimate(flops=flops, bytes_accessed=moved, transcendentals=0),
    )(*operands)
    return got if len(got) > 1 else got[0]


def body(
    pair_rep,
    w_left,
    w_left_gate,
    w_right,
    w_right_gate,
    w_tri_gate,
    w_tri_out,
    w_query,
    w_key,
    w_value,
    w_bias,
    w_att_gate,
    w_att_out,
):
    rows, cols, width = pair_rep.shape
    channels = w_left.shape[1]
    owners, col_parts = lax.axis_size("row"), lax.axis_size("col")
    half = owners // 2
    own = channels // half
    residues = owners * rows
    cells = rows * cols

    left, right, gate, w_tri_out, w_query, w_key, w_value, w_att_gate, w_att_out, w_bias_t = call(
        edges_kernel,
        [
            ((half, own * rows, cols), BF16),
            ((owners, own * rows, cols), BF16),
            ((rows, cols, width), F32),
            *[(w.shape, BF16) for w in (w_tri_out, w_query, w_key, w_value, w_att_gate, w_att_out)],
            (w_bias.shape[::-1], BF16),
        ],
        [
            (pair_rep.shape, BF16),
            ((5, width, channels), BF16),
            (pair_rep.shape, BF16),
            ((cols // LANES, 2, channels * rows, LANES), F32),
            pltpu.SemaphoreType.DMA((13,)),
        ],
        10 * cells * width * channels,
        pair_rep,
        w_left,
        w_left_gate,
        w_right,
        w_right_gate,
        w_tri_gate,
        w_tri_out,
        w_query,
        w_key,
        w_value,
        w_att_gate,
        w_att_out,
        w_bias.T,
        fetched=13,
    )
    right = swap(right, owners)
    left = swap(left, owners)
    flops = 2 * own * half * rows * residues * cols
    if col_parts == 1:
        summed = call(
            functools.partial(triangle_kernel, rows),
            [((half, own * rows, residues), BF16)],
            [],
            flops,
            left,
            right,
        )
    else:
        partial_sums = call(
            functools.partial(partial_kernel, rows),
            [((own, half * rows, residues), F32)],
            [],
            flops,
            left,
            right,
        )
        summed = lax.psum_scatter(partial_sums, "col", scatter_dimension=2, tiled=True).astype(BF16)
        summed = by_slot(summed.reshape(own, half, rows, cols).swapaxes(0, 1))
        summed = summed.reshape(half, own * rows, cols)
    returned = swap(summed, owners)
    first_pass, att_norm, bias_copies = call(
        update_kernel,
        [
            ((rows, cols, width), F32),
            ((rows, cols, width), BF16),
            ((owners, HEADS * rows, cols), BF16),
        ],
        [
            ((cols // LANES, channels * rows, LANES), F32),
            ((HEADS * rows, cols), F32),
            ((4, cols, channels), BF16),
        ],
        2 * cells * channels * width,
        returned,
        gate,
        pair_rep,
        w_tri_out,
        w_bias_t,
    )
    bias = swap(bias_copies, owners)
    projected = [
        ((rows, width, cols), BF16),
        ((rows, cols, width), BF16),
        ((rows, width, cols), BF16),
        ((rows, width, cols), F32),
    ]
    projecting = (att_norm, w_query, w_key, w_value, w_att_gate)
    residues = cols * col_parts
    out = [((rows, cols, width), BF16)]
    held = [
        ((residues, HEADS * cols), F32),
        ((2, residues, HEADS * cols), F32),
        ((2, residues, HEADS * cols), BF16),
        ((4, width, cols), BF16),
    ]
    project_flops, attend_flops = 8 * cells * width * width, 4 * cells * residues * width
    if col_parts == 1:
        flops = project_flops + attend_flops
        given = (first_pass, bias, w_att_out)
        return call(whole_kernel, out, projected + held, flops, *projecting, *given)
    query_t, key, value_t, gate_t = call(project_kernel, projected, [], project_flops, *projecting)
    bias = by_slot(lax.all_to_all(by_rank(bias), "col", split_axis=0, concat_axis=2, tiled=True))
    key = lax.all_gather(key, "col", axis=1, tiled=True)
    value_t = lax.all_gather(value_t, "col", axis=2, tiled=True)
    given = (query_t, key, value_t, gate_t, first_pass, bias, w_att_out)
    return call(attend_kernel, out, held, attend_flops, *given)


def solution(mesh):
    in_specs = (P(("grp", "row"), "col", None),) + (P(),) * 12
    out_specs = P(("grp", "row"), "col", None)
    return jax.shard_map(body, mesh=mesh, in_specs=in_specs, out_specs=out_specs, check_vma=False)
```

```python
import functools

import jax
import jax.numpy as jnp
import numpy as np
from jax import lax
from jax.experimental import pallas as pl
from jax.experimental.pallas import tpu as pltpu
from jax.sharding import PartitionSpec as P

HEADS = 4
HEAD_DIM = 32
LANES = 128
LOG2_E = 1.4426950408889634
F32 = jnp.float32
BF16 = jnp.bfloat16
NN = (((1,), (0,)), ((), ()))
NT = (((1,), (1,)), ((), ()))
TN = (((0,), (0,)), ((), ()))


def dot(left, right, dims=NN):
    return lax.dot_general(left, right, dims, preferred_element_type=F32)


def sigmoid(values):
    return 0.5 * jnp.tanh(0.5 * values) + 0.5


def twice(weight):
    zeros = jnp.zeros_like(weight)
    return jnp.concatenate(
        [jnp.concatenate([weight, zeros], axis=1), jnp.concatenate([zeros, weight], axis=1)], axis=0
    )


def listing(ranks):
    first = ranks - 1 - ranks // 4
    return [first] + [rank for rank in range(ranks - 1, -1, -1) if rank != first]


def slot(rank, ranks):
    return listing(ranks).index(rank)


def swap(blocks, ranks):
    members = blocks.shape[0]
    order = listing(members)
    groups = [[first + member for member in order] for first in range(0, ranks, members)]
    return lax.all_to_all(
        blocks, "row", split_axis=0, concat_axis=0, axis_index_groups=groups, tiled=True
    )


def by_rank(blocks):
    return blocks[np.array([slot(r, blocks.shape[0]) for r in range(blocks.shape[0])])]


def by_slot(blocks):
    return blocks[np.array(listing(blocks.shape[0]))]


def lane_tiles(values):
    lanes = values.shape[1]
    return [(t, slice(t * LANES, (t + 1) * LANES)) for t in range(lanes // LANES)]


def lane_norm(values):
    centered = values - jnp.mean(values, axis=-1, keepdims=True)
    variance = jnp.mean(centered * centered, axis=-1, keepdims=True)
    return (centered * lax.rsqrt(variance + 1e-05)).astype(BF16)


def side_by_side(held, i):
    return jnp.concatenate([held[i], held[i + 1]], axis=1)


def pipeline(rows, *steps):
    for tick in range(len(rows) + len(steps) - 1):
        for late, step in enumerate(steps):
            if 0 <= tick - late < len(rows):
                step(rows[tick - late])


def gated_edges(normed, weight, weight_gate, held):
    rows, cols = normed.shape[0], normed.shape[1]
    channels = weight.shape[1]
    turned = jnp.concatenate([weight[...].T, weight_gate[...].T], axis=0)

    def project(i):
        both = dot(turned, jnp.concatenate([normed[i], normed[i + 1]], axis=0), NT)
        act = sigmoid(both[channels:]) * both[:channels]
        for tile, lanes in lane_tiles(act):
            row, part = divmod(tile, cols // LANES)
            held[part, pl.ds(i + row, channels, stride=rows), :] = act[:, lanes]

    return project


def deal(held, out, members):
    owners, block = out.shape[0], out.shape[1]
    for member in range(members):
        for part in range(held.shape[0]):
            sent = held[part, member * block : (member + 1) * block, :].astype(BF16)
            for owner in range(member, owners, members):
                out[slot(owner, owners), :, part * LANES : (part + 1) * LANES] = sent


def right_kernel(members, *refs):
    given, (right, normed, *staged), (pair, w_right, w_right_gate, held, sems) = refs[:13], refs[13:25], refs[25:]
    targets = [pair, w_right, w_right_gate, *staged]
    copies = [
        pltpu.make_async_copy(source, target, sems.at[n])
        for n, (source, target) in enumerate(zip(given, targets))
    ]
    for copy in copies:
        copy.start()
    for copy in copies[:3]:
        copy.wait()

    def norm(i):
        normed[i] = lane_norm(pair[i].astype(F32))
        normed[i + 1] = lane_norm(pair[i + 1].astype(F32))

    pipeline(range(0, pair.shape[0], 2), norm, gated_edges(normed, w_right, w_right_gate, held))
    deal(held, right, members)
    for copy in copies[3:]:
        copy.wait()


def left_kernel(normed, w_left, w_left_gate, w_tri_gate, left, gate, held):
    width = w_tri_gate.shape[1]
    gate_weight = twice(w_tri_gate[...])

    def open_gate(i):
        opened = sigmoid(dot(side_by_side(normed, i), gate_weight))
        gate[i] = opened[:, :width]
        gate[i + 1] = opened[:, width:]

    step = gated_edges(normed, w_left, w_left_gate, held)
    pipeline(range(0, normed.shape[0], 2), step, open_gate)
    deal(held, left, left.shape[0])


def channel_rows(edges, rows, channel):
    sources = edges.shape[0]
    mine = slice(channel * rows, (channel + 1) * rows)
    both = slice(channel // 2 * 2 * rows, (channel // 2 + 1) * 2 * rows)
    inner = slice(mine.start - both.start, mine.stop - both.start)
    parts = [edges[slot(r, sources), both, :].astype(F32)[inner] for r in range(sources)]
    return jnp.concatenate(parts, axis=0).astype(BF16)


def triangle_product(left, right, rows, channel):
    return dot(channel_rows(left, rows, channel), channel_rows(right, rows, channel), NT)


def triangle_kernel(rows, left, right, out):
    owners = out.shape[0]
    for channel in range(0, out.shape[1] // rows, 2):
        products = [triangle_product(left, right, rows, channel + o) for o in range(2)]
        for owner in range(owners):
            mine = slice(owner * rows, (owner + 1) * rows)
            out[slot(owner, owners), channel * rows : (channel + 2) * rows, :] = jnp.concatenate(
                [p[mine] for p in products], axis=0
            ).astype(BF16)


def partial_kernel(rows, left, right, out):
    for channel in range(out.shape[0]):
        out[channel] = triangle_product(left, right, rows, channel)


def update_kernel(
    returned, gate, pair, w_tri_out, w_bias_t, first_pass, att_norm, bias, held, bias_held, turned
):
    rows, cols, width = pair.shape
    owners, block = returned.shape[0], returned.shape[1]
    channels = owners * block // rows
    total = jnp.zeros((rows, cols), F32)
    for owner in range(owners):
        total += jnp.sum(returned[owner].astype(F32).reshape(block // rows, rows, cols), axis=0)
    average = total / channels
    square = jnp.zeros((rows, cols), F32)
    for owner in range(owners):
        centered = returned[slot(owner, owners)].astype(F32).reshape(block // rows, rows, cols) - average
        square += jnp.sum(centered * centered, axis=0)
        for tile, lanes in lane_tiles(pair):
            held[tile, owner * block : (owner + 1) * block, :] = centered.reshape(block, cols)[:, lanes]
    scale = lax.rsqrt(square / channels + 1e-05)

    weight = twice(w_tri_out[...])

    def turn(i):
        for row in (i, i + 1):
            tri_norm = jnp.concatenate(
                [held[tile, pl.ds(row, channels, stride=rows), :] for tile, _ in lane_tiles(pair)], axis=1
            )
            turned[row % 4] = (tri_norm * scale[row : row + 1]).astype(BF16).T

    def update(i):
        both = dot(side_by_side(turned, i % 4), weight)
        first_pass[i] = pair[i].astype(F32) + gate[i] * both[:, :width]
        first_pass[i + 1] = pair[i + 1].astype(F32) + gate[i + 1] * both[:, width:]

    def norm(i):
        for row in (i, i + 1):
            att_norm[row] = lane_norm(first_pass[row])

    def project_bias(i):
        both = dot(w_bias_t[...], jnp.concatenate([att_norm[i], att_norm[i + 1]], axis=0), NT)
        for row in range(2):
            for head in range(HEADS):
                place = head * rows + i + row
                bias_held[place : place + 1, :] = both[head : head + 1, row * cols : (row + 1) * cols]

    pipeline(range(0, rows, 2), turn, update, norm, project_bias)
    rounded = bias_held[...].astype(BF16)
    for owner in range(bias.shape[0]):
        bias[owner] = rounded


def projector(att_norm, w_query, w_key, w_value, w_att_gate, query_t, key, value_t, gate_t):
    w_turned = jnp.concatenate([w[...].T for w in (w_query, w_value, w_att_gate)], axis=0)
    w_direct = twice(w_key[...])
    cols, width = att_norm.shape[1], w_query.shape[1]

    def project(i):
        if i % 2:
            return
        keys = dot(side_by_side(att_norm, i), w_direct).astype(BF16)
        turned = dot(w_turned, jnp.concatenate([att_norm[i], att_norm[i + 1]], axis=0), NT)
        for row in range(2):
            key[i + row] = keys[:, row * width : (row + 1) * width]
            mine = turned[:, row * cols : (row + 1) * cols]
            query_t[i + row] = mine[:width].astype(BF16)
            value_t[i + row] = mine[width : 2 * width].astype(BF16)
            gate_t[i + row] = sigmoid(mine[2 * width :])

    return project


def project_kernel(*refs):
    pipeline(range(refs[0].shape[0]), projector(*refs))


def whole_kernel(att_norm, w_query, w_key, w_value, w_att_gate, *refs):
    given, projected, held = refs[:4], refs[4:8], refs[8:]
    project = projector(att_norm, w_query, w_key, w_value, w_att_gate, *projected)
    attend_kernel(*projected, *given, *held, before=(project,))


def attend_kernel(
    query_t,
    key,
    value_t,
    gate_t,
    first_pass,
    bias,
    w_att_out,
    out,
    bias_t,
    scores,
    weights,
    gated,
    before=(),
):
    rows, width, cols = query_t.shape
    head_rows = bias.shape[1] // HEADS
    score_scale = LOG2_E / HEAD_DIM**0.5
    ones = jnp.ones((16, key.shape[1]), BF16)
    heads = [
        (slice(h * HEAD_DIM, (h + 1) * HEAD_DIM), slice(h * cols, (h + 1) * cols)) for h in range(HEADS)
    ]

    def score(i):
        blocks = []
        for mine, _ in heads:
            above = jnp.zeros((mine.start, cols), BF16)
            below = jnp.zeros((width - mine.stop, cols), BF16)
            parts = [p for p in (above, query_t[i, mine, :], below) if p.shape[0]]
            blocks.append(jnp.concatenate(parts, axis=0))
        scores[i % 2] = dot(key[i], jnp.concatenate(blocks, axis=1)) * score_scale

    def turn_bias():
        for head, (_, span) in enumerate(heads):
            parts = [
                bias[slot(owner, bias.shape[0])].astype(F32)[head * head_rows : (head + 1) * head_rows]
                for owner in range(bias.shape[0])
            ]
            bias_t[:, span] = jnp.concatenate(parts, axis=0).T * LOG2_E

    def soften(i):
        if i == 0:
            turn_bias()
        for _, span in heads:
            biased = scores[i % 2, :, span] + bias_t[:, span]
            peak = jnp.max(biased, axis=0, keepdims=True)
            weights[i % 2, :, span] = jnp.exp2(biased - peak).astype(BF16)

    def collect(i):
        for head in range(0, HEADS, 2):
            (first, left), (second, right) = heads[head : head + 2]
            values = jnp.concatenate([value_t[i, first.start : second.stop, :], ones], axis=0)
            summed = dot(values, weights[i % 2, :, left.start : right.stop])
            share = 1.0 / summed[2 * HEAD_DIM : 2 * HEAD_DIM + 1]
            for mine, there, lanes in (
                (first, slice(0, HEAD_DIM), slice(0, cols)),
                (second, slice(HEAD_DIM, 2 * HEAD_DIM), slice(cols, 2 * cols)),
            ):
                attended = summed[there, lanes] * share[:, lanes] * gate_t[i, mine, :]
                gated[i % 4, mine, :] = attended.astype(BF16)

    def finish(i):
        if i % 2 == 0:
            return
        turned = jnp.concatenate([gated[(i - 1) % 4].T, gated[i % 4].T], axis=1)
        both = dot(turned, w_last)
        out[i - 1] = (first_pass[i - 1] + both[:, :width]).astype(BF16)
        out[i] = (first_pass[i] + both[:, width:]).astype(BF16)

    w_last = twice(w_att_out[...])
    pipeline(range(rows), *before, score, soften, collect, finish)


def call(kernel, outs, scratch, flops, *operands, fetched=0):
    vmem = pl.BlockSpec(memory_space=pltpu.VMEM)
    far = pl.BlockSpec(memory_space=pltpu.HBM)
    shapes = [jax.ShapeDtypeStruct(shape, dtype) for shape, dtype in outs]
    moved = sum(o.size * o.dtype.itemsize for o in operands)
    operands = [
        pltpu.with_memory_space_constraint(o, pltpu.HBM) if n < fetched else o
        for n, o in enumerate(operands)
    ]
    got = pl.pallas_call(
        kernel,
        out_shape=shapes,
        in_specs=[far] * fetched + [vmem] * (len(operands) - fetched),
        out_specs=[vmem] * len(shapes),
        scratch_shapes=[pltpu.VMEM(*s) if isinstance(s, tuple) else s for s in scratch],
        compiler_params=pltpu.CompilerParams(vmem_limit_bytes=48 * 2**20),
        cost_estimate=pl.CostEstimate(flops=flops, bytes_accessed=moved, transcendentals=0),
    )(*operands)
    return got if len(got) > 1 else got[0]


def body(
    pair_rep,
    w_left,
    w_left_gate,
    w_right,
    w_right_gate,
    w_tri_gate,
    w_tri_out,
    w_query,
    w_key,
    w_value,
    w_bias,
    w_att_gate,
    w_att_out,
):
    rows, cols, width = pair_rep.shape
    channels = w_left.shape[1]
    owners, col_parts = lax.axis_size("row"), lax.axis_size("col")
    half = owners // 2
    own = channels // half
    residues = owners * rows
    cells = rows * cols

    later = (w_left, w_left_gate, w_tri_gate, w_tri_out, w_query, w_key, w_value, w_att_gate, w_att_out)
    right, normed, *later, w_bias_t = call(
        functools.partial(right_kernel, half),
        [
            ((owners, own * rows, cols), BF16),
            (pair_rep.shape, BF16),
            *[(w.shape, BF16) for w in later],
            (w_bias.shape[::-1], BF16),
        ],
        [
            (pair_rep.shape, BF16),
            (w_right.shape, BF16),
            (w_right_gate.shape, BF16),
            ((cols // LANES, channels * rows, LANES), F32),
            pltpu.SemaphoreType.DMA((13,)),
        ],
        4 * cells * width * channels,
        pair_rep,
        w_right,
        w_right_gate,
        *later,
        w_bias.T,
        fetched=13,
    )
    w_left, w_left_gate, w_tri_gate, w_tri_out, w_query, w_key, w_value, w_att_gate, w_att_out = later
    right = swap(right, owners)
    left, gate = call(
        left_kernel,
        [((half, own * rows, cols), BF16), ((rows, cols, width), F32)],
        [((cols // LANES, channels * rows, LANES), F32)],
        6 * cells * width * channels,
        normed,
        w_left,
        w_left_gate,
        w_tri_gate,
    )
    left = swap(left, owners)
    flops = 2 * own * half * rows * residues * cols
    if col_parts == 1:
        summed = call(
            functools.partial(triangle_kernel, rows),
            [((half, own * rows, residues), BF16)],
            [],
            flops,
            left,
            right,
        )
    else:
        partial_sums = call(
            functools.partial(partial_kernel, rows),
            [((own, half * rows, residues), F32)],
            [],
            flops,
            left,
            right,
        )
        summed = lax.psum_scatter(partial_sums, "col", scatter_dimension=2, tiled=True).astype(BF16)
        summed = by_slot(summed.reshape(own, half, rows, cols).swapaxes(0, 1))
        summed = summed.reshape(half, own * rows, cols)
    returned = swap(summed, owners)
    first_pass, att_norm, bias_copies = call(
        update_kernel,
        [
            ((rows, cols, width), F32),
            ((rows, cols, width), BF16),
            ((owners, HEADS * rows, cols), BF16),
        ],
        [
            ((cols // LANES, channels * rows, LANES), F32),
            ((HEADS * rows, cols), F32),
            ((4, cols, channels), BF16),
        ],
        2 * cells * channels * width,
        returned,
        gate,
        pair_rep,
        w_tri_out,
        w_bias_t,
    )
    bias = swap(bias_copies, owners)
    projected = [
        ((rows, width, cols), BF16),
        ((rows, cols, width), BF16),
        ((rows, width, cols), BF16),
        ((rows, width, cols), F32),
    ]
    projecting = (att_norm, w_query, w_key, w_value, w_att_gate)
    residues = cols * col_parts
    out = [((rows, cols, width), BF16)]
    held = [
        ((residues, HEADS * cols), F32),
        ((2, residues, HEADS * cols), F32),
        ((2, residues, HEADS * cols), BF16),
        ((4, width, cols), BF16),
    ]
    project_flops, attend_flops = 8 * cells * width * width, 4 * cells * residues * width
    if col_parts == 1:
        flops = project_flops + attend_flops
        given = (first_pass, bias, w_att_out)
        return call(whole_kernel, out, projected + held, flops, *projecting, *given)
    query_t, key, value_t, gate_t = call(project_kernel, projected, [], project_flops, *projecting)
    bias = by_slot(lax.all_to_all(by_rank(bias), "col", split_axis=0, concat_axis=2, tiled=True))
    key = lax.all_gather(key, "col", axis=1, tiled=True)
    value_t = lax.all_gather(value_t, "col", axis=2, tiled=True)
    given = (query_t, key, value_t, gate_t, first_pass, bias, w_att_out)
    return call(attend_kernel, out, held, attend_flops, *given)


def solution(mesh):
    in_specs = (P(("grp", "row"), "col", None),) + (P(),) * 12
    out_specs = P(("grp", "row"), "col", None)
    return jax.shard_map(body, mesh=mesh, in_specs=in_specs, out_specs=out_specs, check_vma=False)
```

```python
import functools

import jax
import jax.numpy as jnp
import numpy as np
from jax import lax
from jax.experimental import pallas as pl
from jax.experimental.pallas import tpu as pltpu
from jax.sharding import PartitionSpec as P

HEADS = 4
HEAD_DIM = 32
LANES = 128
LOG2_E = 1.4426950408889634
F32 = jnp.float32
BF16 = jnp.bfloat16
NN = (((1,), (0,)), ((), ()))
NT = (((1,), (1,)), ((), ()))
TN = (((0,), (0,)), ((), ()))


def dot(left, right, dims=NN):
    return lax.dot_general(left, right, dims, preferred_element_type=F32)


def sigmoid(values):
    return 0.5 * jnp.tanh(0.5 * values) + 0.5


def twice(weight):
    zeros = jnp.zeros_like(weight)
    return jnp.concatenate(
        [jnp.concatenate([weight, zeros], axis=1), jnp.concatenate([zeros, weight], axis=1)], axis=0
    )


def listing(ranks):
    first = ranks - 1 - ranks // 4
    return [first] + [rank for rank in range(ranks - 1, -1, -1) if rank != first]


def slot(rank, ranks):
    return listing(ranks).index(rank)


def slot_of(rank, ranks):
    first = listing(ranks)[0]
    return jnp.where(rank == first, 0, ranks - 1 - rank + (rank > first).astype(jnp.int32))


def swap(blocks, ranks):
    members = blocks.shape[0]
    order = listing(members)
    groups = [[first + member for member in order] for first in range(0, ranks, members)]
    return lax.all_to_all(
        blocks, "row", split_axis=0, concat_axis=0, axis_index_groups=groups, tiled=True
    )


def by_rank(blocks):
    return blocks[np.array([slot(r, blocks.shape[0]) for r in range(blocks.shape[0])])]


def by_slot(blocks):
    return blocks[np.array(listing(blocks.shape[0]))]


def lane_tiles(values):
    lanes = values.shape[1]
    return [(t, slice(t * LANES, (t + 1) * LANES)) for t in range(lanes // LANES)]


def lane_norm(values):
    centered = values - jnp.mean(values, axis=-1, keepdims=True)
    variance = jnp.mean(centered * centered, axis=-1, keepdims=True)
    return (centered * lax.rsqrt(variance + 1e-05)).astype(BF16)


def side_by_side(held, i):
    return jnp.concatenate([held[i], held[i + 1]], axis=1)


def pipeline(rows, *steps):
    for tick in range(len(rows) + len(steps) - 1):
        for late, step in enumerate(steps):
            if 0 <= tick - late < len(rows):
                step(rows[tick - late])


def gated_edges(normed, weight, weight_gate, held):
    rows, cols = normed.shape[0], normed.shape[1]
    channels = weight.shape[1]
    turned = jnp.concatenate([weight[...].T, weight_gate[...].T], axis=0)

    def project(i):
        both = dot(turned, jnp.concatenate([normed[i], normed[i + 1]], axis=0), NT)
        act = sigmoid(both[channels:]) * both[:channels]
        for tile, lanes in lane_tiles(act):
            row, part = divmod(tile, cols // LANES)
            held[part, pl.ds(i + row, channels, stride=rows), :] = act[:, lanes]

    return project


def right_kernel(members, *refs):
    given, (right, normed, *staged), (pair, w_right, w_right_gate, held, sems) = refs[:13], refs[13:25], refs[25:]
    targets = [pair, w_right, w_right_gate, *staged]
    copies = [
        pltpu.make_async_copy(source, target, sems.at[n])
        for n, (source, target) in enumerate(zip(given, targets))
    ]
    for copy in copies:
        copy.start()
    for copy in copies[:3]:
        copy.wait()

    def norm(i):
        normed[i] = lane_norm(pair[i].astype(F32))
        normed[i + 1] = lane_norm(pair[i + 1].astype(F32))

    pipeline(range(0, pair.shape[0], 2), norm, gated_edges(normed, w_right, w_right_gate, held))
    owners, block = right.shape[0], right.shape[1]
    for member in range(members):
        for part in range(held.shape[0]):
            sent = held[part, member * block : (member + 1) * block, :].astype(BF16)
            for owner in range(member, owners, members):
                right[slot(owner, owners), :, part * LANES : (part + 1) * LANES] = sent
    for copy in copies[3:]:
        copy.wait()


def left_kernel(normed, w_left, w_left_gate, w_tri_gate, gate, *refs):
    left, held = refs[:-1], refs[-1]
    me = lax.rem(lax.axis_index("row"), len(left))
    width = w_tri_gate.shape[1]
    gate_weight = twice(w_tri_gate[...])

    def open_gate(i):
        opened = sigmoid(dot(side_by_side(normed, i), gate_weight))
        gate[i] = opened[:, :width]
        gate[i + 1] = opened[:, width:]

    step = gated_edges(normed, w_left, w_left_gate, held)
    pipeline(range(0, normed.shape[0], 2), step, open_gate)
    for turn, out in enumerate(left):
        block = out.shape[0]
        mine = pl.ds(pl.multiple_of((me ^ turn) * block, block), block)
        for part in range(held.shape[0]):
            out[:, part * LANES : (part + 1) * LANES] = held[part, mine, :].astype(BF16)


def channel_rows(blocks, rows, channel):
    mine = slice(channel * rows, (channel + 1) * rows)
    both = slice(channel // 2 * 2 * rows, (channel // 2 + 1) * 2 * rows)
    inner = slice(mine.start - both.start, mine.stop - both.start)
    parts = [block[both, :].astype(F32)[inner] for block in blocks]
    return jnp.concatenate(parts, axis=0).astype(BF16)


def triangle_product(left, right, rows, channel):
    ranks = right.shape[0]
    by_owner = [right.at[slot(r, ranks)] for r in range(ranks)]
    return dot(channel_rows(left, rows, channel), channel_rows(by_owner, rows, channel), NT)


def triangle_kernel(rows, right, *refs):
    left, out = refs[:-1], refs[-1]
    members = len(left)
    me = lax.rem(lax.axis_index("row"), members)
    for channel in range(0, out.shape[1] // rows, 2):
        products = [triangle_product(left, right, rows, channel + o) for o in range(2)]
        for turn in range(members):
            mine = slice(turn * rows, (turn + 1) * rows)
            out[slot_of(me ^ turn, members), channel * rows : (channel + 2) * rows, :] = jnp.concatenate(
                [p[mine] for p in products], axis=0
            ).astype(BF16)


def partial_kernel(rows, right, *refs):
    left, out = refs[:-1], refs[-1]
    members = len(left)
    me = lax.rem(lax.axis_index("row"), members)
    for channel in range(out.shape[0]):
        product = triangle_product(left, right, rows, channel)
        for turn in range(members):
            place = pl.ds(pl.multiple_of((me ^ turn) * rows, rows), rows)
            out[channel, place, :] = product[turn * rows : (turn + 1) * rows]


def update_kernel(
    returned, gate, pair, w_tri_out, w_bias_t, first_pass, att_norm, bias, held, bias_held, turned
):
    rows, cols, width = pair.shape
    owners, block = returned.shape[0], returned.shape[1]
    channels = owners * block // rows
    total = jnp.zeros((rows, cols), F32)
    for owner in range(owners):
        total += jnp.sum(returned[owner].astype(F32).reshape(block // rows, rows, cols), axis=0)
    average = total / channels
    square = jnp.zeros((rows, cols), F32)
    for owner in range(owners):
        centered = returned[slot(owner, owners)].astype(F32).reshape(block // rows, rows, cols) - average
        square += jnp.sum(centered * centered, axis=0)
        for tile, lanes in lane_tiles(pair):
            held[tile, owner * block : (owner + 1) * block, :] = centered.reshape(block, cols)[:, lanes]
    scale = lax.rsqrt(square / channels + 1e-05)

    weight = twice(w_tri_out[...])

    def turn(i):
        for row in (i, i + 1):
            tri_norm = jnp.concatenate(
                [held[tile, pl.ds(row, channels, stride=rows), :] for tile, _ in lane_tiles(pair)], axis=1
            )
            turned[row % 4] = (tri_norm * scale[row : row + 1]).astype(BF16).T

    def update(i):
        both = dot(side_by_side(turned, i % 4), weight)
        first_pass[i] = pair[i].astype(F32) + gate[i] * both[:, :width]
        first_pass[i + 1] = pair[i + 1].astype(F32) + gate[i + 1] * both[:, width:]

    def norm(i):
        for row in (i, i + 1):
            att_norm[row] = lane_norm(first_pass[row])

    def project_bias(i):
        both = dot(w_bias_t[...], jnp.concatenate([att_norm[i], att_norm[i + 1]], axis=0), NT)
        for row in range(2):
            for head in range(HEADS):
                place = head * rows + i + row
                bias_held[place : place + 1, :] = both[head : head + 1, row * cols : (row + 1) * cols]

    pipeline(range(0, rows, 2), turn, update, norm, project_bias)
    rounded = bias_held[...].astype(BF16)
    for owner in range(bias.shape[0]):
        bias[owner] = rounded


def projector(att_norm, w_query, w_key, w_value, w_att_gate, query_t, key, value_t, gate_t):
    w_turned = jnp.concatenate([w[...].T for w in (w_query, w_value, w_att_gate)], axis=0)
    w_direct = twice(w_key[...])
    cols, width = att_norm.shape[1], w_query.shape[1]

    def project(i):
        if i % 2:
            return
        keys = dot(side_by_side(att_norm, i), w_direct).astype(BF16)
        turned = dot(w_turned, jnp.concatenate([att_norm[i], att_norm[i + 1]], axis=0), NT)
        for row in range(2):
            key[i + row] = keys[:, row * width : (row + 1) * width]
            mine = turned[:, row * cols : (row + 1) * cols]
            query_t[i + row] = mine[:width].astype(BF16)
            value_t[i + row] = mine[width : 2 * width].astype(BF16)
            gate_t[i + row] = sigmoid(mine[2 * width :])

    return project


def project_kernel(*refs):
    pipeline(range(refs[0].shape[0]), projector(*refs))


def whole_kernel(att_norm, w_query, w_key, w_value, w_att_gate, *refs):
    given, projected, held = refs[:4], refs[4:8], refs[8:]
    project = projector(att_norm, w_query, w_key, w_value, w_att_gate, *projected)
    attend_kernel(*projected, *given, *held, before=(project,))


def attend_kernel(
    query_t,
    key,
    value_t,
    gate_t,
    first_pass,
    bias,
    w_att_out,
    out,
    bias_t,
    scores,
    weights,
    gated,
    before=(),
):
    rows, width, cols = query_t.shape
    head_rows = bias.shape[1] // HEADS
    score_scale = LOG2_E / HEAD_DIM**0.5
    ones = jnp.ones((16, key.shape[1]), BF16)
    heads = [
        (slice(h * HEAD_DIM, (h + 1) * HEAD_DIM), slice(h * cols, (h + 1) * cols)) for h in range(HEADS)
    ]

    def score(i):
        blocks = []
        for mine, _ in heads:
            above = jnp.zeros((mine.start, cols), BF16)
            below = jnp.zeros((width - mine.stop, cols), BF16)
            parts = [p for p in (above, query_t[i, mine, :], below) if p.shape[0]]
            blocks.append(jnp.concatenate(parts, axis=0))
        scores[i % 2] = dot(key[i], jnp.concatenate(blocks, axis=1)) * score_scale

    def turn_bias():
        for head, (_, span) in enumerate(heads):
            parts = [
                bias[slot(owner, bias.shape[0])].astype(F32)[head * head_rows : (head + 1) * head_rows]
                for owner in range(bias.shape[0])
            ]
            bias_t[:, span] = jnp.concatenate(parts, axis=0).T * LOG2_E

    def soften(i):
        if i == 0:
            turn_bias()
        for _, span in heads:
            biased = scores[i % 2, :, span] + bias_t[:, span]
            peak = jnp.max(biased, axis=0, keepdims=True)
            weights[i % 2, :, span] = jnp.exp2(biased - peak).astype(BF16)

    def collect(i):
        for head in range(0, HEADS, 2):
            (first, left), (second, right) = heads[head : head + 2]
            values = jnp.concatenate([value_t[i, first.start : second.stop, :], ones], axis=0)
            summed = dot(values, weights[i % 2, :, left.start : right.stop])
            share = 1.0 / summed[2 * HEAD_DIM : 2 * HEAD_DIM + 1]
            for mine, there, lanes in (
                (first, slice(0, HEAD_DIM), slice(0, cols)),
                (second, slice(HEAD_DIM, 2 * HEAD_DIM), slice(cols, 2 * cols)),
            ):
                attended = summed[there, lanes] * share[:, lanes] * gate_t[i, mine, :]
                gated[i % 4, mine, :] = attended.astype(BF16)

    def finish(i):
        if i % 2 == 0:
            return
        turned = jnp.concatenate([gated[(i - 1) % 4].T, gated[i % 4].T], axis=1)
        both = dot(turned, w_last)
        out[i - 1] = (first_pass[i - 1] + both[:, :width]).astype(BF16)
        out[i] = (first_pass[i] + both[:, width:]).astype(BF16)

    w_last = twice(w_att_out[...])
    pipeline(range(rows), *before, score, soften, collect, finish)


def call(kernel, outs, scratch, flops, *operands, fetched=0):
    vmem = pl.BlockSpec(memory_space=pltpu.VMEM)
    far = pl.BlockSpec(memory_space=pltpu.HBM)
    shapes = [jax.ShapeDtypeStruct(shape, dtype) for shape, dtype in outs]
    moved = sum(o.size * o.dtype.itemsize for o in operands)
    operands = [
        pltpu.with_memory_space_constraint(o, pltpu.HBM) if n < fetched else o
        for n, o in enumerate(operands)
    ]
    got = pl.pallas_call(
        kernel,
        out_shape=shapes,
        in_specs=[far] * fetched + [vmem] * (len(operands) - fetched),
        out_specs=[vmem] * len(shapes),
        scratch_shapes=[pltpu.VMEM(*s) if isinstance(s, tuple) else s for s in scratch],
        compiler_params=pltpu.CompilerParams(vmem_limit_bytes=48 * 2**20),
        cost_estimate=pl.CostEstimate(flops=flops, bytes_accessed=moved, transcendentals=0),
    )(*operands)
    return got if len(got) > 1 else got[0]


def body(
    pair_rep,
    w_left,
    w_left_gate,
    w_right,
    w_right_gate,
    w_tri_gate,
    w_tri_out,
    w_query,
    w_key,
    w_value,
    w_bias,
    w_att_gate,
    w_att_out,
):
    rows, cols, width = pair_rep.shape
    channels = w_left.shape[1]
    owners, col_parts = lax.axis_size("row"), lax.axis_size("col")
    half = owners // 2
    own = channels // half
    residues = owners * rows
    cells = rows * cols

    later = (w_left, w_left_gate, w_tri_gate, w_tri_out, w_query, w_key, w_value, w_att_gate, w_att_out)
    right, normed, *later, w_bias_t = call(
        functools.partial(right_kernel, half),
        [
            ((owners, own * rows, cols), BF16),
            (pair_rep.shape, BF16),
            *[(w.shape, BF16) for w in later],
            (w_bias.shape[::-1], BF16),
        ],
        [
            (pair_rep.shape, BF16),
            (w_right.shape, BF16),
            (w_right_gate.shape, BF16),
            ((cols // LANES, channels * rows, LANES), F32),
            pltpu.SemaphoreType.DMA((13,)),
        ],
        4 * cells * width * channels,
        pair_rep,
        w_right,
        w_right_gate,
        *later,
        w_bias.T,
        fetched=13,
    )
    w_left, w_left_gate, w_tri_gate, w_tri_out, w_query, w_key, w_value, w_att_gate, w_att_out = later
    right = swap(right, owners)
    gate, *left = call(
        left_kernel,
        [((rows, cols, width), F32)] + [((own * rows, cols), BF16)] * half,
        [((cols // LANES, channels * rows, LANES), F32)],
        6 * cells * width * channels,
        normed,
        w_left,
        w_left_gate,
        w_tri_gate,
    )
    for turn in range(1, half):
        left[turn] = lax.ppermute(left[turn], "row", [(r, r ^ turn) for r in range(owners)])
    flops = 2 * own * half * rows * residues * cols
    if col_parts == 1:
        summed = call(
            functools.partial(triangle_kernel, rows),
            [((half, own * rows, residues), BF16)],
            [],
            flops,
            right,
            *left,
        )
    else:
        partial_sums = call(
            functools.partial(partial_kernel, rows),
            [((own, half * rows, residues), F32)],
            [],
            flops,
            right,
            *left,
        )
        summed = lax.psum_scatter(partial_sums, "col", scatter_dimension=2, tiled=True).astype(BF16)
        summed = by_slot(summed.reshape(own, half, rows, cols).swapaxes(0, 1))
        summed = summed.reshape(half, own * rows, cols)
    returned = swap(summed, owners)
    first_pass, att_norm, bias_copies = call(
        update_kernel,
        [
            ((rows, cols, width), F32),
            ((rows, cols, width), BF16),
            ((owners, HEADS * rows, cols), BF16),
        ],
        [
            ((cols // LANES, channels * rows, LANES), F32),
            ((HEADS * rows, cols), F32),
            ((4, cols, channels), BF16),
        ],
        2 * cells * channels * width,
        returned,
        gate,
        pair_rep,
        w_tri_out,
        w_bias_t,
    )
    bias = swap(bias_copies, owners)
    projected = [
        ((rows, width, cols), BF16),
        ((rows, cols, width), BF16),
        ((rows, width, cols), BF16),
        ((rows, width, cols), F32),
    ]
    projecting = (att_norm, w_query, w_key, w_value, w_att_gate)
    residues = cols * col_parts
    out = [((rows, cols, width), BF16)]
    held = [
        ((residues, HEADS * cols), F32),
        ((2, residues, HEADS * cols), F32),
        ((2, residues, HEADS * cols), BF16),
        ((4, width, cols), BF16),
    ]
    project_flops, attend_flops = 8 * cells * width * width, 4 * cells * residues * width
    if col_parts == 1:
        flops = project_flops + attend_flops
        given = (first_pass, bias, w_att_out)
        return call(whole_kernel, out, projected + held, flops, *projecting, *given)
    query_t, key, value_t, gate_t = call(project_kernel, projected, [], project_flops, *projecting)
    bias = by_slot(lax.all_to_all(by_rank(bias), "col", split_axis=0, concat_axis=2, tiled=True))
    key = lax.all_gather(key, "col", axis=1, tiled=True)
    value_t = lax.all_gather(value_t, "col", axis=2, tiled=True)
    given = (query_t, key, value_t, gate_t, first_pass, bias, w_att_out)
    return call(attend_kernel, out, held, attend_flops, *given)


def solution(mesh):
    in_specs = (P(("grp", "row"), "col", None),) + (P(),) * 12
    out_specs = P(("grp", "row"), "col", None)
    return jax.shard_map(body, mesh=mesh, in_specs=in_specs, out_specs=out_specs, check_vma=False)
```

```python
import functools

import jax
import jax.numpy as jnp
import numpy as np
from jax import lax
from jax.experimental import pallas as pl
from jax.experimental.pallas import tpu as pltpu
from jax.sharding import PartitionSpec as P

HEADS = 4
HEAD_DIM = 32
LANES = 128
LOG2_E = 1.4426950408889634
F32 = jnp.float32
BF16 = jnp.bfloat16
NN = (((1,), (0,)), ((), ()))
NT = (((1,), (1,)), ((), ()))
TN = (((0,), (0,)), ((), ()))


def dot(left, right, dims=NN):
    return lax.dot_general(left, right, dims, preferred_element_type=F32)


def sigmoid(values):
    return 0.5 * jnp.tanh(0.5 * values) + 0.5


def twice(weight):
    zeros = jnp.zeros_like(weight)
    return jnp.concatenate(
        [jnp.concatenate([weight, zeros], axis=1), jnp.concatenate([zeros, weight], axis=1)], axis=0
    )


def listing(ranks):
    first = ranks - 1 - ranks // 4
    return [first] + [rank for rank in range(ranks - 1, -1, -1) if rank != first]


def slot(rank, ranks):
    return listing(ranks).index(rank)


def slot_of(rank, ranks):
    first = listing(ranks)[0]
    return jnp.where(rank == first, 0, ranks - 1 - rank + (rank > first).astype(jnp.int32))


def swap(blocks, ranks):
    members = blocks.shape[0]
    order = listing(members)
    groups = [[first + member for member in order] for first in range(0, ranks, members)]
    return lax.all_to_all(
        blocks, "row", split_axis=0, concat_axis=0, axis_index_groups=groups, tiled=True
    )


def by_rank(blocks):
    return blocks[np.array([slot(r, blocks.shape[0]) for r in range(blocks.shape[0])])]


def by_slot(blocks):
    return blocks[np.array(listing(blocks.shape[0]))]


def lane_tiles(values):
    lanes = values.shape[1]
    return [(t, slice(t * LANES, (t + 1) * LANES)) for t in range(lanes // LANES)]


def lane_norm(values):
    centered = values - jnp.mean(values, axis=-1, keepdims=True)
    variance = jnp.mean(centered * centered, axis=-1, keepdims=True)
    return (centered * lax.rsqrt(variance + 1e-05)).astype(BF16)


def side_by_side(held, i):
    return jnp.concatenate([held[i], held[i + 1]], axis=1)


def pipeline(rows, *steps):
    for tick in range(len(rows) + len(steps) - 1):
        for late, step in enumerate(steps):
            if 0 <= tick - late < len(rows):
                step(rows[tick - late])


def gated_edges(normed, weight, weight_gate, held):
    rows, cols = normed.shape[0], normed.shape[1]
    channels = weight.shape[1]
    turned = jnp.concatenate([weight[...].T, weight_gate[...].T], axis=0)

    def project(i):
        both = dot(turned, jnp.concatenate([normed[i], normed[i + 1]], axis=0), NT)
        act = sigmoid(both[channels:]) * both[:channels]
        for tile, lanes in lane_tiles(act):
            row, part = divmod(tile, cols // LANES)
            held[part, pl.ds(i + row, channels, stride=rows), :] = act[:, lanes]

    return project


def right_kernel(members, *refs):
    given, (right, normed, *staged), (pair, w_right, w_right_gate, held, sems) = refs[:13], refs[13:25], refs[25:]
    targets = [pair, w_right, w_right_gate, *staged]
    copies = [
        pltpu.make_async_copy(source, target, sems.at[n])
        for n, (source, target) in enumerate(zip(given, targets))
    ]
    for copy in copies:
        copy.start()
    for copy in copies[:3]:
        copy.wait()

    def norm(i):
        normed[i] = lane_norm(pair[i].astype(F32))
        normed[i + 1] = lane_norm(pair[i + 1].astype(F32))

    pipeline(range(0, pair.shape[0], 2), norm, gated_edges(normed, w_right, w_right_gate, held))
    owners, block = right.shape[0], right.shape[1]
    for member in range(members):
        for part in range(held.shape[0]):
            sent = held[part, member * block : (member + 1) * block, :].astype(BF16)
            for owner in range(member, owners, members):
                right[slot(owner, owners), :, part * LANES : (part + 1) * LANES] = sent
    for copy in copies[3:]:
        copy.wait()


def left_kernel(normed, w_left, w_left_gate, w_tri_gate, gate, *refs):
    left, held = refs[:-1], refs[-1]
    near = len(left)
    me = lax.rem(lax.axis_index("row"), 2 * near)
    width = w_tri_gate.shape[1]
    gate_weight = twice(w_tri_gate[...])

    def open_gate(i):
        opened = sigmoid(dot(side_by_side(normed, i), gate_weight))
        gate[i] = opened[:, :width]
        gate[i + 1] = opened[:, width:]

    step = gated_edges(normed, w_left, w_left_gate, held)
    pipeline(range(0, normed.shape[0], 2), step, open_gate)
    for turn in range(2 * near):
        block = left[0].shape[1]
        mine = pl.ds(pl.multiple_of((me ^ turn) * block, block), block)
        for part in range(held.shape[0]):
            lanes = slice(part * LANES, (part + 1) * LANES)
            left[turn % near][turn // near, :, lanes] = held[part, mine, :].astype(BF16)


def channel_rows(blocks, rows, channel):
    mine = slice(channel * rows, (channel + 1) * rows)
    both = slice(channel // 2 * 2 * rows, (channel // 2 + 1) * 2 * rows)
    inner = slice(mine.start - both.start, mine.stop - both.start)
    parts = [block[both, :].astype(F32)[inner] for block in blocks]
    return jnp.concatenate(parts, axis=0).astype(BF16)


def triangle_product(left, right, rows, channel):
    ranks = right.shape[0]
    by_owner = [right.at[slot(r, ranks)] for r in range(ranks)]
    return dot(channel_rows(left, rows, channel), channel_rows(by_owner, rows, channel), NT)


def left_blocks(refs):
    *near, far = refs
    return [block.at[0] for block in near] + [far.at[s] for s in range(len(near))]


def triangle_kernel(rows, right, *refs):
    left, out = left_blocks(refs[:-1]), refs[-1]
    members = len(left)
    me = lax.rem(lax.axis_index("row"), members)
    for channel in range(0, out.shape[1] // rows, 2):
        products = [triangle_product(left, right, rows, channel + o) for o in range(2)]
        for turn in range(members):
            mine = slice(turn * rows, (turn + 1) * rows)
            out[slot_of(me ^ turn, members), channel * rows : (channel + 2) * rows, :] = jnp.concatenate(
                [p[mine] for p in products], axis=0
            ).astype(BF16)


def partial_kernel(rows, right, *refs):
    left, out = left_blocks(refs[:-1]), refs[-1]
    members = len(left)
    me = lax.rem(lax.axis_index("row"), members)
    for channel in range(out.shape[0]):
        product = triangle_product(left, right, rows, channel)
        for turn in range(members):
            place = pl.ds(pl.multiple_of((me ^ turn) * rows, rows), rows)
            out[channel, place, :] = product[turn * rows : (turn + 1) * rows]


def update_kernel(
    returned, gate, pair, w_tri_out, w_bias_t, first_pass, att_norm, bias, held, bias_held, turned
):
    rows, cols, width = pair.shape
    owners, block = returned.shape[0], returned.shape[1]
    channels = owners * block // rows
    total = jnp.zeros((rows, cols), F32)
    for owner in range(owners):
        total += jnp.sum(returned[owner].astype(F32).reshape(block // rows, rows, cols), axis=0)
    average = total / channels
    square = jnp.zeros((rows, cols), F32)
    for owner in range(owners):
        centered = returned[slot(owner, owners)].astype(F32).reshape(block // rows, rows, cols) - average
        square += jnp.sum(centered * centered, axis=0)
        for tile, lanes in lane_tiles(pair):
            held[tile, owner * block : (owner + 1) * block, :] = centered.reshape(block, cols)[:, lanes]
    scale = lax.rsqrt(square / channels + 1e-05)

    weight = twice(w_tri_out[...])

    def turn(i):
        for row in (i, i + 1):
            tri_norm = jnp.concatenate(
                [held[tile, pl.ds(row, channels, stride=rows), :] for tile, _ in lane_tiles(pair)], axis=1
            )
            turned[row % 4] = (tri_norm * scale[row : row + 1]).astype(BF16).T

    def update(i):
        both = dot(side_by_side(turned, i % 4), weight)
        first_pass[i] = pair[i].astype(F32) + gate[i] * both[:, :width]
        first_pass[i + 1] = pair[i + 1].astype(F32) + gate[i + 1] * both[:, width:]

    def norm(i):
        for row in (i, i + 1):
            att_norm[row] = lane_norm(first_pass[row])

    def project_bias(i):
        both = dot(w_bias_t[...], jnp.concatenate([att_norm[i], att_norm[i + 1]], axis=0), NT)
        for row in range(2):
            for head in range(HEADS):
                place = head * rows + i + row
                bias_held[place : place + 1, :] = both[head : head + 1, row * cols : (row + 1) * cols]

    pipeline(range(0, rows, 2), turn, update, norm, project_bias)
    rounded = bias_held[...].astype(BF16)
    for owner in range(bias.shape[0]):
        bias[owner] = rounded


def projector(att_norm, w_query, w_key, w_value, w_att_gate, query_t, key, value_t, gate_t):
    w_turned = jnp.concatenate([w[...].T for w in (w_query, w_value, w_att_gate)], axis=0)
    w_direct = twice(w_key[...])
    cols, width = att_norm.shape[1], w_query.shape[1]

    def project(i):
        if i % 2:
            return
        keys = dot(side_by_side(att_norm, i), w_direct).astype(BF16)
        turned = dot(w_turned, jnp.concatenate([att_norm[i], att_norm[i + 1]], axis=0), NT)
        for row in range(2):
            key[i + row] = keys[:, row * width : (row + 1) * width]
            mine = turned[:, row * cols : (row + 1) * cols]
            query_t[i + row] = mine[:width].astype(BF16)
            value_t[i + row] = mine[width : 2 * width].astype(BF16)
            gate_t[i + row] = sigmoid(mine[2 * width :])

    return project


def project_kernel(*refs):
    pipeline(range(refs[0].shape[0]), projector(*refs))


def whole_kernel(att_norm, w_query, w_key, w_value, w_att_gate, *refs):
    given, projected, held = refs[:4], refs[4:8], refs[8:]
    project = projector(att_norm, w_query, w_key, w_value, w_att_gate, *projected)
    attend_kernel(*projected, *given, *held, before=(project,))


def attend_kernel(
    query_t,
    key,
    value_t,
    gate_t,
    first_pass,
    bias,
    w_att_out,
    out,
    bias_t,
    scores,
    weights,
    gated,
    before=(),
):
    rows, width, cols = query_t.shape
    head_rows = bias.shape[1] // HEADS
    score_scale = LOG2_E / HEAD_DIM**0.5
    ones = jnp.ones((16, key.shape[1]), BF16)
    heads = [
        (slice(h * HEAD_DIM, (h + 1) * HEAD_DIM), slice(h * cols, (h + 1) * cols)) for h in range(HEADS)
    ]

    def score(i):
        blocks = []
        for mine, _ in heads:
            above = jnp.zeros((mine.start, cols), BF16)
            below = jnp.zeros((width - mine.stop, cols), BF16)
            parts = [p for p in (above, query_t[i, mine, :], below) if p.shape[0]]
            blocks.append(jnp.concatenate(parts, axis=0))
        scores[i % 2] = dot(key[i], jnp.concatenate(blocks, axis=1)) * score_scale

    def turn_bias():
        for head, (_, span) in enumerate(heads):
            parts = [
                bias[slot(owner, bias.shape[0])].astype(F32)[head * head_rows : (head + 1) * head_rows]
                for owner in range(bias.shape[0])
            ]
            bias_t[:, span] = jnp.concatenate(parts, axis=0).T * LOG2_E

    def soften(i):
        if i == 0:
            turn_bias()
        for _, span in heads:
            biased = scores[i % 2, :, span] + bias_t[:, span]
            peak = jnp.max(biased, axis=0, keepdims=True)
            weights[i % 2, :, span] = jnp.exp2(biased - peak).astype(BF16)

    def collect(i):
        for head in range(0, HEADS, 2):
            (first, left), (second, right) = heads[head : head + 2]
            values = jnp.concatenate([value_t[i, first.start : second.stop, :], ones], axis=0)
            summed = dot(values, weights[i % 2, :, left.start : right.stop])
            share = 1.0 / summed[2 * HEAD_DIM : 2 * HEAD_DIM + 1]
            for mine, there, lanes in (
                (first, slice(0, HEAD_DIM), slice(0, cols)),
                (second, slice(HEAD_DIM, 2 * HEAD_DIM), slice(cols, 2 * cols)),
            ):
                attended = summed[there, lanes] * share[:, lanes] * gate_t[i, mine, :]
                gated[i % 4, mine, :] = attended.astype(BF16)

    def finish(i):
        if i % 2 == 0:
            return
        turned = jnp.concatenate([gated[(i - 1) % 4].T, gated[i % 4].T], axis=1)
        both = dot(turned, w_last)
        out[i - 1] = (first_pass[i - 1] + both[:, :width]).astype(BF16)
        out[i] = (first_pass[i] + both[:, width:]).astype(BF16)

    w_last = twice(w_att_out[...])
    pipeline(range(rows), *before, score, soften, collect, finish)


def call(kernel, outs, scratch, flops, *operands, fetched=0):
    vmem = pl.BlockSpec(memory_space=pltpu.VMEM)
    far = pl.BlockSpec(memory_space=pltpu.HBM)
    shapes = [jax.ShapeDtypeStruct(shape, dtype) for shape, dtype in outs]
    moved = sum(o.size * o.dtype.itemsize for o in operands)
    operands = [
        pltpu.with_memory_space_constraint(o, pltpu.HBM) if n < fetched else o
        for n, o in enumerate(operands)
    ]
    got = pl.pallas_call(
        kernel,
        out_shape=shapes,
        in_specs=[far] * fetched + [vmem] * (len(operands) - fetched),
        out_specs=[vmem] * len(shapes),
        scratch_shapes=[pltpu.VMEM(*s) if isinstance(s, tuple) else s for s in scratch],
        compiler_params=pltpu.CompilerParams(vmem_limit_bytes=48 * 2**20),
        cost_estimate=pl.CostEstimate(flops=flops, bytes_accessed=moved, transcendentals=0),
    )(*operands)
    return got if len(got) > 1 else got[0]


def body(
    pair_rep,
    w_left,
    w_left_gate,
    w_right,
    w_right_gate,
    w_tri_gate,
    w_tri_out,
    w_query,
    w_key,
    w_value,
    w_bias,
    w_att_gate,
    w_att_out,
):
    rows, cols, width = pair_rep.shape
    channels = w_left.shape[1]
    owners, col_parts = lax.axis_size("row"), lax.axis_size("col")
    half = owners // 2
    near = half // 2
    own = channels // half
    residues = owners * rows
    cells = rows * cols

    later = (w_left, w_left_gate, w_tri_gate, w_tri_out, w_query, w_key, w_value, w_att_gate, w_att_out)
    right, normed, *later, w_bias_t = call(
        functools.partial(right_kernel, half),
        [
            ((owners, own * rows, cols), BF16),
            (pair_rep.shape, BF16),
            *[(w.shape, BF16) for w in later],
            (w_bias.shape[::-1], BF16),
        ],
        [
            (pair_rep.shape, BF16),
            (w_right.shape, BF16),
            (w_right_gate.shape, BF16),
            ((cols // LANES, channels * rows, LANES), F32),
            pltpu.SemaphoreType.DMA((13,)),
        ],
        4 * cells * width * channels,
        pair_rep,
        w_right,
        w_right_gate,
        *later,
        w_bias.T,
        fetched=13,
    )
    w_left, w_left_gate, w_tri_gate, w_tri_out, w_query, w_key, w_value, w_att_gate, w_att_out = later
    right = swap(right, owners)
    gate, *left = call(
        left_kernel,
        [((rows, cols, width), F32)] + [((2, own * rows, cols), BF16)] * near,
        [((cols // LANES, channels * rows, LANES), F32)],
        6 * cells * width * channels,
        normed,
        w_left,
        w_left_gate,
        w_tri_gate,
    )
    for turn in range(1, near):
        left[turn] = lax.ppermute(left[turn], "row", [(r, r ^ turn) for r in range(owners)])
    passed_on = jnp.stack([block[1] for block in left])
    left.append(lax.ppermute(passed_on, "row", [(r, r ^ near) for r in range(owners)]))
    flops = 2 * own * half * rows * residues * cols
    if col_parts == 1:
        summed = call(
            functools.partial(triangle_kernel, rows),
            [((half, own * rows, residues), BF16)],
            [],
            flops,
            right,
            *left,
        )
    else:
        partial_sums = call(
            functools.partial(partial_kernel, rows),
            [((own, half * rows, residues), F32)],
            [],
            flops,
            right,
            *left,
        )
        summed = lax.psum_scatter(partial_sums, "col", scatter_dimension=2, tiled=True).astype(BF16)
        summed = by_slot(summed.reshape(own, half, rows, cols).swapaxes(0, 1))
        summed = summed.reshape(half, own * rows, cols)
    returned = swap(summed, owners)
    first_pass, att_norm, bias_copies = call(
        update_kernel,
        [
            ((rows, cols, width), F32),
            ((rows, cols, width), BF16),
            ((owners, HEADS * rows, cols), BF16),
        ],
        [
            ((cols // LANES, channels * rows, LANES), F32),
            ((HEADS * rows, cols), F32),
            ((4, cols, channels), BF16),
        ],
        2 * cells * channels * width,
        returned,
        gate,
        pair_rep,
        w_tri_out,
        w_bias_t,
    )
    bias = swap(bias_copies, owners)
    projected = [
        ((rows, width, cols), BF16),
        ((rows, cols, width), BF16),
        ((rows, width, cols), BF16),
        ((rows, width, cols), F32),
    ]
    projecting = (att_norm, w_query, w_key, w_value, w_att_gate)
    residues = cols * col_parts
    out = [((rows, cols, width), BF16)]
    held = [
        ((residues, HEADS * cols), F32),
        ((2, residues, HEADS * cols), F32),
        ((2, residues, HEADS * cols), BF16),
        ((4, width, cols), BF16),
    ]
    project_flops, attend_flops = 8 * cells * width * width, 4 * cells * residues * width
    if col_parts == 1:
        flops = project_flops + attend_flops
        given = (first_pass, bias, w_att_out)
        return call(whole_kernel, out, projected + held, flops, *projecting, *given)
    query_t, key, value_t, gate_t = call(project_kernel, projected, [], project_flops, *projecting)
    bias = by_slot(lax.all_to_all(by_rank(bias), "col", split_axis=0, concat_axis=2, tiled=True))
    key = lax.all_gather(key, "col", axis=1, tiled=True)
    value_t = lax.all_gather(value_t, "col", axis=2, tiled=True)
    given = (query_t, key, value_t, gate_t, first_pass, bias, w_att_out)
    return call(attend_kernel, out, held, attend_flops, *given)


def solution(mesh):
    in_specs = (P(("grp", "row"), "col", None),) + (P(),) * 12
    out_specs = P(("grp", "row"), "col", None)
    return jax.shard_map(body, mesh=mesh, in_specs=in_specs, out_specs=out_specs, check_vma=False)
```

```python
import functools

import jax
import jax.numpy as jnp
import numpy as np
from jax import lax
from jax.experimental import pallas as pl
from jax.experimental.pallas import tpu as pltpu
from jax.sharding import PartitionSpec as P

HEADS = 4
HEAD_DIM = 32
LANES = 128
LOG2_E = 1.4426950408889634
F32 = jnp.float32
BF16 = jnp.bfloat16
NN = (((1,), (0,)), ((), ()))
NT = (((1,), (1,)), ((), ()))
TN = (((0,), (0,)), ((), ()))


def dot(left, right, dims=NN):
    return lax.dot_general(left, right, dims, preferred_element_type=F32)


def sigmoid(values):
    return 0.5 * jnp.tanh(0.5 * values) + 0.5


def twice(weight):
    zeros = jnp.zeros_like(weight)
    return jnp.concatenate(
        [jnp.concatenate([weight, zeros], axis=1), jnp.concatenate([zeros, weight], axis=1)], axis=0
    )


def listing(ranks):
    first = ranks - 1 - ranks // 4
    return [first] + [rank for rank in range(ranks - 1, -1, -1) if rank != first]


def slot(rank, ranks):
    return listing(ranks).index(rank)


def swap(blocks):
    return lax.all_to_all(
        blocks,
        "row",
        split_axis=0,
        concat_axis=0,
        axis_index_groups=[listing(blocks.shape[0])],
        tiled=True,
    )


def by_rank(blocks):
    return blocks[np.array([slot(r, blocks.shape[0]) for r in range(blocks.shape[0])])]


def by_slot(blocks):
    return blocks[np.array(listing(blocks.shape[0]))]


def lane_tiles(values):
    lanes = values.shape[1]
    return [(t, slice(t * LANES, (t + 1) * LANES)) for t in range(lanes // LANES)]


def lane_norm(values):
    centered = values - jnp.mean(values, axis=-1, keepdims=True)
    variance = jnp.mean(centered * centered, axis=-1, keepdims=True)
    return (centered * lax.rsqrt(variance + 1e-05)).astype(BF16)


def side_by_side(held, i):
    return jnp.concatenate([held[i], held[i + 1]], axis=1)


def pipeline(rows, *steps):
    for tick in range(len(rows) + len(steps) - 1):
        for late, step in enumerate(steps):
            if 0 <= tick - late < len(rows):
                step(rows[tick - late])


def looped(rows, *steps):
    def tick(now, carry):
        for late, step in reversed(list(enumerate(steps))):
            step(jnp.clip(now - late, 0, rows - 1))
        return carry

    lax.fori_loop(0, rows + len(steps) - 1, tick, 0)


def edges_kernel(*refs):
    given, (out, gate, *staged), (pair, weights, normed, held, sems) = refs[:13], refs[13:22], refs[22:]
    targets = [pair, *(weights.at[n] for n in range(5)), *staged]
    copies = [
        pltpu.make_async_copy(source, target, sems.at[n])
        for n, (source, target) in enumerate(zip(given, targets))
    ]
    for copy in copies:
        copy.start()
    for copy in copies[:6]:
        copy.wait()
    rows, width = pair.shape[0], pair.shape[2]
    channels = weights.shape[2]
    cols = pair.shape[1]
    turned = jnp.concatenate([weights[n].T for n in range(4)], axis=0)
    gate_weight = twice(weights[4])

    def norm(i):
        normed[i] = lane_norm(pair[i].astype(F32))
        normed[i + 1] = lane_norm(pair[i + 1].astype(F32))

    def project(i):
        both = dot(turned, jnp.concatenate([normed[i], normed[i + 1]], axis=0), NT)
        for side in range(2):
            base = 2 * side * channels
            act = sigmoid(both[base + channels : base + 2 * channels]) * both[base : base + channels]
            for tile, lanes in lane_tiles(act):
                row, part = divmod(tile, cols // LANES)
                place = pl.ds(side * rows + i + row, channels, stride=2 * rows)
                held[part, place, :] = act[:, lanes]
        opened = sigmoid(dot(side_by_side(normed, i), gate_weight))
        gate[i] = opened[:, :width]
        gate[i + 1] = opened[:, width:]

    pipeline(range(0, rows, 2), norm, project)
    owners, block = out.shape[0], out.shape[1]
    for owner in range(owners):
        for tile, lanes in lane_tiles(pair):
            out[slot(owner, owners), :, lanes] = held[tile, owner * block : (owner + 1) * block, :].astype(BF16)
    for copy in copies[6:]:
        copy.wait()


def triangle_sides(edges, rows, channel):
    sides = [[], []]
    sources = edges.shape[0]
    for source in range(sources):
        block = edges[slot(source, sources), channel * 2 * rows : (channel + 1) * 2 * rows, :].astype(F32)
        sides[0].append(block[:rows])
        sides[1].append(block[rows:])
    return [jnp.concatenate(side, axis=0).astype(BF16) for side in sides]


def triangle_kernel(rows, edges, out):
    for pair_of in range(0, out.shape[1] // rows, 2):
        products = [dot(*triangle_sides(edges, rows, pair_of + o), NT) for o in range(2)]
        owners = out.shape[0]
        for owner in range(owners):
            mine = slice(owner * rows, (owner + 1) * rows)
            out[slot(owner, owners), pair_of * rows : (pair_of + 2) * rows, :] = jnp.concatenate(
                [p[mine] for p in products], axis=0
            ).astype(BF16)


def partial_kernel(rows, edges, out):
    for channel in range(out.shape[0]):
        out[channel] = dot(*triangle_sides(edges, rows, channel), NT)


def update_kernel(
    returned, gate, pair, w_tri_out, w_bias_t, first_pass, att_norm, bias, held, bias_held, turned
):
    rows, cols, width = pair.shape
    owners, block = returned.shape[0], returned.shape[1]
    channels = owners * block // rows
    total = jnp.zeros((rows, cols), F32)
    for owner in range(owners):
        total += jnp.sum(returned[owner].astype(F32).reshape(block // rows, rows, cols), axis=0)
    average = total / channels
    square = jnp.zeros((rows, cols), F32)
    for owner in range(owners):
        centered = returned[slot(owner, owners)].astype(F32).reshape(block // rows, rows, cols) - average
        square += jnp.sum(centered * centered, axis=0)
        for tile, lanes in lane_tiles(pair):
            held[tile, owner * block : (owner + 1) * block, :] = centered.reshape(block, cols)[:, lanes]
    scale = lax.rsqrt(square / channels + 1e-05)

    weight = twice(w_tri_out[...])

    def turn(i):
        for row in (i, i + 1):
            tri_norm = jnp.concatenate(
                [held[tile, pl.ds(row, channels, stride=rows), :] for tile, _ in lane_tiles(pair)], axis=1
            )
            turned[row % 4] = (tri_norm * scale[row : row + 1]).astype(BF16).T

    def update(i):
        both = dot(side_by_side(turned, i % 4), weight)
        first_pass[i] = pair[i].astype(F32) + gate[i] * both[:, :width]
        first_pass[i + 1] = pair[i + 1].astype(F32) + gate[i + 1] * both[:, width:]

    def norm(i):
        for row in (i, i + 1):
            att_norm[row] = lane_norm(first_pass[row])

    def project_bias(i):
        both = dot(w_bias_t[...], jnp.concatenate([att_norm[i], att_norm[i + 1]], axis=0), NT)
        for row in range(2):
            for head in range(HEADS):
                place = head * rows + i + row
                bias_held[place : place + 1, :] = both[head : head + 1, row * cols : (row + 1) * cols]

    pipeline(range(0, rows, 2), turn, update, norm, project_bias)
    rounded = bias_held[...].astype(BF16)
    for owner in range(bias.shape[0]):
        bias[owner] = rounded


def projector(att_norm, w_query, w_key, w_value, w_att_gate, query_t, key, value_t, gate_t):
    w_turned = jnp.concatenate([w[...].T for w in (w_query, w_value, w_att_gate)], axis=0)
    width = w_query.shape[1]

    def project(i):
        normed = att_norm[i]
        key[i] = dot(normed, w_key[...]).astype(BF16)
        turned = dot(w_turned, normed, NT)
        query_t[i] = turned[:width].astype(BF16)
        value_t[i] = turned[width : 2 * width].astype(BF16)
        gate_t[i] = sigmoid(turned[2 * width :])

    return project


def project_kernel(*refs):
    looped(refs[0].shape[0], projector(*refs))


def whole_kernel(att_norm, w_query, w_key, w_value, w_att_gate, *refs):
    given, projected, held = refs[:4], refs[4:8], refs[8:]
    project = projector(att_norm, w_query, w_key, w_value, w_att_gate, *projected)
    attend_kernel(*projected, *given, *held, before=(project,))


def attend_kernel(
    query_t,
    key,
    value_t,
    gate_t,
    first_pass,
    bias,
    w_att_out,
    out,
    bias_t,
    scores,
    weights,
    gated,
    before=(),
):
    rows, width, cols = query_t.shape
    head_rows = bias.shape[1] // HEADS
    score_scale = LOG2_E / HEAD_DIM**0.5
    ones = jnp.ones((16, key.shape[1]), BF16)
    heads = [
        (slice(h * HEAD_DIM, (h + 1) * HEAD_DIM), slice(h * cols, (h + 1) * cols)) for h in range(HEADS)
    ]

    def score(i):
        blocks = []
        for mine, _ in heads:
            above = jnp.zeros((mine.start, cols), BF16)
            below = jnp.zeros((width - mine.stop, cols), BF16)
            parts = [p for p in (above, query_t[i, mine, :], below) if p.shape[0]]
            blocks.append(jnp.concatenate(parts, axis=0))
        scores[lax.rem(i, 2)] = dot(key[i], jnp.concatenate(blocks, axis=1)) * score_scale

    def soften(i):
        for _, span in heads:
            biased = scores[lax.rem(i, 2), :, span] + bias_t[:, span]
            peak = jnp.max(biased, axis=0, keepdims=True)
            weights[lax.rem(i, 2), :, span] = jnp.exp2(biased - peak).astype(BF16)

    def collect(i):
        for head in range(0, HEADS, 2):
            (first, left), (second, right) = heads[head : head + 2]
            values = jnp.concatenate([value_t[i, first.start : second.stop, :], ones], axis=0)
            summed = dot(values, weights[lax.rem(i, 2), :, left.start : right.stop])
            share = 1.0 / summed[2 * HEAD_DIM : 2 * HEAD_DIM + 1]
            for mine, there, lanes in (
                (first, slice(0, HEAD_DIM), slice(0, cols)),
                (second, slice(HEAD_DIM, 2 * HEAD_DIM), slice(cols, 2 * cols)),
            ):
                attended = summed[there, lanes] * share[:, lanes] * gate_t[i, mine, :]
                gated[lax.rem(i, 2), mine, :] = attended.astype(BF16)

    def finish(i):
        turned = gated[lax.rem(i, 2)].T
        out[i] = (first_pass[i] + dot(turned, w_att_out[...])).astype(BF16)

    for head, (_, span) in enumerate(heads):
        parts = [
            bias[slot(owner, bias.shape[0])].astype(F32)[head * head_rows : (head + 1) * head_rows]
            for owner in range(bias.shape[0])
        ]
        bias_t[:, span] = jnp.concatenate(parts, axis=0).T * LOG2_E
    looped(rows, *before, score, soften, collect, finish)


def call(kernel, outs, scratch, flops, *operands, fetched=0):
    vmem = pl.BlockSpec(memory_space=pltpu.VMEM)
    far = pl.BlockSpec(memory_space=pltpu.HBM)
    shapes = [jax.ShapeDtypeStruct(shape, dtype) for shape, dtype in outs]
    moved = sum(o.size * o.dtype.itemsize for o in operands)
    operands = [
        pltpu.with_memory_space_constraint(o, pltpu.HBM) if n < fetched else o
        for n, o in enumerate(operands)
    ]
    got = pl.pallas_call(
        kernel,
        out_shape=shapes,
        in_specs=[far] * fetched + [vmem] * (len(operands) - fetched),
        out_specs=[vmem] * len(shapes),
        scratch_shapes=[pltpu.VMEM(*s) if isinstance(s, tuple) else s for s in scratch],
        compiler_params=pltpu.CompilerParams(vmem_limit_bytes=48 * 2**20),
        cost_estimate=pl.CostEstimate(flops=flops, bytes_accessed=moved, transcendentals=0),
    )(*operands)
    return got if len(got) > 1 else got[0]


def body(
    pair_rep,
    w_left,
    w_left_gate,
    w_right,
    w_right_gate,
    w_tri_gate,
    w_tri_out,
    w_query,
    w_key,
    w_value,
    w_bias,
    w_att_gate,
    w_att_out,
):
    rows, cols, width = pair_rep.shape
    channels = w_left.shape[1]
    owners, col_parts = lax.axis_size("row"), lax.axis_size("col")
    own = channels // owners
    residues = owners * rows
    cells = rows * cols

    edges, gate, w_tri_out, w_query, w_key, w_value, w_att_gate, w_att_out, w_bias_t = call(
        edges_kernel,
        [
            ((owners, own * 2 * rows, cols), BF16),
            ((rows, cols, width), F32),
            *[(w.shape, BF16) for w in (w_tri_out, w_query, w_key, w_value, w_att_gate, w_att_out)],
            (w_bias.shape[::-1], BF16),
        ],
        [
            (pair_rep.shape, BF16),
            ((5, width, channels), BF16),
            (pair_rep.shape, BF16),
            ((cols // LANES, channels * 2 * rows, LANES), F32),
            pltpu.SemaphoreType.DMA((13,)),
        ],
        10 * cells * width * channels,
        pair_rep,
        w_left,
        w_left_gate,
        w_right,
        w_right_gate,
        w_tri_gate,
        w_tri_out,
        w_query,
        w_key,
        w_value,
        w_att_gate,
        w_att_out,
        w_bias.T,
        fetched=13,
    )
    spread = swap(edges)
    flops = 2 * own * residues * residues * cols
    if col_parts == 1:
        summed = call(
            functools.partial(triangle_kernel, rows),
            [((owners, own * rows, residues), BF16)],
            [],
            flops,
            spread,
        )
    else:
        partial_sums = call(
            functools.partial(partial_kernel, rows),
            [((own, residues, residues), F32)],
            [],
            flops,
            spread,
        )
        summed = lax.psum_scatter(partial_sums, "col", scatter_dimension=2, tiled=True).astype(BF16)
        summed = by_slot(summed.reshape(own, owners, rows, cols).swapaxes(0, 1))
        summed = summed.reshape(owners, own * rows, cols)
    returned = swap(summed)
    first_pass, att_norm, bias_copies = call(
        update_kernel,
        [
            ((rows, cols, width), F32),
            ((rows, cols, width), BF16),
            ((owners, HEADS * rows, cols), BF16),
        ],
        [
            ((cols // LANES, channels * rows, LANES), F32),
            ((HEADS * rows, cols), F32),
            ((4, cols, channels), BF16),
        ],
        2 * cells * channels * width,
        returned,
        gate,
        pair_rep,
        w_tri_out,
        w_bias_t,
    )
    bias = swap(bias_copies)
    projected = [
        ((rows, width, cols), BF16),
        ((rows, cols, width), BF16),
        ((rows, width, cols), BF16),
        ((rows, width, cols), F32),
    ]
    projecting = (att_norm, w_query, w_key, w_value, w_att_gate)
    residues = cols * col_parts
    out = [((rows, cols, width), BF16)]
    held = [
        ((residues, HEADS * cols), F32),
        ((2, residues, HEADS * cols), F32),
        ((2, residues, HEADS * cols), BF16),
        ((2, width, cols), BF16),
    ]
    project_flops, attend_flops = 8 * cells * width * width, 4 * cells * residues * width
    if col_parts == 1:
        flops = project_flops + attend_flops
        given = (first_pass, bias, w_att_out)
        return call(whole_kernel, out, projected + held, flops, *projecting, *given)
    query_t, key, value_t, gate_t = call(project_kernel, projected, [], project_flops, *projecting)
    bias = by_slot(lax.all_to_all(by_rank(bias), "col", split_axis=0, concat_axis=2, tiled=True))
    key = lax.all_gather(key, "col", axis=1, tiled=True)
    value_t = lax.all_gather(value_t, "col", axis=2, tiled=True)
    given = (query_t, key, value_t, gate_t, first_pass, bias, w_att_out)
    return call(attend_kernel, out, held, attend_flops, *given)


def solution(mesh):
    in_specs = (P(("grp", "row"), "col", None),) + (P(),) * 12
    out_specs = P(("grp", "row"), "col", None)
    return jax.shard_map(body, mesh=mesh, in_specs=in_specs, out_specs=out_specs, check_vma=False)
```

```python
import functools

import jax
import jax.numpy as jnp
import numpy as np
from jax import lax
from jax.experimental import pallas as pl
from jax.experimental.pallas import tpu as pltpu
from jax.sharding import PartitionSpec as P

HEADS = 4
HEAD_DIM = 32
LANES = 128
LOG2_E = 1.4426950408889634
F32 = jnp.float32
BF16 = jnp.bfloat16
NN = (((1,), (0,)), ((), ()))
NT = (((1,), (1,)), ((), ()))
TN = (((0,), (0,)), ((), ()))


def dot(left, right, dims=NN):
    return lax.dot_general(left, right, dims, preferred_element_type=F32)


def sigmoid(values):
    return 0.5 * jnp.tanh(0.5 * values) + 0.5


def twice(weight):
    zeros = jnp.zeros_like(weight)
    return jnp.concatenate(
        [jnp.concatenate([weight, zeros], axis=1), jnp.concatenate([zeros, weight], axis=1)], axis=0
    )


def listing(ranks):
    first = ranks - 1 - ranks // 4
    return [first] + [rank for rank in range(ranks - 1, -1, -1) if rank != first]


def slot(rank, ranks):
    return listing(ranks).index(rank)


def swap(blocks):
    return lax.all_to_all(
        blocks,
        "row",
        split_axis=0,
        concat_axis=0,
        axis_index_groups=[listing(blocks.shape[0])],
        tiled=True,
    )


def by_rank(blocks):
    return blocks[np.array([slot(r, blocks.shape[0]) for r in range(blocks.shape[0])])]


def by_slot(blocks):
    return blocks[np.array(listing(blocks.shape[0]))]


def lane_tiles(values):
    lanes = values.shape[1]
    return [(t, slice(t * LANES, (t + 1) * LANES)) for t in range(lanes // LANES)]


def lane_norm(values):
    centered = values - jnp.mean(values, axis=-1, keepdims=True)
    variance = jnp.mean(centered * centered, axis=-1, keepdims=True)
    return (centered * lax.rsqrt(variance + 1e-05)).astype(BF16)


def side_by_side(held, i):
    return jnp.concatenate([held[i], held[i + 1]], axis=1)


def pipeline(rows, *steps):
    for tick in range(len(rows) + len(steps) - 1):
        for late, step in enumerate(steps):
            if 0 <= tick - late < len(rows):
                step(rows[tick - late])


def edges_kernel(*refs):
    given, (out, gate, *staged), (pair, weights, normed, held, sems) = refs[:13], refs[13:22], refs[22:]
    targets = [pair, *(weights.at[n] for n in range(5)), *staged]
    copies = [
        pltpu.make_async_copy(source, target, sems.at[n])
        for n, (source, target) in enumerate(zip(given, targets))
    ]
    for copy in copies:
        copy.start()
    for copy in copies[:6]:
        copy.wait()
    rows, width = pair.shape[0], pair.shape[2]
    channels = weights.shape[2]
    cols = pair.shape[1]
    turned = jnp.concatenate([weights[n].T for n in range(4)], axis=0)
    gate_weight = twice(weights[4])

    def norm(i):
        normed[i] = lane_norm(pair[i].astype(F32))
        normed[i + 1] = lane_norm(pair[i + 1].astype(F32))

    def project(i):
        both = dot(turned, jnp.concatenate([normed[i], normed[i + 1]], axis=0), NT)
        for side in range(2):
            base = 2 * side * channels
            act = sigmoid(both[base + channels : base + 2 * channels]) * both[base : base + channels]
            for tile, lanes in lane_tiles(act):
                row, part = divmod(tile, cols // LANES)
                place = pl.ds(side * rows + i + row, channels, stride=2 * rows)
                held[part, place, :] = act[:, lanes]
        opened = sigmoid(dot(side_by_side(normed, i), gate_weight))
        gate[i] = opened[:, :width]
        gate[i + 1] = opened[:, width:]

    pipeline(range(0, rows, 2), norm, project)
    owners, block = out.shape[0], out.shape[1]
    for owner in range(owners):
        for tile, lanes in lane_tiles(pair):
            out[slot(owner, owners), :, lanes] = held[tile, owner * block : (owner + 1) * block, :].astype(BF16)
    for copy in copies[6:]:
        copy.wait()


def triangle_sides(edges, rows, channel):
    sides = [[], []]
    sources = edges.shape[0]
    for source in range(sources):
        block = edges[slot(source, sources), channel * 2 * rows : (channel + 1) * 2 * rows, :].astype(F32)
        sides[0].append(block[:rows])
        sides[1].append(block[rows:])
    return [jnp.concatenate(side, axis=0).astype(BF16) for side in sides]


def triangle_kernel(rows, edges, out):
    for pair_of in range(0, out.shape[1] // rows, 2):
        products = [dot(*triangle_sides(edges, rows, pair_of + o), NT) for o in range(2)]
        owners = out.shape[0]
        for owner in range(owners):
            mine = slice(owner * rows, (owner + 1) * rows)
            out[slot(owner, owners), pair_of * rows : (pair_of + 2) * rows, :] = jnp.concatenate(
                [p[mine] for p in products], axis=0
            ).astype(BF16)


def partial_kernel(rows, edges, out):
    for channel in range(out.shape[0]):
        out[channel] = dot(*triangle_sides(edges, rows, channel), NT)


def update_kernel(
    returned, gate, pair, w_tri_out, w_bias_t, first_pass, att_norm, bias, held, bias_held, turned
):
    rows, cols, width = pair.shape
    owners, block = returned.shape[0], returned.shape[1]
    channels = owners * block // rows
    total = jnp.zeros((rows, cols), F32)
    for owner in range(owners):
        total += jnp.sum(returned[owner].astype(F32).reshape(block // rows, rows, cols), axis=0)
    average = total / channels
    square = jnp.zeros((rows, cols), F32)
    for owner in range(owners):
        centered = returned[slot(owner, owners)].astype(F32).reshape(block // rows, rows, cols) - average
        square += jnp.sum(centered * centered, axis=0)
        for tile, lanes in lane_tiles(pair):
            held[tile, owner * block : (owner + 1) * block, :] = centered.reshape(block, cols)[:, lanes]
    scale = lax.rsqrt(square / channels + 1e-05)

    weight = twice(w_tri_out[...])

    def turn(i):
        for row in (i, i + 1):
            tri_norm = jnp.concatenate(
                [held[tile, pl.ds(row, channels, stride=rows), :] for tile, _ in lane_tiles(pair)], axis=1
            )
            turned[row % 4] = (tri_norm * scale[row : row + 1]).astype(BF16).T

    def update(i):
        both = dot(side_by_side(turned, i % 4), weight)
        first_pass[i] = pair[i].astype(F32) + gate[i] * both[:, :width]
        first_pass[i + 1] = pair[i + 1].astype(F32) + gate[i + 1] * both[:, width:]

    def norm(i):
        for row in (i, i + 1):
            att_norm[row] = lane_norm(first_pass[row])

    def project_bias(i):
        both = dot(w_bias_t[...], jnp.concatenate([att_norm[i], att_norm[i + 1]], axis=0), NT)
        for row in range(2):
            for head in range(HEADS):
                place = head * rows + i + row
                bias_held[place : place + 1, :] = both[head : head + 1, row * cols : (row + 1) * cols]

    pipeline(range(0, rows, 2), turn, update, norm, project_bias)
    rounded = bias_held[...].astype(BF16)
    for owner in range(bias.shape[0]):
        bias[owner] = rounded


def projector(att_norm, w_query, w_key, w_value, w_att_gate, query_t, key, value_t, gate_t):
    w_turned = jnp.concatenate([w[...].T for w in (w_query, w_value, w_att_gate)], axis=0)
    w_direct = twice(w_key[...])
    cols, width = att_norm.shape[1], w_query.shape[1]

    def project(i):
        keys = dot(side_by_side(att_norm, i), w_direct).astype(BF16)
        turned = dot(w_turned, jnp.concatenate([att_norm[i], att_norm[i + 1]], axis=0), NT)
        for row in range(2):
            key[i + row] = keys[:, row * width : (row + 1) * width]
            mine = turned[:, row * cols : (row + 1) * cols]
            query_t[i + row] = mine[:width].astype(BF16)
            value_t[i + row] = mine[width : 2 * width].astype(BF16)
            gate_t[i + row] = sigmoid(mine[2 * width :])

    return project


def project_kernel(*refs):
    pipeline(range(0, refs[0].shape[0], 2), projector(*refs))


def whole_kernel(att_norm, w_query, w_key, w_value, w_att_gate, *refs):
    given, projected, held = refs[:4], refs[4:8], refs[8:]
    project = projector(att_norm, w_query, w_key, w_value, w_att_gate, *projected)
    attend_kernel(*projected, *given, *held, before=(project,))


def attend_kernel(
    query_t,
    key,
    value_t,
    gate_t,
    first_pass,
    bias,
    w_att_out,
    out,
    bias_t,
    scores,
    peaks,
    weights,
    gated,
    done,
    sems,
    before=(),
):
    rows, width, cols = query_t.shape
    head_rows = bias.shape[1] // HEADS
    score_scale = LOG2_E / HEAD_DIM**0.5
    ones = jnp.ones((16, key.shape[1]), BF16)
    heads = [
        (slice(h * HEAD_DIM, (h + 1) * HEAD_DIM), slice(h * cols, (h + 1) * cols)) for h in range(HEADS)
    ]

    def score(i):
        for row in (i, i + 1):
            blocks = []
            for mine, _ in heads:
                above = jnp.zeros((mine.start, cols), BF16)
                below = jnp.zeros((width - mine.stop, cols), BF16)
                parts = [p for p in (above, query_t[row, mine, :], below) if p.shape[0]]
                blocks.append(jnp.concatenate(parts, axis=0))
            raw = dot(key[row], jnp.concatenate(blocks, axis=1))
            for _, span in heads:
                biased = raw[:, span] * score_scale + bias_t[:, span]
                scores[row % 4, :, span] = biased
                peaks[row % 4, :, span] = jnp.max(biased, axis=0, keepdims=True)

    def soften(i):
        for row in (i, i + 1):
            for _, span in heads:
                lowered = scores[row % 4, :, span] - peaks[row % 4, :, span]
                weights[row % 4, :, span] = jnp.exp2(lowered).astype(BF16)

    def collect(i):
        for row in (i, i + 1):
            for head in range(0, HEADS, 2):
                (first, left), (second, right) = heads[head : head + 2]
                values = jnp.concatenate([value_t[row, first.start : second.stop, :], ones], axis=0)
                summed = dot(values, weights[row % 4, :, left.start : right.stop])
                share = 1.0 / summed[2 * HEAD_DIM : 2 * HEAD_DIM + 1]
                for mine, there, lanes in (
                    (first, slice(0, HEAD_DIM), slice(0, cols)),
                    (second, slice(HEAD_DIM, 2 * HEAD_DIM), slice(cols, 2 * cols)),
                ):
                    attended = summed[there, lanes] * share[:, lanes] * gate_t[row, mine, :]
                    gated[row % 4, mine, :] = attended.astype(BF16)

    def finish(i):
        turned = jnp.concatenate([gated[i % 4].T, gated[(i + 1) % 4].T], axis=1)
        both = dot(turned, w_last)
        done[i] = (first_pass[i] + both[:, :width]).astype(BF16)
        done[i + 1] = (first_pass[i + 1] + both[:, width:]).astype(BF16)
        copy = pltpu.make_async_copy(done.at[pl.ds(i, 2)], out.at[pl.ds(i, 2)], sems.at[i // 2])
        copy.start()
        copies.append(copy)

    copies = []
    w_last = twice(w_att_out[...])
    for head, (_, span) in enumerate(heads):
        parts = [
            bias[slot(owner, bias.shape[0])].astype(F32)[head * head_rows : (head + 1) * head_rows]
            for owner in range(bias.shape[0])
        ]
        bias_t[:, span] = jnp.concatenate(parts, axis=0).T * LOG2_E
    pipeline(range(0, rows, 2), *before, score, soften, collect, finish)
    for copy in copies:
        copy.wait()


def call(kernel, outs, scratch, flops, *operands, fetched=0, sent=False):
    vmem = pl.BlockSpec(memory_space=pltpu.VMEM)
    far = pl.BlockSpec(memory_space=pltpu.HBM)
    shapes = [jax.ShapeDtypeStruct(shape, dtype) for shape, dtype in outs]
    moved = sum(o.size * o.dtype.itemsize for o in operands)
    operands = [
        pltpu.with_memory_space_constraint(o, pltpu.HBM) if n < fetched else o
        for n, o in enumerate(operands)
    ]
    got = pl.pallas_call(
        kernel,
        out_shape=shapes,
        in_specs=[far] * fetched + [vmem] * (len(operands) - fetched),
        out_specs=[far if sent else vmem] * len(shapes),
        scratch_shapes=[pltpu.VMEM(*s) if isinstance(s, tuple) else s for s in scratch],
        compiler_params=pltpu.CompilerParams(vmem_limit_bytes=48 * 2**20),
        cost_estimate=pl.CostEstimate(flops=flops, bytes_accessed=moved, transcendentals=0),
    )(*operands)
    return got if len(got) > 1 else got[0]


def body(
    pair_rep,
    w_left,
    w_left_gate,
    w_right,
    w_right_gate,
    w_tri_gate,
    w_tri_out,
    w_query,
    w_key,
    w_value,
    w_bias,
    w_att_gate,
    w_att_out,
):
    rows, cols, width = pair_rep.shape
    channels = w_left.shape[1]
    owners, col_parts = lax.axis_size("row"), lax.axis_size("col")
    own = channels // owners
    residues = owners * rows
    cells = rows * cols

    edges, gate, w_tri_out, w_query, w_key, w_value, w_att_gate, w_att_out, w_bias_t = call(
        edges_kernel,
        [
            ((owners, own * 2 * rows, cols), BF16),
            ((rows, cols, width), F32),
            *[(w.shape, BF16) for w in (w_tri_out, w_query, w_key, w_value, w_att_gate, w_att_out)],
            (w_bias.shape[::-1], BF16),
        ],
        [
            (pair_rep.shape, BF16),
            ((5, width, channels), BF16),
            (pair_rep.shape, BF16),
            ((cols // LANES, channels * 2 * rows, LANES), F32),
            pltpu.SemaphoreType.DMA((13,)),
        ],
        10 * cells * width * channels,
        pair_rep,
        w_left,
        w_left_gate,
        w_right,
        w_right_gate,
        w_tri_gate,
        w_tri_out,
        w_query,
        w_key,
        w_value,
        w_att_gate,
        w_att_out,
        w_bias.T,
        fetched=13,
    )
    spread = swap(edges)
    flops = 2 * own * residues * residues * cols
    if col_parts == 1:
        summed = call(
            functools.partial(triangle_kernel, rows),
            [((owners, own * rows, residues), BF16)],
            [],
            flops,
            spread,
        )
    else:
        partial_sums = call(
            functools.partial(partial_kernel, rows),
            [((own, residues, residues), F32)],
            [],
            flops,
            spread,
        )
        summed = lax.psum_scatter(partial_sums, "col", scatter_dimension=2, tiled=True).astype(BF16)
        summed = by_slot(summed.reshape(own, owners, rows, cols).swapaxes(0, 1))
        summed = summed.reshape(owners, own * rows, cols)
    returned = swap(summed)
    first_pass, att_norm, bias_copies = call(
        update_kernel,
        [
            ((rows, cols, width), F32),
            ((rows, cols, width), BF16),
            ((owners, HEADS * rows, cols), BF16),
        ],
        [
            ((cols // LANES, channels * rows, LANES), F32),
            ((HEADS * rows, cols), F32),
            ((4, cols, channels), BF16),
        ],
        2 * cells * channels * width,
        returned,
        gate,
        pair_rep,
        w_tri_out,
        w_bias_t,
    )
    bias = swap(bias_copies)
    projected = [
        ((rows, width, cols), BF16),
        ((rows, cols, width), BF16),
        ((rows, width, cols), BF16),
        ((rows, width, cols), F32),
    ]
    projecting = (att_norm, w_query, w_key, w_value, w_att_gate)
    residues = cols * col_parts
    out = [((rows, cols, width), BF16)]
    held = [
        ((residues, HEADS * cols), F32),
        ((4, residues, HEADS * cols), F32),
        ((4, 1, HEADS * cols), F32),
        ((4, residues, HEADS * cols), BF16),
        ((4, width, cols), BF16),
        ((rows, cols, width), BF16),
        pltpu.SemaphoreType.DMA((rows // 2,)),
    ]
    project_flops, attend_flops = 8 * cells * width * width, 4 * cells * residues * width
    if col_parts == 1:
        flops = project_flops + attend_flops
        given = (first_pass, bias, w_att_out)
        return call(whole_kernel, out, projected + held, flops, *projecting, *given, sent=True)
    query_t, key, value_t, gate_t = call(project_kernel, projected, [], project_flops, *projecting)
    bias = by_slot(lax.all_to_all(by_rank(bias), "col", split_axis=0, concat_axis=2, tiled=True))
    key = lax.all_gather(key, "col", axis=1, tiled=True)
    value_t = lax.all_gather(value_t, "col", axis=2, tiled=True)
    given = (query_t, key, value_t, gate_t, first_pass, bias, w_att_out)
    return call(attend_kernel, out, held, attend_flops, *given, sent=True)


def solution(mesh):
    in_specs = (P(("grp", "row"), "col", None),) + (P(),) * 12
    out_specs = P(("grp", "row"), "col", None)
    return jax.shard_map(body, mesh=mesh, in_specs=in_specs, out_specs=out_specs, check_vma=False)
```

```python
import functools

import jax
import jax.numpy as jnp
import numpy as np
from jax import lax
from jax.experimental import pallas as pl
from jax.experimental.pallas import tpu as pltpu
from jax.sharding import PartitionSpec as P

HEADS = 4
HEAD_DIM = 32
LANES = 128
LOG2_E = 1.4426950408889634
F32 = jnp.float32
BF16 = jnp.bfloat16
NN = (((1,), (0,)), ((), ()))
NT = (((1,), (1,)), ((), ()))
TN = (((0,), (0,)), ((), ()))


def dot(left, right, dims=NN):
    return lax.dot_general(left, right, dims, preferred_element_type=F32)


def sigmoid(values):
    return 0.5 * jnp.tanh(0.5 * values) + 0.5


def twice(weight):
    zeros = jnp.zeros_like(weight)
    return jnp.concatenate(
        [jnp.concatenate([weight, zeros], axis=1), jnp.concatenate([zeros, weight], axis=1)], axis=0
    )


def listing(ranks):
    first = ranks - 1 - ranks // 4
    return [first] + [rank for rank in range(ranks - 1, -1, -1) if rank != first]


def slot(rank, ranks):
    return listing(ranks).index(rank)


def slot_of(rank, ranks):
    first = listing(ranks)[0]
    return jnp.where(rank == first, 0, ranks - 1 - rank + (rank > first).astype(jnp.int32))


def swap(blocks, ranks):
    members = blocks.shape[0]
    order = listing(members)
    groups = [[first + member for member in order] for first in range(0, ranks, members)]
    return lax.all_to_all(
        blocks, "row", split_axis=0, concat_axis=0, axis_index_groups=groups, tiled=True
    )


def by_rank(blocks):
    return blocks[np.array([slot(r, blocks.shape[0]) for r in range(blocks.shape[0])])]


def by_slot(blocks):
    return blocks[np.array(listing(blocks.shape[0]))]


def lane_tiles(values):
    lanes = values.shape[1]
    return [(t, slice(t * LANES, (t + 1) * LANES)) for t in range(lanes // LANES)]


def lane_norm(values):
    centered = values - jnp.mean(values, axis=-1, keepdims=True)
    variance = jnp.mean(centered * centered, axis=-1, keepdims=True)
    return (centered * lax.rsqrt(variance + 1e-05)).astype(BF16)


def side_by_side(held, i):
    return jnp.concatenate([held[i], held[i + 1]], axis=1)


def pipeline(rows, *steps):
    for tick in range(len(rows) + len(steps) - 1):
        for late, step in enumerate(steps):
            if 0 <= tick - late < len(rows):
                step(rows[tick - late])


def gated_edges(normed, weight, weight_gate, held):
    rows, cols = normed.shape[0], normed.shape[1]
    channels = weight.shape[1]
    turned = jnp.concatenate([weight[...].T, weight_gate[...].T], axis=0)

    def project(i):
        both = dot(turned, jnp.concatenate([normed[i], normed[i + 1]], axis=0), NT)
        act = sigmoid(both[channels:]) * both[:channels]
        for tile, lanes in lane_tiles(act):
            row, part = divmod(tile, cols // LANES)
            held[part, pl.ds(i + row, channels, stride=rows), :] = act[:, lanes]

    return project


def edges_kernel(*refs):
    given, (right, far, near, normed, *staged) = refs[:13], refs[13:25]
    pair, weights, held, sems = refs[25:]
    targets = [pair, *(weights.at[n] for n in range(4)), *staged]
    copies = [
        pltpu.make_async_copy(source, target, sems.at[n])
        for n, (source, target) in enumerate(zip(given, targets))
    ]
    for copy in copies:
        copy.start()
    for copy in copies[:5]:
        copy.wait()

    def norm(i):
        normed[i] = lane_norm(pair[i].astype(F32))
        normed[i + 1] = lane_norm(pair[i + 1].astype(F32))

    steps = [gated_edges(normed, weights.at[2 * n], weights.at[2 * n + 1], held.at[n]) for n in range(2)]
    pipeline(range(0, pair.shape[0], 2), norm, *steps)
    owners, block, parts = right.shape[0], right.shape[1], held.shape[1]
    members, turns = owners // 2, near.shape[0]
    me = lax.rem(lax.axis_index("row"), members)
    for member in range(members):
        mine = pl.ds(pl.multiple_of((me ^ member) * block, block), block)
        out = (near, far)[member // turns]
        for part in range(parts):
            lanes = slice(part * LANES, (part + 1) * LANES)
            out[member % turns, :, lanes] = held[0, part, mine, :].astype(BF16)
    for member in range(members):
        for part in range(parts):
            lanes = slice(part * LANES, (part + 1) * LANES)
            sent = held[1, part, member * block : (member + 1) * block, :].astype(BF16)
            for owner in range(member, owners, members):
                right[slot(owner, owners), :, lanes] = sent
    for copy in copies[5:]:
        copy.wait()


def merge_kernel(normed, w_tri_gate, near, passed, gate, *left):
    for turn, out in enumerate(left):
        out[0] = near[turn]
        out[1] = passed[turn]
    width = w_tri_gate.shape[1]
    gate_weight = twice(w_tri_gate[...])
    for i in range(0, normed.shape[0], 2):
        opened = sigmoid(dot(side_by_side(normed, i), gate_weight))
        gate[i] = opened[:, :width]
        gate[i + 1] = opened[:, width:]


def channel_rows(blocks, rows, channel):
    mine = slice(channel * rows, (channel + 1) * rows)
    both = slice(channel // 2 * 2 * rows, (channel // 2 + 1) * 2 * rows)
    inner = slice(mine.start - both.start, mine.stop - both.start)
    parts = [block[both, :].astype(F32)[inner] for block in blocks]
    return jnp.concatenate(parts, axis=0).astype(BF16)


def triangle_product(left, right, rows, channel):
    ranks = right.shape[0]
    by_owner = [right.at[slot(r, ranks)] for r in range(ranks)]
    return dot(channel_rows(left, rows, channel), channel_rows(by_owner, rows, channel), NT)


def left_blocks(refs):
    return [block.at[0] for block in refs] + [block.at[1] for block in refs]


def triangle_kernel(rows, right, *refs):
    left, out = left_blocks(refs[:-1]), refs[-1]
    members = len(left)
    me = lax.rem(lax.axis_index("row"), members)
    for channel in range(0, out.shape[1] // rows, 2):
        products = [triangle_product(left, right, rows, channel + o) for o in range(2)]
        for turn in range(members):
            mine = slice(turn * rows, (turn + 1) * rows)
            out[slot_of(me ^ turn, members), channel * rows : (channel + 2) * rows, :] = jnp.concatenate(
                [p[mine] for p in products], axis=0
            ).astype(BF16)


def partial_kernel(rows, right, *refs):
    left, out = left_blocks(refs[:-1]), refs[-1]
    members = len(left)
    me = lax.rem(lax.axis_index("row"), members)
    for channel in range(out.shape[0]):
        product = triangle_product(left, right, rows, channel)
        for turn in range(members):
            place = pl.ds(pl.multiple_of((me ^ turn) * rows, rows), rows)
            out[channel, place, :] = product[turn * rows : (turn + 1) * rows]


def update_kernel(
    returned, gate, pair, w_tri_out, w_bias_t, first_pass, att_norm, bias, held, bias_held, turned
):
    rows, cols, width = pair.shape
    owners, block = returned.shape[0], returned.shape[1]
    channels = owners * block // rows
    total = jnp.zeros((rows, cols), F32)
    for owner in range(owners):
        total += jnp.sum(returned[owner].astype(F32).reshape(block // rows, rows, cols), axis=0)
    average = total / channels
    square = jnp.zeros((rows, cols), F32)
    for owner in range(owners):
        centered = returned[slot(owner, owners)].astype(F32).reshape(block // rows, rows, cols) - average
        square += jnp.sum(centered * centered, axis=0)
        for tile, lanes in lane_tiles(pair):
            held[tile, owner * block : (owner + 1) * block, :] = centered.reshape(block, cols)[:, lanes]
    scale = lax.rsqrt(square / channels + 1e-05)

    weight = twice(w_tri_out[...])

    def turn(i):
        for row in (i, i + 1):
            tri_norm = jnp.concatenate(
                [held[tile, pl.ds(row, channels, stride=rows), :] for tile, _ in lane_tiles(pair)], axis=1
            )
            turned[row % 4] = (tri_norm * scale[row : row + 1]).astype(BF16).T

    def update(i):
        both = dot(side_by_side(turned, i % 4), weight)
        first_pass[i] = pair[i].astype(F32) + gate[i] * both[:, :width]
        first_pass[i + 1] = pair[i + 1].astype(F32) + gate[i + 1] * both[:, width:]

    def norm(i):
        for row in (i, i + 1):
            att_norm[row] = lane_norm(first_pass[row])

    def project_bias(i):
        both = dot(w_bias_t[...], jnp.concatenate([att_norm[i], att_norm[i + 1]], axis=0), NT)
        for row in range(2):
            for head in range(HEADS):
                place = head * rows + i + row
                bias_held[place : place + 1, :] = both[head : head + 1, row * cols : (row + 1) * cols]

    pipeline(range(0, rows, 2), turn, update, norm, project_bias)
    rounded = bias_held[...].astype(BF16)
    for owner in range(bias.shape[0]):
        bias[owner] = rounded


def projector(att_norm, w_query, w_key, w_value, w_att_gate, query_t, key, value_t, gate_t):
    w_turned = jnp.concatenate([w[...].T for w in (w_query, w_value, w_att_gate)], axis=0)
    w_direct = twice(w_key[...])
    cols, width = att_norm.shape[1], w_query.shape[1]

    def project(i):
        keys = dot(side_by_side(att_norm, i), w_direct).astype(BF16)
        turned = dot(w_turned, jnp.concatenate([att_norm[i], att_norm[i + 1]], axis=0), NT)
        for row in range(2):
            key[i + row] = keys[:, row * width : (row + 1) * width]
            mine = turned[:, row * cols : (row + 1) * cols]
            query_t[i + row] = mine[:width].astype(BF16)
            value_t[i + row] = mine[width : 2 * width].astype(BF16)
            gate_t[i + row] = sigmoid(mine[2 * width :])

    return project


def project_kernel(*refs):
    pipeline(range(0, refs[0].shape[0], 2), projector(*refs))


def whole_kernel(att_norm, w_query, w_key, w_value, w_att_gate, *refs):
    given, projected, held = refs[:4], refs[4:8], refs[8:]
    project = projector(att_norm, w_query, w_key, w_value, w_att_gate, *projected)
    attend_kernel(*projected, *given, *held, before=(project,))


def attend_kernel(
    query_t,
    key,
    value_t,
    gate_t,
    first_pass,
    bias,
    w_att_out,
    out,
    bias_t,
    scores,
    peaks,
    weights,
    gated,
    done,
    sems,
    before=(),
):
    rows, width, cols = query_t.shape
    head_rows = bias.shape[1] // HEADS
    score_scale = LOG2_E / HEAD_DIM**0.5
    ones = jnp.ones((16, key.shape[1]), BF16)
    heads = [
        (slice(h * HEAD_DIM, (h + 1) * HEAD_DIM), slice(h * cols, (h + 1) * cols)) for h in range(HEADS)
    ]

    def score(i):
        for row in (i, i + 1):
            blocks = []
            for mine, _ in heads:
                above = jnp.zeros((mine.start, cols), BF16)
                below = jnp.zeros((width - mine.stop, cols), BF16)
                parts = [p for p in (above, query_t[row, mine, :], below) if p.shape[0]]
                blocks.append(jnp.concatenate(parts, axis=0))
            raw = dot(key[row], jnp.concatenate(blocks, axis=1))
            for _, span in heads:
                biased = raw[:, span] * score_scale + bias_t[:, span]
                scores[row % 4, :, span] = biased
                peaks[row % 4, :, span] = jnp.max(biased, axis=0, keepdims=True)

    def soften(i):
        for row in (i, i + 1):
            for _, span in heads:
                lowered = scores[row % 4, :, span] - peaks[row % 4, :, span]
                weights[row % 4, :, span] = jnp.exp2(lowered).astype(BF16)

    def collect(i):
        for row in (i, i + 1):
            for head in range(0, HEADS, 2):
                (first, left), (second, right) = heads[head : head + 2]
                values = jnp.concatenate([value_t[row, first.start : second.stop, :], ones], axis=0)
                summed = dot(values, weights[row % 4, :, left.start : right.stop])
                share = 1.0 / summed[2 * HEAD_DIM : 2 * HEAD_DIM + 1]
                for mine, there, lanes in (
                    (first, slice(0, HEAD_DIM), slice(0, cols)),
                    (second, slice(HEAD_DIM, 2 * HEAD_DIM), slice(cols, 2 * cols)),
                ):
                    attended = summed[there, lanes] * share[:, lanes] * gate_t[row, mine, :]
                    gated[row % 4, mine, :] = attended.astype(BF16)

    def finish(i):
        turned = jnp.concatenate([gated[i % 4].T, gated[(i + 1) % 4].T], axis=1)
        both = dot(turned, w_last)
        done[i] = (first_pass[i] + both[:, :width]).astype(BF16)
        done[i + 1] = (first_pass[i + 1] + both[:, width:]).astype(BF16)
        copy = pltpu.make_async_copy(done.at[pl.ds(i, 2)], out.at[pl.ds(i, 2)], sems.at[i // 2])
        copy.start()
        copies.append(copy)

    copies = []
    w_last = twice(w_att_out[...])
    for head, (_, span) in enumerate(heads):
        parts = [
            bias[slot(owner, bias.shape[0])].astype(F32)[head * head_rows : (head + 1) * head_rows]
            for owner in range(bias.shape[0])
        ]
        bias_t[:, span] = jnp.concatenate(parts, axis=0).T * LOG2_E
    pipeline(range(0, rows, 2), *before, score, soften, collect, finish)
    for copy in copies:
        copy.wait()


def call(kernel, outs, scratch, flops, *operands, fetched=0, sent=False):
    vmem = pl.BlockSpec(memory_space=pltpu.VMEM)
    far = pl.BlockSpec(memory_space=pltpu.HBM)
    shapes = [jax.ShapeDtypeStruct(shape, dtype) for shape, dtype in outs]
    moved = sum(o.size * o.dtype.itemsize for o in operands)
    operands = [
        pltpu.with_memory_space_constraint(o, pltpu.HBM) if n < fetched else o
        for n, o in enumerate(operands)
    ]
    got = pl.pallas_call(
        kernel,
        out_shape=shapes,
        in_specs=[far] * fetched + [vmem] * (len(operands) - fetched),
        out_specs=[far if sent else vmem] * len(shapes),
        scratch_shapes=[pltpu.VMEM(*s) if isinstance(s, tuple) else s for s in scratch],
        compiler_params=pltpu.CompilerParams(vmem_limit_bytes=48 * 2**20),
        cost_estimate=pl.CostEstimate(flops=flops, bytes_accessed=moved, transcendentals=0),
    )(*operands)
    return got if len(got) > 1 else got[0]


def body(
    pair_rep,
    w_left,
    w_left_gate,
    w_right,
    w_right_gate,
    w_tri_gate,
    w_tri_out,
    w_query,
    w_key,
    w_value,
    w_bias,
    w_att_gate,
    w_att_out,
):
    rows, cols, width = pair_rep.shape
    channels = w_left.shape[1]
    owners, col_parts = lax.axis_size("row"), lax.axis_size("col")
    half = owners // 2
    near = half // 2
    own = channels // half
    residues = owners * rows
    cells = rows * cols

    later = (w_tri_gate, w_tri_out, w_query, w_key, w_value, w_att_gate, w_att_out)
    right, far, left, normed, *later, w_bias_t = call(
        edges_kernel,
        [
            ((owners, own * rows, cols), BF16),
            ((near, own * rows, cols), BF16),
            ((near, own * rows, cols), BF16),
            (pair_rep.shape, BF16),
            *[(w.shape, BF16) for w in later],
            (w_bias.shape[::-1], BF16),
        ],
        [
            (pair_rep.shape, BF16),
            ((4, width, channels), BF16),
            ((2, cols // LANES, channels * rows, LANES), F32),
            pltpu.SemaphoreType.DMA((13,)),
        ],
        8 * cells * width * channels,
        pair_rep,
        w_left,
        w_left_gate,
        w_right,
        w_right_gate,
        *later,
        w_bias.T,
        fetched=13,
    )
    w_tri_gate, w_tri_out, w_query, w_key, w_value, w_att_gate, w_att_out = later
    passed = lax.ppermute(far, "row", [(r, r ^ near) for r in range(owners)])
    right = swap(right, owners)
    gate, *left = call(
        merge_kernel,
        [((rows, cols, width), F32)] + [((2, own * rows, cols), BF16)] * near,
        [],
        2 * cells * width * channels,
        normed,
        w_tri_gate,
        left,
        passed,
    )
    for turn in range(1, near):
        left[turn] = lax.ppermute(left[turn], "row", [(r, r ^ turn) for r in range(owners)])
    flops = 2 * own * half * rows * residues * cols
    if col_parts == 1:
        summed = call(
            functools.partial(triangle_kernel, rows),
            [((half, own * rows, residues), BF16)],
            [],
            flops,
            right,
            *left,
        )
    else:
        partial_sums = call(
            functools.partial(partial_kernel, rows),
            [((own, half * rows, residues), F32)],
            [],
            flops,
            right,
            *left,
        )
        summed = lax.psum_scatter(partial_sums, "col", scatter_dimension=2, tiled=True).astype(BF16)
        summed = by_slot(summed.reshape(own, half, rows, cols).swapaxes(0, 1))
        summed = summed.reshape(half, own * rows, cols)
    returned = swap(summed, owners)
    first_pass, att_norm, bias_copies = call(
        update_kernel,
        [
            ((rows, cols, width), F32),
            ((rows, cols, width), BF16),
            ((owners, HEADS * rows, cols), BF16),
        ],
        [
            ((cols // LANES, channels * rows, LANES), F32),
            ((HEADS * rows, cols), F32),
            ((4, cols, channels), BF16),
        ],
        2 * cells * channels * width,
        returned,
        gate,
        pair_rep,
        w_tri_out,
        w_bias_t,
    )
    bias = swap(bias_copies, owners)
    projected = [
        ((rows, width, cols), BF16),
        ((rows, cols, width), BF16),
        ((rows, width, cols), BF16),
        ((rows, width, cols), F32),
    ]
    projecting = (att_norm, w_query, w_key, w_value, w_att_gate)
    residues = cols * col_parts
    out = [((rows, cols, width), BF16)]
    held = [
        ((residues, HEADS * cols), F32),
        ((4, residues, HEADS * cols), F32),
        ((4, 1, HEADS * cols), F32),
        ((4, residues, HEADS * cols), BF16),
        ((4, width, cols), BF16),
        ((rows, cols, width), BF16),
        pltpu.SemaphoreType.DMA((rows // 2,)),
    ]
    project_flops, attend_flops = 8 * cells * width * width, 4 * cells * residues * width
    if col_parts == 1:
        flops = project_flops + attend_flops
        given = (first_pass, bias, w_att_out)
        return call(whole_kernel, out, projected + held, flops, *projecting, *given, sent=True)
    query_t, key, value_t, gate_t = call(project_kernel, projected, [], project_flops, *projecting)
    bias = by_slot(lax.all_to_all(by_rank(bias), "col", split_axis=0, concat_axis=2, tiled=True))
    key = lax.all_gather(key, "col", axis=1, tiled=True)
    value_t = lax.all_gather(value_t, "col", axis=2, tiled=True)
    given = (query_t, key, value_t, gate_t, first_pass, bias, w_att_out)
    return call(attend_kernel, out, held, attend_flops, *given, sent=True)


def solution(mesh):
    in_specs = (P(("grp", "row"), "col", None),) + (P(),) * 12
    out_specs = P(("grp", "row"), "col", None)
    return jax.shard_map(body, mesh=mesh, in_specs=in_specs, out_specs=out_specs, check_vma=False)
```

```python
import functools

import jax
import jax.numpy as jnp
import numpy as np
from jax import lax
from jax.experimental import pallas as pl
from jax.experimental.pallas import tpu as pltpu
from jax.sharding import PartitionSpec as P

HEADS = 4
HEAD_DIM = 32
LANES = 128
LOG2_E = 1.4426950408889634
F32 = jnp.float32
BF16 = jnp.bfloat16
NN = (((1,), (0,)), ((), ()))
NT = (((1,), (1,)), ((), ()))
TN = (((0,), (0,)), ((), ()))


def dot(left, right, dims=NN):
    return lax.dot_general(left, right, dims, preferred_element_type=F32)


def sigmoid(values):
    return 0.5 * jnp.tanh(0.5 * values) + 0.5


def twice(weight):
    zeros = jnp.zeros_like(weight)
    return jnp.concatenate(
        [jnp.concatenate([weight, zeros], axis=1), jnp.concatenate([zeros, weight], axis=1)], axis=0
    )


def listing(ranks):
    first = ranks - 1 - ranks // 4
    return [first] + [rank for rank in range(ranks - 1, -1, -1) if rank != first]


def slot(rank, ranks):
    return listing(ranks).index(rank)


def swap(blocks):
    return lax.all_to_all(
        blocks,
        "row",
        split_axis=0,
        concat_axis=0,
        axis_index_groups=[listing(blocks.shape[0])],
        tiled=True,
    )


def swap_apart(blocks):
    ranks, groups = blocks.shape[0], lax.axis_size("grp")
    orders = [listing(ranks), list(range(ranks))]
    return lax.all_to_all(
        blocks,
        ("grp", "row"),
        split_axis=0,
        concat_axis=0,
        axis_index_groups=[[g * ranks + r for r in orders[g % 2]] for g in range(groups)],
        tiled=True,
    )


def slot_apart(rank, ranks):
    return jnp.where(lax.rem(lax.axis_index("grp"), 2) == 0, slot(rank, ranks), rank)


def by_rank(blocks):
    return blocks[np.array([slot(r, blocks.shape[0]) for r in range(blocks.shape[0])])]


def by_slot(blocks):
    return blocks[np.array(listing(blocks.shape[0]))]


def lane_tiles(values):
    lanes = values.shape[1]
    return [(t, slice(t * LANES, (t + 1) * LANES)) for t in range(lanes // LANES)]


def lane_norm(values):
    centered = values - jnp.mean(values, axis=-1, keepdims=True)
    variance = jnp.mean(centered * centered, axis=-1, keepdims=True)
    return (centered * lax.rsqrt(variance + 1e-05)).astype(BF16)


def side_by_side(held, i):
    return jnp.concatenate([held[i], held[i + 1]], axis=1)


def pipeline(rows, *steps):
    for tick in range(len(rows) + len(steps) - 1):
        for late, step in enumerate(steps):
            if 0 <= tick - late < len(rows):
                step(rows[tick - late])


def edges_kernel(*refs):
    given, (out, gate, *staged), (pair, weights, normed, held, sems) = refs[:13], refs[13:22], refs[22:]
    targets = [pair, *(weights.at[n] for n in range(5)), *staged]
    copies = [
        pltpu.make_async_copy(source, target, sems.at[n])
        for n, (source, target) in enumerate(zip(given, targets))
    ]
    for copy in copies:
        copy.start()
    for copy in copies[:6]:
        copy.wait()
    rows, width = pair.shape[0], pair.shape[2]
    channels = weights.shape[2]
    cols = pair.shape[1]
    turned = jnp.concatenate([weights[n].T for n in range(4)], axis=0)
    gate_weight = twice(weights[4])

    def norm(i):
        normed[i] = lane_norm(pair[i].astype(F32))
        normed[i + 1] = lane_norm(pair[i + 1].astype(F32))

    def project(i):
        both = dot(turned, jnp.concatenate([normed[i], normed[i + 1]], axis=0), NT)
        for side in range(2):
            base = 2 * side * channels
            act = sigmoid(both[base + channels : base + 2 * channels]) * both[base : base + channels]
            for tile, lanes in lane_tiles(act):
                row, part = divmod(tile, cols // LANES)
                place = pl.ds(side * rows + i + row, channels, stride=2 * rows)
                held[part, place, :] = act[:, lanes]
        opened = sigmoid(dot(side_by_side(normed, i), gate_weight))
        gate[i] = opened[:, :width]
        gate[i + 1] = opened[:, width:]

    pipeline(range(0, rows, 2), norm, project)
    owners, block = out.shape[0], out.shape[1]
    for owner in range(owners):
        place = slot_apart(owner, owners)
        for tile, lanes in lane_tiles(pair):
            out[place, :, lanes] = held[tile, owner * block : (owner + 1) * block, :].astype(BF16)
    for copy in copies[6:]:
        copy.wait()


def triangle_sides(edges, rows, channel):
    sides = [[], []]
    sources = edges.shape[0]
    for source in range(sources):
        block = edges[slot_apart(source, sources), channel * 2 * rows : (channel + 1) * 2 * rows, :].astype(F32)
        sides[0].append(block[:rows])
        sides[1].append(block[rows:])
    return [jnp.concatenate(side, axis=0).astype(BF16) for side in sides]


def triangle_kernel(rows, edges, out):
    for pair_of in range(0, out.shape[1] // rows, 2):
        products = [dot(*triangle_sides(edges, rows, pair_of + o), NT) for o in range(2)]
        owners = out.shape[0]
        for owner in range(owners):
            mine = slice(owner * rows, (owner + 1) * rows)
            out[slot(owner, owners), pair_of * rows : (pair_of + 2) * rows, :] = jnp.concatenate(
                [p[mine] for p in products], axis=0
            ).astype(BF16)


def partial_kernel(rows, edges, out):
    for channel in range(out.shape[0]):
        out[channel] = dot(*triangle_sides(edges, rows, channel), NT)


def update_kernel(
    returned, gate, pair, w_tri_out, w_bias_t, first_pass, att_norm, bias, held, bias_held, turned
):
    rows, cols, width = pair.shape
    owners, block = returned.shape[0], returned.shape[1]
    channels = owners * block // rows
    total = jnp.zeros((rows, cols), F32)
    for owner in range(owners):
        total += jnp.sum(returned[owner].astype(F32).reshape(block // rows, rows, cols), axis=0)
    average = total / channels
    square = jnp.zeros((rows, cols), F32)
    for owner in range(owners):
        centered = returned[slot(owner, owners)].astype(F32).reshape(block // rows, rows, cols) - average
        square += jnp.sum(centered * centered, axis=0)
        for tile, lanes in lane_tiles(pair):
            held[tile, owner * block : (owner + 1) * block, :] = centered.reshape(block, cols)[:, lanes]
    scale = lax.rsqrt(square / channels + 1e-05)

    weight = twice(w_tri_out[...])

    def turn(i):
        for row in (i, i + 1):
            tri_norm = jnp.concatenate(
                [held[tile, pl.ds(row, channels, stride=rows), :] for tile, _ in lane_tiles(pair)], axis=1
            )
            turned[row % 4] = (tri_norm * scale[row : row + 1]).astype(BF16).T

    def update(i):
        both = dot(side_by_side(turned, i % 4), weight)
        first_pass[i] = pair[i].astype(F32) + gate[i] * both[:, :width]
        first_pass[i + 1] = pair[i + 1].astype(F32) + gate[i + 1] * both[:, width:]

    def norm(i):
        for row in (i, i + 1):
            att_norm[row] = lane_norm(first_pass[row])

    def project_bias(i):
        both = dot(w_bias_t[...], jnp.concatenate([att_norm[i], att_norm[i + 1]], axis=0), NT)
        for row in range(2):
            for head in range(HEADS):
                place = head * rows + i + row
                bias_held[place : place + 1, :] = both[head : head + 1, row * cols : (row + 1) * cols]

    pipeline(range(0, rows, 2), turn, update, norm, project_bias)
    rounded = bias_held[...].astype(BF16)
    for owner in range(bias.shape[0]):
        bias[owner] = rounded


def projector(att_norm, w_query, w_key, w_value, w_att_gate, query_t, key, value_t, gate_t):
    w_turned = jnp.concatenate([w[...].T for w in (w_query, w_value, w_att_gate)], axis=0)
    w_direct = twice(w_key[...])
    cols, width = att_norm.shape[1], w_query.shape[1]

    def project(i):
        keys = dot(side_by_side(att_norm, i), w_direct).astype(BF16)
        turned = dot(w_turned, jnp.concatenate([att_norm[i], att_norm[i + 1]], axis=0), NT)
        for row in range(2):
            key[i + row] = keys[:, row * width : (row + 1) * width]
            mine = turned[:, row * cols : (row + 1) * cols]
            query_t[i + row] = mine[:width].astype(BF16)
            value_t[i + row] = mine[width : 2 * width].astype(BF16)
            gate_t[i + row] = sigmoid(mine[2 * width :])

    return project


def project_kernel(*refs):
    pipeline(range(0, refs[0].shape[0], 2), projector(*refs))


def whole_kernel(att_norm, w_query, w_key, w_value, w_att_gate, *refs):
    given, projected, held = refs[:4], refs[4:8], refs[8:]
    project = projector(att_norm, w_query, w_key, w_value, w_att_gate, *projected)
    attend_kernel(*projected, *given, *held, before=(project,))


def attend_kernel(
    query_t,
    key,
    value_t,
    gate_t,
    first_pass,
    bias,
    w_att_out,
    out,
    bias_t,
    scores,
    peaks,
    weights,
    gated,
    done,
    sems,
    before=(),
):
    rows, width, cols = query_t.shape
    head_rows = bias.shape[1] // HEADS
    score_scale = LOG2_E / HEAD_DIM**0.5
    ones = jnp.ones((16, key.shape[1]), BF16)
    heads = [
        (slice(h * HEAD_DIM, (h + 1) * HEAD_DIM), slice(h * cols, (h + 1) * cols)) for h in range(HEADS)
    ]

    def score(i):
        for row in (i, i + 1):
            blocks = []
            for mine, _ in heads:
                above = jnp.zeros((mine.start, cols), BF16)
                below = jnp.zeros((width - mine.stop, cols), BF16)
                parts = [p for p in (above, query_t[row, mine, :], below) if p.shape[0]]
                blocks.append(jnp.concatenate(parts, axis=0))
            raw = dot(key[row], jnp.concatenate(blocks, axis=1))
            for _, span in heads:
                biased = raw[:, span] * score_scale + bias_t[:, span]
                scores[row % 4, :, span] = biased
                peaks[row % 4, :, span] = jnp.max(biased, axis=0, keepdims=True)

    def soften(i):
        for row in (i, i + 1):
            for _, span in heads:
                lowered = scores[row % 4, :, span] - peaks[row % 4, :, span]
                weights[row % 4, :, span] = jnp.exp2(lowered).astype(BF16)

    def collect(i):
        for row in (i, i + 1):
            for head in range(0, HEADS, 2):
                (first, left), (second, right) = heads[head : head + 2]
                values = jnp.concatenate([value_t[row, first.start : second.stop, :], ones], axis=0)
                summed = dot(values, weights[row % 4, :, left.start : right.stop])
                share = 1.0 / summed[2 * HEAD_DIM : 2 * HEAD_DIM + 1]
                for mine, there, lanes in (
                    (first, slice(0, HEAD_DIM), slice(0, cols)),
                    (second, slice(HEAD_DIM, 2 * HEAD_DIM), slice(cols, 2 * cols)),
                ):
                    attended = summed[there, lanes] * share[:, lanes] * gate_t[row, mine, :]
                    gated[row % 4, mine, :] = attended.astype(BF16)

    def finish(i):
        turned = jnp.concatenate([gated[i % 4].T, gated[(i + 1) % 4].T], axis=1)
        both = dot(turned, w_last)
        done[i] = (first_pass[i] + both[:, :width]).astype(BF16)
        done[i + 1] = (first_pass[i + 1] + both[:, width:]).astype(BF16)
        copy = pltpu.make_async_copy(done.at[pl.ds(i, 2)], out.at[pl.ds(i, 2)], sems.at[i // 2])
        copy.start()
        copies.append(copy)

    copies = []
    w_last = twice(w_att_out[...])
    for head, (_, span) in enumerate(heads):
        parts = [
            bias[slot(owner, bias.shape[0])].astype(F32)[head * head_rows : (head + 1) * head_rows]
            for owner in range(bias.shape[0])
        ]
        bias_t[:, span] = jnp.concatenate(parts, axis=0).T * LOG2_E
    pipeline(range(0, rows, 2), *before, score, soften, collect, finish)
    for copy in copies:
        copy.wait()


def call(kernel, outs, scratch, flops, *operands, fetched=0, sent=False):
    vmem = pl.BlockSpec(memory_space=pltpu.VMEM)
    far = pl.BlockSpec(memory_space=pltpu.HBM)
    shapes = [jax.ShapeDtypeStruct(shape, dtype) for shape, dtype in outs]
    moved = sum(o.size * o.dtype.itemsize for o in operands)
    operands = [
        pltpu.with_memory_space_constraint(o, pltpu.HBM) if n < fetched else o
        for n, o in enumerate(operands)
    ]
    got = pl.pallas_call(
        kernel,
        out_shape=shapes,
        in_specs=[far] * fetched + [vmem] * (len(operands) - fetched),
        out_specs=[far if sent else vmem] * len(shapes),
        scratch_shapes=[pltpu.VMEM(*s) if isinstance(s, tuple) else s for s in scratch],
        compiler_params=pltpu.CompilerParams(vmem_limit_bytes=48 * 2**20),
        cost_estimate=pl.CostEstimate(flops=flops, bytes_accessed=moved, transcendentals=0),
    )(*operands)
    return got if len(got) > 1 else got[0]


def body(
    pair_rep,
    w_left,
    w_left_gate,
    w_right,
    w_right_gate,
    w_tri_gate,
    w_tri_out,
    w_query,
    w_key,
    w_value,
    w_bias,
    w_att_gate,
    w_att_out,
):
    rows, cols, width = pair_rep.shape
    channels = w_left.shape[1]
    owners, col_parts = lax.axis_size("row"), lax.axis_size("col")
    own = channels // owners
    residues = owners * rows
    cells = rows * cols

    edges, gate, w_tri_out, w_query, w_key, w_value, w_att_gate, w_att_out, w_bias_t = call(
        edges_kernel,
        [
            ((owners, own * 2 * rows, cols), BF16),
            ((rows, cols, width), F32),
            *[(w.shape, BF16) for w in (w_tri_out, w_query, w_key, w_value, w_att_gate, w_att_out)],
            (w_bias.shape[::-1], BF16),
        ],
        [
            (pair_rep.shape, BF16),
            ((5, width, channels), BF16),
            (pair_rep.shape, BF16),
            ((cols // LANES, channels * 2 * rows, LANES), F32),
            pltpu.SemaphoreType.DMA((13,)),
        ],
        10 * cells * width * channels,
        pair_rep,
        w_left,
        w_left_gate,
        w_right,
        w_right_gate,
        w_tri_gate,
        w_tri_out,
        w_query,
        w_key,
        w_value,
        w_att_gate,
        w_att_out,
        w_bias.T,
        fetched=13,
    )
    spread = swap_apart(edges)
    flops = 2 * own * residues * residues * cols
    if col_parts == 1:
        summed = call(
            functools.partial(triangle_kernel, rows),
            [((owners, own * rows, residues), BF16)],
            [],
            flops,
            spread,
        )
    else:
        partial_sums = call(
            functools.partial(partial_kernel, rows),
            [((own, residues, residues), F32)],
            [],
            flops,
            spread,
        )
        summed = lax.psum_scatter(partial_sums, "col", scatter_dimension=2, tiled=True).astype(BF16)
        summed = by_slot(summed.reshape(own, owners, rows, cols).swapaxes(0, 1))
        summed = summed.reshape(owners, own * rows, cols)
    returned = swap(summed)
    first_pass, att_norm, bias_copies = call(
        update_kernel,
        [
            ((rows, cols, width), F32),
            ((rows, cols, width), BF16),
            ((owners, HEADS * rows, cols), BF16),
        ],
        [
            ((cols // LANES, channels * rows, LANES), F32),
            ((HEADS * rows, cols), F32),
            ((4, cols, channels), BF16),
        ],
        2 * cells * channels * width,
        returned,
        gate,
        pair_rep,
        w_tri_out,
        w_bias_t,
    )
    bias = swap(bias_copies)
    projected = [
        ((rows, width, cols), BF16),
        ((rows, cols, width), BF16),
        ((rows, width, cols), BF16),
        ((rows, width, cols), F32),
    ]
    projecting = (att_norm, w_query, w_key, w_value, w_att_gate)
    residues = cols * col_parts
    out = [((rows, cols, width), BF16)]
    held = [
        ((residues, HEADS * cols), F32),
        ((4, residues, HEADS * cols), F32),
        ((4, 1, HEADS * cols), F32),
        ((4, residues, HEADS * cols), BF16),
        ((4, width, cols), BF16),
        ((rows, cols, width), BF16),
        pltpu.SemaphoreType.DMA((rows // 2,)),
    ]
    project_flops, attend_flops = 8 * cells * width * width, 4 * cells * residues * width
    if col_parts == 1:
        flops = project_flops + attend_flops
        given = (first_pass, bias, w_att_out)
        return call(whole_kernel, out, projected + held, flops, *projecting, *given, sent=True)
    query_t, key, value_t, gate_t = call(project_kernel, projected, [], project_flops, *projecting)
    bias = by_slot(lax.all_to_all(by_rank(bias), "col", split_axis=0, concat_axis=2, tiled=True))
    key = lax.all_gather(key, "col", axis=1, tiled=True)
    value_t = lax.all_gather(value_t, "col", axis=2, tiled=True)
    given = (query_t, key, value_t, gate_t, first_pass, bias, w_att_out)
    return call(attend_kernel, out, held, attend_flops, *given, sent=True)


def solution(mesh):
    in_specs = (P(("grp", "row"), "col", None),) + (P(),) * 12
    out_specs = P(("grp", "row"), "col", None)
    return jax.shard_map(body, mesh=mesh, in_specs=in_specs, out_specs=out_specs, check_vma=False)
```

```python
import functools

import jax
import jax.numpy as jnp
import numpy as np
from jax import lax
from jax.experimental import pallas as pl
from jax.experimental.pallas import tpu as pltpu
from jax.sharding import PartitionSpec as P

HEADS = 4
HEAD_DIM = 32
LANES = 128
LOG2_E = 1.4426950408889634
F32 = jnp.float32
BF16 = jnp.bfloat16
NN = (((1,), (0,)), ((), ()))
NT = (((1,), (1,)), ((), ()))
TN = (((0,), (0,)), ((), ()))


def dot(left, right, dims=NN):
    return lax.dot_general(left, right, dims, preferred_element_type=F32)


def sigmoid(values):
    return 0.5 * jnp.tanh(0.5 * values) + 0.5


def twice(weight):
    zeros = jnp.zeros_like(weight)
    return jnp.concatenate(
        [jnp.concatenate([weight, zeros], axis=1), jnp.concatenate([zeros, weight], axis=1)], axis=0
    )


def listing(ranks):
    first = ranks - 1 - ranks // 4
    return [first] + [rank for rank in range(ranks - 1, -1, -1) if rank != first]


def slot(rank, ranks):
    return listing(ranks).index(rank)


def swap(blocks):
    return lax.all_to_all(
        blocks,
        "row",
        split_axis=0,
        concat_axis=0,
        axis_index_groups=[listing(blocks.shape[0])],
        tiled=True,
    )


def swap_apart(blocks):
    ranks, groups = blocks.shape[0], lax.axis_size("grp")
    orders = [listing(ranks), list(range(ranks))]
    return lax.all_to_all(
        blocks,
        ("grp", "row"),
        split_axis=0,
        concat_axis=0,
        axis_index_groups=[[g * ranks + r for r in orders[g % 2]] for g in range(groups)],
        tiled=True,
    )


def in_odd_group():
    return lax.rem(lax.axis_index("grp"), 2) == 1


def slots_apart(ranks):
    odd = in_odd_group()
    return [jnp.where(odd, rank, slot(rank, ranks)) for rank in range(ranks)]


def by_rank(blocks):
    return blocks[np.array([slot(r, blocks.shape[0]) for r in range(blocks.shape[0])])]


def by_slot(blocks):
    return blocks[np.array(listing(blocks.shape[0]))]


def lane_tiles(values):
    lanes = values.shape[1]
    return [(t, slice(t * LANES, (t + 1) * LANES)) for t in range(lanes // LANES)]


def lane_norm(values):
    centered = values - jnp.mean(values, axis=-1, keepdims=True)
    variance = jnp.mean(centered * centered, axis=-1, keepdims=True)
    return (centered * lax.rsqrt(variance + 1e-05)).astype(BF16)


def side_by_side(held, i):
    return jnp.concatenate([held[i], held[i + 1]], axis=1)


def pipeline(rows, *steps):
    for tick in range(len(rows) + len(steps) - 1):
        for late, step in enumerate(steps):
            if 0 <= tick - late < len(rows):
                step(rows[tick - late])


def edges_kernel(*refs):
    given, (out, gate, *staged), (pair, weights, normed, held, sems) = refs[:13], refs[13:22], refs[22:]
    targets = [pair, *(weights.at[n] for n in range(5)), *staged]
    copies = [
        pltpu.make_async_copy(source, target, sems.at[n])
        for n, (source, target) in enumerate(zip(given, targets))
    ]
    for copy in copies:
        copy.start()
    for copy in copies[:6]:
        copy.wait()
    rows, width = pair.shape[0], pair.shape[2]
    channels = weights.shape[2]
    cols = pair.shape[1]
    turned = jnp.concatenate([weights[n].T for n in range(4)], axis=0)
    gate_weight = twice(weights[4])

    def norm(i):
        normed[i] = lane_norm(pair[i].astype(F32))
        normed[i + 1] = lane_norm(pair[i + 1].astype(F32))

    def project(i):
        both = dot(turned, jnp.concatenate([normed[i], normed[i + 1]], axis=0), NT)
        for side in range(2):
            base = 2 * side * channels
            act = sigmoid(both[base + channels : base + 2 * channels]) * both[base : base + channels]
            for tile, lanes in lane_tiles(act):
                row, part = divmod(tile, cols // LANES)
                place = pl.ds(side * rows + i + row, channels, stride=2 * rows)
                held[part, place, :] = act[:, lanes]
        opened = sigmoid(dot(side_by_side(normed, i), gate_weight))
        gate[i] = opened[:, :width]
        gate[i + 1] = opened[:, width:]

    pipeline(range(0, rows, 2), norm, project)
    owners, block = out.shape[0], out.shape[1]
    for owner in range(owners):
        for tile, lanes in lane_tiles(pair):
            out[slot(owner, owners), :, lanes] = held[tile, owner * block : (owner + 1) * block, :].astype(BF16)
    for copy in copies[6:]:
        copy.wait()


def triangle_sides(edges, rows, channel):
    sides = [[], []]
    sources = edges.shape[0]
    for source in range(sources):
        block = edges[slot(source, sources), channel * 2 * rows : (channel + 1) * 2 * rows, :].astype(F32)
        sides[0].append(block[:rows])
        sides[1].append(block[rows:])
    return [jnp.concatenate(side, axis=0).astype(BF16) for side in sides]


def triangle_kernel(rows, edges, out):
    places = slots_apart(out.shape[0])
    for pair_of in range(0, out.shape[1] // rows, 2):
        products = [dot(*triangle_sides(edges, rows, pair_of + o), NT) for o in range(2)]
        for owner, place in enumerate(places):
            mine = slice(owner * rows, (owner + 1) * rows)
            out[place, pair_of * rows : (pair_of + 2) * rows, :] = jnp.concatenate(
                [p[mine] for p in products], axis=0
            ).astype(BF16)


def partial_kernel(rows, edges, out):
    for channel in range(out.shape[0]):
        out[channel] = dot(*triangle_sides(edges, rows, channel), NT)


def update_kernel(
    returned, gate, pair, w_tri_out, w_bias_t, first_pass, att_norm, bias, held, bias_held, turned
):
    rows, cols, width = pair.shape
    owners, block = returned.shape[0], returned.shape[1]
    places = slots_apart(owners)
    channels = owners * block // rows
    total = jnp.zeros((rows, cols), F32)
    for owner in range(owners):
        total += jnp.sum(returned[owner].astype(F32).reshape(block // rows, rows, cols), axis=0)
    average = total / channels
    square = jnp.zeros((rows, cols), F32)
    for owner in range(owners):
        centered = returned[places[owner]].astype(F32).reshape(block // rows, rows, cols) - average
        square += jnp.sum(centered * centered, axis=0)
        for tile, lanes in lane_tiles(pair):
            held[tile, owner * block : (owner + 1) * block, :] = centered.reshape(block, cols)[:, lanes]
    scale = lax.rsqrt(square / channels + 1e-05)

    weight = twice(w_tri_out[...])

    def turn(i):
        for row in (i, i + 1):
            tri_norm = jnp.concatenate(
                [held[tile, pl.ds(row, channels, stride=rows), :] for tile, _ in lane_tiles(pair)], axis=1
            )
            turned[row % 4] = (tri_norm * scale[row : row + 1]).astype(BF16).T

    def update(i):
        both = dot(side_by_side(turned, i % 4), weight)
        first_pass[i] = pair[i].astype(F32) + gate[i] * both[:, :width]
        first_pass[i + 1] = pair[i + 1].astype(F32) + gate[i + 1] * both[:, width:]

    def norm(i):
        for row in (i, i + 1):
            att_norm[row] = lane_norm(first_pass[row])

    def project_bias(i):
        both = dot(w_bias_t[...], jnp.concatenate([att_norm[i], att_norm[i + 1]], axis=0), NT)
        for row in range(2):
            for head in range(HEADS):
                place = head * rows + i + row
                bias_held[place : place + 1, :] = both[head : head + 1, row * cols : (row + 1) * cols]

    pipeline(range(0, rows, 2), turn, update, norm, project_bias)
    rounded = bias_held[...].astype(BF16)
    for owner in range(bias.shape[0]):
        bias[owner] = rounded


def projector(att_norm, w_query, w_key, w_value, w_att_gate, query_t, key, value_t, gate_t):
    w_turned = jnp.concatenate([w[...].T for w in (w_query, w_value, w_att_gate)], axis=0)
    w_direct = twice(w_key[...])
    cols, width = att_norm.shape[1], w_query.shape[1]

    def project(i):
        keys = dot(side_by_side(att_norm, i), w_direct).astype(BF16)
        turned = dot(w_turned, jnp.concatenate([att_norm[i], att_norm[i + 1]], axis=0), NT)
        for row in range(2):
            key[i + row] = keys[:, row * width : (row + 1) * width]
            mine = turned[:, row * cols : (row + 1) * cols]
            query_t[i + row] = mine[:width].astype(BF16)
            value_t[i + row] = mine[width : 2 * width].astype(BF16)
            gate_t[i + row] = sigmoid(mine[2 * width :])

    return project


def project_kernel(*refs):
    pipeline(range(0, refs[0].shape[0], 2), projector(*refs))


def whole_kernel(att_norm, w_query, w_key, w_value, w_att_gate, *refs):
    given, projected, held = refs[:4], refs[4:8], refs[8:]
    project = projector(att_norm, w_query, w_key, w_value, w_att_gate, *projected)
    attend_kernel(*projected, *given, *held, before=(project,))


def attend_kernel(
    query_t,
    key,
    value_t,
    gate_t,
    first_pass,
    bias,
    w_att_out,
    out,
    bias_t,
    scores,
    peaks,
    weights,
    gated,
    done,
    sems,
    before=(),
):
    rows, width, cols = query_t.shape
    head_rows = bias.shape[1] // HEADS
    score_scale = LOG2_E / HEAD_DIM**0.5
    ones = jnp.ones((16, key.shape[1]), BF16)
    heads = [
        (slice(h * HEAD_DIM, (h + 1) * HEAD_DIM), slice(h * cols, (h + 1) * cols)) for h in range(HEADS)
    ]

    def score(i):
        for row in (i, i + 1):
            blocks = []
            for mine, _ in heads:
                above = jnp.zeros((mine.start, cols), BF16)
                below = jnp.zeros((width - mine.stop, cols), BF16)
                parts = [p for p in (above, query_t[row, mine, :], below) if p.shape[0]]
                blocks.append(jnp.concatenate(parts, axis=0))
            raw = dot(key[row], jnp.concatenate(blocks, axis=1))
            for _, span in heads:
                biased = raw[:, span] * score_scale + bias_t[:, span]
                scores[row % 4, :, span] = biased
                peaks[row % 4, :, span] = jnp.max(biased, axis=0, keepdims=True)

    def soften(i):
        for row in (i, i + 1):
            for _, span in heads:
                lowered = scores[row % 4, :, span] - peaks[row % 4, :, span]
                weights[row % 4, :, span] = jnp.exp2(lowered).astype(BF16)

    def collect(i):
        for row in (i, i + 1):
            for head in range(0, HEADS, 2):
                (first, left), (second, right) = heads[head : head + 2]
                values = jnp.concatenate([value_t[row, first.start : second.stop, :], ones], axis=0)
                summed = dot(values, weights[row % 4, :, left.start : right.stop])
                share = 1.0 / summed[2 * HEAD_DIM : 2 * HEAD_DIM + 1]
                for mine, there, lanes in (
                    (first, slice(0, HEAD_DIM), slice(0, cols)),
                    (second, slice(HEAD_DIM, 2 * HEAD_DIM), slice(cols, 2 * cols)),
                ):
                    attended = summed[there, lanes] * share[:, lanes] * gate_t[row, mine, :]
                    gated[row % 4, mine, :] = attended.astype(BF16)

    def finish(i):
        turned = jnp.concatenate([gated[i % 4].T, gated[(i + 1) % 4].T], axis=1)
        both = dot(turned, w_last)
        done[i] = (first_pass[i] + both[:, :width]).astype(BF16)
        done[i + 1] = (first_pass[i + 1] + both[:, width:]).astype(BF16)
        copy = pltpu.make_async_copy(done.at[pl.ds(i, 2)], out.at[pl.ds(i, 2)], sems.at[i // 2])
        copy.start()
        copies.append(copy)

    copies = []
    w_last = twice(w_att_out[...])
    for head, (_, span) in enumerate(heads):
        parts = [
            bias[slot(owner, bias.shape[0])].astype(F32)[head * head_rows : (head + 1) * head_rows]
            for owner in range(bias.shape[0])
        ]
        bias_t[:, span] = jnp.concatenate(parts, axis=0).T * LOG2_E
    pipeline(range(0, rows, 2), *before, score, soften, collect, finish)
    for copy in copies:
        copy.wait()


def call(kernel, outs, scratch, flops, *operands, fetched=0, sent=False):
    vmem = pl.BlockSpec(memory_space=pltpu.VMEM)
    far = pl.BlockSpec(memory_space=pltpu.HBM)
    shapes = [jax.ShapeDtypeStruct(shape, dtype) for shape, dtype in outs]
    moved = sum(o.size * o.dtype.itemsize for o in operands)
    operands = [
        pltpu.with_memory_space_constraint(o, pltpu.HBM) if n < fetched else o
        for n, o in enumerate(operands)
    ]
    got = pl.pallas_call(
        kernel,
        out_shape=shapes,
        in_specs=[far] * fetched + [vmem] * (len(operands) - fetched),
        out_specs=[far if sent else vmem] * len(shapes),
        scratch_shapes=[pltpu.VMEM(*s) if isinstance(s, tuple) else s for s in scratch],
        compiler_params=pltpu.CompilerParams(vmem_limit_bytes=48 * 2**20),
        cost_estimate=pl.CostEstimate(flops=flops, bytes_accessed=moved, transcendentals=0),
    )(*operands)
    return got if len(got) > 1 else got[0]


def body(
    pair_rep,
    w_left,
    w_left_gate,
    w_right,
    w_right_gate,
    w_tri_gate,
    w_tri_out,
    w_query,
    w_key,
    w_value,
    w_bias,
    w_att_gate,
    w_att_out,
):
    rows, cols, width = pair_rep.shape
    channels = w_left.shape[1]
    owners, col_parts = lax.axis_size("row"), lax.axis_size("col")
    own = channels // owners
    residues = owners * rows
    cells = rows * cols

    edges, gate, w_tri_out, w_query, w_key, w_value, w_att_gate, w_att_out, w_bias_t = call(
        edges_kernel,
        [
            ((owners, own * 2 * rows, cols), BF16),
            ((rows, cols, width), F32),
            *[(w.shape, BF16) for w in (w_tri_out, w_query, w_key, w_value, w_att_gate, w_att_out)],
            (w_bias.shape[::-1], BF16),
        ],
        [
            (pair_rep.shape, BF16),
            ((5, width, channels), BF16),
            (pair_rep.shape, BF16),
            ((cols // LANES, channels * 2 * rows, LANES), F32),
            pltpu.SemaphoreType.DMA((13,)),
        ],
        10 * cells * width * channels,
        pair_rep,
        w_left,
        w_left_gate,
        w_right,
        w_right_gate,
        w_tri_gate,
        w_tri_out,
        w_query,
        w_key,
        w_value,
        w_att_gate,
        w_att_out,
        w_bias.T,
        fetched=13,
    )
    spread = swap(edges)
    flops = 2 * own * residues * residues * cols
    if col_parts == 1:
        summed = call(
            functools.partial(triangle_kernel, rows),
            [((owners, own * rows, residues), BF16)],
            [],
            flops,
            spread,
        )
    else:
        partial_sums = call(
            functools.partial(partial_kernel, rows),
            [((own, residues, residues), F32)],
            [],
            flops,
            spread,
        )
        summed = lax.psum_scatter(partial_sums, "col", scatter_dimension=2, tiled=True).astype(BF16)
        summed = summed.reshape(own, owners, rows, cols).swapaxes(0, 1)
        summed = jnp.where(in_odd_group(), summed, by_slot(summed))
        summed = summed.reshape(owners, own * rows, cols)
    returned = swap_apart(summed)
    first_pass, att_norm, bias_copies = call(
        update_kernel,
        [
            ((rows, cols, width), F32),
            ((rows, cols, width), BF16),
            ((owners, HEADS * rows, cols), BF16),
        ],
        [
            ((cols // LANES, channels * rows, LANES), F32),
            ((HEADS * rows, cols), F32),
            ((4, cols, channels), BF16),
        ],
        2 * cells * channels * width,
        returned,
        gate,
        pair_rep,
        w_tri_out,
        w_bias_t,
    )
    bias = swap(bias_copies)
    projected = [
        ((rows, width, cols), BF16),
        ((rows, cols, width), BF16),
        ((rows, width, cols), BF16),
        ((rows, width, cols), F32),
    ]
    projecting = (att_norm, w_query, w_key, w_value, w_att_gate)
    residues = cols * col_parts
    out = [((rows, cols, width), BF16)]
    held = [
        ((residues, HEADS * cols), F32),
        ((4, residues, HEADS * cols), F32),
        ((4, 1, HEADS * cols), F32),
        ((4, residues, HEADS * cols), BF16),
        ((4, width, cols), BF16),
        ((rows, cols, width), BF16),
        pltpu.SemaphoreType.DMA((rows // 2,)),
    ]
    project_flops, attend_flops = 8 * cells * width * width, 4 * cells * residues * width
    if col_parts == 1:
        flops = project_flops + attend_flops
        given = (first_pass, bias, w_att_out)
        return call(whole_kernel, out, projected + held, flops, *projecting, *given, sent=True)
    query_t, key, value_t, gate_t = call(project_kernel, projected, [], project_flops, *projecting)
    bias = by_slot(lax.all_to_all(by_rank(bias), "col", split_axis=0, concat_axis=2, tiled=True))
    key = lax.all_gather(key, "col", axis=1, tiled=True)
    value_t = lax.all_gather(value_t, "col", axis=2, tiled=True)
    given = (query_t, key, value_t, gate_t, first_pass, bias, w_att_out)
    return call(attend_kernel, out, held, attend_flops, *given, sent=True)


def solution(mesh):
    in_specs = (P(("grp", "row"), "col", None),) + (P(),) * 12
    out_specs = P(("grp", "row"), "col", None)
    return jax.shard_map(body, mesh=mesh, in_specs=in_specs, out_specs=out_specs, check_vma=False)
```

```python
import functools
import math

import jax
import jax.numpy as jnp
import numpy as np
from jax import lax
from jax.experimental import pallas as pl
from jax.experimental.pallas import tpu as pltpu
from jax.sharding import PartitionSpec as P

HEADS = 4
HEAD_DIM = 32
LANES = 128
LOG2_E = 1.4426950408889634
F32 = jnp.float32
BF16 = jnp.bfloat16
NN = (((1,), (0,)), ((), ()))
NT = (((1,), (1,)), ((), ()))
TN = (((0,), (0,)), ((), ()))


def dot(left, right, dims=NN):
    return lax.dot_general(left, right, dims, preferred_element_type=F32)


def sigmoid(values):
    return 0.5 * jnp.tanh(0.5 * values) + 0.5


def twice(weight):
    zeros = jnp.zeros_like(weight)
    return jnp.concatenate(
        [jnp.concatenate([weight, zeros], axis=1), jnp.concatenate([zeros, weight], axis=1)], axis=0
    )


def listing(ranks):
    first, stride = ranks - 1 - ranks // 4, 5
    assert math.gcd(stride, ranks) == 1
    return [(first + stride * n) % ranks for n in range(ranks)]


def slot(rank, ranks):
    return listing(ranks).index(rank)


def swap(blocks):
    return lax.all_to_all(
        blocks,
        "row",
        split_axis=0,
        concat_axis=0,
        axis_index_groups=[listing(blocks.shape[0])],
        tiled=True,
    )


def by_rank(blocks):
    return blocks[np.array([slot(r, blocks.shape[0]) for r in range(blocks.shape[0])])]


def by_slot(blocks):
    return blocks[np.array(listing(blocks.shape[0]))]


def lane_tiles(values):
    lanes = values.shape[1]
    return [(t, slice(t * LANES, (t + 1) * LANES)) for t in range(lanes // LANES)]


def lane_norm(values):
    centered = values - jnp.mean(values, axis=-1, keepdims=True)
    variance = jnp.mean(centered * centered, axis=-1, keepdims=True)
    return (centered * lax.rsqrt(variance + 1e-05)).astype(BF16)


def side_by_side(held, i):
    return jnp.concatenate([held[i], held[i + 1]], axis=1)


def pipeline(rows, *steps):
    for tick in range(len(rows) + len(steps) - 1):
        for late, step in enumerate(steps):
            if 0 <= tick - late < len(rows):
                step(rows[tick - late])


def edges_kernel(*refs):
    given, (out, gate, *staged), (pair, weights, normed, held, sems) = refs[:13], refs[13:22], refs[22:]
    targets = [pair, *(weights.at[n] for n in range(5)), *staged]
    copies = [
        pltpu.make_async_copy(source, target, sems.at[n])
        for n, (source, target) in enumerate(zip(given, targets))
    ]
    for copy in copies:
        copy.start()
    for copy in copies[:6]:
        copy.wait()
    rows, width = pair.shape[0], pair.shape[2]
    channels = weights.shape[2]
    cols = pair.shape[1]
    turned = jnp.concatenate([weights[n].T for n in range(4)], axis=0)
    gate_weight = twice(weights[4])

    def norm(i):
        normed[i] = lane_norm(pair[i].astype(F32))
        normed[i + 1] = lane_norm(pair[i + 1].astype(F32))

    def project(i):
        both = dot(turned, jnp.concatenate([normed[i], normed[i + 1]], axis=0), NT)
        for side in range(2):
            base = 2 * side * channels
            act = sigmoid(both[base + channels : base + 2 * channels]) * both[base : base + channels]
            for tile, lanes in lane_tiles(act):
                row, part = divmod(tile, cols // LANES)
                place = pl.ds(side * rows + i + row, channels, stride=2 * rows)
                held[part, place, :] = act[:, lanes]
        opened = sigmoid(dot(side_by_side(normed, i), gate_weight))
        gate[i] = opened[:, :width]
        gate[i + 1] = opened[:, width:]

    pipeline(range(0, rows, 2), norm, project)
    owners, block = out.shape[0], out.shape[1]
    for owner in range(owners):
        for tile, lanes in lane_tiles(pair):
            out[slot(owner, owners), :, lanes] = held[tile, owner * block : (owner + 1) * block, :].astype(BF16)
    for copy in copies[6:]:
        copy.wait()


def triangle_sides(edges, rows, channel):
    sides = [[], []]
    sources = edges.shape[0]
    for source in range(sources):
        block = edges[slot(source, sources), channel * 2 * rows : (channel + 1) * 2 * rows, :].astype(F32)
        sides[0].append(block[:rows])
        sides[1].append(block[rows:])
    return [jnp.concatenate(side, axis=0).astype(BF16) for side in sides]


def triangle_kernel(rows, edges, out):
    for pair_of in range(0, out.shape[1] // rows, 2):
        products = [dot(*triangle_sides(edges, rows, pair_of + o), NT) for o in range(2)]
        owners = out.shape[0]
        for owner in range(owners):
            mine = slice(owner * rows, (owner + 1) * rows)
            out[slot(owner, owners), pair_of * rows : (pair_of + 2) * rows, :] = jnp.concatenate(
                [p[mine] for p in products], axis=0
            ).astype(BF16)


def partial_kernel(rows, edges, out):
    for channel in range(out.shape[0]):
        out[channel] = dot(*triangle_sides(edges, rows, channel), NT)


def update_kernel(
    returned, gate, pair, w_tri_out, w_bias_t, first_pass, att_norm, bias, held, bias_held, turned
):
    rows, cols, width = pair.shape
    owners, block = returned.shape[0], returned.shape[1]
    channels = owners * block // rows
    total = jnp.zeros((rows, cols), F32)
    for owner in range(owners):
        total += jnp.sum(returned[owner].astype(F32).reshape(block // rows, rows, cols), axis=0)
    average = total / channels
    square = jnp.zeros((rows, cols), F32)
    for owner in range(owners):
        centered = returned[slot(owner, owners)].astype(F32).reshape(block // rows, rows, cols) - average
        square += jnp.sum(centered * centered, axis=0)
        for tile, lanes in lane_tiles(pair):
            held[tile, owner * block : (owner + 1) * block, :] = centered.reshape(block, cols)[:, lanes]
    scale = lax.rsqrt(square / channels + 1e-05)

    weight = twice(w_tri_out[...])

    def turn(i):
        for row in (i, i + 1):
            tri_norm = jnp.concatenate(
                [held[tile, pl.ds(row, channels, stride=rows), :] for tile, _ in lane_tiles(pair)], axis=1
            )
            turned[row % 4] = (tri_norm * scale[row : row + 1]).astype(BF16).T

    def update(i):
        both = dot(side_by_side(turned, i % 4), weight)
        first_pass[i] = pair[i].astype(F32) + gate[i] * both[:, :width]
        first_pass[i + 1] = pair[i + 1].astype(F32) + gate[i + 1] * both[:, width:]

    def norm(i):
        for row in (i, i + 1):
            att_norm[row] = lane_norm(first_pass[row])

    def project_bias(i):
        both = dot(w_bias_t[...], jnp.concatenate([att_norm[i], att_norm[i + 1]], axis=0), NT)
        for row in range(2):
            for head in range(HEADS):
                place = head * rows + i + row
                bias_held[place : place + 1, :] = both[head : head + 1, row * cols : (row + 1) * cols]

    pipeline(range(0, rows, 2), turn, update, norm, project_bias)
    rounded = bias_held[...].astype(BF16)
    for owner in range(bias.shape[0]):
        bias[owner] = rounded


def projector(att_norm, w_query, w_key, w_value, w_att_gate, query_t, key, value_t, gate_t):
    w_turned = jnp.concatenate([w[...].T for w in (w_query, w_value, w_att_gate)], axis=0)
    w_direct = twice(w_key[...])
    cols, width = att_norm.shape[1], w_query.shape[1]

    def project(i):
        keys = dot(side_by_side(att_norm, i), w_direct).astype(BF16)
        turned = dot(w_turned, jnp.concatenate([att_norm[i], att_norm[i + 1]], axis=0), NT)
        for row in range(2):
            key[i + row] = keys[:, row * width : (row + 1) * width]
            mine = turned[:, row * cols : (row + 1) * cols]
            query_t[i + row] = mine[:width].astype(BF16)
            value_t[i + row] = mine[width : 2 * width].astype(BF16)
            gate_t[i + row] = sigmoid(mine[2 * width :])

    return project


def project_kernel(*refs):
    pipeline(range(0, refs[0].shape[0], 2), projector(*refs))


def whole_kernel(att_norm, w_query, w_key, w_value, w_att_gate, *refs):
    given, projected, held = refs[:4], refs[4:8], refs[8:]
    project = projector(att_norm, w_query, w_key, w_value, w_att_gate, *projected)
    attend_kernel(*projected, *given, *held, before=(project,))


def attend_kernel(
    query_t,
    key,
    value_t,
    gate_t,
    first_pass,
    bias,
    w_att_out,
    out,
    bias_t,
    scores,
    peaks,
    weights,
    gated,
    done,
    sems,
    before=(),
):
    rows, width, cols = query_t.shape
    head_rows = bias.shape[1] // HEADS
    score_scale = LOG2_E / HEAD_DIM**0.5
    ones = jnp.ones((16, key.shape[1]), BF16)
    heads = [
        (slice(h * HEAD_DIM, (h + 1) * HEAD_DIM), slice(h * cols, (h + 1) * cols)) for h in range(HEADS)
    ]

    def score(i):
        for row in (i, i + 1):
            blocks = []
            for mine, _ in heads:
                above = jnp.zeros((mine.start, cols), BF16)
                below = jnp.zeros((width - mine.stop, cols), BF16)
                parts = [p for p in (above, query_t[row, mine, :], below) if p.shape[0]]
                blocks.append(jnp.concatenate(parts, axis=0))
            raw = dot(key[row], jnp.concatenate(blocks, axis=1))
            for _, span in heads:
                biased = raw[:, span] * score_scale + bias_t[:, span]
                scores[row % 4, :, span] = biased
                peaks[row % 4, :, span] = jnp.max(biased, axis=0, keepdims=True)

    def soften(i):
        for row in (i, i + 1):
            for _, span in heads:
                lowered = scores[row % 4, :, span] - peaks[row % 4, :, span]
                weights[row % 4, :, span] = jnp.exp2(lowered).astype(BF16)

    def collect(i):
        for row in (i, i + 1):
            for head in range(0, HEADS, 2):
                (first, left), (second, right) = heads[head : head + 2]
                values = jnp.concatenate([value_t[row, first.start : second.stop, :], ones], axis=0)
                summed = dot(values, weights[row % 4, :, left.start : right.stop])
                share = 1.0 / summed[2 * HEAD_DIM : 2 * HEAD_DIM + 1]
                for mine, there, lanes in (
                    (first, slice(0, HEAD_DIM), slice(0, cols)),
                    (second, slice(HEAD_DIM, 2 * HEAD_DIM), slice(cols, 2 * cols)),
                ):
                    attended = summed[there, lanes] * share[:, lanes] * gate_t[row, mine, :]
                    gated[row % 4, mine, :] = attended.astype(BF16)

    def finish(i):
        turned = jnp.concatenate([gated[i % 4].T, gated[(i + 1) % 4].T], axis=1)
        both = dot(turned, w_last)
        done[i] = (first_pass[i] + both[:, :width]).astype(BF16)
        done[i + 1] = (first_pass[i + 1] + both[:, width:]).astype(BF16)
        copy = pltpu.make_async_copy(done.at[pl.ds(i, 2)], out.at[pl.ds(i, 2)], sems.at[i // 2])
        copy.start()
        copies.append(copy)

    copies = []
    w_last = twice(w_att_out[...])
    for head, (_, span) in enumerate(heads):
        parts = [
            bias[slot(owner, bias.shape[0])].astype(F32)[head * head_rows : (head + 1) * head_rows]
            for owner in range(bias.shape[0])
        ]
        bias_t[:, span] = jnp.concatenate(parts, axis=0).T * LOG2_E
    pipeline(range(0, rows, 2), *before, score, soften, collect, finish)
    for copy in copies:
        copy.wait()


def call(kernel, outs, scratch, flops, *operands, fetched=0, sent=False):
    vmem = pl.BlockSpec(memory_space=pltpu.VMEM)
    far = pl.BlockSpec(memory_space=pltpu.HBM)
    shapes = [jax.ShapeDtypeStruct(shape, dtype) for shape, dtype in outs]
    moved = sum(o.size * o.dtype.itemsize for o in operands)
    operands = [
        pltpu.with_memory_space_constraint(o, pltpu.HBM) if n < fetched else o
        for n, o in enumerate(operands)
    ]
    got = pl.pallas_call(
        kernel,
        out_shape=shapes,
        in_specs=[far] * fetched + [vmem] * (len(operands) - fetched),
        out_specs=[far if sent else vmem] * len(shapes),
        scratch_shapes=[pltpu.VMEM(*s) if isinstance(s, tuple) else s for s in scratch],
        compiler_params=pltpu.CompilerParams(vmem_limit_bytes=48 * 2**20),
        cost_estimate=pl.CostEstimate(flops=flops, bytes_accessed=moved, transcendentals=0),
    )(*operands)
    return got if len(got) > 1 else got[0]


def body(
    pair_rep,
    w_left,
    w_left_gate,
    w_right,
    w_right_gate,
    w_tri_gate,
    w_tri_out,
    w_query,
    w_key,
    w_value,
    w_bias,
    w_att_gate,
    w_att_out,
):
    rows, cols, width = pair_rep.shape
    channels = w_left.shape[1]
    owners, col_parts = lax.axis_size("row"), lax.axis_size("col")
    own = channels // owners
    residues = owners * rows
    cells = rows * cols

    edges, gate, w_tri_out, w_query, w_key, w_value, w_att_gate, w_att_out, w_bias_t = call(
        edges_kernel,
        [
            ((owners, own * 2 * rows, cols), BF16),
            ((rows, cols, width), F32),
            *[(w.shape, BF16) for w in (w_tri_out, w_query, w_key, w_value, w_att_gate, w_att_out)],
            (w_bias.shape[::-1], BF16),
        ],
        [
            (pair_rep.shape, BF16),
            ((5, width, channels), BF16),
            (pair_rep.shape, BF16),
            ((cols // LANES, channels * 2 * rows, LANES), F32),
            pltpu.SemaphoreType.DMA((13,)),
        ],
        10 * cells * width * channels,
        pair_rep,
        w_left,
        w_left_gate,
        w_right,
        w_right_gate,
        w_tri_gate,
        w_tri_out,
        w_query,
        w_key,
        w_value,
        w_att_gate,
        w_att_out,
        w_bias.T,
        fetched=13,
    )
    spread = swap(edges)
    flops = 2 * own * residues * residues * cols
    if col_parts == 1:
        summed = call(
            functools.partial(triangle_kernel, rows),
            [((owners, own * rows, residues), BF16)],
            [],
            flops,
            spread,
        )
    else:
        partial_sums = call(
            functools.partial(partial_kernel, rows),
            [((own, residues, residues), F32)],
            [],
            flops,
            spread,
        )
        summed = lax.psum_scatter(partial_sums, "col", scatter_dimension=2, tiled=True).astype(BF16)
        summed = by_slot(summed.reshape(own, owners, rows, cols).swapaxes(0, 1))
        summed = summed.reshape(owners, own * rows, cols)
    returned = swap(summed)
    first_pass, att_norm, bias_copies = call(
        update_kernel,
        [
            ((rows, cols, width), F32),
            ((rows, cols, width), BF16),
            ((owners, HEADS * rows, cols), BF16),
        ],
        [
            ((cols // LANES, channels * rows, LANES), F32),
            ((HEADS * rows, cols), F32),
            ((4, cols, channels), BF16),
        ],
        2 * cells * channels * width,
        returned,
        gate,
        pair_rep,
        w_tri_out,
        w_bias_t,
    )
    bias = swap(bias_copies)
    projected = [
        ((rows, width, cols), BF16),
        ((rows, cols, width), BF16),
        ((rows, width, cols), BF16),
        ((rows, width, cols), F32),
    ]
    projecting = (att_norm, w_query, w_key, w_value, w_att_gate)
    residues = cols * col_parts
    out = [((rows, cols, width), BF16)]
    held = [
        ((residues, HEADS * cols), F32),
        ((4, residues, HEADS * cols), F32),
        ((4, 1, HEADS * cols), F32),
        ((4, residues, HEADS * cols), BF16),
        ((4, width, cols), BF16),
        ((rows, cols, width), BF16),
        pltpu.SemaphoreType.DMA((rows // 2,)),
    ]
    project_flops, attend_flops = 8 * cells * width * width, 4 * cells * residues * width
    if col_parts == 1:
        flops = project_flops + attend_flops
        given = (first_pass, bias, w_att_out)
        return call(whole_kernel, out, projected + held, flops, *projecting, *given, sent=True)
    query_t, key, value_t, gate_t = call(project_kernel, projected, [], project_flops, *projecting)
    bias = by_slot(lax.all_to_all(by_rank(bias), "col", split_axis=0, concat_axis=2, tiled=True))
    key = lax.all_gather(key, "col", axis=1, tiled=True)
    value_t = lax.all_gather(value_t, "col", axis=2, tiled=True)
    given = (query_t, key, value_t, gate_t, first_pass, bias, w_att_out)
    return call(attend_kernel, out, held, attend_flops, *given, sent=True)


def solution(mesh):
    in_specs = (P(("grp", "row"), "col", None),) + (P(),) * 12
    out_specs = P(("grp", "row"), "col", None)
    return jax.shard_map(body, mesh=mesh, in_specs=in_specs, out_specs=out_specs, check_vma=False)
```

```python
import functools
import math

import jax
import jax.numpy as jnp
import numpy as np
from jax import lax
from jax.experimental import pallas as pl
from jax.experimental.pallas import tpu as pltpu
from jax.sharding import PartitionSpec as P

HEADS = 4
HEAD_DIM = 32
LANES = 128
LOG2_E = 1.4426950408889634
F32 = jnp.float32
BF16 = jnp.bfloat16
NN = (((1,), (0,)), ((), ()))
NT = (((1,), (1,)), ((), ()))
TN = (((0,), (0,)), ((), ()))


def dot(left, right, dims=NN):
    return lax.dot_general(left, right, dims, preferred_element_type=F32)


def sigmoid(values):
    return 0.5 * jnp.tanh(0.5 * values) + 0.5


def twice(weight):
    zeros = jnp.zeros_like(weight)
    return jnp.concatenate(
        [jnp.concatenate([weight, zeros], axis=1), jnp.concatenate([zeros, weight], axis=1)], axis=0
    )


def listing(ranks):
    first, stride = ranks - 1 - ranks // 4, 5
    assert math.gcd(stride, ranks) == 1
    return [(first + stride * n) % ranks for n in range(ranks)]


def slot(rank, ranks):
    return listing(ranks).index(rank)


def swap(blocks):
    return lax.all_to_all(
        blocks,
        "row",
        split_axis=0,
        concat_axis=0,
        axis_index_groups=[listing(blocks.shape[0])],
        tiled=True,
    )


def by_rank(blocks):
    return blocks[np.array([slot(r, blocks.shape[0]) for r in range(blocks.shape[0])])]


def by_slot(blocks):
    return blocks[np.array(listing(blocks.shape[0]))]


def lane_tiles(values):
    lanes = values.shape[1]
    return [(t, slice(t * LANES, (t + 1) * LANES)) for t in range(lanes // LANES)]


def lane_norm(values):
    centered = values - jnp.mean(values, axis=-1, keepdims=True)
    variance = jnp.mean(centered * centered, axis=-1, keepdims=True)
    return (centered * lax.rsqrt(variance + 1e-05)).astype(BF16)


def side_by_side(held, i):
    return jnp.concatenate([held[i], held[i + 1]], axis=1)


def pipeline(rows, *steps):
    for tick in range(len(rows) + len(steps) - 1):
        for late, step in enumerate(steps):
            if 0 <= tick - late < len(rows):
                step(rows[tick - late])


def edges_kernel(*refs):
    given, (out, gate, *staged), (pair, weights, normed, held, sems) = refs[:13], refs[13:22], refs[22:]
    targets = [*(weights.at[n] for n in range(5)), *staged]
    copies = [
        pltpu.make_async_copy(source, target, sems.at[n])
        for n, (source, target) in enumerate(zip(given[1:], targets))
    ]
    arrivals = []
    for n in range(pair.shape[0] // 2):
        two = pl.ds(2 * n, 2)
        arrivals.append(pltpu.make_async_copy(given[0].at[two], pair.at[two], sems.at[len(copies) + n]))
    for copy in copies[:4] + arrivals + copies[4:]:
        copy.start()
    for copy in copies[:4]:
        copy.wait()
    rows, width = pair.shape[0], pair.shape[2]
    channels = weights.shape[2]
    cols = pair.shape[1]
    turned = jnp.concatenate([weights[n].T for n in range(4)], axis=0)
    copies[4].wait()
    gate_weight = twice(weights[4])

    def norm(i):
        arrivals[i // 2].wait()
        normed[i] = lane_norm(pair[i].astype(F32))
        normed[i + 1] = lane_norm(pair[i + 1].astype(F32))

    def project(i):
        both = dot(turned, jnp.concatenate([normed[i], normed[i + 1]], axis=0), NT)
        gates = dot(side_by_side(normed, i), gate_weight)
        for side in range(2):
            base = 2 * side * channels
            act = sigmoid(both[base + channels : base + 2 * channels]) * both[base : base + channels]
            for tile, lanes in lane_tiles(act):
                row, part = divmod(tile, cols // LANES)
                place = pl.ds(side * rows + i + row, channels, stride=2 * rows)
                held[part, place, :] = act[:, lanes]
        opened = sigmoid(gates)
        gate[i] = opened[:, :width]
        gate[i + 1] = opened[:, width:]

    pipeline(range(0, rows, 2), norm, project)
    owners, block = out.shape[0], out.shape[1]
    for owner in range(owners):
        for tile, lanes in lane_tiles(pair):
            out[slot(owner, owners), :, lanes] = held[tile, owner * block : (owner + 1) * block, :].astype(BF16)
    for copy in copies[5:]:
        copy.wait()


def triangle_sides(edges, rows, channel):
    sides = [[], []]
    sources = edges.shape[0]
    for source in range(sources):
        block = edges[slot(source, sources), channel * 2 * rows : (channel + 1) * 2 * rows, :].astype(F32)
        sides[0].append(block[:rows])
        sides[1].append(block[rows:])
    return [jnp.concatenate(side, axis=0).astype(BF16) for side in sides]


def triangle_kernel(rows, edges, out):
    for pair_of in range(0, out.shape[1] // rows, 2):
        products = [dot(*triangle_sides(edges, rows, pair_of + o), NT) for o in range(2)]
        owners = out.shape[0]
        for owner in range(owners):
            mine = slice(owner * rows, (owner + 1) * rows)
            out[slot(owner, owners), pair_of * rows : (pair_of + 2) * rows, :] = jnp.concatenate(
                [p[mine] for p in products], axis=0
            ).astype(BF16)


def partial_kernel(rows, edges, out):
    for channel in range(out.shape[0]):
        out[channel] = dot(*triangle_sides(edges, rows, channel), NT)


def update_kernel(
    returned, gate, pair, w_tri_out, w_bias_t, first_pass, att_norm, bias, held, bias_held, turned
):
    rows, cols, width = pair.shape
    owners, block = returned.shape[0], returned.shape[1]
    channels = owners * block // rows
    total = jnp.zeros((rows, cols), F32)
    for owner in range(owners):
        total += jnp.sum(returned[owner].astype(F32).reshape(block // rows, rows, cols), axis=0)
    average = total / channels
    square = jnp.zeros((rows, cols), F32)
    for owner in range(owners):
        centered = returned[slot(owner, owners)].astype(F32).reshape(block // rows, rows, cols) - average
        square += jnp.sum(centered * centered, axis=0)
        for tile, lanes in lane_tiles(pair):
            held[tile, owner * block : (owner + 1) * block, :] = centered.reshape(block, cols)[:, lanes]
    scale = lax.rsqrt(square / channels + 1e-05)

    weight = twice(w_tri_out[...])

    def turn(i):
        for row in (i, i + 1):
            tri_norm = jnp.concatenate(
                [held[tile, pl.ds(row, channels, stride=rows), :] for tile, _ in lane_tiles(pair)], axis=1
            )
            turned[row % 4] = (tri_norm * scale[row : row + 1]).astype(BF16).T

    def update(i):
        both = dot(side_by_side(turned, i % 4), weight)
        first_pass[i] = pair[i].astype(F32) + gate[i] * both[:, :width]
        first_pass[i + 1] = pair[i + 1].astype(F32) + gate[i + 1] * both[:, width:]

    def norm(i):
        for row in (i, i + 1):
            att_norm[row] = lane_norm(first_pass[row])

    def project_bias(i):
        both = dot(w_bias_t[...], jnp.concatenate([att_norm[i], att_norm[i + 1]], axis=0), NT)
        for row in range(2):
            for head in range(HEADS):
                place = head * rows + i + row
                bias_held[place : place + 1, :] = both[head : head + 1, row * cols : (row + 1) * cols]

    pipeline(range(0, rows, 2), turn, update, norm, project_bias)
    rounded = bias_held[...].astype(BF16)
    for owner in range(bias.shape[0]):
        bias[owner] = rounded


def projector(att_norm, w_query, w_key, w_value, w_att_gate, query_t, key, value_t, gate_t):
    w_turned = jnp.concatenate([w[...].T for w in (w_query, w_value, w_att_gate)], axis=0)
    w_direct = twice(w_key[...])
    cols, width = att_norm.shape[1], w_query.shape[1]

    def project(i):
        keys = dot(side_by_side(att_norm, i), w_direct)
        turned = dot(w_turned, jnp.concatenate([att_norm[i], att_norm[i + 1]], axis=0), NT)
        keys = keys.astype(BF16)
        for row in range(2):
            key[i + row] = keys[:, row * width : (row + 1) * width]
            mine = turned[:, row * cols : (row + 1) * cols]
            query_t[i + row] = mine[:width].astype(BF16)
            value_t[i + row] = mine[width : 2 * width].astype(BF16)
            gate_t[i + row] = sigmoid(mine[2 * width :])

    return project


def project_kernel(*refs):
    pipeline(range(0, refs[0].shape[0], 2), projector(*refs))


def whole_kernel(att_norm, w_query, w_key, w_value, w_att_gate, *refs):
    given, projected, held = refs[:4], refs[4:8], refs[8:]
    project = projector(att_norm, w_query, w_key, w_value, w_att_gate, *projected)
    attend_kernel(*projected, *given, *held, before=(project,))


def attend_kernel(
    query_t,
    key,
    value_t,
    gate_t,
    first_pass,
    bias,
    w_att_out,
    out,
    bias_t,
    scores,
    peaks,
    weights,
    gated,
    done,
    sems,
    before=(),
):
    rows, width, cols = query_t.shape
    head_rows = bias.shape[1] // HEADS
    score_scale = LOG2_E / HEAD_DIM**0.5
    ones = jnp.ones((16, key.shape[1]), BF16)
    heads = [
        (slice(h * HEAD_DIM, (h + 1) * HEAD_DIM), slice(h * cols, (h + 1) * cols)) for h in range(HEADS)
    ]

    def raw_scores(row):
        blocks = []
        for mine, _ in heads:
            above = jnp.zeros((mine.start, cols), BF16)
            below = jnp.zeros((width - mine.stop, cols), BF16)
            parts = [p for p in (above, query_t[row, mine, :], below) if p.shape[0]]
            blocks.append(jnp.concatenate(parts, axis=0))
        return dot(key[row], jnp.concatenate(blocks, axis=1))

    def score(i):
        raw = [raw_scores(i), raw_scores(i + 1)]
        for row in (i, i + 1):
            for _, span in heads:
                biased = raw[row - i][:, span] * score_scale + bias_t[:, span]
                scores[row % 4, :, span] = biased
                peaks[row % 4, :, span] = jnp.max(biased, axis=0, keepdims=True)

    def soften(i):
        for row in (i, i + 1):
            for _, span in heads:
                lowered = scores[row % 4, :, span] - peaks[row % 4, :, span]
                weights[row % 4, :, span] = jnp.exp2(lowered).astype(BF16)

    def collect(i):
        pairs = [(row, heads[head], heads[head + 1]) for row in (i, i + 1) for head in range(0, HEADS, 2)]
        sums = []
        for row, (first, left), (second, right) in pairs:
            values = jnp.concatenate([value_t[row, first.start : second.stop, :], ones], axis=0)
            sums.append(dot(values, weights[row % 4, :, left.start : right.stop]))
        for (row, (first, _), (second, _)), summed in zip(pairs, sums):
            share = 1.0 / summed[2 * HEAD_DIM : 2 * HEAD_DIM + 1]
            for mine, there, lanes in (
                (first, slice(0, HEAD_DIM), slice(0, cols)),
                (second, slice(HEAD_DIM, 2 * HEAD_DIM), slice(cols, 2 * cols)),
            ):
                attended = summed[there, lanes] * share[:, lanes] * gate_t[row, mine, :]
                gated[row % 4, mine, :] = attended.astype(BF16)

    def finish(i):
        turned = jnp.concatenate([gated[i % 4].T, gated[(i + 1) % 4].T], axis=1)
        both = dot(turned, w_last)
        done[i] = (first_pass[i] + both[:, :width]).astype(BF16)
        done[i + 1] = (first_pass[i + 1] + both[:, width:]).astype(BF16)
        copy = pltpu.make_async_copy(done.at[pl.ds(i, 2)], out.at[pl.ds(i, 2)], sems.at[i // 2])
        copy.start()
        copies.append(copy)

    copies = []
    w_last = twice(w_att_out[...])
    for head, (_, span) in enumerate(heads):
        parts = [
            bias[slot(owner, bias.shape[0])].astype(F32)[head * head_rows : (head + 1) * head_rows]
            for owner in range(bias.shape[0])
        ]
        bias_t[:, span] = jnp.concatenate(parts, axis=0).T * LOG2_E
    pipeline(range(0, rows, 2), *before, score, soften, collect, finish)
    for copy in copies:
        copy.wait()


def call(kernel, outs, scratch, flops, *operands, fetched=0, sent=False):
    vmem = pl.BlockSpec(memory_space=pltpu.VMEM)
    far = pl.BlockSpec(memory_space=pltpu.HBM)
    shapes = [jax.ShapeDtypeStruct(shape, dtype) for shape, dtype in outs]
    moved = sum(o.size * o.dtype.itemsize for o in operands)
    operands = [
        pltpu.with_memory_space_constraint(o, pltpu.HBM) if n < fetched else o
        for n, o in enumerate(operands)
    ]
    got = pl.pallas_call(
        kernel,
        out_shape=shapes,
        in_specs=[far] * fetched + [vmem] * (len(operands) - fetched),
        out_specs=[far if sent else vmem] * len(shapes),
        scratch_shapes=[pltpu.VMEM(*s) if isinstance(s, tuple) else s for s in scratch],
        compiler_params=pltpu.CompilerParams(vmem_limit_bytes=48 * 2**20),
        cost_estimate=pl.CostEstimate(flops=flops, bytes_accessed=moved, transcendentals=0),
    )(*operands)
    return got if len(got) > 1 else got[0]


def body(
    pair_rep,
    w_left,
    w_left_gate,
    w_right,
    w_right_gate,
    w_tri_gate,
    w_tri_out,
    w_query,
    w_key,
    w_value,
    w_bias,
    w_att_gate,
    w_att_out,
):
    rows, cols, width = pair_rep.shape
    channels = w_left.shape[1]
    owners, col_parts = lax.axis_size("row"), lax.axis_size("col")
    own = channels // owners
    residues = owners * rows
    cells = rows * cols

    edges, gate, w_tri_out, w_query, w_key, w_value, w_att_gate, w_att_out, w_bias_t = call(
        edges_kernel,
        [
            ((owners, own * 2 * rows, cols), BF16),
            ((rows, cols, width), F32),
            *[(w.shape, BF16) for w in (w_tri_out, w_query, w_key, w_value, w_att_gate, w_att_out)],
            (w_bias.shape[::-1], BF16),
        ],
        [
            (pair_rep.shape, BF16),
            ((5, width, channels), BF16),
            (pair_rep.shape, BF16),
            ((cols // LANES, channels * 2 * rows, LANES), F32),
            pltpu.SemaphoreType.DMA((12 + rows // 2,)),
        ],
        10 * cells * width * channels,
        pair_rep,
        w_left,
        w_left_gate,
        w_right,
        w_right_gate,
        w_tri_gate,
        w_tri_out,
        w_query,
        w_key,
        w_value,
        w_att_gate,
        w_att_out,
        w_bias.T,
        fetched=13,
    )
    spread = swap(edges)
    flops = 2 * own * residues * residues * cols
    if col_parts == 1:
        summed = call(
            functools.partial(triangle_kernel, rows),
            [((owners, own * rows, residues), BF16)],
            [],
            flops,
            spread,
        )
    else:
        partial_sums = call(
            functools.partial(partial_kernel, rows),
            [((own, residues, residues), F32)],
            [],
            flops,
            spread,
        )
        summed = lax.psum_scatter(partial_sums, "col", scatter_dimension=2, tiled=True).astype(BF16)
        summed = by_slot(summed.reshape(own, owners, rows, cols).swapaxes(0, 1))
        summed = summed.reshape(owners, own * rows, cols)
    returned = swap(summed)
    first_pass, att_norm, bias_copies = call(
        update_kernel,
        [
            ((rows, cols, width), F32),
            ((rows, cols, width), BF16),
            ((owners, HEADS * rows, cols), BF16),
        ],
        [
            ((cols // LANES, channels * rows, LANES), F32),
            ((HEADS * rows, cols), F32),
            ((4, cols, channels), BF16),
        ],
        2 * cells * channels * width,
        returned,
        gate,
        pair_rep,
        w_tri_out,
        w_bias_t,
    )
    bias = swap(bias_copies)
    projected = [
        ((rows, width, cols), BF16),
        ((rows, cols, width), BF16),
        ((rows, width, cols), BF16),
        ((rows, width, cols), F32),
    ]
    projecting = (att_norm, w_query, w_key, w_value, w_att_gate)
    residues = cols * col_parts
    out = [((rows, cols, width), BF16)]
    held = [
        ((residues, HEADS * cols), F32),
        ((4, residues, HEADS * cols), F32),
        ((4, 1, HEADS * cols), F32),
        ((4, residues, HEADS * cols), BF16),
        ((4, width, cols), BF16),
        ((rows, cols, width), BF16),
        pltpu.SemaphoreType.DMA((rows // 2,)),
    ]
    project_flops, attend_flops = 8 * cells * width * width, 4 * cells * residues * width
    if col_parts == 1:
        flops = project_flops + attend_flops
        given = (first_pass, bias, w_att_out)
        return call(whole_kernel, out, projected + held, flops, *projecting, *given, sent=True)
    query_t, key, value_t, gate_t = call(project_kernel, projected, [], project_flops, *projecting)
    bias = by_slot(lax.all_to_all(by_rank(bias), "col", split_axis=0, concat_axis=2, tiled=True))
    key = lax.all_gather(key, "col", axis=1, tiled=True)
    value_t = lax.all_gather(value_t, "col", axis=2, tiled=True)
    given = (query_t, key, value_t, gate_t, first_pass, bias, w_att_out)
    return call(attend_kernel, out, held, attend_flops, *given, sent=True)


def solution(mesh):
    in_specs = (P(("grp", "row"), "col", None),) + (P(),) * 12
    out_specs = P(("grp", "row"), "col", None)
    return jax.shard_map(body, mesh=mesh, in_specs=in_specs, out_specs=out_specs, check_vma=False)
```

```python
import functools
import math

import jax
import jax.numpy as jnp
import numpy as np
from jax import lax
from jax.experimental import pallas as pl
from jax.experimental.pallas import tpu as pltpu
from jax.sharding import PartitionSpec as P

HEADS = 4
HEAD_DIM = 32
LANES = 128
LOG2_E = 1.4426950408889634
F32 = jnp.float32
BF16 = jnp.bfloat16
NN = (((1,), (0,)), ((), ()))
NT = (((1,), (1,)), ((), ()))
TN = (((0,), (0,)), ((), ()))


def dot(left, right, dims=NN):
    return lax.dot_general(left, right, dims, preferred_element_type=F32)


def sigmoid(values):
    return 0.5 * jnp.tanh(0.5 * values) + 0.5


def twice(weight):
    zeros = jnp.zeros_like(weight)
    return jnp.concatenate(
        [jnp.concatenate([weight, zeros], axis=1), jnp.concatenate([zeros, weight], axis=1)], axis=0
    )


def listing(step, ranks):
    first, stride = {"edges": ranks - 1, "triangle": ranks // 2, "bias": ranks // 4}[step], 5
    assert math.gcd(stride, ranks) == 1
    return [(first + stride * n) % ranks for n in range(ranks)]


def slot(step, rank, ranks):
    return listing(step, ranks).index(rank)


def swap(step, blocks):
    return lax.all_to_all(
        blocks,
        "row",
        split_axis=0,
        concat_axis=0,
        axis_index_groups=[listing(step, blocks.shape[0])],
        tiled=True,
    )


def by_rank(step, blocks):
    return blocks[np.array([slot(step, r, blocks.shape[0]) for r in range(blocks.shape[0])])]


def by_slot(step, blocks):
    return blocks[np.array(listing(step, blocks.shape[0]))]


def lane_tiles(values):
    lanes = values.shape[1]
    return [(t, slice(t * LANES, (t + 1) * LANES)) for t in range(lanes // LANES)]


def lane_norm(values):
    centered = values - jnp.mean(values, axis=-1, keepdims=True)
    variance = jnp.mean(centered * centered, axis=-1, keepdims=True)
    return (centered * lax.rsqrt(variance + 1e-05)).astype(BF16)


def side_by_side(held, i):
    return jnp.concatenate([held[i], held[i + 1]], axis=1)


def pipeline(rows, *steps):
    for tick in range(len(rows) + len(steps) - 1):
        for late, step in enumerate(steps):
            if 0 <= tick - late < len(rows):
                step(rows[tick - late])


def edges_kernel(*refs):
    given, (out, gate, *staged), (pair, weights, normed, held, sems) = refs[:13], refs[13:22], refs[22:]
    targets = [pair, *(weights.at[n] for n in range(5)), *staged]
    copies = [
        pltpu.make_async_copy(source, target, sems.at[n])
        for n, (source, target) in enumerate(zip(given, targets))
    ]
    for copy in copies:
        copy.start()
    for copy in copies[:6]:
        copy.wait()
    rows, width = pair.shape[0], pair.shape[2]
    channels = weights.shape[2]
    cols = pair.shape[1]
    turned = jnp.concatenate([weights[n].T for n in range(4)], axis=0)
    gate_weight = twice(weights[4])

    def norm(i):
        normed[i] = lane_norm(pair[i].astype(F32))
        normed[i + 1] = lane_norm(pair[i + 1].astype(F32))

    def project(i):
        both = dot(turned, jnp.concatenate([normed[i], normed[i + 1]], axis=0), NT)
        for side in range(2):
            base = 2 * side * channels
            act = sigmoid(both[base + channels : base + 2 * channels]) * both[base : base + channels]
            for tile, lanes in lane_tiles(act):
                row, part = divmod(tile, cols // LANES)
                place = pl.ds(side * rows + i + row, channels, stride=2 * rows)
                held[part, place, :] = act[:, lanes]
        opened = sigmoid(dot(side_by_side(normed, i), gate_weight))
        gate[i] = opened[:, :width]
        gate[i + 1] = opened[:, width:]

    pipeline(range(0, rows, 2), norm, project)
    owners, block = out.shape[0], out.shape[1]
    for owner in range(owners):
        for tile, lanes in lane_tiles(pair):
            out[slot("edges", owner, owners), :, lanes] = held[tile, owner * block : (owner + 1) * block, :].astype(BF16)
    for copy in copies[6:]:
        copy.wait()


def triangle_sides(edges, rows, channel):
    sides = [[], []]
    sources = edges.shape[0]
    for source in range(sources):
        block = edges[slot("edges", source, sources), channel * 2 * rows : (channel + 1) * 2 * rows, :].astype(F32)
        sides[0].append(block[:rows])
        sides[1].append(block[rows:])
    return [jnp.concatenate(side, axis=0).astype(BF16) for side in sides]


def triangle_kernel(rows, edges, out):
    for pair_of in range(0, out.shape[1] // rows, 2):
        products = [dot(*triangle_sides(edges, rows, pair_of + o), NT) for o in range(2)]
        owners = out.shape[0]
        for owner in range(owners):
            mine = slice(owner * rows, (owner + 1) * rows)
            out[slot("triangle", owner, owners), pair_of * rows : (pair_of + 2) * rows, :] = jnp.concatenate(
                [p[mine] for p in products], axis=0
            ).astype(BF16)


def partial_kernel(rows, edges, out):
    for channel in range(out.shape[0]):
        out[channel] = dot(*triangle_sides(edges, rows, channel), NT)


def update_kernel(
    returned, gate, pair, w_tri_out, w_bias_t, first_pass, att_norm, bias, held, bias_held, turned
):
    rows, cols, width = pair.shape
    owners, block = returned.shape[0], returned.shape[1]
    channels = owners * block // rows
    total = jnp.zeros((rows, cols), F32)
    for owner in range(owners):
        total += jnp.sum(returned[owner].astype(F32).reshape(block // rows, rows, cols), axis=0)
    average = total / channels
    square = jnp.zeros((rows, cols), F32)
    for owner in range(owners):
        centered = returned[slot("triangle", owner, owners)].astype(F32).reshape(block // rows, rows, cols) - average
        square += jnp.sum(centered * centered, axis=0)
        for tile, lanes in lane_tiles(pair):
            held[tile, owner * block : (owner + 1) * block, :] = centered.reshape(block, cols)[:, lanes]
    scale = lax.rsqrt(square / channels + 1e-05)

    weight = twice(w_tri_out[...])

    def turn(i):
        for row in (i, i + 1):
            tri_norm = jnp.concatenate(
                [held[tile, pl.ds(row, channels, stride=rows), :] for tile, _ in lane_tiles(pair)], axis=1
            )
            turned[row % 4] = (tri_norm * scale[row : row + 1]).astype(BF16).T

    def update(i):
        both = dot(side_by_side(turned, i % 4), weight)
        first_pass[i] = pair[i].astype(F32) + gate[i] * both[:, :width]
        first_pass[i + 1] = pair[i + 1].astype(F32) + gate[i + 1] * both[:, width:]

    def norm(i):
        for row in (i, i + 1):
            att_norm[row] = lane_norm(first_pass[row])

    def project_bias(i):
        both = dot(w_bias_t[...], jnp.concatenate([att_norm[i], att_norm[i + 1]], axis=0), NT)
        for row in range(2):
            for head in range(HEADS):
                place = head * rows + i + row
                bias_held[place : place + 1, :] = both[head : head + 1, row * cols : (row + 1) * cols]

    pipeline(range(0, rows, 2), turn, update, norm, project_bias)
    rounded = bias_held[...].astype(BF16)
    for owner in range(bias.shape[0]):
        bias[owner] = rounded


def projector(att_norm, w_query, w_key, w_value, w_att_gate, query_t, key, value_t, gate_t):
    w_turned = jnp.concatenate([w[...].T for w in (w_query, w_value, w_att_gate)], axis=0)
    w_direct = twice(w_key[...])
    cols, width = att_norm.shape[1], w_query.shape[1]

    def project(i):
        keys = dot(side_by_side(att_norm, i), w_direct).astype(BF16)
        turned = dot(w_turned, jnp.concatenate([att_norm[i], att_norm[i + 1]], axis=0), NT)
        for row in range(2):
            key[i + row] = keys[:, row * width : (row + 1) * width]
            mine = turned[:, row * cols : (row + 1) * cols]
            query_t[i + row] = mine[:width].astype(BF16)
            value_t[i + row] = mine[width : 2 * width].astype(BF16)
            gate_t[i + row] = sigmoid(mine[2 * width :])

    return project


def project_kernel(*refs):
    pipeline(range(0, refs[0].shape[0], 2), projector(*refs))


def whole_kernel(att_norm, w_query, w_key, w_value, w_att_gate, *refs):
    given, projected, held = refs[:4], refs[4:8], refs[8:]
    project = projector(att_norm, w_query, w_key, w_value, w_att_gate, *projected)
    attend_kernel(*projected, *given, *held, before=(project,))


def attend_kernel(
    query_t,
    key,
    value_t,
    gate_t,
    first_pass,
    bias,
    w_att_out,
    out,
    bias_t,
    scores,
    peaks,
    weights,
    gated,
    done,
    sems,
    before=(),
):
    rows, width, cols = query_t.shape
    head_rows = bias.shape[1] // HEADS
    score_scale = LOG2_E / HEAD_DIM**0.5
    ones = jnp.ones((16, key.shape[1]), BF16)
    heads = [
        (slice(h * HEAD_DIM, (h + 1) * HEAD_DIM), slice(h * cols, (h + 1) * cols)) for h in range(HEADS)
    ]

    def score(i):
        if i == 0:
            turn_bias()
        for row in (i, i + 1):
            blocks = []
            for mine, _ in heads:
                above = jnp.zeros((mine.start, cols), BF16)
                below = jnp.zeros((width - mine.stop, cols), BF16)
                parts = [p for p in (above, query_t[row, mine, :], below) if p.shape[0]]
                blocks.append(jnp.concatenate(parts, axis=0))
            raw = dot(key[row], jnp.concatenate(blocks, axis=1))
            for _, span in heads:
                biased = raw[:, span] * score_scale + bias_t[:, span]
                scores[row % 4, :, span] = biased
                peaks[row % 4, :, span] = jnp.max(biased, axis=0, keepdims=True)

    def soften(i):
        for row in (i, i + 1):
            for _, span in heads:
                lowered = scores[row % 4, :, span] - peaks[row % 4, :, span]
                weights[row % 4, :, span] = jnp.exp2(lowered).astype(BF16)

    def collect(i):
        for row in (i, i + 1):
            for head in range(0, HEADS, 2):
                (first, left), (second, right) = heads[head : head + 2]
                values = jnp.concatenate([value_t[row, first.start : second.stop, :], ones], axis=0)
                summed = dot(values, weights[row % 4, :, left.start : right.stop])
                share = 1.0 / summed[2 * HEAD_DIM : 2 * HEAD_DIM + 1]
                for mine, there, lanes in (
                    (first, slice(0, HEAD_DIM), slice(0, cols)),
                    (second, slice(HEAD_DIM, 2 * HEAD_DIM), slice(cols, 2 * cols)),
                ):
                    attended = summed[there, lanes] * share[:, lanes] * gate_t[row, mine, :]
                    gated[row % 4, mine, :] = attended.astype(BF16)

    def finish(i):
        turned = jnp.concatenate([gated[i % 4].T, gated[(i + 1) % 4].T], axis=1)
        both = dot(turned, w_last)
        done[i] = (first_pass[i] + both[:, :width]).astype(BF16)
        done[i + 1] = (first_pass[i + 1] + both[:, width:]).astype(BF16)
        copy = pltpu.make_async_copy(done.at[pl.ds(i, 2)], out.at[pl.ds(i, 2)], sems.at[i // 2])
        copy.start()
        copies.append(copy)

    def turn_bias():
        for head, (_, span) in enumerate(heads):
            parts = [
                bias[slot("bias", owner, bias.shape[0])].astype(F32)[head * head_rows : (head + 1) * head_rows]
                for owner in range(bias.shape[0])
            ]
            bias_t[:, span] = jnp.concatenate(parts, axis=0).T * LOG2_E

    copies = []
    w_last = twice(w_att_out[...])
    pipeline(range(0, rows, 2), *before, score, soften, collect, finish)
    for copy in copies:
        copy.wait()


def call(kernel, outs, scratch, flops, *operands, fetched=0, sent=False):
    vmem = pl.BlockSpec(memory_space=pltpu.VMEM)
    far = pl.BlockSpec(memory_space=pltpu.HBM)
    shapes = [jax.ShapeDtypeStruct(shape, dtype) for shape, dtype in outs]
    moved = sum(o.size * o.dtype.itemsize for o in operands)
    operands = [
        pltpu.with_memory_space_constraint(o, pltpu.HBM) if n < fetched else o
        for n, o in enumerate(operands)
    ]
    got = pl.pallas_call(
        kernel,
        out_shape=shapes,
        in_specs=[far] * fetched + [vmem] * (len(operands) - fetched),
        out_specs=[far if sent else vmem] * len(shapes),
        scratch_shapes=[pltpu.VMEM(*s) if isinstance(s, tuple) else s for s in scratch],
        compiler_params=pltpu.CompilerParams(vmem_limit_bytes=48 * 2**20),
        cost_estimate=pl.CostEstimate(flops=flops, bytes_accessed=moved, transcendentals=0),
    )(*operands)
    return got if len(got) > 1 else got[0]


def body(
    pair_rep,
    w_left,
    w_left_gate,
    w_right,
    w_right_gate,
    w_tri_gate,
    w_tri_out,
    w_query,
    w_key,
    w_value,
    w_bias,
    w_att_gate,
    w_att_out,
):
    rows, cols, width = pair_rep.shape
    channels = w_left.shape[1]
    owners, col_parts = lax.axis_size("row"), lax.axis_size("col")
    own = channels // owners
    residues = owners * rows
    cells = rows * cols

    edges, gate, w_tri_out, w_query, w_key, w_value, w_att_gate, w_att_out, w_bias_t = call(
        edges_kernel,
        [
            ((owners, own * 2 * rows, cols), BF16),
            ((rows, cols, width), F32),
            *[(w.shape, BF16) for w in (w_tri_out, w_query, w_key, w_value, w_att_gate, w_att_out)],
            (w_bias.shape[::-1], BF16),
        ],
        [
            (pair_rep.shape, BF16),
            ((5, width, channels), BF16),
            (pair_rep.shape, BF16),
            ((cols // LANES, channels * 2 * rows, LANES), F32),
            pltpu.SemaphoreType.DMA((13,)),
        ],
        10 * cells * width * channels,
        pair_rep,
        w_left,
        w_left_gate,
        w_right,
        w_right_gate,
        w_tri_gate,
        w_tri_out,
        w_query,
        w_key,
        w_value,
        w_att_gate,
        w_att_out,
        w_bias.T,
        fetched=13,
    )
    spread = swap("edges", edges)
    flops = 2 * own * residues * residues * cols
    if col_parts == 1:
        summed = call(
            functools.partial(triangle_kernel, rows),
            [((owners, own * rows, residues), BF16)],
            [],
            flops,
            spread,
        )
    else:
        partial_sums = call(
            functools.partial(partial_kernel, rows),
            [((own, residues, residues), F32)],
            [],
            flops,
            spread,
        )
        summed = lax.psum_scatter(partial_sums, "col", scatter_dimension=2, tiled=True).astype(BF16)
        summed = by_slot("triangle", summed.reshape(own, owners, rows, cols).swapaxes(0, 1))
        summed = summed.reshape(owners, own * rows, cols)
    returned = swap("triangle", summed)
    first_pass, att_norm, bias_copies = call(
        update_kernel,
        [
            ((rows, cols, width), F32),
            ((rows, cols, width), BF16),
            ((owners, HEADS * rows, cols), BF16),
        ],
        [
            ((cols // LANES, channels * rows, LANES), F32),
            ((HEADS * rows, cols), F32),
            ((4, cols, channels), BF16),
        ],
        2 * cells * channels * width,
        returned,
        gate,
        pair_rep,
        w_tri_out,
        w_bias_t,
    )
    bias = swap("bias", bias_copies)
    projected = [
        ((rows, width, cols), BF16),
        ((rows, cols, width), BF16),
        ((rows, width, cols), BF16),
        ((rows, width, cols), F32),
    ]
    projecting = (att_norm, w_query, w_key, w_value, w_att_gate)
    residues = cols * col_parts
    out = [((rows, cols, width), BF16)]
    held = [
        ((residues, HEADS * cols), F32),
        ((4, residues, HEADS * cols), F32),
        ((4, 1, HEADS * cols), F32),
        ((4, residues, HEADS * cols), BF16),
        ((4, width, cols), BF16),
        ((rows, cols, width), BF16),
        pltpu.SemaphoreType.DMA((rows // 2,)),
    ]
    project_flops, attend_flops = 8 * cells * width * width, 4 * cells * residues * width
    if col_parts == 1:
        flops = project_flops + attend_flops
        given = (first_pass, bias, w_att_out)
        return call(whole_kernel, out, projected + held, flops, *projecting, *given, sent=True)
    query_t, key, value_t, gate_t = call(project_kernel, projected, [], project_flops, *projecting)
    bias = by_slot(
        "bias", lax.all_to_all(by_rank("bias", bias), "col", split_axis=0, concat_axis=2, tiled=True)
    )
    key = lax.all_gather(key, "col", axis=1, tiled=True)
    value_t = lax.all_gather(value_t, "col", axis=2, tiled=True)
    given = (query_t, key, value_t, gate_t, first_pass, bias, w_att_out)
    return call(attend_kernel, out, held, attend_flops, *given, sent=True)


def solution(mesh):
    in_specs = (P(("grp", "row"), "col", None),) + (P(),) * 12
    out_specs = P(("grp", "row"), "col", None)
    return jax.shard_map(body, mesh=mesh, in_specs=in_specs, out_specs=out_specs, check_vma=False)
```

```python
import functools
import math

import jax
import jax.numpy as jnp
import numpy as np
from jax import lax
from jax.experimental import pallas as pl
from jax.experimental.pallas import tpu as pltpu
from jax.sharding import PartitionSpec as P

HEADS = 4
HEAD_DIM = 32
LANES = 128
LOG2_E = 1.4426950408889634
F32 = jnp.float32
BF16 = jnp.bfloat16
NN = (((1,), (0,)), ((), ()))
NT = (((1,), (1,)), ((), ()))
TN = (((0,), (0,)), ((), ()))


def dot(left, right, dims=NN):
    return lax.dot_general(left, right, dims, preferred_element_type=F32)


def sigmoid(values):
    return 0.5 * jnp.tanh(0.5 * values) + 0.5


def twice(weight):
    zeros = jnp.zeros_like(weight)
    return jnp.concatenate(
        [jnp.concatenate([weight, zeros], axis=1), jnp.concatenate([zeros, weight], axis=1)], axis=0
    )


def listing(step, ranks):
    first, stride = ranks - 1 - ranks // 4, 5
    if step == "triangle":
        return [first] + [rank for rank in range(ranks - 1, -1, -1) if rank != first]
    assert math.gcd(stride, ranks) == 1
    return [(first + stride * n) % ranks for n in range(ranks)]


def slot(step, rank, ranks):
    return listing(step, ranks).index(rank)


def swap(step, blocks):
    return lax.all_to_all(
        blocks,
        "row",
        split_axis=0,
        concat_axis=0,
        axis_index_groups=[listing(step, blocks.shape[0])],
        tiled=True,
    )


def by_rank(step, blocks):
    return blocks[np.array([slot(step, r, blocks.shape[0]) for r in range(blocks.shape[0])])]


def by_slot(step, blocks):
    return blocks[np.array(listing(step, blocks.shape[0]))]


def lane_tiles(values):
    lanes = values.shape[1]
    return [(t, slice(t * LANES, (t + 1) * LANES)) for t in range(lanes // LANES)]


def lane_norm(values):
    centered = values - jnp.mean(values, axis=-1, keepdims=True)
    variance = jnp.mean(centered * centered, axis=-1, keepdims=True)
    return (centered * lax.rsqrt(variance + 1e-05)).astype(BF16)


def side_by_side(held, i):
    return jnp.concatenate([held[i], held[i + 1]], axis=1)


def pipeline(rows, *steps):
    for tick in range(len(rows) + len(steps) - 1):
        for late, step in enumerate(steps):
            if 0 <= tick - late < len(rows):
                step(rows[tick - late])


def edges_kernel(*refs):
    given, (out, gate, *staged), (pair, weights, normed, held, sems) = refs[:13], refs[13:22], refs[22:]
    targets = [pair, *(weights.at[n] for n in range(5)), *staged]
    copies = [
        pltpu.make_async_copy(source, target, sems.at[n])
        for n, (source, target) in enumerate(zip(given, targets))
    ]
    for copy in copies:
        copy.start()
    for copy in copies[:6]:
        copy.wait()
    rows, width = pair.shape[0], pair.shape[2]
    channels = weights.shape[2]
    cols = pair.shape[1]
    turned = jnp.concatenate([weights[n].T for n in range(4)], axis=0)
    gate_weight = twice(weights[4])

    def norm(i):
        normed[i] = lane_norm(pair[i].astype(F32))
        normed[i + 1] = lane_norm(pair[i + 1].astype(F32))

    def project(i):
        both = dot(turned, jnp.concatenate([normed[i], normed[i + 1]], axis=0), NT)
        for side in range(2):
            base = 2 * side * channels
            act = sigmoid(both[base + channels : base + 2 * channels]) * both[base : base + channels]
            for tile, lanes in lane_tiles(act):
                row, part = divmod(tile, cols // LANES)
                place = pl.ds(side * rows + i + row, channels, stride=2 * rows)
                held[part, place, :] = act[:, lanes]
        opened = sigmoid(dot(side_by_side(normed, i), gate_weight))
        gate[i] = opened[:, :width]
        gate[i + 1] = opened[:, width:]

    pipeline(range(0, rows, 2), norm, project)
    owners, block = out.shape[0], out.shape[1]
    for owner in range(owners):
        for tile, lanes in lane_tiles(pair):
            out[slot("edges", owner, owners), :, lanes] = held[tile, owner * block : (owner + 1) * block, :].astype(BF16)
    for copy in copies[6:]:
        copy.wait()


def triangle_sides(edges, rows, channel):
    sides = [[], []]
    sources = edges.shape[0]
    for source in range(sources):
        block = edges[slot("edges", source, sources), channel * 2 * rows : (channel + 1) * 2 * rows, :].astype(F32)
        sides[0].append(block[:rows])
        sides[1].append(block[rows:])
    return [jnp.concatenate(side, axis=0).astype(BF16) for side in sides]


def triangle_kernel(rows, edges, out):
    for pair_of in range(0, out.shape[1] // rows, 2):
        products = [dot(*triangle_sides(edges, rows, pair_of + o), NT) for o in range(2)]
        owners = out.shape[0]
        for owner in range(owners):
            mine = slice(owner * rows, (owner + 1) * rows)
            out[slot("triangle", owner, owners), pair_of * rows : (pair_of + 2) * rows, :] = jnp.concatenate(
                [p[mine] for p in products], axis=0
            ).astype(BF16)


def partial_kernel(rows, edges, out):
    for channel in range(out.shape[0]):
        out[channel] = dot(*triangle_sides(edges, rows, channel), NT)


def update_kernel(
    returned, gate, pair, w_tri_out, w_bias_t, first_pass, att_norm, bias, held, bias_held, turned
):
    rows, cols, width = pair.shape
    owners, block = returned.shape[0], returned.shape[1]
    channels = owners * block // rows
    total = jnp.zeros((rows, cols), F32)
    for owner in range(owners):
        total += jnp.sum(returned[owner].astype(F32).reshape(block // rows, rows, cols), axis=0)
    average = total / channels
    square = jnp.zeros((rows, cols), F32)
    for owner in range(owners):
        centered = returned[slot("triangle", owner, owners)].astype(F32).reshape(block // rows, rows, cols) - average
        square += jnp.sum(centered * centered, axis=0)
        for tile, lanes in lane_tiles(pair):
            held[tile, owner * block : (owner + 1) * block, :] = centered.reshape(block, cols)[:, lanes]
    scale = lax.rsqrt(square / channels + 1e-05)

    weight = twice(w_tri_out[...])

    def turn(i):
        for row in (i, i + 1):
            tri_norm = jnp.concatenate(
                [held[tile, pl.ds(row, channels, stride=rows), :] for tile, _ in lane_tiles(pair)], axis=1
            )
            turned[row % 4] = (tri_norm * scale[row : row + 1]).astype(BF16).T

    def update(i):
        both = dot(side_by_side(turned, i % 4), weight)
        first_pass[i] = pair[i].astype(F32) + gate[i] * both[:, :width]
        first_pass[i + 1] = pair[i + 1].astype(F32) + gate[i + 1] * both[:, width:]

    def norm(i):
        for row in (i, i + 1):
            att_norm[row] = lane_norm(first_pass[row])

    def project_bias(i):
        both = dot(w_bias_t[...], jnp.concatenate([att_norm[i], att_norm[i + 1]], axis=0), NT)
        for row in range(2):
            for head in range(HEADS):
                place = head * rows + i + row
                bias_held[place : place + 1, :] = both[head : head + 1, row * cols : (row + 1) * cols]

    pipeline(range(0, rows, 2), turn, update, norm, project_bias)
    rounded = bias_held[...].astype(BF16)
    for owner in range(bias.shape[0]):
        bias[owner] = rounded


def projector(att_norm, w_query, w_key, w_value, w_att_gate, query_t, key, value_t, gate_t):
    w_turned = jnp.concatenate([w[...].T for w in (w_query, w_value, w_att_gate)], axis=0)
    w_direct = twice(w_key[...])
    cols, width = att_norm.shape[1], w_query.shape[1]

    def project(i):
        keys = dot(side_by_side(att_norm, i), w_direct).astype(BF16)
        turned = dot(w_turned, jnp.concatenate([att_norm[i], att_norm[i + 1]], axis=0), NT)
        for row in range(2):
            key[i + row] = keys[:, row * width : (row + 1) * width]
            mine = turned[:, row * cols : (row + 1) * cols]
            query_t[i + row] = mine[:width].astype(BF16)
            value_t[i + row] = mine[width : 2 * width].astype(BF16)
            gate_t[i + row] = sigmoid(mine[2 * width :])

    return project


def project_kernel(*refs):
    pipeline(range(0, refs[0].shape[0], 2), projector(*refs))


def whole_kernel(att_norm, w_query, w_key, w_value, w_att_gate, *refs):
    given, projected, held = refs[:4], refs[4:8], refs[8:]
    project = projector(att_norm, w_query, w_key, w_value, w_att_gate, *projected)
    attend_kernel(*projected, *given, *held, before=(project,))


def attend_kernel(
    query_t,
    key,
    value_t,
    gate_t,
    first_pass,
    bias,
    w_att_out,
    out,
    bias_t,
    scores,
    peaks,
    weights,
    gated,
    done,
    sems,
    before=(),
):
    rows, width, cols = query_t.shape
    head_rows = bias.shape[1] // HEADS
    score_scale = LOG2_E / HEAD_DIM**0.5
    ones = jnp.ones((16, key.shape[1]), BF16)
    heads = [
        (slice(h * HEAD_DIM, (h + 1) * HEAD_DIM), slice(h * cols, (h + 1) * cols)) for h in range(HEADS)
    ]

    def score(i):
        for row in (i, i + 1):
            blocks = []
            for mine, _ in heads:
                above = jnp.zeros((mine.start, cols), BF16)
                below = jnp.zeros((width - mine.stop, cols), BF16)
                parts = [p for p in (above, query_t[row, mine, :], below) if p.shape[0]]
                blocks.append(jnp.concatenate(parts, axis=0))
            raw = dot(key[row], jnp.concatenate(blocks, axis=1))
            for _, span in heads:
                biased = raw[:, span] * score_scale + bias_t[:, span]
                scores[row % 4, :, span] = biased
                peaks[row % 4, :, span] = jnp.max(biased, axis=0, keepdims=True)

    def soften(i):
        for row in (i, i + 1):
            for _, span in heads:
                lowered = scores[row % 4, :, span] - peaks[row % 4, :, span]
                weights[row % 4, :, span] = jnp.exp2(lowered).astype(BF16)

    def collect(i):
        for row in (i, i + 1):
            for head in range(0, HEADS, 2):
                (first, left), (second, right) = heads[head : head + 2]
                values = jnp.concatenate([value_t[row, first.start : second.stop, :], ones], axis=0)
                summed = dot(values, weights[row % 4, :, left.start : right.stop])
                share = 1.0 / summed[2 * HEAD_DIM : 2 * HEAD_DIM + 1]
                for mine, there, lanes in (
                    (first, slice(0, HEAD_DIM), slice(0, cols)),
                    (second, slice(HEAD_DIM, 2 * HEAD_DIM), slice(cols, 2 * cols)),
                ):
                    attended = summed[there, lanes] * share[:, lanes] * gate_t[row, mine, :]
                    gated[row % 4, mine, :] = attended.astype(BF16)

    def finish(i):
        turned = jnp.concatenate([gated[i % 4].T, gated[(i + 1) % 4].T], axis=1)
        both = dot(turned, w_last)
        done[i] = (first_pass[i] + both[:, :width]).astype(BF16)
        done[i + 1] = (first_pass[i + 1] + both[:, width:]).astype(BF16)
        copy = pltpu.make_async_copy(done.at[pl.ds(i, 2)], out.at[pl.ds(i, 2)], sems.at[i // 2])
        copy.start()
        copies.append(copy)

    copies = []
    w_last = twice(w_att_out[...])
    for head, (_, span) in enumerate(heads):
        parts = [
            bias[slot("bias", owner, bias.shape[0])].astype(F32)[head * head_rows : (head + 1) * head_rows]
            for owner in range(bias.shape[0])
        ]
        bias_t[:, span] = jnp.concatenate(parts, axis=0).T * LOG2_E
    pipeline(range(0, rows, 2), *before, score, soften, collect, finish)
    for copy in copies:
        copy.wait()


def call(kernel, outs, scratch, flops, *operands, fetched=0, sent=False):
    vmem = pl.BlockSpec(memory_space=pltpu.VMEM)
    far = pl.BlockSpec(memory_space=pltpu.HBM)
    shapes = [jax.ShapeDtypeStruct(shape, dtype) for shape, dtype in outs]
    moved = sum(o.size * o.dtype.itemsize for o in operands)
    operands = [
        pltpu.with_memory_space_constraint(o, pltpu.HBM) if n < fetched else o
        for n, o in enumerate(operands)
    ]
    got = pl.pallas_call(
        kernel,
        out_shape=shapes,
        in_specs=[far] * fetched + [vmem] * (len(operands) - fetched),
        out_specs=[far if sent else vmem] * len(shapes),
        scratch_shapes=[pltpu.VMEM(*s) if isinstance(s, tuple) else s for s in scratch],
        compiler_params=pltpu.CompilerParams(vmem_limit_bytes=48 * 2**20),
        cost_estimate=pl.CostEstimate(flops=flops, bytes_accessed=moved, transcendentals=0),
    )(*operands)
    return got if len(got) > 1 else got[0]


def body(
    pair_rep,
    w_left,
    w_left_gate,
    w_right,
    w_right_gate,
    w_tri_gate,
    w_tri_out,
    w_query,
    w_key,
    w_value,
    w_bias,
    w_att_gate,
    w_att_out,
):
    rows, cols, width = pair_rep.shape
    channels = w_left.shape[1]
    owners, col_parts = lax.axis_size("row"), lax.axis_size("col")
    own = channels // owners
    residues = owners * rows
    cells = rows * cols

    edges, gate, w_tri_out, w_query, w_key, w_value, w_att_gate, w_att_out, w_bias_t = call(
        edges_kernel,
        [
            ((owners, own * 2 * rows, cols), BF16),
            ((rows, cols, width), F32),
            *[(w.shape, BF16) for w in (w_tri_out, w_query, w_key, w_value, w_att_gate, w_att_out)],
            (w_bias.shape[::-1], BF16),
        ],
        [
            (pair_rep.shape, BF16),
            ((5, width, channels), BF16),
            (pair_rep.shape, BF16),
            ((cols // LANES, (channels + 1) * 2 * rows, LANES), F32),
            pltpu.SemaphoreType.DMA((13,)),
        ],
        10 * cells * width * channels,
        pair_rep,
        w_left,
        w_left_gate,
        w_right,
        w_right_gate,
        w_tri_gate,
        w_tri_out,
        w_query,
        w_key,
        w_value,
        w_att_gate,
        w_att_out,
        w_bias.T,
        fetched=13,
    )
    spread = swap("edges", edges)
    flops = 2 * own * residues * residues * cols
    if col_parts == 1:
        summed = call(
            functools.partial(triangle_kernel, rows),
            [((owners, own * rows, residues), BF16)],
            [],
            flops,
            spread,
        )
    else:
        partial_sums = call(
            functools.partial(partial_kernel, rows),
            [((own, residues, residues), F32)],
            [],
            flops,
            spread,
        )
        summed = lax.psum_scatter(partial_sums, "col", scatter_dimension=2, tiled=True).astype(BF16)
        summed = by_slot("triangle", summed.reshape(own, owners, rows, cols).swapaxes(0, 1))
        summed = summed.reshape(owners, own * rows, cols)
    returned = swap("triangle", summed)
    first_pass, att_norm, bias_copies = call(
        update_kernel,
        [
            ((rows, cols, width), F32),
            ((rows, cols, width), BF16),
            ((owners, HEADS * rows, cols), BF16),
        ],
        [
            ((cols // LANES, (channels + 1) * rows, LANES), F32),
            ((HEADS * rows, cols), F32),
            ((4, cols, channels), BF16),
        ],
        2 * cells * channels * width,
        returned,
        gate,
        pair_rep,
        w_tri_out,
        w_bias_t,
    )
    bias = swap("bias", bias_copies)
    projected = [
        ((rows, width, cols), BF16),
        ((rows, cols, width), BF16),
        ((rows, width, cols), BF16),
        ((rows, width, cols), F32),
    ]
    projecting = (att_norm, w_query, w_key, w_value, w_att_gate)
    residues = cols * col_parts
    out = [((rows, cols, width), BF16)]
    held = [
        ((residues, HEADS * cols), F32),
        ((4, residues, HEADS * cols), F32),
        ((4, 1, HEADS * cols), F32),
        ((4, residues, HEADS * cols), BF16),
        ((4, width, cols), BF16),
        ((rows, cols, width), BF16),
        pltpu.SemaphoreType.DMA((rows // 2,)),
    ]
    project_flops, attend_flops = 8 * cells * width * width, 4 * cells * residues * width
    if col_parts == 1:
        flops = project_flops + attend_flops
        given = (first_pass, bias, w_att_out)
        return call(whole_kernel, out, projected + held, flops, *projecting, *given, sent=True)
    query_t, key, value_t, gate_t = call(project_kernel, projected, [], project_flops, *projecting)
    bias = by_slot(
        "bias", lax.all_to_all(by_rank("bias", bias), "col", split_axis=0, concat_axis=2, tiled=True)
    )
    key = lax.all_gather(key, "col", axis=1, tiled=True)
    value_t = lax.all_gather(value_t, "col", axis=2, tiled=True)
    given = (query_t, key, value_t, gate_t, first_pass, bias, w_att_out)
    return call(attend_kernel, out, held, attend_flops, *given, sent=True)


def solution(mesh):
    in_specs = (P(("grp", "row"), "col", None),) + (P(),) * 12
    out_specs = P(("grp", "row"), "col", None)
    return jax.shard_map(body, mesh=mesh, in_specs=in_specs, out_specs=out_specs, check_vma=False)
```

```python
import functools
import math

import jax
import jax.numpy as jnp
import numpy as np
from jax import lax
from jax.experimental import pallas as pl
from jax.experimental.pallas import tpu as pltpu
from jax.sharding import PartitionSpec as P

HEADS = 4
HEAD_DIM = 32
LANES = 128
LOG2_E = 1.4426950408889634
F32 = jnp.float32
BF16 = jnp.bfloat16
NN = (((1,), (0,)), ((), ()))
NT = (((1,), (1,)), ((), ()))
TN = (((0,), (0,)), ((), ()))


def dot(left, right, dims=NN):
    return lax.dot_general(left, right, dims, preferred_element_type=F32)


def sigmoid(values):
    return 0.5 * jnp.tanh(0.5 * values) + 0.5


def twice(weight):
    zeros = jnp.zeros_like(weight)
    return jnp.concatenate(
        [jnp.concatenate([weight, zeros], axis=1), jnp.concatenate([zeros, weight], axis=1)], axis=0
    )


def listing(ranks, mixed=False):
    first, stride = ranks - 1 - ranks // 4, 5
    if not mixed:
        return [first] + [rank for rank in range(ranks - 1, -1, -1) if rank != first]
    assert math.gcd(stride, ranks) == 1
    return [(first + stride * n) % ranks for n in range(ranks)]


def slot(rank, ranks, mixed=False):
    return listing(ranks, mixed).index(rank)


def slot_of(rank, ranks):
    first = listing(ranks)[0]
    return jnp.where(rank == first, 0, ranks - 1 - rank + (rank > first).astype(jnp.int32))


def swap(blocks, ranks, mixed=False):
    members = blocks.shape[0]
    order = listing(members, mixed)
    groups = [[first + member for member in order] for first in range(0, ranks, members)]
    return lax.all_to_all(
        blocks, "row", split_axis=0, concat_axis=0, axis_index_groups=groups, tiled=True
    )


def by_rank(blocks):
    return blocks[np.array([slot(r, blocks.shape[0]) for r in range(blocks.shape[0])])]


def by_slot(blocks):
    return blocks[np.array(listing(blocks.shape[0]))]


def lane_tiles(values):
    lanes = values.shape[1]
    return [(t, slice(t * LANES, (t + 1) * LANES)) for t in range(lanes // LANES)]


def lane_norm(values):
    centered = values - jnp.mean(values, axis=-1, keepdims=True)
    variance = jnp.mean(centered * centered, axis=-1, keepdims=True)
    return (centered * lax.rsqrt(variance + 1e-05)).astype(BF16)


def side_by_side(held, i):
    return jnp.concatenate([held[i], held[i + 1]], axis=1)


def pipeline(rows, *steps):
    for tick in range(len(rows) + len(steps) - 1):
        for late, step in enumerate(steps):
            if 0 <= tick - late < len(rows):
                step(rows[tick - late])


def gated_edges(normed, weight, weight_gate, held):
    rows, cols = normed.shape[0], normed.shape[1]
    channels = weight.shape[1]
    turned = jnp.concatenate([weight[...].T, weight_gate[...].T], axis=0)

    def project(i):
        both = dot(turned, jnp.concatenate([normed[i], normed[i + 1]], axis=0), NT)
        act = sigmoid(both[channels:]) * both[:channels]
        for tile, lanes in lane_tiles(act):
            row, part = divmod(tile, cols // LANES)
            held[part, pl.ds(i + row, channels, stride=rows), :] = act[:, lanes]

    return project


def right_kernel(members, *refs):
    given, (right, normed, *staged), (pair, w_right, w_right_gate, held, sems) = refs[:13], refs[13:25], refs[25:]
    targets = [pair, w_right, w_right_gate, *staged]
    copies = [
        pltpu.make_async_copy(source, target, sems.at[n])
        for n, (source, target) in enumerate(zip(given, targets))
    ]
    for copy in copies:
        copy.start()
    for copy in copies[:3]:
        copy.wait()

    def norm(i):
        normed[i] = lane_norm(pair[i].astype(F32))
        normed[i + 1] = lane_norm(pair[i + 1].astype(F32))

    pipeline(range(0, pair.shape[0], 2), norm, gated_edges(normed, w_right, w_right_gate, held))
    owners, block = right.shape[0], right.shape[1]
    for member in range(members):
        for part in range(held.shape[0]):
            sent = held[part, member * block : (member + 1) * block, :].astype(BF16)
            for owner in range(member, owners, members):
                right[slot(owner, owners, True), :, part * LANES : (part + 1) * LANES] = sent
    for copy in copies[3:]:
        copy.wait()


def left_kernel(normed, w_left, w_left_gate, w_tri_gate, gate, *refs):
    left, held = refs[:-1], refs[-1]
    me = lax.rem(lax.axis_index("row"), len(left))
    width = w_tri_gate.shape[1]
    gate_weight = twice(w_tri_gate[...])

    def open_gate(i):
        opened = sigmoid(dot(side_by_side(normed, i), gate_weight))
        gate[i] = opened[:, :width]
        gate[i + 1] = opened[:, width:]

    step = gated_edges(normed, w_left, w_left_gate, held)
    pipeline(range(0, normed.shape[0], 2), step, open_gate)
    for turn, out in enumerate(left):
        block = out.shape[0]
        mine = pl.ds(pl.multiple_of((me ^ turn) * block, block), block)
        for part in range(held.shape[0]):
            out[:, part * LANES : (part + 1) * LANES] = held[part, mine, :].astype(BF16)


def channel_rows(blocks, rows, channel):
    mine = slice(channel * rows, (channel + 1) * rows)
    both = slice(channel // 2 * 2 * rows, (channel // 2 + 1) * 2 * rows)
    inner = slice(mine.start - both.start, mine.stop - both.start)
    parts = [block[both, :].astype(F32)[inner] for block in blocks]
    return jnp.concatenate(parts, axis=0).astype(BF16)


def triangle_product(left, right, rows, channel):
    ranks = right.shape[0]
    by_owner = [right.at[slot(r, ranks, True)] for r in range(ranks)]
    return dot(channel_rows(left, rows, channel), channel_rows(by_owner, rows, channel), NT)


def triangle_kernel(rows, right, *refs):
    left, out = refs[:-1], refs[-1]
    members = len(left)
    me = lax.rem(lax.axis_index("row"), members)
    for channel in range(0, out.shape[1] // rows, 2):
        products = [triangle_product(left, right, rows, channel + o) for o in range(2)]
        for turn in range(members):
            mine = slice(turn * rows, (turn + 1) * rows)
            out[slot_of(me ^ turn, members), channel * rows : (channel + 2) * rows, :] = jnp.concatenate(
                [p[mine] for p in products], axis=0
            ).astype(BF16)


def partial_kernel(rows, right, *refs):
    left, out = refs[:-1], refs[-1]
    members = len(left)
    me = lax.rem(lax.axis_index("row"), members)
    for channel in range(out.shape[0]):
        product = triangle_product(left, right, rows, channel)
        for turn in range(members):
            place = pl.ds(pl.multiple_of((me ^ turn) * rows, rows), rows)
            out[channel, place, :] = product[turn * rows : (turn + 1) * rows]


def update_kernel(
    returned, gate, pair, w_tri_out, w_bias_t, first_pass, att_norm, bias, held, bias_held, turned
):
    rows, cols, width = pair.shape
    owners, block = returned.shape[0], returned.shape[1]
    channels = owners * block // rows
    total = jnp.zeros((rows, cols), F32)
    for owner in range(owners):
        total += jnp.sum(returned[owner].astype(F32).reshape(block // rows, rows, cols), axis=0)
    average = total / channels
    square = jnp.zeros((rows, cols), F32)
    for owner in range(owners):
        centered = returned[slot(owner, owners)].astype(F32).reshape(block // rows, rows, cols) - average
        square += jnp.sum(centered * centered, axis=0)
        for tile, lanes in lane_tiles(pair):
            held[tile, owner * block : (owner + 1) * block, :] = centered.reshape(block, cols)[:, lanes]
    scale = lax.rsqrt(square / channels + 1e-05)

    weight = twice(w_tri_out[...])

    def turn(i):
        for row in (i, i + 1):
            tri_norm = jnp.concatenate(
                [held[tile, pl.ds(row, channels, stride=rows), :] for tile, _ in lane_tiles(pair)], axis=1
            )
            turned[row % 4] = (tri_norm * scale[row : row + 1]).astype(BF16).T

    def update(i):
        both = dot(side_by_side(turned, i % 4), weight)
        first_pass[i] = pair[i].astype(F32) + gate[i] * both[:, :width]
        first_pass[i + 1] = pair[i + 1].astype(F32) + gate[i + 1] * both[:, width:]

    def norm(i):
        for row in (i, i + 1):
            att_norm[row] = lane_norm(first_pass[row])

    def project_bias(i):
        both = dot(w_bias_t[...], jnp.concatenate([att_norm[i], att_norm[i + 1]], axis=0), NT)
        for row in range(2):
            for head in range(HEADS):
                place = head * rows + i + row
                bias_held[place : place + 1, :] = both[head : head + 1, row * cols : (row + 1) * cols]

    pipeline(range(0, rows, 2), turn, update, norm, project_bias)
    rounded = bias_held[...].astype(BF16)
    for owner in range(bias.shape[0]):
        bias[owner] = rounded


def projector(att_norm, w_query, w_key, w_value, w_att_gate, query_t, key, value_t, gate_t):
    w_turned = jnp.concatenate([w[...].T for w in (w_query, w_value, w_att_gate)], axis=0)
    w_direct = twice(w_key[...])
    cols, width = att_norm.shape[1], w_query.shape[1]

    def project(i):
        keys = dot(side_by_side(att_norm, i), w_direct).astype(BF16)
        turned = dot(w_turned, jnp.concatenate([att_norm[i], att_norm[i + 1]], axis=0), NT)
        for row in range(2):
            key[i + row] = keys[:, row * width : (row + 1) * width]
            mine = turned[:, row * cols : (row + 1) * cols]
            query_t[i + row] = mine[:width].astype(BF16)
            value_t[i + row] = mine[width : 2 * width].astype(BF16)
            gate_t[i + row] = sigmoid(mine[2 * width :])

    return project


def project_kernel(*refs):
    pipeline(range(0, refs[0].shape[0], 2), projector(*refs))


def whole_kernel(att_norm, w_query, w_key, w_value, w_att_gate, *refs):
    given, projected, held = refs[:4], refs[4:8], refs[8:]
    project = projector(att_norm, w_query, w_key, w_value, w_att_gate, *projected)
    attend_kernel(*projected, *given, *held, before=(project,))


def attend_kernel(
    query_t,
    key,
    value_t,
    gate_t,
    first_pass,
    bias,
    w_att_out,
    out,
    bias_t,
    scores,
    peaks,
    weights,
    gated,
    done,
    sems,
    before=(),
):
    rows, width, cols = query_t.shape
    head_rows = bias.shape[1] // HEADS
    score_scale = LOG2_E / HEAD_DIM**0.5
    ones = jnp.ones((16, key.shape[1]), BF16)
    heads = [
        (slice(h * HEAD_DIM, (h + 1) * HEAD_DIM), slice(h * cols, (h + 1) * cols)) for h in range(HEADS)
    ]

    def score(i):
        for row in (i, i + 1):
            blocks = []
            for mine, _ in heads:
                above = jnp.zeros((mine.start, cols), BF16)
                below = jnp.zeros((width - mine.stop, cols), BF16)
                parts = [p for p in (above, query_t[row, mine, :], below) if p.shape[0]]
                blocks.append(jnp.concatenate(parts, axis=0))
            raw = dot(key[row], jnp.concatenate(blocks, axis=1))
            for _, span in heads:
                biased = raw[:, span] * score_scale + bias_t[:, span]
                scores[row % 4, :, span] = biased
                peaks[row % 4, :, span] = jnp.max(biased, axis=0, keepdims=True)

    def soften(i):
        for row in (i, i + 1):
            for _, span in heads:
                lowered = scores[row % 4, :, span] - peaks[row % 4, :, span]
                weights[row % 4, :, span] = jnp.exp2(lowered).astype(BF16)

    def collect(i):
        for row in (i, i + 1):
            for head in range(0, HEADS, 2):
                (first, left), (second, right) = heads[head : head + 2]
                values = jnp.concatenate([value_t[row, first.start : second.stop, :], ones], axis=0)
                summed = dot(values, weights[row % 4, :, left.start : right.stop])
                share = 1.0 / summed[2 * HEAD_DIM : 2 * HEAD_DIM + 1]
                for mine, there, lanes in (
                    (first, slice(0, HEAD_DIM), slice(0, cols)),
                    (second, slice(HEAD_DIM, 2 * HEAD_DIM), slice(cols, 2 * cols)),
                ):
                    attended = summed[there, lanes] * share[:, lanes] * gate_t[row, mine, :]
                    gated[row % 4, mine, :] = attended.astype(BF16)

    def finish(i):
        turned = jnp.concatenate([gated[i % 4].T, gated[(i + 1) % 4].T], axis=1)
        both = dot(turned, w_last)
        done[i] = (first_pass[i] + both[:, :width]).astype(BF16)
        done[i + 1] = (first_pass[i + 1] + both[:, width:]).astype(BF16)
        copy = pltpu.make_async_copy(done.at[pl.ds(i, 2)], out.at[pl.ds(i, 2)], sems.at[i // 2])
        copy.start()
        copies.append(copy)

    copies = []
    w_last = twice(w_att_out[...])
    for head, (_, span) in enumerate(heads):
        parts = [
            bias[slot(owner, bias.shape[0])].astype(F32)[head * head_rows : (head + 1) * head_rows]
            for owner in range(bias.shape[0])
        ]
        bias_t[:, span] = jnp.concatenate(parts, axis=0).T * LOG2_E
    pipeline(range(0, rows, 2), *before, score, soften, collect, finish)
    for copy in copies:
        copy.wait()


def call(kernel, outs, scratch, flops, *operands, fetched=0, sent=False):
    vmem = pl.BlockSpec(memory_space=pltpu.VMEM)
    far = pl.BlockSpec(memory_space=pltpu.HBM)
    shapes = [jax.ShapeDtypeStruct(shape, dtype) for shape, dtype in outs]
    moved = sum(o.size * o.dtype.itemsize for o in operands)
    operands = [
        pltpu.with_memory_space_constraint(o, pltpu.HBM) if n < fetched else o
        for n, o in enumerate(operands)
    ]
    got = pl.pallas_call(
        kernel,
        out_shape=shapes,
        in_specs=[far] * fetched + [vmem] * (len(operands) - fetched),
        out_specs=[far if sent else vmem] * len(shapes),
        scratch_shapes=[pltpu.VMEM(*s) if isinstance(s, tuple) else s for s in scratch],
        compiler_params=pltpu.CompilerParams(vmem_limit_bytes=48 * 2**20),
        cost_estimate=pl.CostEstimate(flops=flops, bytes_accessed=moved, transcendentals=0),
    )(*operands)
    return got if len(got) > 1 else got[0]


def body(
    pair_rep,
    w_left,
    w_left_gate,
    w_right,
    w_right_gate,
    w_tri_gate,
    w_tri_out,
    w_query,
    w_key,
    w_value,
    w_bias,
    w_att_gate,
    w_att_out,
):
    rows, cols, width = pair_rep.shape
    channels = w_left.shape[1]
    owners, col_parts = lax.axis_size("row"), lax.axis_size("col")
    half = owners // 2
    own = channels // half
    residues = owners * rows
    cells = rows * cols

    later = (w_left, w_left_gate, w_tri_gate, w_tri_out, w_query, w_key, w_value, w_att_gate, w_att_out)
    right, normed, *later, w_bias_t = call(
        functools.partial(right_kernel, half),
        [
            ((owners, own * rows, cols), BF16),
            (pair_rep.shape, BF16),
            *[(w.shape, BF16) for w in later],
            (w_bias.shape[::-1], BF16),
        ],
        [
            (pair_rep.shape, BF16),
            (w_right.shape, BF16),
            (w_right_gate.shape, BF16),
            ((cols // LANES, (channels + 1) * rows, LANES), F32),
            pltpu.SemaphoreType.DMA((13,)),
        ],
        4 * cells * width * channels,
        pair_rep,
        w_right,
        w_right_gate,
        *later,
        w_bias.T,
        fetched=13,
    )
    w_left, w_left_gate, w_tri_gate, w_tri_out, w_query, w_key, w_value, w_att_gate, w_att_out = later
    right = swap(right, owners, True)
    gate, *left = call(
        left_kernel,
        [((rows, cols, width), F32)] + [((own * rows, cols), BF16)] * half,
        [((cols // LANES, (channels + 1) * rows, LANES), F32)],
        6 * cells * width * channels,
        normed,
        w_left,
        w_left_gate,
        w_tri_gate,
    )
    for turn in range(half - 1, 0, -1):
        left[turn] = lax.ppermute(left[turn], "row", [(r, r ^ turn) for r in range(owners)])
    flops = 2 * own * half * rows * residues * cols
    if col_parts == 1:
        summed = call(
            functools.partial(triangle_kernel, rows),
            [((half, own * rows, residues), BF16)],
            [],
            flops,
            right,
            *left,
        )
    else:
        partial_sums = call(
            functools.partial(partial_kernel, rows),
            [((own, half * rows, residues), F32)],
            [],
            flops,
            right,
            *left,
        )
        summed = lax.psum_scatter(partial_sums, "col", scatter_dimension=2, tiled=True).astype(BF16)
        summed = by_slot(summed.reshape(own, half, rows, cols).swapaxes(0, 1))
        summed = summed.reshape(half, own * rows, cols)
    returned = swap(summed, owners)
    first_pass, att_norm, bias_copies = call(
        update_kernel,
        [
            ((rows, cols, width), F32),
            ((rows, cols, width), BF16),
            ((owners, HEADS * rows, cols), BF16),
        ],
        [
            ((cols // LANES, (channels + 1) * rows, LANES), F32),
            ((HEADS * rows, cols), F32),
            ((4, cols, channels), BF16),
        ],
        2 * cells * channels * width,
        returned,
        gate,
        pair_rep,
        w_tri_out,
        w_bias_t,
    )
    bias = swap(bias_copies, owners)
    projected = [
        ((rows, width, cols), BF16),
        ((rows, cols, width), BF16),
        ((rows, width, cols), BF16),
        ((rows, width, cols), F32),
    ]
    projecting = (att_norm, w_query, w_key, w_value, w_att_gate)
    residues = cols * col_parts
    out = [((rows, cols, width), BF16)]
    held = [
        ((residues, HEADS * cols), F32),
        ((4, residues, HEADS * cols), F32),
        ((4, 1, HEADS * cols), F32),
        ((4, residues, HEADS * cols), BF16),
        ((4, width, cols), BF16),
        ((rows, cols, width), BF16),
        pltpu.SemaphoreType.DMA((rows // 2,)),
    ]
    project_flops, attend_flops = 8 * cells * width * width, 4 * cells * residues * width
    if col_parts == 1:
        flops = project_flops + attend_flops
        given = (first_pass, bias, w_att_out)
        return call(whole_kernel, out, projected + held, flops, *projecting, *given, sent=True)
    query_t, key, value_t, gate_t = call(project_kernel, projected, [], project_flops, *projecting)
    bias = by_slot(lax.all_to_all(by_rank(bias), "col", split_axis=0, concat_axis=2, tiled=True))
    key = lax.all_gather(key, "col", axis=1, tiled=True)
    value_t = lax.all_gather(value_t, "col", axis=2, tiled=True)
    given = (query_t, key, value_t, gate_t, first_pass, bias, w_att_out)
    return call(attend_kernel, out, held, attend_flops, *given, sent=True)


def solution(mesh):
    in_specs = (P(("grp", "row"), "col", None),) + (P(),) * 12
    out_specs = P(("grp", "row"), "col", None)
    return jax.shard_map(body, mesh=mesh, in_specs=in_specs, out_specs=out_specs, check_vma=False)
```

```python
import functools
import math

import jax
import jax.numpy as jnp
import numpy as np
from jax import lax
from jax.experimental import pallas as pl
from jax.experimental.pallas import tpu as pltpu
from jax.sharding import PartitionSpec as P

HEADS = 4
HEAD_DIM = 32
LANES = 128
LOG2_E = 1.4426950408889634
F32 = jnp.float32
BF16 = jnp.bfloat16
NN = (((1,), (0,)), ((), ()))
NT = (((1,), (1,)), ((), ()))
TN = (((0,), (0,)), ((), ()))


def dot(left, right, dims=NN):
    return lax.dot_general(left, right, dims, preferred_element_type=F32)


def sigmoid(values):
    return 0.5 * jnp.tanh(0.5 * values) + 0.5


def twice(weight):
    zeros = jnp.zeros_like(weight)
    return jnp.concatenate(
        [jnp.concatenate([weight, zeros], axis=1), jnp.concatenate([zeros, weight], axis=1)], axis=0
    )


def listing(ranks, mixed=False):
    first, stride = ranks - 1 - ranks // 4, 5
    if not mixed:
        return [first] + [rank for rank in range(ranks - 1, -1, -1) if rank != first]
    assert math.gcd(stride, ranks) == 1
    return [(first + stride * n) % ranks for n in range(ranks)]


def slot(rank, ranks, mixed=False):
    return listing(ranks, mixed).index(rank)


def slot_of(rank, ranks):
    first = listing(ranks)[0]
    return jnp.where(rank == first, 0, ranks - 1 - rank + (rank > first).astype(jnp.int32))


def swap(blocks, ranks, mixed=False):
    members = blocks.shape[0]
    order = listing(members, mixed)
    groups = [[first + member for member in order] for first in range(0, ranks, members)]
    return lax.all_to_all(
        blocks, "row", split_axis=0, concat_axis=0, axis_index_groups=groups, tiled=True
    )


def by_rank(blocks):
    return blocks[np.array([slot(r, blocks.shape[0]) for r in range(blocks.shape[0])])]


def by_slot(blocks):
    return blocks[np.array(listing(blocks.shape[0]))]


def lane_tiles(values):
    lanes = values.shape[1]
    return [(t, slice(t * LANES, (t + 1) * LANES)) for t in range(lanes // LANES)]


def lane_norm(values):
    centered = values - jnp.mean(values, axis=-1, keepdims=True)
    variance = jnp.mean(centered * centered, axis=-1, keepdims=True)
    return (centered * lax.rsqrt(variance + 1e-05)).astype(BF16)


def side_by_side(held, i):
    return jnp.concatenate([held[i], held[i + 1]], axis=1)


def pipeline(rows, *steps):
    for tick in range(len(rows) + len(steps) - 1):
        for late, step in enumerate(steps):
            if 0 <= tick - late < len(rows):
                step(rows[tick - late])


def gated_edges(normed, weight, weight_gate, held):
    rows, cols = normed.shape[0], normed.shape[1]
    channels = weight.shape[1]
    turned = jnp.concatenate([weight[...].T, weight_gate[...].T], axis=0)

    def project(i):
        both = dot(turned, jnp.concatenate([normed[i], normed[i + 1]], axis=0), NT)
        act = sigmoid(both[channels:]) * both[:channels]
        for tile, lanes in lane_tiles(act):
            row, part = divmod(tile, cols // LANES)
            held[part, pl.ds(i + row, channels, stride=rows), :] = act[:, lanes]

    return project


def right_kernel(members, *refs):
    given, (right, normed, *staged), (pair, w_right, w_right_gate, held, sems) = refs[:13], refs[13:25], refs[25:]
    targets = [pair, w_right, w_right_gate, *staged]
    copies = [
        pltpu.make_async_copy(source, target, sems.at[n])
        for n, (source, target) in enumerate(zip(given, targets))
    ]
    for copy in copies:
        copy.start()
    for copy in copies[:3]:
        copy.wait()

    def norm(i):
        normed[i] = lane_norm(pair[i].astype(F32))
        normed[i + 1] = lane_norm(pair[i + 1].astype(F32))

    pipeline(range(0, pair.shape[0], 2), norm, gated_edges(normed, w_right, w_right_gate, held))
    owners, block = right.shape[0], right.shape[1]
    for member in range(members):
        for part in range(held.shape[0]):
            sent = held[part, member * block : (member + 1) * block, :].astype(BF16)
            for owner in range(member, owners, members):
                right[slot(owner, owners, True), :, part * LANES : (part + 1) * LANES] = sent
    for copy in copies[3:]:
        copy.wait()


def left_kernel(normed, w_left, w_left_gate, w_tri_gate, gate, *refs):
    left, held = refs[:-1], refs[-1]
    me = lax.rem(lax.axis_index("row"), len(left))
    width = w_tri_gate.shape[1]
    gate_weight = twice(w_tri_gate[...])

    def open_gate(i):
        opened = sigmoid(dot(side_by_side(normed, i), gate_weight))
        gate[i] = opened[:, :width]
        gate[i + 1] = opened[:, width:]

    step = gated_edges(normed, w_left, w_left_gate, held)
    pipeline(range(0, normed.shape[0], 2), step, open_gate)
    for turn, out in enumerate(left):
        block = out.shape[0]
        mine = pl.ds(pl.multiple_of((me ^ turn) * block, block), block)
        for part in range(held.shape[0]):
            out[:, part * LANES : (part + 1) * LANES] = held[part, mine, :].astype(BF16)


def channel_rows(blocks, rows, channel):
    mine = slice(channel * rows, (channel + 1) * rows)
    both = slice(channel // 2 * 2 * rows, (channel // 2 + 1) * 2 * rows)
    inner = slice(mine.start - both.start, mine.stop - both.start)
    parts = [block[both, :].astype(F32)[inner] for block in blocks]
    return jnp.concatenate(parts, axis=0).astype(BF16)


def triangle_product(left, right, rows, channel):
    ranks = right.shape[0]
    by_owner = [right.at[slot(r, ranks, True)] for r in range(ranks)]
    return dot(channel_rows(left, rows, channel), channel_rows(by_owner, rows, channel), NT)


def triangle_kernel(rows, right, *refs):
    left, out = refs[-2::-1], refs[-1]
    members = len(left)
    me = lax.rem(lax.axis_index("row"), members)
    for channel in range(0, out.shape[1] // rows, 2):
        products = [triangle_product(left, right, rows, channel + o) for o in range(2)]
        for turn in range(members):
            mine = slice(turn * rows, (turn + 1) * rows)
            out[slot_of(me ^ turn, members), channel * rows : (channel + 2) * rows, :] = jnp.concatenate(
                [p[mine] for p in products], axis=0
            ).astype(BF16)


def partial_kernel(rows, right, *refs):
    left, out = refs[-2::-1], refs[-1]
    members = len(left)
    me = lax.rem(lax.axis_index("row"), members)
    for channel in range(out.shape[0]):
        product = triangle_product(left, right, rows, channel)
        for turn in range(members):
            place = pl.ds(pl.multiple_of((me ^ turn) * rows, rows), rows)
            out[channel, place, :] = product[turn * rows : (turn + 1) * rows]


def update_kernel(
    returned, gate, pair, w_tri_out, w_bias_t, first_pass, att_norm, bias, held, bias_held, turned
):
    rows, cols, width = pair.shape
    owners, block = returned.shape[0], returned.shape[1]
    channels = owners * block // rows
    total = jnp.zeros((rows, cols), F32)
    for owner in range(owners):
        total += jnp.sum(returned[owner].astype(F32).reshape(block // rows, rows, cols), axis=0)
    average = total / channels
    square = jnp.zeros((rows, cols), F32)
    for owner in range(owners):
        centered = returned[slot(owner, owners)].astype(F32).reshape(block // rows, rows, cols) - average
        square += jnp.sum(centered * centered, axis=0)
        for tile, lanes in lane_tiles(pair):
            held[tile, owner * block : (owner + 1) * block, :] = centered.reshape(block, cols)[:, lanes]
    scale = lax.rsqrt(square / channels + 1e-05)

    weight = twice(w_tri_out[...])

    def turn(i):
        for row in (i, i + 1):
            tri_norm = jnp.concatenate(
                [held[tile, pl.ds(row, channels, stride=rows), :] for tile, _ in lane_tiles(pair)], axis=1
            )
            turned[row % 4] = (tri_norm * scale[row : row + 1]).astype(BF16).T

    def update(i):
        both = dot(side_by_side(turned, i % 4), weight)
        first_pass[i] = pair[i].astype(F32) + gate[i] * both[:, :width]
        first_pass[i + 1] = pair[i + 1].astype(F32) + gate[i + 1] * both[:, width:]

    def norm(i):
        for row in (i, i + 1):
            att_norm[row] = lane_norm(first_pass[row])

    def project_bias(i):
        both = dot(w_bias_t[...], jnp.concatenate([att_norm[i], att_norm[i + 1]], axis=0), NT)
        for row in range(2):
            for head in range(HEADS):
                place = head * rows + i + row
                bias_held[place : place + 1, :] = both[head : head + 1, row * cols : (row + 1) * cols]

    pipeline(range(0, rows, 2), turn, update, norm, project_bias)
    rounded = bias_held[...].astype(BF16)
    for owner in range(bias.shape[0]):
        bias[owner] = rounded


def projector(att_norm, w_query, w_key, w_value, w_att_gate, query_t, key, value_t, gate_t):
    w_turned = jnp.concatenate([w[...].T for w in (w_query, w_value, w_att_gate)], axis=0)
    w_direct = twice(w_key[...])
    cols, width = att_norm.shape[1], w_query.shape[1]

    def project(i):
        keys = dot(side_by_side(att_norm, i), w_direct).astype(BF16)
        turned = dot(w_turned, jnp.concatenate([att_norm[i], att_norm[i + 1]], axis=0), NT)
        for row in range(2):
            key[i + row] = keys[:, row * width : (row + 1) * width]
            mine = turned[:, row * cols : (row + 1) * cols]
            query_t[i + row] = mine[:width].astype(BF16)
            value_t[i + row] = mine[width : 2 * width].astype(BF16)
            gate_t[i + row] = sigmoid(mine[2 * width :])

    return project


def project_kernel(*refs):
    pipeline(range(0, refs[0].shape[0], 2), projector(*refs))


def whole_kernel(att_norm, w_query, w_key, w_value, w_att_gate, *refs):
    given, projected, held = refs[:4], refs[4:8], refs[8:]
    project = projector(att_norm, w_query, w_key, w_value, w_att_gate, *projected)
    attend_kernel(*projected, *given, *held, before=(project,))


def attend_kernel(
    query_t,
    key,
    value_t,
    gate_t,
    first_pass,
    bias,
    w_att_out,
    out,
    bias_t,
    scores,
    peaks,
    weights,
    gated,
    done,
    sems,
    before=(),
):
    rows, width, cols = query_t.shape
    head_rows = bias.shape[1] // HEADS
    score_scale = LOG2_E / HEAD_DIM**0.5
    ones = jnp.ones((16, key.shape[1]), BF16)
    heads = [
        (slice(h * HEAD_DIM, (h + 1) * HEAD_DIM), slice(h * cols, (h + 1) * cols)) for h in range(HEADS)
    ]

    def score(i):
        for row in (i, i + 1):
            blocks = []
            for mine, _ in heads:
                above = jnp.zeros((mine.start, cols), BF16)
                below = jnp.zeros((width - mine.stop, cols), BF16)
                parts = [p for p in (above, query_t[row, mine, :], below) if p.shape[0]]
                blocks.append(jnp.concatenate(parts, axis=0))
            raw = dot(key[row], jnp.concatenate(blocks, axis=1))
            for _, span in heads:
                biased = raw[:, span] * score_scale + bias_t[:, span]
                scores[row % 4, :, span] = biased
                peaks[row % 4, :, span] = jnp.max(biased, axis=0, keepdims=True)

    def soften(i):
        for row in (i, i + 1):
            for _, span in heads:
                lowered = scores[row % 4, :, span] - peaks[row % 4, :, span]
                weights[row % 4, :, span] = jnp.exp2(lowered).astype(BF16)

    def collect(i):
        for row in (i, i + 1):
            for head in range(0, HEADS, 2):
                (first, left), (second, right) = heads[head : head + 2]
                values = jnp.concatenate([value_t[row, first.start : second.stop, :], ones], axis=0)
                summed = dot(values, weights[row % 4, :, left.start : right.stop])
                share = 1.0 / summed[2 * HEAD_DIM : 2 * HEAD_DIM + 1]
                for mine, there, lanes in (
                    (first, slice(0, HEAD_DIM), slice(0, cols)),
                    (second, slice(HEAD_DIM, 2 * HEAD_DIM), slice(cols, 2 * cols)),
                ):
                    attended = summed[there, lanes] * share[:, lanes] * gate_t[row, mine, :]
                    gated[row % 4, mine, :] = attended.astype(BF16)

    def finish(i):
        turned = jnp.concatenate([gated[i % 4].T, gated[(i + 1) % 4].T], axis=1)
        both = dot(turned, w_last)
        done[i] = (first_pass[i] + both[:, :width]).astype(BF16)
        done[i + 1] = (first_pass[i + 1] + both[:, width:]).astype(BF16)
        copy = pltpu.make_async_copy(done.at[pl.ds(i, 2)], out.at[pl.ds(i, 2)], sems.at[i // 2])
        copy.start()
        copies.append(copy)

    copies = []
    w_last = twice(w_att_out[...])
    for head, (_, span) in enumerate(heads):
        parts = [
            bias[slot(owner, bias.shape[0])].astype(F32)[head * head_rows : (head + 1) * head_rows]
            for owner in range(bias.shape[0])
        ]
        bias_t[:, span] = jnp.concatenate(parts, axis=0).T * LOG2_E
    pipeline(range(0, rows, 2), *before, score, soften, collect, finish)
    for copy in copies:
        copy.wait()


def call(kernel, outs, scratch, flops, *operands, fetched=0, sent=False):
    vmem = pl.BlockSpec(memory_space=pltpu.VMEM)
    far = pl.BlockSpec(memory_space=pltpu.HBM)
    shapes = [jax.ShapeDtypeStruct(shape, dtype) for shape, dtype in outs]
    moved = sum(o.size * o.dtype.itemsize for o in operands)
    operands = [
        pltpu.with_memory_space_constraint(o, pltpu.HBM) if n < fetched else o
        for n, o in enumerate(operands)
    ]
    got = pl.pallas_call(
        kernel,
        out_shape=shapes,
        in_specs=[far] * fetched + [vmem] * (len(operands) - fetched),
        out_specs=[far if sent else vmem] * len(shapes),
        scratch_shapes=[pltpu.VMEM(*s) if isinstance(s, tuple) else s for s in scratch],
        compiler_params=pltpu.CompilerParams(vmem_limit_bytes=48 * 2**20),
        cost_estimate=pl.CostEstimate(flops=flops, bytes_accessed=moved, transcendentals=0),
    )(*operands)
    return got if len(got) > 1 else got[0]


def body(
    pair_rep,
    w_left,
    w_left_gate,
    w_right,
    w_right_gate,
    w_tri_gate,
    w_tri_out,
    w_query,
    w_key,
    w_value,
    w_bias,
    w_att_gate,
    w_att_out,
):
    rows, cols, width = pair_rep.shape
    channels = w_left.shape[1]
    owners, col_parts = lax.axis_size("row"), lax.axis_size("col")
    half = owners // 2
    own = channels // half
    residues = owners * rows
    cells = rows * cols

    later = (w_left, w_left_gate, w_tri_gate, w_tri_out, w_query, w_key, w_value, w_att_gate, w_att_out)
    right, normed, *later, w_bias_t = call(
        functools.partial(right_kernel, half),
        [
            ((owners, own * rows, cols), BF16),
            (pair_rep.shape, BF16),
            *[(w.shape, BF16) for w in later],
            (w_bias.shape[::-1], BF16),
        ],
        [
            (pair_rep.shape, BF16),
            (w_right.shape, BF16),
            (w_right_gate.shape, BF16),
            ((cols // LANES, (channels + 1) * rows, LANES), F32),
            pltpu.SemaphoreType.DMA((13,)),
        ],
        4 * cells * width * channels,
        pair_rep,
        w_right,
        w_right_gate,
        *later,
        w_bias.T,
        fetched=13,
    )
    w_left, w_left_gate, w_tri_gate, w_tri_out, w_query, w_key, w_value, w_att_gate, w_att_out = later
    right = swap(right, owners, True)
    gate, *left = call(
        left_kernel,
        [((rows, cols, width), F32)] + [((own * rows, cols), BF16)] * half,
        [((cols // LANES, (channels + 1) * rows, LANES), F32)],
        6 * cells * width * channels,
        normed,
        w_left,
        w_left_gate,
        w_tri_gate,
    )
    for turn in range(half - 1, 0, -1):
        left[turn] = lax.ppermute(left[turn], "row", [(r, r ^ turn) for r in range(owners)])
    flops = 2 * own * half * rows * residues * cols
    if col_parts == 1:
        summed = call(
            functools.partial(triangle_kernel, rows),
            [((half, own * rows, residues), BF16)],
            [],
            flops,
            right,
            *left[::-1],
        )
    else:
        partial_sums = call(
            functools.partial(partial_kernel, rows),
            [((own, half * rows, residues), F32)],
            [],
            flops,
            right,
            *left[::-1],
        )
        summed = lax.psum_scatter(partial_sums, "col", scatter_dimension=2, tiled=True).astype(BF16)
        summed = by_slot(summed.reshape(own, half, rows, cols).swapaxes(0, 1))
        summed = summed.reshape(half, own * rows, cols)
    returned = swap(summed, owners)
    first_pass, att_norm, bias_copies = call(
        update_kernel,
        [
            ((rows, cols, width), F32),
            ((rows, cols, width), BF16),
            ((owners, HEADS * rows, cols), BF16),
        ],
        [
            ((cols // LANES, (channels + 1) * rows, LANES), F32),
            ((HEADS * rows, cols), F32),
            ((4, cols, channels), BF16),
        ],
        2 * cells * channels * width,
        returned,
        gate,
        pair_rep,
        w_tri_out,
        w_bias_t,
    )
    bias = swap(bias_copies, owners)
    projected = [
        ((rows, width, cols), BF16),
        ((rows, cols, width), BF16),
        ((rows, width, cols), BF16),
        ((rows, width, cols), F32),
    ]
    projecting = (att_norm, w_query, w_key, w_value, w_att_gate)
    residues = cols * col_parts
    out = [((rows, cols, width), BF16)]
    held = [
        ((residues, HEADS * cols), F32),
        ((4, residues, HEADS * cols), F32),
        ((4, 1, HEADS * cols), F32),
        ((4, residues, HEADS * cols), BF16),
        ((4, width, cols), BF16),
        ((rows, cols, width), BF16),
        pltpu.SemaphoreType.DMA((rows // 2,)),
    ]
    project_flops, attend_flops = 8 * cells * width * width, 4 * cells * residues * width
    if col_parts == 1:
        flops = project_flops + attend_flops
        given = (first_pass, bias, w_att_out)
        return call(whole_kernel, out, projected + held, flops, *projecting, *given, sent=True)
    query_t, key, value_t, gate_t = call(project_kernel, projected, [], project_flops, *projecting)
    bias = by_slot(lax.all_to_all(by_rank(bias), "col", split_axis=0, concat_axis=2, tiled=True))
    key = lax.all_gather(key, "col", axis=1, tiled=True)
    value_t = lax.all_gather(value_t, "col", axis=2, tiled=True)
    given = (query_t, key, value_t, gate_t, first_pass, bias, w_att_out)
    return call(attend_kernel, out, held, attend_flops, *given, sent=True)


def solution(mesh):
    in_specs = (P(("grp", "row"), "col", None),) + (P(),) * 12
    out_specs = P(("grp", "row"), "col", None)
    return jax.shard_map(body, mesh=mesh, in_specs=in_specs, out_specs=out_specs, check_vma=False)
```

```python
import functools
import math

import jax
import jax.numpy as jnp
import numpy as np
from jax import lax
from jax.experimental import pallas as pl
from jax.experimental.pallas import tpu as pltpu
from jax.sharding import PartitionSpec as P

HEADS = 4
HEAD_DIM = 32
LANES = 128
RING = 8
LOG2_E = 1.4426950408889634
F32 = jnp.float32
BF16 = jnp.bfloat16
NN = (((1,), (0,)), ((), ()))
NT = (((1,), (1,)), ((), ()))
TN = (((0,), (0,)), ((), ()))


def dot(left, right, dims=NN):
    return lax.dot_general(left, right, dims, preferred_element_type=F32)


def sigmoid(values):
    return 0.5 * jnp.tanh(0.5 * values) + 0.5


def twice(weight):
    zeros = jnp.zeros_like(weight)
    return jnp.concatenate(
        [jnp.concatenate([weight, zeros], axis=1), jnp.concatenate([zeros, weight], axis=1)], axis=0
    )


def listing(step, ranks):
    first, stride = ranks - 1 - ranks // 4, 5
    if step == "triangle":
        return [first] + [rank for rank in range(ranks - 1, -1, -1) if rank != first]
    assert math.gcd(stride, ranks) == 1
    return [(first + stride * n) % ranks for n in range(ranks)]


def slot(step, rank, ranks):
    return listing(step, ranks).index(rank)


def swap(step, blocks):
    return lax.all_to_all(
        blocks,
        "row",
        split_axis=0,
        concat_axis=0,
        axis_index_groups=[listing(step, blocks.shape[0])],
        tiled=True,
    )


def by_rank(step, blocks):
    return blocks[np.array([slot(step, r, blocks.shape[0]) for r in range(blocks.shape[0])])]


def by_slot(step, blocks):
    return blocks[np.array(listing(step, blocks.shape[0]))]


def lane_tiles(values):
    lanes = values.shape[1]
    return [(t, slice(t * LANES, (t + 1) * LANES)) for t in range(lanes // LANES)]


def lane_norm(values):
    centered = values - jnp.mean(values, axis=-1, keepdims=True)
    variance = jnp.mean(centered * centered, axis=-1, keepdims=True)
    return (centered * lax.rsqrt(variance + 1e-05)).astype(BF16)


def side_by_side(held, i):
    return jnp.concatenate([held[i], held[i + 1]], axis=1)


def pipeline(rows, *steps):
    for tick in range(len(rows) + len(steps) - 1):
        for late, step in enumerate(steps):
            if 0 <= tick - late < len(rows):
                step(rows[tick - late])


def doubled(step):
    def both(i):
        step(i)
        step(i + 2)

    return both


def edges_kernel(*refs):
    given, (out, gate, *staged), (pair, weights, normed, held, sems) = refs[:13], refs[13:22], refs[22:]
    targets = [pair, *(weights.at[n] for n in range(5)), *staged]
    copies = [
        pltpu.make_async_copy(source, target, sems.at[n])
        for n, (source, target) in enumerate(zip(given, targets))
    ]
    for copy in copies:
        copy.start()
    for copy in copies[:6]:
        copy.wait()
    rows, width = pair.shape[0], pair.shape[2]
    channels = weights.shape[2]
    cols = pair.shape[1]
    turned = jnp.concatenate([weights[n].T for n in range(4)], axis=0)
    gate_weight = twice(weights[4])

    def norm(i):
        normed[i] = lane_norm(pair[i].astype(F32))
        normed[i + 1] = lane_norm(pair[i + 1].astype(F32))

    def project(i):
        both = dot(turned, jnp.concatenate([normed[i], normed[i + 1]], axis=0), NT)
        for side in range(2):
            base = 2 * side * channels
            act = sigmoid(both[base + channels : base + 2 * channels]) * both[base : base + channels]
            for tile, lanes in lane_tiles(act):
                row, part = divmod(tile, cols // LANES)
                place = pl.ds(side * rows + i + row, channels, stride=2 * rows)
                held[part, place, :] = act[:, lanes]
        opened = sigmoid(dot(side_by_side(normed, i), gate_weight))
        gate[i] = opened[:, :width]
        gate[i + 1] = opened[:, width:]

    pipeline(range(0, rows, 2), norm, project)
    owners, block = out.shape[0], out.shape[1]
    for owner in range(owners):
        for tile, lanes in lane_tiles(pair):
            out[slot("edges", owner, owners), :, lanes] = held[tile, owner * block : (owner + 1) * block, :].astype(BF16)
    for copy in copies[6:]:
        copy.wait()


def triangle_sides(edges, rows, channel):
    sides = [[], []]
    sources = edges.shape[0]
    for source in range(sources):
        block = edges[slot("edges", source, sources), channel * 2 * rows : (channel + 1) * 2 * rows, :].astype(F32)
        sides[0].append(block[:rows])
        sides[1].append(block[rows:])
    return [jnp.concatenate(side, axis=0).astype(BF16) for side in sides]


def triangle_kernel(rows, edges, out):
    for pair_of in range(0, out.shape[1] // rows, 2):
        products = [dot(*triangle_sides(edges, rows, pair_of + o), NT) for o in range(2)]
        owners = out.shape[0]
        for owner in range(owners):
            mine = slice(owner * rows, (owner + 1) * rows)
            out[slot("triangle", owner, owners), pair_of * rows : (pair_of + 2) * rows, :] = jnp.concatenate(
                [p[mine] for p in products], axis=0
            ).astype(BF16)


def partial_kernel(rows, edges, out):
    for channel in range(out.shape[0]):
        out[channel] = dot(*triangle_sides(edges, rows, channel), NT)


def update_kernel(
    returned, gate, pair, w_tri_out, w_bias_t, first_pass, att_norm, bias, held, bias_held, turned
):
    rows, cols, width = pair.shape
    owners, block = returned.shape[0], returned.shape[1]
    channels = owners * block // rows
    total = jnp.zeros((rows, cols), F32)
    for owner in range(owners):
        total += jnp.sum(returned[owner].astype(F32).reshape(block // rows, rows, cols), axis=0)
    average = total / channels
    square = jnp.zeros((rows, cols), F32)
    for owner in range(owners):
        centered = returned[slot("triangle", owner, owners)].astype(F32).reshape(block // rows, rows, cols) - average
        square += jnp.sum(centered * centered, axis=0)
        for tile, lanes in lane_tiles(pair):
            held[tile, owner * block : (owner + 1) * block, :] = centered.reshape(block, cols)[:, lanes]
    scale = lax.rsqrt(square / channels + 1e-05)

    weight = twice(w_tri_out[...])

    def turn(i):
        for row in (i, i + 1):
            tri_norm = jnp.concatenate(
                [held[tile, pl.ds(row, channels, stride=rows), :] for tile, _ in lane_tiles(pair)], axis=1
            )
            turned[row % 4] = (tri_norm * scale[row : row + 1]).astype(BF16).T

    def update(i):
        both = dot(side_by_side(turned, i % 4), weight)
        first_pass[i] = pair[i].astype(F32) + gate[i] * both[:, :width]
        first_pass[i + 1] = pair[i + 1].astype(F32) + gate[i + 1] * both[:, width:]

    def norm(i):
        for row in (i, i + 1):
            att_norm[row] = lane_norm(first_pass[row])

    def project_bias(i):
        both = dot(w_bias_t[...], jnp.concatenate([att_norm[i], att_norm[i + 1]], axis=0), NT)
        for row in range(2):
            for head in range(HEADS):
                place = head * rows + i + row
                bias_held[place : place + 1, :] = both[head : head + 1, row * cols : (row + 1) * cols]

    pipeline(range(0, rows, 2), turn, update, norm, project_bias)
    rounded = bias_held[...].astype(BF16)
    for owner in range(bias.shape[0]):
        bias[owner] = rounded


def projector(att_norm, w_query, w_key, w_value, w_att_gate, query_t, key, value_t, gate_t):
    w_turned = jnp.concatenate([w[...].T for w in (w_query, w_value, w_att_gate)], axis=0)
    w_direct = twice(w_key[...])
    cols, width = att_norm.shape[1], w_query.shape[1]

    def project(i):
        keys = dot(side_by_side(att_norm, i), w_direct).astype(BF16)
        turned = dot(w_turned, jnp.concatenate([att_norm[i], att_norm[i + 1]], axis=0), NT)
        for row in range(2):
            key[i + row] = keys[:, row * width : (row + 1) * width]
            mine = turned[:, row * cols : (row + 1) * cols]
            query_t[i + row] = mine[:width].astype(BF16)
            value_t[i + row] = mine[width : 2 * width].astype(BF16)
            gate_t[i + row] = sigmoid(mine[2 * width :])

    return project


def project_kernel(*refs):
    pipeline(range(0, refs[0].shape[0], 2), projector(*refs))


def whole_kernel(att_norm, w_query, w_key, w_value, w_att_gate, *refs):
    given, projected, held = refs[:4], refs[4:8], refs[8:]
    project = projector(att_norm, w_query, w_key, w_value, w_att_gate, *projected)
    attend_kernel(*projected, *given, *held, before=(project,))


def attend_kernel(
    query_t,
    key,
    value_t,
    gate_t,
    first_pass,
    bias,
    w_att_out,
    out,
    bias_t,
    scores,
    peaks,
    weights,
    gated,
    done,
    sems,
    before=(),
):
    rows, width, cols = query_t.shape
    head_rows = bias.shape[1] // HEADS
    score_scale = LOG2_E / HEAD_DIM**0.5
    ones = jnp.ones((16, key.shape[1]), BF16)
    heads = [
        (slice(h * HEAD_DIM, (h + 1) * HEAD_DIM), slice(h * cols, (h + 1) * cols)) for h in range(HEADS)
    ]

    def score(i):
        for row in (i, i + 1):
            blocks = []
            for mine, _ in heads:
                above = jnp.zeros((mine.start, cols), BF16)
                below = jnp.zeros((width - mine.stop, cols), BF16)
                parts = [p for p in (above, query_t[row, mine, :], below) if p.shape[0]]
                blocks.append(jnp.concatenate(parts, axis=0))
            raw = dot(key[row], jnp.concatenate(blocks, axis=1))
            for _, span in heads:
                biased = raw[:, span] * score_scale + bias_t[:, span]
                scores[row % RING, :, span] = biased
                peaks[row % RING, :, span] = jnp.max(biased, axis=0, keepdims=True)

    def soften(i):
        for row in (i, i + 1):
            for _, span in heads:
                lowered = scores[row % RING, :, span] - peaks[row % RING, :, span]
                weights[row % RING, :, span] = jnp.exp2(lowered).astype(BF16)

    def collect(i):
        for row in (i, i + 1):
            for head in range(0, HEADS, 2):
                (first, left), (second, right) = heads[head : head + 2]
                values = jnp.concatenate([value_t[row, first.start : second.stop, :], ones], axis=0)
                summed = dot(values, weights[row % RING, :, left.start : right.stop])
                share = 1.0 / summed[2 * HEAD_DIM : 2 * HEAD_DIM + 1]
                for mine, there, lanes in (
                    (first, slice(0, HEAD_DIM), slice(0, cols)),
                    (second, slice(HEAD_DIM, 2 * HEAD_DIM), slice(cols, 2 * cols)),
                ):
                    attended = summed[there, lanes] * share[:, lanes] * gate_t[row, mine, :]
                    gated[row % RING, mine, :] = attended.astype(BF16)

    def finish(i):
        turned = jnp.concatenate([gated[i % RING].T, gated[(i + 1) % RING].T], axis=1)
        both = dot(turned, w_last)
        done[i] = (first_pass[i] + both[:, :width]).astype(BF16)
        done[i + 1] = (first_pass[i + 1] + both[:, width:]).astype(BF16)
        copy = pltpu.make_async_copy(done.at[pl.ds(i, 2)], out.at[pl.ds(i, 2)], sems.at[i // 2])
        copy.start()
        copies.append(copy)

    copies = []
    w_last = twice(w_att_out[...])
    for head, (_, span) in enumerate(heads):
        parts = [
            bias[slot("bias", owner, bias.shape[0])].astype(F32)[head * head_rows : (head + 1) * head_rows]
            for owner in range(bias.shape[0])
        ]
        bias_t[:, span] = jnp.concatenate(parts, axis=0).T * LOG2_E
    steps = [doubled(step) for step in (*before, score, soften, collect, finish)]
    pipeline(range(0, rows, 4), *steps)
    for copy in copies:
        copy.wait()


def call(kernel, outs, scratch, flops, *operands, fetched=0, sent=False):
    vmem = pl.BlockSpec(memory_space=pltpu.VMEM)
    far = pl.BlockSpec(memory_space=pltpu.HBM)
    shapes = [jax.ShapeDtypeStruct(shape, dtype) for shape, dtype in outs]
    moved = sum(o.size * o.dtype.itemsize for o in operands)
    operands = [
        pltpu.with_memory_space_constraint(o, pltpu.HBM) if n < fetched else o
        for n, o in enumerate(operands)
    ]
    got = pl.pallas_call(
        kernel,
        out_shape=shapes,
        in_specs=[far] * fetched + [vmem] * (len(operands) - fetched),
        out_specs=[far if sent else vmem] * len(shapes),
        scratch_shapes=[pltpu.VMEM(*s) if isinstance(s, tuple) else s for s in scratch],
        compiler_params=pltpu.CompilerParams(vmem_limit_bytes=48 * 2**20),
        cost_estimate=pl.CostEstimate(flops=flops, bytes_accessed=moved, transcendentals=0),
    )(*operands)
    return got if len(got) > 1 else got[0]


def body(
    pair_rep,
    w_left,
    w_left_gate,
    w_right,
    w_right_gate,
    w_tri_gate,
    w_tri_out,
    w_query,
    w_key,
    w_value,
    w_bias,
    w_att_gate,
    w_att_out,
):
    rows, cols, width = pair_rep.shape
    channels = w_left.shape[1]
    owners, col_parts = lax.axis_size("row"), lax.axis_size("col")
    own = channels // owners
    residues = owners * rows
    cells = rows * cols

    edges, gate, w_tri_out, w_query, w_key, w_value, w_att_gate, w_att_out, w_bias_t = call(
        edges_kernel,
        [
            ((owners, own * 2 * rows, cols), BF16),
            ((rows, cols, width), F32),
            *[(w.shape, BF16) for w in (w_tri_out, w_query, w_key, w_value, w_att_gate, w_att_out)],
            (w_bias.shape[::-1], BF16),
        ],
        [
            (pair_rep.shape, BF16),
            ((5, width, channels), BF16),
            (pair_rep.shape, BF16),
            ((cols // LANES, (channels + 1) * 2 * rows, LANES), F32),
            pltpu.SemaphoreType.DMA((13,)),
        ],
        10 * cells * width * channels,
        pair_rep,
        w_left,
        w_left_gate,
        w_right,
        w_right_gate,
        w_tri_gate,
        w_tri_out,
        w_query,
        w_key,
        w_value,
        w_att_gate,
        w_att_out,
        w_bias.T,
        fetched=13,
    )
    spread = swap("edges", edges)
    flops = 2 * own * residues * residues * cols
    if col_parts == 1:
        summed = call(
            functools.partial(triangle_kernel, rows),
            [((owners, own * rows, residues), BF16)],
            [],
            flops,
            spread,
        )
    else:
        partial_sums = call(
            functools.partial(partial_kernel, rows),
            [((own, residues, residues), F32)],
            [],
            flops,
            spread,
        )
        summed = lax.psum_scatter(partial_sums, "col", scatter_dimension=2, tiled=True).astype(BF16)
        summed = by_slot("triangle", summed.reshape(own, owners, rows, cols).swapaxes(0, 1))
        summed = summed.reshape(owners, own * rows, cols)
    returned = swap("triangle", summed)
    first_pass, att_norm, bias_copies = call(
        update_kernel,
        [
            ((rows, cols, width), F32),
            ((rows, cols, width), BF16),
            ((owners, HEADS * rows, cols), BF16),
        ],
        [
            ((cols // LANES, (channels + 1) * rows, LANES), F32),
            ((HEADS * rows, cols), F32),
            ((4, cols, channels), BF16),
        ],
        2 * cells * channels * width,
        returned,
        gate,
        pair_rep,
        w_tri_out,
        w_bias_t,
    )
    bias = swap("bias", bias_copies)
    projected = [
        ((rows, width, cols), BF16),
        ((rows, cols, width), BF16),
        ((rows, width, cols), BF16),
        ((rows, width, cols), F32),
    ]
    projecting = (att_norm, w_query, w_key, w_value, w_att_gate)
    residues = cols * col_parts
    out = [((rows, cols, width), BF16)]
    held = [
        ((residues, HEADS * cols), F32),
        ((RING, residues, HEADS * cols), F32),
        ((RING, 1, HEADS * cols), F32),
        ((RING, residues, HEADS * cols), BF16),
        ((RING, width, cols), BF16),
        ((rows, cols, width), BF16),
        pltpu.SemaphoreType.DMA((rows // 2,)),
    ]
    project_flops, attend_flops = 8 * cells * width * width, 4 * cells * residues * width
    if col_parts == 1:
        flops = project_flops + attend_flops
        given = (first_pass, bias, w_att_out)
        return call(whole_kernel, out, projected + held, flops, *projecting, *given, sent=True)
    query_t, key, value_t, gate_t = call(project_kernel, projected, [], project_flops, *projecting)
    bias = by_slot(
        "bias", lax.all_to_all(by_rank("bias", bias), "col", split_axis=0, concat_axis=2, tiled=True)
    )
    key = lax.all_gather(key, "col", axis=1, tiled=True)
    value_t = lax.all_gather(value_t, "col", axis=2, tiled=True)
    given = (query_t, key, value_t, gate_t, first_pass, bias, w_att_out)
    return call(attend_kernel, out, held, attend_flops, *given, sent=True)


def solution(mesh):
    in_specs = (P(("grp", "row"), "col", None),) + (P(),) * 12
    out_specs = P(("grp", "row"), "col", None)
    return jax.shard_map(body, mesh=mesh, in_specs=in_specs, out_specs=out_specs, check_vma=False)
```

```python
import functools
import math

import jax
import jax.numpy as jnp
import numpy as np
from jax import lax
from jax.experimental import pallas as pl
from jax.experimental.pallas import tpu as pltpu
from jax.sharding import PartitionSpec as P

HEADS = 4
HEAD_DIM = 32
LANES = 128
LOG2_E = 1.4426950408889634
F32 = jnp.float32
BF16 = jnp.bfloat16
NN = (((1,), (0,)), ((), ()))
NT = (((1,), (1,)), ((), ()))
TN = (((0,), (0,)), ((), ()))


def dot(left, right, dims=NN):
    return lax.dot_general(left, right, dims, preferred_element_type=F32)


def sigmoid(values):
    return 0.5 * jnp.tanh(0.5 * values) + 0.5


def twice(weight):
    zeros = jnp.zeros_like(weight)
    return jnp.concatenate(
        [jnp.concatenate([weight, zeros], axis=1), jnp.concatenate([zeros, weight], axis=1)], axis=0
    )


def listing(step, ranks):
    first, stride = ranks - 1 - ranks // 4, 5
    if step == "triangle":
        return [first] + [rank for rank in range(ranks - 1, -1, -1) if rank != first]
    assert math.gcd(stride, ranks) == 1
    return [(first + stride * n) % ranks for n in range(ranks)]


def slot(step, rank, ranks):
    return listing(step, ranks).index(rank)


def swap(step, blocks):
    return lax.all_to_all(
        blocks,
        "row",
        split_axis=0,
        concat_axis=0,
        axis_index_groups=[listing(step, blocks.shape[0])],
        tiled=True,
    )


def by_rank(step, blocks):
    return blocks[np.array([slot(step, r, blocks.shape[0]) for r in range(blocks.shape[0])])]


def by_slot(step, blocks):
    return blocks[np.array(listing(step, blocks.shape[0]))]


def lane_tiles(values):
    lanes = values.shape[1]
    return [(t, slice(t * LANES, (t + 1) * LANES)) for t in range(lanes // LANES)]


def lane_norm(values):
    centered = values - jnp.mean(values, axis=-1, keepdims=True)
    variance = jnp.mean(centered * centered, axis=-1, keepdims=True)
    return (centered * lax.rsqrt(variance + 1e-05)).astype(BF16)


def side_by_side(held, i):
    return jnp.concatenate([held[i], held[i + 1]], axis=1)


def pipeline(rows, *steps):
    for tick in range(len(rows) + len(steps) - 1):
        for late, step in reversed(list(enumerate(steps))):
            if 0 <= tick - late < len(rows):
                step(rows[tick - late])


def edges_kernel(*refs):
    given, (out, gate, *staged), (pair, weights, normed, held, sems) = refs[:13], refs[13:22], refs[22:]
    targets = [pair, *(weights.at[n] for n in range(5)), *staged]
    copies = [
        pltpu.make_async_copy(source, target, sems.at[n])
        for n, (source, target) in enumerate(zip(given, targets))
    ]
    for copy in copies:
        copy.start()
    for copy in copies[:6]:
        copy.wait()
    rows, width = pair.shape[0], pair.shape[2]
    channels = weights.shape[2]
    cols = pair.shape[1]
    turned = jnp.concatenate([weights[n].T for n in range(4)], axis=0)
    gate_weight = twice(weights[4])

    def norm(i):
        normed[i] = lane_norm(pair[i].astype(F32))
        normed[i + 1] = lane_norm(pair[i + 1].astype(F32))

    def project(i):
        both = dot(turned, jnp.concatenate([normed[i], normed[i + 1]], axis=0), NT)
        for side in range(2):
            base = 2 * side * channels
            act = sigmoid(both[base + channels : base + 2 * channels]) * both[base : base + channels]
            for tile, lanes in lane_tiles(act):
                row, part = divmod(tile, cols // LANES)
                place = pl.ds(side * rows + i + row, channels, stride=2 * rows)
                held[part, place, :] = act[:, lanes]
        opened = sigmoid(dot(side_by_side(normed, i), gate_weight))
        gate[i] = opened[:, :width]
        gate[i + 1] = opened[:, width:]

    pipeline(range(0, rows, 2), norm, project)
    owners, block = out.shape[0], out.shape[1]
    for owner in range(owners):
        for tile, lanes in lane_tiles(pair):
            out[slot("edges", owner, owners), :, lanes] = held[tile, owner * block : (owner + 1) * block, :].astype(BF16)
    for copy in copies[6:]:
        copy.wait()


def triangle_sides(edges, rows, channel):
    sides = [[], []]
    sources = edges.shape[0]
    for source in range(sources):
        block = edges[slot("edges", source, sources), channel * 2 * rows : (channel + 1) * 2 * rows, :].astype(F32)
        sides[0].append(block[:rows])
        sides[1].append(block[rows:])
    return [jnp.concatenate(side, axis=0).astype(BF16) for side in sides]


def triangle_kernel(rows, edges, out):
    for pair_of in range(0, out.shape[1] // rows, 2):
        products = [dot(*triangle_sides(edges, rows, pair_of + o), NT) for o in range(2)]
        owners = out.shape[0]
        for owner in range(owners):
            mine = slice(owner * rows, (owner + 1) * rows)
            out[slot("triangle", owner, owners), pair_of * rows : (pair_of + 2) * rows, :] = jnp.concatenate(
                [p[mine] for p in products], axis=0
            ).astype(BF16)


def partial_kernel(rows, edges, out):
    for channel in range(out.shape[0]):
        out[channel] = dot(*triangle_sides(edges, rows, channel), NT)


def update_kernel(
    returned, gate, pair, w_tri_out, w_bias_t, first_pass, att_norm, bias, held, bias_held, turned
):
    rows, cols, width = pair.shape
    owners, block = returned.shape[0], returned.shape[1]
    channels = owners * block // rows
    total = jnp.zeros((rows, cols), F32)
    for owner in range(owners):
        total += jnp.sum(returned[owner].astype(F32).reshape(block // rows, rows, cols), axis=0)
    average = total / channels
    square = jnp.zeros((rows, cols), F32)
    for owner in range(owners):
        centered = returned[slot("triangle", owner, owners)].astype(F32).reshape(block // rows, rows, cols) - average
        square += jnp.sum(centered * centered, axis=0)
        for tile, lanes in lane_tiles(pair):
            held[tile, owner * block : (owner + 1) * block, :] = centered.reshape(block, cols)[:, lanes]
    scale = lax.rsqrt(square / channels + 1e-05)

    weight = twice(w_tri_out[...])

    def turn(i):
        for row in (i, i + 1):
            tri_norm = jnp.concatenate(
                [held[tile, pl.ds(row, channels, stride=rows), :] for tile, _ in lane_tiles(pair)], axis=1
            )
            turned[row % 4] = (tri_norm * scale[row : row + 1]).astype(BF16).T

    def update(i):
        both = dot(side_by_side(turned, i % 4), weight)
        first_pass[i] = pair[i].astype(F32) + gate[i] * both[:, :width]
        first_pass[i + 1] = pair[i + 1].astype(F32) + gate[i + 1] * both[:, width:]

    def norm(i):
        for row in (i, i + 1):
            att_norm[row] = lane_norm(first_pass[row])

    def project_bias(i):
        both = dot(w_bias_t[...], jnp.concatenate([att_norm[i], att_norm[i + 1]], axis=0), NT)
        for row in range(2):
            for head in range(HEADS):
                place = head * rows + i + row
                bias_held[place : place + 1, :] = both[head : head + 1, row * cols : (row + 1) * cols]

    pipeline(range(0, rows, 2), turn, update, norm, project_bias)
    rounded = bias_held[...].astype(BF16)
    for owner in range(bias.shape[0]):
        bias[owner] = rounded


def projector(att_norm, w_query, w_key, w_value, w_att_gate, query_t, key, value_t, gate_t):
    w_turned = jnp.concatenate([w[...].T for w in (w_query, w_value, w_att_gate)], axis=0)
    w_direct = twice(w_key[...])
    cols, width = att_norm.shape[1], w_query.shape[1]

    def project(i):
        keys = dot(side_by_side(att_norm, i), w_direct).astype(BF16)
        turned = dot(w_turned, jnp.concatenate([att_norm[i], att_norm[i + 1]], axis=0), NT)
        for row in range(2):
            key[i + row] = keys[:, row * width : (row + 1) * width]
            mine = turned[:, row * cols : (row + 1) * cols]
            query_t[i + row] = mine[:width].astype(BF16)
            value_t[i + row] = mine[width : 2 * width].astype(BF16)
            gate_t[i + row] = sigmoid(mine[2 * width :])

    return project


def project_kernel(*refs):
    pipeline(range(0, refs[0].shape[0], 2), projector(*refs))


def whole_kernel(att_norm, w_query, w_key, w_value, w_att_gate, *refs):
    given, projected, held = refs[:4], refs[4:8], refs[8:]
    project = projector(att_norm, w_query, w_key, w_value, w_att_gate, *projected)
    attend_kernel(*projected, *given, *held, before=(project,))


def attend_kernel(
    query_t,
    key,
    value_t,
    gate_t,
    first_pass,
    bias,
    w_att_out,
    out,
    bias_t,
    scores,
    peaks,
    weights,
    gated,
    done,
    sems,
    before=(),
):
    rows, width, cols = query_t.shape
    head_rows = bias.shape[1] // HEADS
    score_scale = LOG2_E / HEAD_DIM**0.5
    ones = jnp.ones((16, key.shape[1]), BF16)
    heads = [
        (slice(h * HEAD_DIM, (h + 1) * HEAD_DIM), slice(h * cols, (h + 1) * cols)) for h in range(HEADS)
    ]

    def score(i):
        for row in (i, i + 1):
            blocks = []
            for mine, _ in heads:
                above = jnp.zeros((mine.start, cols), BF16)
                below = jnp.zeros((width - mine.stop, cols), BF16)
                parts = [p for p in (above, query_t[row, mine, :], below) if p.shape[0]]
                blocks.append(jnp.concatenate(parts, axis=0))
            raw = dot(key[row], jnp.concatenate(blocks, axis=1))
            for _, span in heads:
                biased = raw[:, span] * score_scale + bias_t[:, span]
                scores[row % 4, :, span] = biased
                peaks[row % 4, :, span] = jnp.max(biased, axis=0, keepdims=True)

    def soften(i):
        for row in (i, i + 1):
            for _, span in heads:
                lowered = scores[row % 4, :, span] - peaks[row % 4, :, span]
                weights[row % 4, :, span] = jnp.exp2(lowered).astype(BF16)

    def collect(i):
        for row in (i, i + 1):
            for head in range(0, HEADS, 2):
                (first, left), (second, right) = heads[head : head + 2]
                values = jnp.concatenate([value_t[row, first.start : second.stop, :], ones], axis=0)
                summed = dot(values, weights[row % 4, :, left.start : right.stop])
                share = 1.0 / summed[2 * HEAD_DIM : 2 * HEAD_DIM + 1]
                for mine, there, lanes in (
                    (first, slice(0, HEAD_DIM), slice(0, cols)),
                    (second, slice(HEAD_DIM, 2 * HEAD_DIM), slice(cols, 2 * cols)),
                ):
                    attended = summed[there, lanes] * share[:, lanes] * gate_t[row, mine, :]
                    gated[row % 4, mine, :] = attended.astype(BF16)

    def finish(i):
        turned = jnp.concatenate([gated[i % 4].T, gated[(i + 1) % 4].T], axis=1)
        both = dot(turned, w_last)
        done[i] = (first_pass[i] + both[:, :width]).astype(BF16)
        done[i + 1] = (first_pass[i + 1] + both[:, width:]).astype(BF16)
        copy = pltpu.make_async_copy(done.at[pl.ds(i, 2)], out.at[pl.ds(i, 2)], sems.at[i // 2])
        copy.start()
        copies.append(copy)

    copies = []
    w_last = twice(w_att_out[...])
    for head, (_, span) in enumerate(heads):
        parts = [
            bias[slot("bias", owner, bias.shape[0])].astype(F32)[head * head_rows : (head + 1) * head_rows]
            for owner in range(bias.shape[0])
        ]
        bias_t[:, span] = jnp.concatenate(parts, axis=0).T * LOG2_E
    pipeline(range(0, rows, 2), *before, score, soften, collect, finish)
    for copy in copies:
        copy.wait()


def call(kernel, outs, scratch, flops, *operands, fetched=0, sent=False):
    vmem = pl.BlockSpec(memory_space=pltpu.VMEM)
    far = pl.BlockSpec(memory_space=pltpu.HBM)
    shapes = [jax.ShapeDtypeStruct(shape, dtype) for shape, dtype in outs]
    moved = sum(o.size * o.dtype.itemsize for o in operands)
    operands = [
        pltpu.with_memory_space_constraint(o, pltpu.HBM) if n < fetched else o
        for n, o in enumerate(operands)
    ]
    got = pl.pallas_call(
        kernel,
        out_shape=shapes,
        in_specs=[far] * fetched + [vmem] * (len(operands) - fetched),
        out_specs=[far if sent else vmem] * len(shapes),
        scratch_shapes=[pltpu.VMEM(*s) if isinstance(s, tuple) else s for s in scratch],
        compiler_params=pltpu.CompilerParams(vmem_limit_bytes=48 * 2**20),
        cost_estimate=pl.CostEstimate(flops=flops, bytes_accessed=moved, transcendentals=0),
    )(*operands)
    return got if len(got) > 1 else got[0]


def body(
    pair_rep,
    w_left,
    w_left_gate,
    w_right,
    w_right_gate,
    w_tri_gate,
    w_tri_out,
    w_query,
    w_key,
    w_value,
    w_bias,
    w_att_gate,
    w_att_out,
):
    rows, cols, width = pair_rep.shape
    channels = w_left.shape[1]
    owners, col_parts = lax.axis_size("row"), lax.axis_size("col")
    own = channels // owners
    residues = owners * rows
    cells = rows * cols

    edges, gate, w_tri_out, w_query, w_key, w_value, w_att_gate, w_att_out, w_bias_t = call(
        edges_kernel,
        [
            ((owners, own * 2 * rows, cols), BF16),
            ((rows, cols, width), F32),
            *[(w.shape, BF16) for w in (w_tri_out, w_query, w_key, w_value, w_att_gate, w_att_out)],
            (w_bias.shape[::-1], BF16),
        ],
        [
            (pair_rep.shape, BF16),
            ((5, width, channels), BF16),
            (pair_rep.shape, BF16),
            ((cols // LANES, (channels + 1) * 2 * rows, LANES), F32),
            pltpu.SemaphoreType.DMA((13,)),
        ],
        10 * cells * width * channels,
        pair_rep,
        w_left,
        w_left_gate,
        w_right,
        w_right_gate,
        w_tri_gate,
        w_tri_out,
        w_query,
        w_key,
        w_value,
        w_att_gate,
        w_att_out,
        w_bias.T,
        fetched=13,
    )
    spread = swap("edges", edges)
    flops = 2 * own * residues * residues * cols
    if col_parts == 1:
        summed = call(
            functools.partial(triangle_kernel, rows),
            [((owners, own * rows, residues), BF16)],
            [],
            flops,
            spread,
        )
    else:
        partial_sums = call(
            functools.partial(partial_kernel, rows),
            [((own, residues, residues), F32)],
            [],
            flops,
            spread,
        )
        summed = lax.psum_scatter(partial_sums, "col", scatter_dimension=2, tiled=True).astype(BF16)
        summed = by_slot("triangle", summed.reshape(own, owners, rows, cols).swapaxes(0, 1))
        summed = summed.reshape(owners, own * rows, cols)
    returned = swap("triangle", summed)
    first_pass, att_norm, bias_copies = call(
        update_kernel,
        [
            ((rows, cols, width), F32),
            ((rows, cols, width), BF16),
            ((owners, HEADS * rows, cols), BF16),
        ],
        [
            ((cols // LANES, (channels + 1) * rows, LANES), F32),
            ((HEADS * rows, cols), F32),
            ((4, cols, channels), BF16),
        ],
        2 * cells * channels * width,
        returned,
        gate,
        pair_rep,
        w_tri_out,
        w_bias_t,
    )
    bias = swap("bias", bias_copies)
    projected = [
        ((rows, width, cols), BF16),
        ((rows, cols, width), BF16),
        ((rows, width, cols), BF16),
        ((rows, width, cols), F32),
    ]
    projecting = (att_norm, w_query, w_key, w_value, w_att_gate)
    residues = cols * col_parts
    out = [((rows, cols, width), BF16)]
    held = [
        ((residues, HEADS * cols), F32),
        ((4, residues, HEADS * cols), F32),
        ((4, 1, HEADS * cols), F32),
        ((4, residues, HEADS * cols), BF16),
        ((4, width, cols), BF16),
        ((rows, cols, width), BF16),
        pltpu.SemaphoreType.DMA((rows // 2,)),
    ]
    project_flops, attend_flops = 8 * cells * width * width, 4 * cells * residues * width
    if col_parts == 1:
        flops = project_flops + attend_flops
        given = (first_pass, bias, w_att_out)
        return call(whole_kernel, out, projected + held, flops, *projecting, *given, sent=True)
    query_t, key, value_t, gate_t = call(project_kernel, projected, [], project_flops, *projecting)
    bias = by_slot(
        "bias", lax.all_to_all(by_rank("bias", bias), "col", split_axis=0, concat_axis=2, tiled=True)
    )
    key = lax.all_gather(key, "col", axis=1, tiled=True)
    value_t = lax.all_gather(value_t, "col", axis=2, tiled=True)
    given = (query_t, key, value_t, gate_t, first_pass, bias, w_att_out)
    return call(attend_kernel, out, held, attend_flops, *given, sent=True)


def solution(mesh):
    in_specs = (P(("grp", "row"), "col", None),) + (P(),) * 12
    out_specs = P(("grp", "row"), "col", None)
    return jax.shard_map(body, mesh=mesh, in_specs=in_specs, out_specs=out_specs, check_vma=False)
```

```python
import functools
import math

import jax
import jax.numpy as jnp
import numpy as np
from jax import lax
from jax.experimental import pallas as pl
from jax.experimental.pallas import tpu as pltpu
from jax.sharding import PartitionSpec as P

HEADS = 4
HEAD_DIM = 32
LANES = 128
LOG2_E = 1.4426950408889634
F32 = jnp.float32
BF16 = jnp.bfloat16
NN = (((1,), (0,)), ((), ()))
NT = (((1,), (1,)), ((), ()))
TN = (((0,), (0,)), ((), ()))


def dot(left, right, dims=NN):
    return lax.dot_general(left, right, dims, preferred_element_type=F32)


def sigmoid(values):
    return 0.5 * jnp.tanh(0.5 * values) + 0.5


def twice(weight):
    zeros = jnp.zeros_like(weight)
    return jnp.concatenate(
        [jnp.concatenate([weight, zeros], axis=1), jnp.concatenate([zeros, weight], axis=1)], axis=0
    )


def listing(step, ranks):
    first, stride = ranks - 1 - ranks // 4, 5
    if step == "triangle":
        return [first] + [rank for rank in range(ranks - 1, -1, -1) if rank != first]
    assert math.gcd(stride, ranks) == 1
    return [(first + stride * n) % ranks for n in range(ranks)]


def slot(step, rank, ranks):
    return listing(step, ranks).index(rank)


def swap(step, blocks):
    return lax.all_to_all(
        blocks,
        "row",
        split_axis=0,
        concat_axis=0,
        axis_index_groups=[listing(step, blocks.shape[0])],
        tiled=True,
    )


def by_rank(step, blocks):
    return blocks[np.array([slot(step, r, blocks.shape[0]) for r in range(blocks.shape[0])])]


def by_slot(step, blocks):
    return blocks[np.array(listing(step, blocks.shape[0]))]


def lane_tiles(values):
    lanes = values.shape[1]
    return [(t, slice(t * LANES, (t + 1) * LANES)) for t in range(lanes // LANES)]


def lane_norm(values):
    centered = values - jnp.mean(values, axis=-1, keepdims=True)
    variance = jnp.mean(centered * centered, axis=-1, keepdims=True)
    return (centered * lax.rsqrt(variance + 1e-05)).astype(BF16)


def side_by_side(held, i):
    return jnp.concatenate([held[i], held[i + 1]], axis=1)


def pipeline(rows, *steps):
    for tick in range(len(rows) + len(steps) - 1):
        for late, step in enumerate(steps):
            if 0 <= tick - late < len(rows):
                step(rows[tick - late])


def edges_kernel(*refs):
    given, (out, gate, *staged), (pair, weights, normed, held, sems) = refs[:13], refs[13:22], refs[22:]
    targets = [pair, *(weights.at[n] for n in range(5)), *staged]
    copies = [
        pltpu.make_async_copy(source, target, sems.at[n])
        for n, (source, target) in enumerate(zip(given, targets))
    ]
    for copy in copies:
        copy.start()
    for copy in copies[:6]:
        copy.wait()
    rows, width = pair.shape[0], pair.shape[2]
    channels = weights.shape[2]
    cols = pair.shape[1]
    turned = jnp.concatenate([weights[n].T for n in range(4)], axis=0)
    gate_weight = twice(weights[4])

    def norm(i):
        normed[i] = lane_norm(pair[i].astype(F32))
        normed[i + 1] = lane_norm(pair[i + 1].astype(F32))

    def project(i):
        both = dot(turned, jnp.concatenate([normed[i], normed[i + 1]], axis=0), NT)
        gates = dot(side_by_side(normed, i), gate_weight)
        for side in range(2):
            base = 2 * side * channels
            act = sigmoid(both[base + channels : base + 2 * channels]) * both[base : base + channels]
            for tile, lanes in lane_tiles(act):
                row, part = divmod(tile, cols // LANES)
                place = pl.ds(side * rows + i + row, channels, stride=2 * rows)
                held[part, place, :] = act[:, lanes]
        opened = sigmoid(gates)
        gate[i] = opened[:, :width]
        gate[i + 1] = opened[:, width:]

    pipeline(range(0, rows, 2), norm, project)
    owners, block = out.shape[0], out.shape[1]
    for owner in range(owners):
        for tile, lanes in lane_tiles(pair):
            out[slot("edges", owner, owners), :, lanes] = held[tile, owner * block : (owner + 1) * block, :].astype(BF16)
    for copy in copies[6:]:
        copy.wait()


def triangle_sides(edges, rows, channel):
    sides = [[], []]
    sources = edges.shape[0]
    for source in range(sources):
        block = edges[slot("edges", source, sources), channel * 2 * rows : (channel + 1) * 2 * rows, :].astype(F32)
        sides[0].append(block[:rows])
        sides[1].append(block[rows:])
    return [jnp.concatenate(side, axis=0).astype(BF16) for side in sides]


def triangle_kernel(rows, edges, out):
    for pair_of in range(0, out.shape[1] // rows, 2):
        products = [dot(*triangle_sides(edges, rows, pair_of + o), NT) for o in range(2)]
        owners = out.shape[0]
        for owner in range(owners):
            mine = slice(owner * rows, (owner + 1) * rows)
            out[slot("triangle", owner, owners), pair_of * rows : (pair_of + 2) * rows, :] = jnp.concatenate(
                [p[mine] for p in products], axis=0
            ).astype(BF16)


def partial_kernel(rows, edges, out):
    for channel in range(out.shape[0]):
        out[channel] = dot(*triangle_sides(edges, rows, channel), NT)


def update_kernel(
    returned, gate, pair, w_tri_out, w_bias_t, first_pass, att_norm, bias, held, bias_held, turned
):
    rows, cols, width = pair.shape
    owners, block = returned.shape[0], returned.shape[1]
    channels = owners * block // rows
    total = jnp.zeros((rows, cols), F32)
    for owner in range(owners):
        total += jnp.sum(returned[owner].astype(F32).reshape(block // rows, rows, cols), axis=0)
    average = total / channels
    square = jnp.zeros((rows, cols), F32)
    for owner in range(owners):
        centered = returned[slot("triangle", owner, owners)].astype(F32).reshape(block // rows, rows, cols) - average
        square += jnp.sum(centered * centered, axis=0)
        for tile, lanes in lane_tiles(pair):
            held[tile, owner * block : (owner + 1) * block, :] = centered.reshape(block, cols)[:, lanes]
    scale = lax.rsqrt(square / channels + 1e-05)

    weight = twice(w_tri_out[...])

    def turn(i):
        for row in (i, i + 1):
            tri_norm = jnp.concatenate(
                [held[tile, pl.ds(row, channels, stride=rows), :] for tile, _ in lane_tiles(pair)], axis=1
            )
            turned[row % 4] = (tri_norm * scale[row : row + 1]).astype(BF16).T

    def update(i):
        both = dot(side_by_side(turned, i % 4), weight)
        first_pass[i] = pair[i].astype(F32) + gate[i] * both[:, :width]
        first_pass[i + 1] = pair[i + 1].astype(F32) + gate[i + 1] * both[:, width:]

    def norm(i):
        for row in (i, i + 1):
            att_norm[row] = lane_norm(first_pass[row])

    def project_bias(i):
        both = dot(w_bias_t[...], jnp.concatenate([att_norm[i], att_norm[i + 1]], axis=0), NT)
        for row in range(2):
            for head in range(HEADS):
                place = head * rows + i + row
                bias_held[place : place + 1, :] = both[head : head + 1, row * cols : (row + 1) * cols]

    pipeline(range(0, rows, 2), turn, update, norm, project_bias)
    rounded = bias_held[...].astype(BF16)
    for owner in range(bias.shape[0]):
        bias[owner] = rounded


def projector(att_norm, w_query, w_key, w_value, w_att_gate, query_t, key, value_t, gate_t):
    w_turned = jnp.concatenate([w[...].T for w in (w_query, w_value, w_att_gate)], axis=0)
    w_direct = twice(w_key[...])
    cols, width = att_norm.shape[1], w_query.shape[1]

    def project(i):
        keys = dot(side_by_side(att_norm, i), w_direct).astype(BF16)
        turned = dot(w_turned, jnp.concatenate([att_norm[i], att_norm[i + 1]], axis=0), NT)
        for row in range(2):
            key[i + row] = keys[:, row * width : (row + 1) * width]
            mine = turned[:, row * cols : (row + 1) * cols]
            query_t[i + row] = mine[:width].astype(BF16)
            value_t[i + row] = mine[width : 2 * width].astype(BF16)
            gate_t[i + row] = sigmoid(mine[2 * width :])

    return project


def project_kernel(*refs):
    pipeline(range(0, refs[0].shape[0], 2), projector(*refs))


def whole_kernel(att_norm, w_query, w_key, w_value, w_att_gate, *refs):
    given, projected, held = refs[:4], refs[4:8], refs[8:]
    project = projector(att_norm, w_query, w_key, w_value, w_att_gate, *projected)
    attend_kernel(*projected, *given, *held, before=(project,))


def attend_kernel(
    query_t,
    key,
    value_t,
    gate_t,
    first_pass,
    bias,
    w_att_out,
    out,
    bias_t,
    scores,
    peaks,
    weights,
    gated,
    done,
    sems,
    before=(),
):
    rows, width, cols = query_t.shape
    head_rows = bias.shape[1] // HEADS
    score_scale = LOG2_E / HEAD_DIM**0.5
    ones = jnp.ones((16, key.shape[1]), BF16)
    heads = [
        (slice(h * HEAD_DIM, (h + 1) * HEAD_DIM), slice(h * cols, (h + 1) * cols)) for h in range(HEADS)
    ]

    def score(i):
        for row in (i, i + 1):
            blocks = []
            for mine, _ in heads:
                above = jnp.zeros((mine.start, cols), BF16)
                below = jnp.zeros((width - mine.stop, cols), BF16)
                parts = [p for p in (above, query_t[row, mine, :], below) if p.shape[0]]
                blocks.append(jnp.concatenate(parts, axis=0))
            raw = dot(key[row], jnp.concatenate(blocks, axis=1))
            for _, span in heads:
                biased = raw[:, span] * score_scale + bias_t[:, span]
                scores[row % 4, :, span] = biased
                peaks[row % 4, :, span] = jnp.max(biased, axis=0, keepdims=True)

    def soften(i):
        for row in (i, i + 1):
            for _, span in heads:
                lowered = scores[row % 4, :, span] - peaks[row % 4, :, span]
                weights[row % 4, :, span] = jnp.exp2(lowered).astype(BF16)

    def collect(i):
        for row in (i, i + 1):
            for head in range(0, HEADS, 2):
                (first, left), (second, right) = heads[head : head + 2]
                values = jnp.concatenate([value_t[row, first.start : second.stop, :], ones], axis=0)
                summed = dot(values, weights[row % 4, :, left.start : right.stop])
                share = 1.0 / summed[2 * HEAD_DIM : 2 * HEAD_DIM + 1]
                for mine, there, lanes in (
                    (first, slice(0, HEAD_DIM), slice(0, cols)),
                    (second, slice(HEAD_DIM, 2 * HEAD_DIM), slice(cols, 2 * cols)),
                ):
                    attended = summed[there, lanes] * share[:, lanes] * gate_t[row, mine, :]
                    gated[row % 4, mine, :] = attended.astype(BF16)

    def finish(i):
        turned = jnp.concatenate([gated[i % 4].T, gated[(i + 1) % 4].T], axis=1)
        both = dot(turned, w_last)
        done[i] = (first_pass[i] + both[:, :width]).astype(BF16)
        done[i + 1] = (first_pass[i + 1] + both[:, width:]).astype(BF16)
        copy = pltpu.make_async_copy(done.at[pl.ds(i, 2)], out.at[pl.ds(i, 2)], sems.at[i // 2])
        copy.start()
        copies.append(copy)

    copies = []
    w_last = twice(w_att_out[...])
    for head, (_, span) in enumerate(heads):
        parts = [
            bias[slot("bias", owner, bias.shape[0])].astype(F32)[head * head_rows : (head + 1) * head_rows]
            for owner in range(bias.shape[0])
        ]
        bias_t[:, span] = jnp.concatenate(parts, axis=0).T * LOG2_E
    pipeline(range(0, rows, 2), *before, score, soften, collect, finish)
    for copy in copies:
        copy.wait()


def call(kernel, outs, scratch, flops, *operands, fetched=0, sent=False):
    vmem = pl.BlockSpec(memory_space=pltpu.VMEM)
    far = pl.BlockSpec(memory_space=pltpu.HBM)
    shapes = [jax.ShapeDtypeStruct(shape, dtype) for shape, dtype in outs]
    moved = sum(o.size * o.dtype.itemsize for o in operands)
    operands = [
        pltpu.with_memory_space_constraint(o, pltpu.HBM) if n < fetched else o
        for n, o in enumerate(operands)
    ]
    got = pl.pallas_call(
        kernel,
        out_shape=shapes,
        in_specs=[far] * fetched + [vmem] * (len(operands) - fetched),
        out_specs=[far if sent else vmem] * len(shapes),
        scratch_shapes=[pltpu.VMEM(*s) if isinstance(s, tuple) else s for s in scratch],
        compiler_params=pltpu.CompilerParams(vmem_limit_bytes=48 * 2**20),
        cost_estimate=pl.CostEstimate(flops=flops, bytes_accessed=moved, transcendentals=0),
    )(*operands)
    return got if len(got) > 1 else got[0]


def body(
    pair_rep,
    w_left,
    w_left_gate,
    w_right,
    w_right_gate,
    w_tri_gate,
    w_tri_out,
    w_query,
    w_key,
    w_value,
    w_bias,
    w_att_gate,
    w_att_out,
):
    rows, cols, width = pair_rep.shape
    channels = w_left.shape[1]
    owners, col_parts = lax.axis_size("row"), lax.axis_size("col")
    own = channels // owners
    residues = owners * rows
    cells = rows * cols

    edges, gate, w_tri_out, w_query, w_key, w_value, w_att_gate, w_att_out, w_bias_t = call(
        edges_kernel,
        [
            ((owners, own * 2 * rows, cols), BF16),
            ((rows, cols, width), F32),
            *[(w.shape, BF16) for w in (w_tri_out, w_query, w_key, w_value, w_att_gate, w_att_out)],
            (w_bias.shape[::-1], BF16),
        ],
        [
            (pair_rep.shape, BF16),
            ((5, width, channels), BF16),
            (pair_rep.shape, BF16),
            ((cols // LANES, (channels + 1) * 2 * rows, LANES), F32),
            pltpu.SemaphoreType.DMA((13,)),
        ],
        10 * cells * width * channels,
        pair_rep,
        w_left,
        w_left_gate,
        w_right,
        w_right_gate,
        w_tri_gate,
        w_tri_out,
        w_query,
        w_key,
        w_value,
        w_att_gate,
        w_att_out,
        w_bias.T,
        fetched=13,
    )
    spread = swap("edges", edges)
    flops = 2 * own * residues * residues * cols
    if col_parts == 1:
        summed = call(
            functools.partial(triangle_kernel, rows),
            [((owners, own * rows, residues), BF16)],
            [],
            flops,
            spread,
        )
    else:
        partial_sums = call(
            functools.partial(partial_kernel, rows),
            [((own, residues, residues), F32)],
            [],
            flops,
            spread,
        )
        summed = lax.psum_scatter(partial_sums, "col", scatter_dimension=2, tiled=True).astype(BF16)
        summed = by_slot("triangle", summed.reshape(own, owners, rows, cols).swapaxes(0, 1))
        summed = summed.reshape(owners, own * rows, cols)
    returned = swap("triangle", summed)
    first_pass, att_norm, bias_copies = call(
        update_kernel,
        [
            ((rows, cols, width), F32),
            ((rows, cols, width), BF16),
            ((owners, HEADS * rows, cols), BF16),
        ],
        [
            ((cols // LANES, (channels + 1) * rows, LANES), F32),
            ((HEADS * rows, cols), F32),
            ((4, cols, channels), BF16),
        ],
        2 * cells * channels * width,
        returned,
        gate,
        pair_rep,
        w_tri_out,
        w_bias_t,
    )
    bias = swap("bias", bias_copies)
    projected = [
        ((rows, width, cols), BF16),
        ((rows, cols, width), BF16),
        ((rows, width, cols), BF16),
        ((rows, width, cols), F32),
    ]
    projecting = (att_norm, w_query, w_key, w_value, w_att_gate)
    residues = cols * col_parts
    out = [((rows, cols, width), BF16)]
    held = [
        ((residues, HEADS * cols), F32),
        ((4, residues, HEADS * cols), F32),
        ((4, 1, HEADS * cols), F32),
        ((4, residues, HEADS * cols), BF16),
        ((4, width, cols), BF16),
        ((rows, cols, width), BF16),
        pltpu.SemaphoreType.DMA((rows // 2,)),
    ]
    project_flops, attend_flops = 8 * cells * width * width, 4 * cells * residues * width
    if col_parts == 1:
        flops = project_flops + attend_flops
        given = (first_pass, bias, w_att_out)
        return call(whole_kernel, out, projected + held, flops, *projecting, *given, sent=True)
    query_t, key, value_t, gate_t = call(project_kernel, projected, [], project_flops, *projecting)
    bias = by_slot(
        "bias", lax.all_to_all(by_rank("bias", bias), "col", split_axis=0, concat_axis=2, tiled=True)
    )
    key = lax.all_gather(key, "col", axis=1, tiled=True)
    value_t = lax.all_gather(value_t, "col", axis=2, tiled=True)
    given = (query_t, key, value_t, gate_t, first_pass, bias, w_att_out)
    return call(attend_kernel, out, held, attend_flops, *given, sent=True)


def solution(mesh):
    in_specs = (P(("grp", "row"), "col", None),) + (P(),) * 12
    out_specs = P(("grp", "row"), "col", None)
    return jax.shard_map(body, mesh=mesh, in_specs=in_specs, out_specs=out_specs, check_vma=False)
```

```python
import functools
import math

import jax
import jax.numpy as jnp
import numpy as np
from jax import lax
from jax.experimental import pallas as pl
from jax.experimental.pallas import tpu as pltpu
from jax.sharding import PartitionSpec as P

HEADS = 4
HEAD_DIM = 32
LANES = 128
LOG2_E = 1.4426950408889634
F32 = jnp.float32
BF16 = jnp.bfloat16
NN = (((1,), (0,)), ((), ()))
NT = (((1,), (1,)), ((), ()))
TN = (((0,), (0,)), ((), ()))


def dot(left, right, dims=NN):
    return lax.dot_general(left, right, dims, preferred_element_type=F32)


def sigmoid(values):
    return 0.5 * jnp.tanh(0.5 * values) + 0.5


def twice(weight):
    zeros = jnp.zeros_like(weight)
    return jnp.concatenate(
        [jnp.concatenate([weight, zeros], axis=1), jnp.concatenate([zeros, weight], axis=1)], axis=0
    )


def listing(step, ranks):
    first, stride = ranks - 1 - ranks // 4, 5
    if step == "triangle":
        return [first] + [rank for rank in range(ranks - 1, -1, -1) if rank != first]
    assert math.gcd(stride, ranks) == 1
    return [(first + stride * n) % ranks for n in range(ranks)]


def slot(step, rank, ranks):
    return listing(step, ranks).index(rank)


def swap(step, blocks):
    return lax.all_to_all(
        blocks,
        "row",
        split_axis=0,
        concat_axis=0,
        axis_index_groups=[listing(step, blocks.shape[0])],
        tiled=True,
    )


def by_rank(step, blocks):
    return blocks[np.array([slot(step, r, blocks.shape[0]) for r in range(blocks.shape[0])])]


def by_slot(step, blocks):
    return blocks[np.array(listing(step, blocks.shape[0]))]


def lane_tiles(values):
    lanes = values.shape[1]
    return [(t, slice(t * LANES, (t + 1) * LANES)) for t in range(lanes // LANES)]


def lane_norm(values):
    centered = values - jnp.mean(values, axis=-1, keepdims=True)
    variance = jnp.mean(centered * centered, axis=-1, keepdims=True)
    return (centered * lax.rsqrt(variance + 1e-05)).astype(BF16)


def side_by_side(held, i):
    return jnp.concatenate([held[i], held[i + 1]], axis=1)


def pipeline(rows, *steps):
    for tick in range(len(rows) + len(steps) - 1):
        for late, step in enumerate(steps):
            if 0 <= tick - late < len(rows):
                step(rows[tick - late])


def edges_kernel(*refs):
    given, (out, gate, *staged), (pair, weights, normed, held, sems) = refs[:13], refs[13:22], refs[22:]
    targets = [pair, *(weights.at[n] for n in range(5)), *staged]
    copies = [
        pltpu.make_async_copy(source, target, sems.at[n])
        for n, (source, target) in enumerate(zip(given, targets))
    ]
    for copy in copies[:6]:
        copy.start()
    for copy in copies[:6]:
        copy.wait()
    for copy in copies[6:]:
        copy.start()
    rows, width = pair.shape[0], pair.shape[2]
    channels = weights.shape[2]
    cols = pair.shape[1]
    turned = jnp.concatenate([weights[n].T for n in range(4)], axis=0)
    gate_weight = twice(weights[4])

    def norm(i):
        normed[i] = lane_norm(pair[i].astype(F32))
        normed[i + 1] = lane_norm(pair[i + 1].astype(F32))

    def project(i):
        both = dot(turned, jnp.concatenate([normed[i], normed[i + 1]], axis=0), NT)
        gates = dot(side_by_side(normed, i), gate_weight)
        for side in range(2):
            base = 2 * side * channels
            act = sigmoid(both[base + channels : base + 2 * channels]) * both[base : base + channels]
            for tile, lanes in lane_tiles(act):
                row, part = divmod(tile, cols // LANES)
                place = pl.ds(side * rows + i + row, channels, stride=2 * rows)
                held[part, place, :] = act[:, lanes]
        opened = sigmoid(gates)
        gate[i] = opened[:, :width]
        gate[i + 1] = opened[:, width:]

    pipeline(range(0, rows, 2), norm, project)
    owners, block = out.shape[0], out.shape[1]
    for owner in range(owners):
        for tile, lanes in lane_tiles(pair):
            out[slot("edges", owner, owners), :, lanes] = held[tile, owner * block : (owner + 1) * block, :].astype(BF16)
    for copy in copies[6:]:
        copy.wait()


def triangle_sides(edges, rows, channel):
    sides = [[], []]
    sources = edges.shape[0]
    for source in range(sources):
        block = edges[slot("edges", source, sources), channel * 2 * rows : (channel + 1) * 2 * rows, :].astype(F32)
        sides[0].append(block[:rows])
        sides[1].append(block[rows:])
    return [jnp.concatenate(side, axis=0).astype(BF16) for side in sides]


def triangle_kernel(rows, edges, out):
    for pair_of in range(0, out.shape[1] // rows, 2):
        products = [dot(*triangle_sides(edges, rows, pair_of + o), NT) for o in range(2)]
        owners = out.shape[0]
        for owner in range(owners):
            mine = slice(owner * rows, (owner + 1) * rows)
            out[slot("triangle", owner, owners), pair_of * rows : (pair_of + 2) * rows, :] = jnp.concatenate(
                [p[mine] for p in products], axis=0
            ).astype(BF16)


def partial_kernel(rows, edges, out):
    for channel in range(out.shape[0]):
        out[channel] = dot(*triangle_sides(edges, rows, channel), NT)


def update_kernel(
    returned, gate, pair, w_tri_out, w_bias_t, first_pass, att_norm, bias, held, bias_held, turned
):
    rows, cols, width = pair.shape
    owners, block = returned.shape[0], returned.shape[1]
    channels = owners * block // rows
    total = jnp.zeros((rows, cols), F32)
    for owner in range(owners):
        total += jnp.sum(returned[owner].astype(F32).reshape(block // rows, rows, cols), axis=0)
    average = total / channels
    square = jnp.zeros((rows, cols), F32)
    for owner in range(owners):
        centered = returned[slot("triangle", owner, owners)].astype(F32).reshape(block // rows, rows, cols) - average
        square += jnp.sum(centered * centered, axis=0)
        for tile, lanes in lane_tiles(pair):
            held[tile, owner * block : (owner + 1) * block, :] = centered.reshape(block, cols)[:, lanes]
    scale = lax.rsqrt(square / channels + 1e-05)

    weight = twice(w_tri_out[...])

    def turn(i):
        for row in (i, i + 1):
            tri_norm = jnp.concatenate(
                [held[tile, pl.ds(row, channels, stride=rows), :] for tile, _ in lane_tiles(pair)], axis=1
            )
            turned[row % 4] = (tri_norm * scale[row : row + 1]).astype(BF16).T

    def update(i):
        both = dot(side_by_side(turned, i % 4), weight)
        first_pass[i] = pair[i].astype(F32) + gate[i] * both[:, :width]
        first_pass[i + 1] = pair[i + 1].astype(F32) + gate[i + 1] * both[:, width:]

    def norm(i):
        for row in (i, i + 1):
            att_norm[row] = lane_norm(first_pass[row])

    def project_bias(i):
        both = dot(w_bias_t[...], jnp.concatenate([att_norm[i], att_norm[i + 1]], axis=0), NT)
        for row in range(2):
            for head in range(HEADS):
                place = head * rows + i + row
                bias_held[place : place + 1, :] = both[head : head + 1, row * cols : (row + 1) * cols]

    pipeline(range(0, rows, 2), turn, update, norm, project_bias)
    rounded = bias_held[...].astype(BF16)
    for owner in range(bias.shape[0]):
        bias[owner] = rounded


def projector(att_norm, w_query, w_key, w_value, w_att_gate, query_t, key, value_t, gate_t):
    w_turned = jnp.concatenate([w[...].T for w in (w_query, w_value, w_att_gate)], axis=0)
    w_direct = twice(w_key[...])
    cols, width = att_norm.shape[1], w_query.shape[1]

    def project(i):
        keys = dot(side_by_side(att_norm, i), w_direct).astype(BF16)
        turned = dot(w_turned, jnp.concatenate([att_norm[i], att_norm[i + 1]], axis=0), NT)
        for row in range(2):
            key[i + row] = keys[:, row * width : (row + 1) * width]
            mine = turned[:, row * cols : (row + 1) * cols]
            query_t[i + row] = mine[:width].astype(BF16)
            value_t[i + row] = mine[width : 2 * width].astype(BF16)
            gate_t[i + row] = sigmoid(mine[2 * width :])

    return project


def project_kernel(*refs):
    pipeline(range(0, refs[0].shape[0], 2), projector(*refs))


def whole_kernel(att_norm, w_query, w_key, w_value, w_att_gate, *refs):
    given, projected, held = refs[:4], refs[4:8], refs[8:]
    project = projector(att_norm, w_query, w_key, w_value, w_att_gate, *projected)
    attend_kernel(*projected, *given, *held, before=(project,))


def attend_kernel(
    query_t,
    key,
    value_t,
    gate_t,
    first_pass,
    bias,
    w_att_out,
    out,
    bias_t,
    scores,
    peaks,
    weights,
    gated,
    done,
    sems,
    before=(),
):
    rows, width, cols = query_t.shape
    head_rows = bias.shape[1] // HEADS
    score_scale = LOG2_E / HEAD_DIM**0.5
    ones = jnp.ones((16, key.shape[1]), BF16)
    heads = [
        (slice(h * HEAD_DIM, (h + 1) * HEAD_DIM), slice(h * cols, (h + 1) * cols)) for h in range(HEADS)
    ]

    def score(i):
        for row in (i, i + 1):
            blocks = []
            for mine, _ in heads:
                above = jnp.zeros((mine.start, cols), BF16)
                below = jnp.zeros((width - mine.stop, cols), BF16)
                parts = [p for p in (above, query_t[row, mine, :], below) if p.shape[0]]
                blocks.append(jnp.concatenate(parts, axis=0))
            raw = dot(key[row], jnp.concatenate(blocks, axis=1))
            for _, span in heads:
                biased = raw[:, span] * score_scale + bias_t[:, span]
                scores[row % 4, :, span] = biased
                peaks[row % 4, :, span] = jnp.max(biased, axis=0, keepdims=True)

    def soften(i):
        for row in (i, i + 1):
            for _, span in heads:
                lowered = scores[row % 4, :, span] - peaks[row % 4, :, span]
                weights[row % 4, :, span] = jnp.exp2(lowered).astype(BF16)

    def collect(i):
        for row in (i, i + 1):
            for head in range(0, HEADS, 2):
                (first, left), (second, right) = heads[head : head + 2]
                values = jnp.concatenate([value_t[row, first.start : second.stop, :], ones], axis=0)
                summed = dot(values, weights[row % 4, :, left.start : right.stop])
                share = 1.0 / summed[2 * HEAD_DIM : 2 * HEAD_DIM + 1]
                for mine, there, lanes in (
                    (first, slice(0, HEAD_DIM), slice(0, cols)),
                    (second, slice(HEAD_DIM, 2 * HEAD_DIM), slice(cols, 2 * cols)),
                ):
                    attended = summed[there, lanes] * share[:, lanes] * gate_t[row, mine, :]
                    gated[row % 4, mine, :] = attended.astype(BF16)

    def finish(i):
        turned = jnp.concatenate([gated[i % 4].T, gated[(i + 1) % 4].T], axis=1)
        both = dot(turned, w_last)
        done[i] = (first_pass[i] + both[:, :width]).astype(BF16)
        done[i + 1] = (first_pass[i + 1] + both[:, width:]).astype(BF16)
        copy = pltpu.make_async_copy(done.at[pl.ds(i, 2)], out.at[pl.ds(i, 2)], sems.at[i // 2])
        copy.start()
        copies.append(copy)

    copies = []
    w_last = twice(w_att_out[...])
    for head, (_, span) in enumerate(heads):
        parts = [
            bias[slot("bias", owner, bias.shape[0])].astype(F32)[head * head_rows : (head + 1) * head_rows]
            for owner in range(bias.shape[0])
        ]
        bias_t[:, span] = jnp.concatenate(parts, axis=0).T * LOG2_E
    pipeline(range(0, rows, 2), *before, score, soften, collect, finish)
    for copy in copies:
        copy.wait()


def call(kernel, outs, scratch, flops, *operands, fetched=0, sent=False):
    vmem = pl.BlockSpec(memory_space=pltpu.VMEM)
    far = pl.BlockSpec(memory_space=pltpu.HBM)
    shapes = [jax.ShapeDtypeStruct(shape, dtype) for shape, dtype in outs]
    moved = sum(o.size * o.dtype.itemsize for o in operands)
    operands = [
        pltpu.with_memory_space_constraint(o, pltpu.HBM) if n < fetched else o
        for n, o in enumerate(operands)
    ]
    got = pl.pallas_call(
        kernel,
        out_shape=shapes,
        in_specs=[far] * fetched + [vmem] * (len(operands) - fetched),
        out_specs=[far if sent else vmem] * len(shapes),
        scratch_shapes=[pltpu.VMEM(*s) if isinstance(s, tuple) else s for s in scratch],
        compiler_params=pltpu.CompilerParams(vmem_limit_bytes=48 * 2**20),
        cost_estimate=pl.CostEstimate(flops=flops, bytes_accessed=moved, transcendentals=0),
    )(*operands)
    return got if len(got) > 1 else got[0]


def body(
    pair_rep,
    w_left,
    w_left_gate,
    w_right,
    w_right_gate,
    w_tri_gate,
    w_tri_out,
    w_query,
    w_key,
    w_value,
    w_bias,
    w_att_gate,
    w_att_out,
):
    rows, cols, width = pair_rep.shape
    channels = w_left.shape[1]
    owners, col_parts = lax.axis_size("row"), lax.axis_size("col")
    own = channels // owners
    residues = owners * rows
    cells = rows * cols

    edges, gate, w_tri_out, w_query, w_key, w_value, w_att_gate, w_att_out, w_bias_t = call(
        edges_kernel,
        [
            ((owners, own * 2 * rows, cols), BF16),
            ((rows, cols, width), F32),
            *[(w.shape, BF16) for w in (w_tri_out, w_query, w_key, w_value, w_att_gate, w_att_out)],
            (w_bias.shape[::-1], BF16),
        ],
        [
            (pair_rep.shape, BF16),
            ((5, width, channels), BF16),
            (pair_rep.shape, BF16),
            ((cols // LANES, (channels + 1) * 2 * rows, LANES), F32),
            pltpu.SemaphoreType.DMA((13,)),
        ],
        10 * cells * width * channels,
        pair_rep,
        w_left,
        w_left_gate,
        w_right,
        w_right_gate,
        w_tri_gate,
        w_tri_out,
        w_query,
        w_key,
        w_value,
        w_att_gate,
        w_att_out,
        w_bias.T,
        fetched=13,
    )
    spread = swap("edges", edges)
    flops = 2 * own * residues * residues * cols
    if col_parts == 1:
        summed = call(
            functools.partial(triangle_kernel, rows),
            [((owners, own * rows, residues), BF16)],
            [],
            flops,
            spread,
        )
    else:
        partial_sums = call(
            functools.partial(partial_kernel, rows),
            [((own, residues, residues), F32)],
            [],
            flops,
            spread,
        )
        summed = lax.psum_scatter(partial_sums, "col", scatter_dimension=2, tiled=True).astype(BF16)
        summed = by_slot("triangle", summed.reshape(own, owners, rows, cols).swapaxes(0, 1))
        summed = summed.reshape(owners, own * rows, cols)
    returned = swap("triangle", summed)
    first_pass, att_norm, bias_copies = call(
        update_kernel,
        [
            ((rows, cols, width), F32),
            ((rows, cols, width), BF16),
            ((owners, HEADS * rows, cols), BF16),
        ],
        [
            ((cols // LANES, (channels + 1) * rows, LANES), F32),
            ((HEADS * rows, cols), F32),
            ((4, cols, channels), BF16),
        ],
        2 * cells * channels * width,
        returned,
        gate,
        pair_rep,
        w_tri_out,
        w_bias_t,
    )
    bias = swap("bias", bias_copies)
    projected = [
        ((rows, width, cols), BF16),
        ((rows, cols, width), BF16),
        ((rows, width, cols), BF16),
        ((rows, width, cols), F32),
    ]
    projecting = (att_norm, w_query, w_key, w_value, w_att_gate)
    residues = cols * col_parts
    out = [((rows, cols, width), BF16)]
    held = [
        ((residues, HEADS * cols), F32),
        ((4, residues, HEADS * cols), F32),
        ((4, 1, HEADS * cols), F32),
        ((4, residues, HEADS * cols), BF16),
        ((4, width, cols), BF16),
        ((rows, cols, width), BF16),
        pltpu.SemaphoreType.DMA((rows // 2,)),
    ]
    project_flops, attend_flops = 8 * cells * width * width, 4 * cells * residues * width
    if col_parts == 1:
        flops = project_flops + attend_flops
        given = (first_pass, bias, w_att_out)
        return call(whole_kernel, out, projected + held, flops, *projecting, *given, sent=True)
    query_t, key, value_t, gate_t = call(project_kernel, projected, [], project_flops, *projecting)
    bias = by_slot(
        "bias", lax.all_to_all(by_rank("bias", bias), "col", split_axis=0, concat_axis=2, tiled=True)
    )
    key = lax.all_gather(key, "col", axis=1, tiled=True)
    value_t = lax.all_gather(value_t, "col", axis=2, tiled=True)
    given = (query_t, key, value_t, gate_t, first_pass, bias, w_att_out)
    return call(attend_kernel, out, held, attend_flops, *given, sent=True)


def solution(mesh):
    in_specs = (P(("grp", "row"), "col", None),) + (P(),) * 12
    out_specs = P(("grp", "row"), "col", None)
    return jax.shard_map(body, mesh=mesh, in_specs=in_specs, out_specs=out_specs, check_vma=False)
```
